32 devices in a mesh: dp: 8 (over z, x), tensor: 4 (over y, core).
Axes of the slice: x: 2, y: 2, z: 4, core: 2. Of those that a mesh axis runs over, the one named last changes fastest.
Arguments:
- states_in: float32 [8192, 1536], P(('dp', 'tensor')), may hold values from -6 to 6
- documents: int32 [8192], P('dp'), may hold values from 0 to 2, as said below
- attnorm_one: float32 [1536], P('dp'), may hold values from 0.1 to 1.9
- query_one: float32 [1536, 1536], P('dp', 'tensor'), may hold values from -0.15625 to 0.15625
- key_one: float32 [1536, 768], P('dp', 'tensor'), may hold values from -0.15625 to 0.15625
- value_one: float32 [1536, 768], P('dp', 'tensor'), may hold values from -0.15625 to 0.15625
- output_one: float32 [1536, 1536], P('tensor', 'dp'), may hold values from -1.75 to 1.75
- mlpnorm_one: float32 [1536], P('dp'), may hold values from 0.1 to 1.9
- gate_one: float32 [1536, 4096], P('dp', 'tensor'), may hold values from -0.15625 to 0.15625
- up_one: float32 [1536, 4096], P('dp', 'tensor'), may hold values from -0.15625 to 0.15625
- down_one: float32 [4096, 1536], P('tensor', 'dp'), may hold values from -0.125 to 0.125
- attnorm_two: float32 [1536], P('dp'), may hold values from 0.1 to 1.9
- query_two: float32 [1536, 1536], P('dp', 'tensor'), may hold values from -0.15625 to 0.15625
- key_two: float32 [1536, 768], P('dp', 'tensor'), may hold values from -0.15625 to 0.15625
- value_two: float32 [1536, 768], P('dp', 'tensor'), may hold values from -0.15625 to 0.15625
- output_two: float32 [1536, 1536], P('tensor', 'dp'), may hold values from -1.75 to 1.75
- mlpnorm_two: float32 [1536], P('dp'), may hold values from 0.1 to 1.9
- gate_two: float32 [1536, 4096], P('dp', 'tensor'), may hold values from -0.15625 to 0.15625
- up_two: float32 [1536, 4096], P('dp', 'tensor'), may hold values from -0.15625 to 0.15625
- down_two: float32 [4096, 1536], P('tensor', 'dp'), may hold values from -0.09375 to 0.09375
- cotangent: float32 [8192, 1536], P(('dp', 'tensor')), may hold values from -6 to 6
Outputs:
- states_out: float32 [8192, 1536], P(('dp', 'tensor'))
- grad_input: float32 [8192, 1536], P(('dp', 'tensor'))
- dattnorm_one: float32 [1536], P('dp')
- dquery_one: float32 [1536, 1536], P('dp', 'tensor')
- dkey_one: float32 [1536, 768], P('dp', 'tensor')
- dvalue_one: float32 [1536, 768], P('dp', 'tensor')
- doutput_one: float32 [1536, 1536], P('tensor', 'dp')
- dmlpnorm_one: float32 [1536], P('dp')
- dgate_one: float32 [1536, 4096], P('dp', 'tensor')
- dup_one: float32 [1536, 4096], P('dp', 'tensor')
- ddown_one: float32 [4096, 1536], P('tensor', 'dp')
- dattnorm_two: float32 [1536], P('dp')
- dquery_two: float32 [1536, 1536], P('dp', 'tensor')
- dkey_two: float32 [1536, 768], P('dp', 'tensor')
- dvalue_two: float32 [1536, 768], P('dp', 'tensor')
- doutput_two: float32 [1536, 1536], P('tensor', 'dp')
- dmlpnorm_two: float32 [1536], P('dp')
- dgate_two: float32 [1536, 4096], P('dp', 'tensor')
- dup_two: float32 [1536, 4096], P('dp', 'tensor')
- ddown_two: float32 [4096, 1536], P('tensor', 'dp')
The draws below stay inside these ranges and needn't reach their ends.
Inputs may be any that keep to these rules, and one draw needn't show every extreme that they name: In each aligned run of 1024 tokens the document numbers are 0, 1, 2 in order, never falling; documents 0 and 2 each have 1 to 127 tokens.
All inputs are finite; a program needn't handle non-finite values.
Results may differ from the reference program's by a relative error of at most 0.035.
Values may be sent and summed in bfloat16 or wider, within the bound.
A program may use at most 256 MiB of HBM per device.

```python
import math
import jax
import jax.numpy as jnp
from jax import lax

D = 1536
HEADS = 16
KV_HEADS = 8
HEAD_DIM = 96
FF = 4096
LEN = 1024
BLOCK = 256
TOKENS = 8192


def draw_documents(key, part):
    groups = TOKENS // LEN
    key_head, key_tail = jax.random.split(key)
    head_len = jax.random.randint(key_head, (groups, 1), 1, LEN // 8, dtype=jnp.int32)
    tail_len = jax.random.randint(key_tail, (groups, 1), 1, LEN // 8, dtype=jnp.int32)
    places = jnp.arange(LEN, dtype=jnp.int32)[None, :]
    doc_ids = (places >= head_len).astype(jnp.int32) + (places >= LEN - tail_len).astype(jnp.int32)
    return doc_ids.reshape(TOKENS)


def raised(values, own_key, source, target, shards_of, factor):
    owner, partner = [(jnp.arange(values.shape[axis_at]) // (values.shape[axis_at] // shards_of)).reshape([-1 if axis == axis_at else 1 for axis in range(values.ndim)]) for axis_at in (source, target)]
    chosen = jax.random.permutation(own_key, shards_of)[partner]
    strong = (owner == chosen) | (owner == (partner + shards_of // 2) % shards_of)
    return jnp.where(strong, factor * values, values)


def levels(key, shape, pieces, smallest, top_value):
    loudness = 1.0
    for position, parts in pieces:
        heights = jax.random.uniform(jax.random.fold_in(jax.random.fold_in(key, 6), position), (parts,), jnp.float32, smallest / len(pieces), top_value / len(pieces))
        loudness = loudness * jnp.repeat(jnp.exp(heights), shape[position] // parts).reshape((-1,) + (1,) * (len(shape) - 1 - position))
    return loudness


def scatter_about(own_key, shape, width, most, shards=(), held_as=jnp.bfloat16):
    drawn = width * jax.random.normal(own_key, shape, jnp.float32)
    if shards:
        drawn = drawn * levels(own_key, shape, shards, -0.22, 0.18)
    return jnp.clip(drawn, -most, most).astype(held_as)


def heavy_noise(stream_key, extent, width, reach, shards, heavy, held_as=jnp.bfloat16):
    array = width * jax.random.normal(stream_key, extent, jnp.float32)
    if shards:
        array = array * levels(stream_key, extent, shards, -0.22, 0.18)
    return jnp.clip(raised(array, jax.random.fold_in(stream_key, 3), *heavy), -reach, reach).astype(held_as)


def setup_inputs(seed: int = 0) -> dict:
    key_list = jax.random.split(jax.random.key(seed), 22)
    return {
        "states_in": heavy_noise(key_list[0], (TOKENS, D), 1.0, 6.0, ((0, 32),), (0, 1, 32, 2.75), jnp.float32),
        "documents": draw_documents(jax.random.fold_in(key_list[21], 71), 0),
        "attnorm_one": jnp.clip(1.0 + 0.18 * jax.random.normal(key_list[2], (D,), jnp.float32), 0.1, 1.9),
        "query_one": scatter_about(key_list[3], (D, HEADS * HEAD_DIM), D ** -0.5, 0.15625, ((0, 8), (1, 4)), jnp.float32),
        "key_one": scatter_about(key_list[4], (D, KV_HEADS * HEAD_DIM), D ** -0.5, 0.15625, ((0, 8), (1, 4)), jnp.float32),
        "value_one": scatter_about(key_list[5], (D, KV_HEADS * HEAD_DIM), D ** -0.5, 0.15625, ((0, 8), (1, 4)), jnp.float32),
        "output_one": scatter_about(key_list[6], (HEADS * HEAD_DIM, D), (max(4, HEADS * HEAD_DIM // 128)) ** -0.5, 1.75, ((0, 4), (1, 8)), jnp.float32),
        "mlpnorm_one": jnp.clip(1.0 + 0.18 * jax.random.normal(key_list[7], (D,), jnp.float32), 0.1, 1.9),
        "gate_one": scatter_about(key_list[8], (D, FF), D ** -0.5, 0.15625, ((0, 8), (1, 4)), jnp.float32),
        "up_one": scatter_about(key_list[9], (D, FF), D ** -0.5, 0.15625, ((0, 8), (1, 4)), jnp.float32),
        "down_one": heavy_noise(key_list[10], (FF, D), FF ** -0.5, 0.125, ((0, 4), (1, 8)), (0, 1, 8, 2.0), jnp.float32),
        "attnorm_two": jnp.clip(1.0 + 0.18 * jax.random.normal(key_list[11], (D,), jnp.float32), 0.1, 1.9),
        "query_two": scatter_about(key_list[12], (D, HEADS * HEAD_DIM), D ** -0.5, 0.15625, ((0, 8), (1, 4)), jnp.float32),
        "key_two": scatter_about(key_list[13], (D, KV_HEADS * HEAD_DIM), D ** -0.5, 0.15625, ((0, 8), (1, 4)), jnp.float32),
        "value_two": scatter_about(key_list[14], (D, KV_HEADS * HEAD_DIM), D ** -0.5, 0.15625, ((0, 8), (1, 4)), jnp.float32),
        "output_two": scatter_about(key_list[15], (HEADS * HEAD_DIM, D), (max(4, HEADS * HEAD_DIM // 128)) ** -0.5, 1.75, ((0, 4), (1, 8)), jnp.float32),
        "mlpnorm_two": jnp.clip(1.0 + 0.18 * jax.random.normal(key_list[16], (D,), jnp.float32), 0.1, 1.9),
        "gate_two": scatter_about(key_list[17], (D, FF), D ** -0.5, 0.15625, ((0, 8), (1, 4)), jnp.float32),
        "up_two": scatter_about(key_list[18], (D, FF), D ** -0.5, 0.15625, ((0, 8), (1, 4)), jnp.float32),
        "down_two": scatter_about(key_list[19], (FF, D), FF ** -0.5, 0.09375, ((0, 4), (1, 8)), jnp.float32),
        "cotangent": heavy_noise(key_list[20], (TOKENS, D), 1.0, 6.0, ((0, 32),), (0, 1, 32, 2.75), jnp.float32),
    }


@jax.custom_vjp
def low(v):
    return lax.optimization_barrier(v.astype(jnp.bfloat16)).astype(jnp.float32)

@jax.custom_vjp
def low_back(v):
    return v

def low_keep(v):
    return (low(v), None)

def low_pass(kept, grad):
    return (grad,)

def back_keep(v):
    return (v, None)

def back_low(kept, grad):
    return (low(grad),)
low.defvjp(low_keep, low_pass)
low_back.defvjp(back_keep, back_low)
highest = lax.Precision.HIGHEST
epsilon = 1e-05
rope_base = 100000.0
masked_value = -1e+30

def matmul(left, right):
    return jnp.dot(left, right, precision=highest, preferred_element_type=jnp.float32)

def layout(documents):
    length = documents.shape[0]
    places = jnp.arange(length, dtype=jnp.int32)
    change = jnp.concatenate([jnp.ones((1,), dtype=jnp.bool_), documents[1:] != documents[:-1]])
    starts = lax.cummax(jnp.where(change, places, 0), axis=0)
    offset = places - starts
    blocks = offset // BLOCK
    allowed = (documents[:, None] == documents[None, :]) & (blocks[None, :] <= blocks[:, None])
    half_dim = HEAD_DIM // 2
    freqs = jnp.exp(jnp.arange(half_dim, dtype=jnp.float32) * (-2.0 * math.log(rope_base) / HEAD_DIM))
    angles = offset.astype(jnp.float32)[:, None] * freqs[None, :]
    return (allowed, jnp.cos(angles), jnp.sin(angles))

def rotate(values, cosine, sine):
    half_dim = values.shape[-1] // 2
    front_half = values[..., :half_dim]
    back_half = values[..., half_dim:]
    cos_b = cosine[:, None, :]
    sin_b = sine[:, None, :]
    return jnp.concatenate([front_half * cos_b - back_half * sin_b, back_half * cos_b + front_half * sin_b], axis=-1)

def normalize(values):
    return values * lax.rsqrt(lax.optimization_barrier(jnp.mean(values * values, axis=-1, keepdims=True)) + epsilon)

def layer(states, weights, allowed, cosine, sine):
    gain_attn, w_query, w_key, w_value, w_output, gain_mlp, w_gate, w_up, w_down = [low(item) for item in weights]
    length = states.shape[0]
    group = HEADS // KV_HEADS
    normed = low(normalize(states) * gain_attn)
    q_lin = low_back(matmul(normed, w_query))
    k_lin = low_back(matmul(normed, w_key))
    v_lin = low_back(matmul(normed, w_value))
    queries = low(rotate(q_lin.reshape(length, HEADS, HEAD_DIM), cosine, sine))
    keys = low(rotate(k_lin.reshape(length, KV_HEADS, HEAD_DIM), cosine, sine))
    values = low(v_lin.reshape(length, KV_HEADS, HEAD_DIM))
    queries = queries.reshape(length, KV_HEADS, group, HEAD_DIM)
    scores = low_back(jnp.einsum('qngd,knd->ngqk', queries, keys, precision=highest) / math.sqrt(HEAD_DIM))
    scores = jnp.where(allowed[None, None], scores, masked_value)
    row_max = lax.optimization_barrier(jnp.max(scores, axis=-1, keepdims=True))
    exponent = jnp.exp(scores - row_max)
    probs = low(exponent / lax.optimization_barrier(jnp.sum(exponent, axis=-1, keepdims=True)))
    mixed = low(low_back(jnp.einsum('ngqk,knd->qngd', probs, values, precision=highest)))
    attended = low_back(matmul(mixed.reshape(length, HEADS * HEAD_DIM), w_output))
    middle = states + attended
    normed_mlp = low(normalize(middle) * gain_mlp)
    gate_pre = low_back(matmul(normed_mlp, w_gate))
    up_pre = low_back(matmul(normed_mlp, w_up))
    hidden = low(jax.nn.silu(gate_pre) * up_pre)
    return middle + low_back(matmul(hidden, w_down))

def run_group(states, documents, weights_one, weights_two):
    allowed, cosine, sine = layout(documents)
    between = layer(states, weights_one, allowed, cosine, sine)
    return layer(between, weights_two, allowed, cosine, sine)

def reference(states_in, documents, attnorm_one, query_one, key_one, value_one, output_one, mlpnorm_one, gate_one, up_one, down_one, attnorm_two, query_two, key_two, value_two, output_two, mlpnorm_two, gate_two, up_two, down_two, cotangent):
    groups = TOKENS // LEN
    doc_groups = documents.reshape(groups, LEN)

    def whole(states, weights_one, weights_two):

        def one_group(inputs_pair):
            return run_group(inputs_pair[0], inputs_pair[1], weights_one, weights_two)
        mapped = lax.map(jax.checkpoint(one_group), (states.reshape(groups, LEN, D), doc_groups))
        return mapped.reshape(TOKENS, D)
    weights_one = (attnorm_one, query_one, key_one, value_one, output_one, mlpnorm_one, gate_one, up_one, down_one)
    weights_two = (attnorm_two, query_two, key_two, value_two, output_two, mlpnorm_two, gate_two, up_two, down_two)
    result, pull = jax.vjp(whole, states_in, weights_one, weights_two)
    grad_states, grads_one, grads_two = pull(cotangent)
    return (result, grad_states, grads_one[0], grads_one[1], grads_one[2], grads_one[3], grads_one[4], grads_one[5], grads_one[6], grads_one[7], grads_one[8], grads_two[0], grads_two[1], grads_two[2], grads_two[3], grads_two[4], grads_two[5], grads_two[6], grads_two[7], grads_two[8])
```

```python
import functools
import math

import jax
import jax.numpy as jnp
import numpy as np
from jax import lax
from jax.experimental import pallas as pl
from jax.experimental.pallas import tpu as pltpu
from jax.sharding import PartitionSpec as P

HEAD_DIM = 96
HALF = HEAD_DIM // 2
BLOCK = 256
PAD = 128
GAIN_ROWS = 16
LIMIT = 60 * 1024 * 1024

epsilon = 1e-05
rope_base = 100000.0
masked_value = -1e30
scale = 1.0 / math.sqrt(HEAD_DIM)

BF = jnp.bfloat16
F32 = jnp.float32
MESH = pl.DeviceIdType.MESH
ANY = pl.BlockSpec(memory_space=pl.ANY)
VM = pl.BlockSpec(memory_space=pltpu.VMEM)


def nn(left, right):
    return lax.dot_general(left, right, (((1,), (0,)), ((), ())), preferred_element_type=F32)


def nt(left, right):
    return lax.dot_general(left, right, (((1,), (1,)), ((), ())), preferred_element_type=F32)


def tn(left, right):
    return lax.dot_general(left, right, (((0,), (0,)), ((), ())), preferred_element_type=F32)


def tile(index, size):
    return pl.ds(pl.multiple_of(index * size, size), size)


def each(count, body):
    def step(index, carry):
        body(index)
        return carry

    lax.fori_loop(0, count, step, 0)


class Group:
    def __init__(self):
        self.me = lax.axis_index("tensor")
        self.core_bit = lax.rem(self.me, 2)
        self.chip = self.me // 2
        self.core = self.me + 1 - 2 * self.core_bit
        self.other = lax.rem(self.me + 2, 4)

    def greet(self):
        barrier = pltpu.get_barrier_semaphore()
        for near in (self.core, self.other):
            pl.semaphore_signal(barrier, inc=1, device_id={"tensor": near}, device_id_type=MESH)
        pl.semaphore_wait(barrier, 2)

    def remote(self, source, target, send, recv, device):
        return pltpu.make_async_remote_copy(
            src_ref=source,
            dst_ref=target,
            send_sem=send,
            recv_sem=recv,
            device_id={"tensor": device},
            device_id_type=MESH,
        )


class Gather:
    def __init__(self, group, full, send, recv):
        self.group, self.full, self.send, self.recv = group, full, send, recv
        half = full.shape[1] // 2
        mine = full.at[group.me]
        self.to_core = group.remote(mine, mine, send.at[0], recv.at[0], group.core)
        self.to_other = []
        self.onward = []
        for part in range(2):
            piece = full.at[group.me, pl.ds(part * half, half)]
            self.to_other.append(
                group.remote(piece, piece, send.at[1 + part], recv.at[1 + part], group.other)
            )
            piece = full.at[group.other, pl.ds(part * half, half)]
            self.onward.append(
                group.remote(piece, piece, send.at[3 + part], recv.at[3 + part], group.core)
            )

    def start(self):
        for copy in self.to_other:
            copy.start()
        self.to_core.start()

    def wait_chip(self):
        self.to_core.wait_recv()

    def forward(self):
        for here, there in zip(self.to_other, self.onward):
            here.wait_recv()
            there.start()

    def wait_other(self):
        for copy in self.onward:
            copy.wait_recv()

    def finish(self):
        self.to_core.wait_send()
        for copy in self.to_other + self.onward:
            copy.wait_send()


class Scatter:
    def __init__(self, group, parts, near, away, landed, send, recv):
        self.group, self.parts, self.near = group, parts, near
        self.away, self.landed = away, landed
        self.to_core = [
            group.remote(
                parts.at[turn, 1 - group.core_bit], near.at[turn], send.at[turn], recv.at[turn], group.core
            )
            for turn in range(2)
        ]
        half = away.shape[0] // 2
        self.to_other = [
            group.remote(
                away.at[pl.ds(part * half, half)],
                landed.at[pl.ds(part * half, half)],
                send.at[2 + part],
                recv.at[2 + part],
                group.other,
            )
            for part in range(2)
        ]

    def rows_of(self, turn):
        return 1 - self.group.chip if turn == 0 else self.group.chip

    def send_core(self, turn):
        self.to_core[turn].start()

    def send_away(self):
        self.to_core[0].wait_recv()
        half = self.away.shape[0] // 2
        for part in range(2):

            def add(index):
                rows = pl.ds(pl.multiple_of(part * half + index * 32, 32), 32)
                total = self.parts[0, self.group.core_bit, rows, :].astype(F32) + self.near[
                    0, rows, :
                ].astype(F32)
                self.away[rows, :] = total.astype(BF)

            each(half // 32, add)
            self.to_other[part].start()

    def wait(self):
        self.to_core[1].wait_recv()
        for copy in self.to_other:
            copy.wait_recv()

    def total(self, rows):
        return (
            self.parts[1, self.group.core_bit, rows, :].astype(F32)
            + self.near[1, rows, :].astype(F32)
            + self.landed[rows, :].astype(F32)
        )

    def finish(self):
        for copy in self.to_core + self.to_other:
            copy.wait_send()


def comm_scratch(rows, width):
    return [
        pltpu.VMEM((4, rows, width), BF),
        pltpu.VMEM((2, 2, rows, width), BF),
        pltpu.VMEM((2, rows, width), BF),
        pltpu.VMEM((rows, width), BF),
        pltpu.VMEM((rows, width), BF),
        pltpu.SemaphoreType.DMA((5,)),
        pltpu.SemaphoreType.DMA((5,)),
        pltpu.SemaphoreType.DMA((4,)),
        pltpu.SemaphoreType.DMA((4,)),
    ]


def source_block(index, n_dp):
    mine = lax.axis_index("dp")
    high, low = mine // 2, lax.rem(mine, 2)
    shift, side = index // 2, lax.rem(index, 2)
    count = n_dp // 2
    return lax.rem(high + count - shift, count) * 2 + lax.rem(low + side, 2)


def target_block(index, n_dp):
    mine = lax.axis_index("dp")
    high, low = mine // 2, lax.rem(mine, 2)
    shift, side = index // 2, lax.rem(index, 2)
    count = n_dp // 2
    return lax.rem(high + shift, count) * 2 + lax.rem(low + side, 2)


class Weights:
    def __init__(self, shards, held, sems, low_gains=None, gain_sems=None):
        n_dp = len(shards)
        depth = held.shape[0] // n_dp
        self.copies = []
        for index, shard in enumerate(shards):
            block = source_block(index, n_dp)
            rows = pl.ds(pl.multiple_of(block * depth, GAIN_ROWS), depth)
            self.copies.append(
                pltpu.make_async_copy(shard.at[pl.ds(0, depth)], held.at[rows], sems.at[index])
            )
            if low_gains is not None:
                self.copies.append(
                    pltpu.make_async_copy(
                        shard.at[pl.ds(depth, GAIN_ROWS), pl.ds(0, low_gains.shape[2])],
                        low_gains.at[block],
                        gain_sems.at[index],
                    )
                )

    def start(self):
        for copy in self.copies:
            copy.start()

    def wait(self):
        for copy in self.copies:
            copy.wait()


def spread(block, depth, lanes, width):
    row = lax.broadcasted_iota(jnp.int32, (lanes, width), 0)
    column = lax.broadcasted_iota(jnp.int32, (lanes, width), 1)
    hit = (column - row == block * depth) & (row < depth)
    return jnp.where(hit, 1.0, 0.0).astype(BF)


def turn_half(values):
    return pltpu.roll(values, PAD // 2, 1)


def out_columns(group, scatter, turn, left_rows, right_tile, columns):
    product = nt(left_rows, right_tile)
    rows = product.shape[0] // 2
    scatter.parts[turn, 0, :, columns] = product[:rows].astype(BF)
    scatter.parts[turn, 1, :, columns] = product[rows:].astype(BF)


def attn_forward_kernel(n_dp, depth, *refs):
    x_ref, cos_ref, sin_ref, span_ref, place_ref = refs[:5]
    shards = refs[5 : 5 + n_dp]
    refs = refs[5 + n_dp :]
    mid_ref, gains_ref, a_out, qkv_out, o_out = refs[:5]
    p_outs = refs[5:9]
    (full, parts, near, away, landed, g_send, g_recv, s_send, s_recv) = refs[9:18]
    (held, low_gains, padded, qkv, mixed, compact, p0, p1, p2, p3, w_sems, gain_sems, out_sems) = refs[18:]
    probs = (p0, p1, p2, p3)
    rows, width = x_ref.shape
    length = 4 * rows
    group = Group()
    weights = Weights(shards, held, w_sems, low_gains, gain_sems)
    weights.start()
    weights.wait()
    gains_ref[...] = jnp.zeros_like(gains_ref)

    def gather_gain(block):
        gains_ref[...] += nn(
            low_gains[block], spread(block, depth, low_gains.shape[2], width)
        )

    each(n_dp, gather_gain)
    gather = Gather(group, full, g_send, g_recv)
    scatter = Scatter(group, parts, near, away, landed, s_send, s_recv)
    gain = gains_ref[0:1, :]

    def norm(index):
        part = tile(index, 32)
        values = x_ref[part, :]
        factor = lax.rsqrt(jnp.mean(values * values, axis=-1, keepdims=True) + epsilon)
        full[group.me, part, :] = (values * factor * gain).astype(BF)

    each(rows // 32, norm)
    group.greet()
    gather.start()
    place = place_ref[...]
    heads = place.shape[1] // PAD
    compact_width = place.shape[0]
    head_width = place.shape[1]

    def pad(index):
        part = tile(index, 256)
        padded[part, 0:head_width] = nn(held[part, 0:compact_width], place).astype(BF)
        padded[part, head_width : 2 * head_width] = nn(
            held[part, compact_width : 2 * compact_width], place
        ).astype(BF)

    each(width // 256, pad)

    def project(chip):
        left = full[pl.ds(2 * chip, 2)].reshape(2 * rows, width)
        where = tile(chip, 2 * rows)
        cosine, sine = cos_ref[where, :], sin_ref[where, :]

        def turned(index):
            columns = tile(index, 2 * PAD)
            product = nn(left, padded[:, columns])
            for half in range(2):
                u = product[:, half * PAD : (half + 1) * PAD]
                qkv[where, tile(2 * index + half, PAD)] = (u * cosine + turn_half(u) * sine).astype(BF)

        each(3 * heads // 4, turned)
        columns = pl.ds(3 * heads // 2 * PAD, heads // 2 * PAD)
        qkv[where, columns] = nn(left, padded[:, columns]).astype(BF)

    gather.wait_chip()
    project(group.chip)
    gather.forward()
    gather.wait_other()
    project(1 - group.chip)
    copies = [
        pltpu.make_async_copy(full, a_out, out_sems.at[0]),
        pltpu.make_async_copy(qkv, qkv_out, out_sems.at[1]),
    ]
    for copy in copies:
        copy.start()
    kv_at = heads * PAD
    value_at = kv_at + heads // 2 * PAD
    for turn, prob in enumerate(probs):
        reach = prob.shape[2]
        where = pl.ds(turn * rows, rows)

        def attend(head):
            query = qkv[where, tile(head, PAD)]
            key = qkv[0:reach, pl.ds(pl.multiple_of(kv_at + head // 2 * PAD, PAD), PAD)]
            value = qkv[0:reach, pl.ds(pl.multiple_of(value_at + head // 2 * PAD, PAD), PAD)]
            scores = nt(query, key) * scale
            place_of = lax.broadcasted_iota(jnp.int32, scores.shape, 1)
            first = span_ref[where, 0:1]
            last = span_ref[where, 1:2]
            scores = jnp.where((place_of >= first) & (place_of < last), scores, masked_value)
            exponent = jnp.exp(scores - jnp.max(scores, axis=-1, keepdims=True))
            summed = jnp.sum(exponent, axis=-1, keepdims=True)
            low = (exponent * (1.0 / summed)).astype(BF)
            prob[head] = low
            mixed[where, tile(head, PAD)] = nn(low, value).astype(BF)

        each(heads, attend)
        copy = pltpu.make_async_copy(prob, p_outs[turn], out_sems.at[2 + turn])
        copy.start()
        copies.append(copy)
        compact[where, :] = nt(mixed[where, :], place).astype(BF)
    copy = pltpu.make_async_copy(compact, o_out, out_sems.at[6])
    copy.start()
    copies.append(copy)
    for turn in range(2):
        left = compact[tile(scatter.rows_of(turn), 2 * rows), :]

        def part_of(index):
            columns = tile(index, 256)
            out_columns(group, scatter, turn, left, held[columns, 2 * compact_width :], columns)

        each(width // 256, part_of)
        scatter.send_core(turn)
        if turn == 0:
            scatter.send_away()
    scatter.wait()

    def close(index):
        part = tile(index, 32)
        mid_ref[part, :] = x_ref[part, :] + scatter.total(part)

    each(rows // 32, close)
    gather.finish()
    scatter.finish()
    for copy in copies:
        copy.wait()


def mlp_forward_kernel(n_dp, *refs):
    mid_ref, gains_ref = refs[:2]
    shards = refs[2 : 2 + n_dp]
    refs = refs[2 + n_dp :]
    y_ref, m_out, gu_out, hid_out = refs[:4]
    (full, parts, near, away, landed, g_send, g_recv, s_send, s_recv) = refs[4:13]
    held, gu, hid, w_sems, out_sems = refs[13:]
    rows, width = mid_ref.shape
    units = hid.shape[1]
    group = Group()
    weights = Weights(shards, held, w_sems)
    weights.start()
    gather = Gather(group, full, g_send, g_recv)
    scatter = Scatter(group, parts, near, away, landed, s_send, s_recv)
    gain = gains_ref[1:2, :]

    def norm(index):
        part = tile(index, 32)
        values = mid_ref[part, :]
        factor = lax.rsqrt(jnp.mean(values * values, axis=-1, keepdims=True) + epsilon)
        full[group.me, part, :] = (values * factor * gain).astype(BF)

    each(rows // 32, norm)
    group.greet()
    gather.start()
    weights.wait()

    def expand(chip):
        left = full[pl.ds(2 * chip, 2)].reshape(2 * rows, width)
        where = tile(chip, 2 * rows)

        def unit(index):
            columns = tile(index, 256)
            further = pl.ds(pl.multiple_of(units + index * 256, 256), 256)
            gate = nn(left, held[:, columns])
            up = nn(left, held[:, further])
            hid[where, columns] = (gate / (1.0 + jnp.exp(-gate)) * up).astype(BF)
            gu[where, columns] = gate.astype(BF)
            gu[where, further] = up.astype(BF)

        each(units // 256, unit)

    gather.wait_chip()
    expand(group.chip)
    gather.forward()
    gather.wait_other()
    expand(1 - group.chip)
    copies = [
        pltpu.make_async_copy(full, m_out, out_sems.at[0]),
        pltpu.make_async_copy(gu, gu_out, out_sems.at[1]),
        pltpu.make_async_copy(hid, hid_out, out_sems.at[2]),
    ]
    for copy in copies:
        copy.start()
    for turn in range(2):
        left = hid[tile(scatter.rows_of(turn), 2 * rows), :]

        def part_of(index):
            columns = tile(index, 256)
            out_columns(group, scatter, turn, left, held[columns, 2 * units :], columns)

        each(width // 256, part_of)
        scatter.send_core(turn)
        if turn == 0:
            scatter.send_away()
    scatter.wait()

    def close(index):
        part = tile(index, 32)
        y_ref[part, :] = mid_ref[part, :] + scatter.total(part)

    each(rows // 32, close)
    gather.finish()
    scatter.finish()
    for copy in copies:
        copy.wait()


def flip(source, target, slot, rows, width):
    def block(index):
        columns = tile(index, 256)
        target[columns, slot * rows : (slot + 1) * rows] = source[slot, :, columns].T

    each(width // 256, block)


def close_back(scatter, grad_ref, state_ref, gain, grad_out, dgain):
    rows = state_ref.shape[0]
    dgain[...] = jnp.zeros_like(dgain)

    def close(index):
        part = tile(index, 32)
        values = state_ref[part, :]
        factor = lax.rsqrt(jnp.mean(values * values, axis=-1, keepdims=True) + epsilon)
        normed = values * factor
        grad_in = scatter.total(part)
        dgain[...] += jnp.sum((grad_in * normed).reshape(4, 8, -1), axis=0)
        grad_norm = grad_in * gain
        inner = jnp.mean(grad_norm * normed, axis=-1, keepdims=True)
        grad_out[part, :] = grad_ref[part, :] + factor * (grad_norm - normed * inner)

    each(rows // 32, close)


def mlp_backward_kernel(n_dp, depth, *refs):
    grad_ref, mid_ref, gains_ref, m_in, gu_in, hid_in = refs[:6]
    shards = refs[6 : 6 + n_dp]
    refs = refs[6 + n_dp :]
    out_ref, dgain_ref = refs[:2]
    g_outs = refs[2 : 2 + n_dp]
    refs = refs[2 + n_dp :]
    (full, parts, near, away, landed, g_send, g_recv, s_send, s_recv) = refs[:9]
    held, m_full, flipped, gu, hid, grad_gu, grads, w_sems, in_sems, out_sems = refs[9:]
    rows, width = mid_ref.shape
    units = hid.shape[1]
    group = Group()
    weights = Weights(shards, held, w_sems)
    fetches = [
        pltpu.make_async_copy(m_in, m_full, in_sems.at[0]),
        pltpu.make_async_copy(gu_in, gu, in_sems.at[1]),
        pltpu.make_async_copy(hid_in, hid, in_sems.at[2]),
    ]
    gather = Gather(group, full, g_send, g_recv)
    scatter = Scatter(group, parts, near, away, landed, s_send, s_recv)
    fetches[0].start()
    weights.start()
    fetches[1].start()
    fetches[2].start()
    full[group.me] = grad_ref[...].astype(BF)
    group.greet()
    gather.start()
    fetches[0].wait()
    for slot in range(4):
        flip(m_full, flipped, slot, rows, width)
    weights.wait()
    for copy in fetches[1:]:
        copy.wait()

    def inward(chip):
        left = full[pl.ds(2 * chip, 2)].reshape(2 * rows, width)
        where = tile(chip, 2 * rows)

        def unit(index):
            columns = tile(index, 256)
            further = pl.ds(pl.multiple_of(units + index * 256, 256), 256)
            last = pl.ds(pl.multiple_of(2 * units + index * 256, 256), 256)
            grad = nn(left, held[:, last])
            gate = gu[where, columns].astype(F32)
            up = gu[where, further].astype(F32)
            sig = 1.0 / (1.0 + jnp.exp(-gate))
            grad_gu[where, columns] = (grad * up * sig * (1.0 + gate * (1.0 - sig))).astype(BF)
            grad_gu[where, further] = (grad * gate * sig).astype(BF)

        each(units // 256, unit)

    gather.wait_chip()
    inward(group.chip)
    gather.forward()
    gather.wait_other()
    inward(1 - group.chip)
    for turn in range(2):
        where = tile(scatter.rows_of(turn), 2 * rows)

        def part_of(index):
            columns = tile(index, 256)
            out_columns(group, scatter, turn, grad_gu[where, :], held[columns, 0 : 2 * units], columns)

        each(width // 256, part_of)
        scatter.send_core(turn)
        if turn == 0:
            scatter.send_away()
    def grad_of(order, first, count, right):
        block = target_block(order, n_dp)
        left = flipped[pl.ds(pl.multiple_of(block * depth, GAIN_ROWS), depth), :]

        def some(index):
            columns = pl.ds(pl.multiple_of(first + index * 512, 512), 512)
            grads[order, :, columns] = nn(left, right[:, tile(index, 512)]).astype(BF)

        each(count // 512, some)

    each(n_dp, lambda order: grad_of(order, 0, 2 * units, grad_gu))
    for slot in range(4):
        flip(full, flipped, slot, rows, width)
    each(n_dp, lambda order: grad_of(order, 2 * units, units, hid))
    copies = []
    for order in range(n_dp):
        copy = pltpu.make_async_copy(grads.at[order], g_outs[order], out_sems.at[order])
        copy.start()
        copies.append(copy)
    scatter.wait()
    close_back(scatter, grad_ref, mid_ref, gains_ref[1:2, :], out_ref, dgain_ref)
    gather.finish()
    scatter.finish()
    for copy in copies:
        copy.wait()


def attn_backward_kernel(n_dp, depth, *refs):
    grad_ref, x_ref, gains_ref, dmlp_ref, cos_ref, sin_ref, place_ref, a_in, qkv_in, o_in = refs[:10]
    p_ins = refs[10:14]
    shards = refs[14 : 14 + n_dp]
    refs = refs[14 + n_dp :]
    out_ref = refs[0]
    g_outs = refs[1 : 1 + n_dp]
    refs = refs[1 + n_dp :]
    (full, parts, near, away, landed, g_send, g_recv, s_send, s_recv) = refs[:9]
    held, a_full, flipped, qkv, compact, p0, p1, p2, p3 = refs[9:18]
    (grad_mixed, grad_q, grad_kv, grad_k, grad_v, grad_low, grads, dgain, w_sems, in_sems, out_sems) = refs[18:]
    probs = (p0, p1, p2, p3)
    rows, width = x_ref.shape
    length = 4 * rows
    group = Group()
    weights = Weights(shards, held, w_sems)
    fetches = [
        pltpu.make_async_copy(a_in, a_full, in_sems.at[0]),
        pltpu.make_async_copy(qkv_in, qkv, in_sems.at[1]),
        pltpu.make_async_copy(o_in, compact, in_sems.at[2]),
    ] + [pltpu.make_async_copy(p_ins[i], probs[i], in_sems.at[3 + i]) for i in range(4)]
    gather = Gather(group, full, g_send, g_recv)
    scatter = Scatter(group, parts, near, away, landed, s_send, s_recv)
    fetches[0].start()
    weights.start()
    for copy in fetches[1:]:
        copy.start()
    full[group.me] = grad_ref[...].astype(BF)
    group.greet()
    gather.start()
    fetches[0].wait()
    for slot in range(4):
        flip(a_full, flipped, slot, rows, width)
    weights.wait()
    for copy in fetches[1:]:
        copy.wait()
    place = place_ref[...]
    heads = place.shape[1] // PAD
    compact_width = place.shape[0]
    head_width = place.shape[1]

    def inward(chip):
        left = full[pl.ds(2 * chip, 2)].reshape(2 * rows, width)
        where = tile(chip, 2 * rows)
        grad = nn(left, held[:, 2 * compact_width :]).astype(BF)
        grad_mixed[where, :] = nn(grad, place).astype(BF)

    gather.wait_chip()
    inward(group.chip)
    gather.forward()
    gather.wait_other()
    inward(1 - group.chip)
    kv_at = heads * PAD
    value_at = kv_at + heads // 2 * PAD
    grad_k[...] = jnp.zeros_like(grad_k)
    grad_v[...] = jnp.zeros_like(grad_v)
    for turn, prob in enumerate(probs):
        reach = prob.shape[2]
        where = pl.ds(turn * rows, rows)
        cosine, sine = cos_ref[where, :], sin_ref[where, :]

        def attend(head):
            mine = tile(head, PAD)
            shared = tile(head // 2, PAD)
            query = qkv[where, mine]
            key = qkv[0:reach, pl.ds(pl.multiple_of(kv_at + head // 2 * PAD, PAD), PAD)]
            value = qkv[0:reach, pl.ds(pl.multiple_of(value_at + head // 2 * PAD, PAD), PAD)]
            grad = grad_mixed[where, mine]
            low = prob[head]
            grad_prob = nt(grad, value)
            weight = low.astype(F32)
            inner = jnp.sum(weight * grad_prob, axis=-1, keepdims=True)
            grad_score = (weight * (grad_prob - inner)).astype(BF)
            u = nn(grad_score, key) * scale
            grad_q[where, mine] = (u * cosine - turn_half(u) * sine).astype(BF)
            grad_k[0:reach, shared] += tn(grad_score, query)
            grad_v[0:reach, shared] += tn(low, grad)

        each(heads, attend)
    for pair in range(heads // 2):
        columns = pl.ds(pair * PAD, PAD)
        u = grad_k[:, columns] * scale
        grad_kv[:, columns] = (u * cos_ref[...] - turn_half(u) * sin_ref[...]).astype(BF)
        grad_kv[:, pl.ds((heads // 2 + pair) * PAD, PAD)] = grad_v[:, columns].astype(BF)
    grad_low[:, 0:compact_width] = nt(grad_q[...], place).astype(BF)
    grad_low[:, compact_width : 2 * compact_width] = nt(grad_kv[...], place).astype(BF)
    for turn in range(2):
        where = tile(scatter.rows_of(turn), 2 * rows)

        def part_of(index):
            columns = tile(index, 256)
            out_columns(
                group, scatter, turn, grad_low[where, :], held[columns, 0 : 2 * compact_width], columns
            )

        each(width // 256, part_of)
        scatter.send_core(turn)
        if turn == 0:
            scatter.send_away()

    def grad_of(order, first, right):
        block = target_block(order, n_dp)
        left = flipped[pl.ds(pl.multiple_of(block * depth, GAIN_ROWS), depth), :]
        grads[order, 0:depth, first : first + right.shape[1]] = nn(left, right[...]).astype(BF)

    each(n_dp, lambda order: grad_of(order, 0, grad_low))
    for slot in range(4):
        flip(full, flipped, slot, rows, width)
    each(n_dp, lambda order: grad_of(order, 2 * compact_width, compact))
    scatter.wait()
    close_back(scatter, grad_ref, x_ref, gains_ref[0:1, :], out_ref, dgain)
    both = jnp.concatenate(
        [
            jnp.sum(dgain[...], axis=0, keepdims=True),
            jnp.sum(dmlp_ref[...], axis=0, keepdims=True),
            jnp.zeros((GAIN_ROWS - 2, width), F32),
        ],
        axis=0,
    ).astype(BF)

    def gain_rows(order):
        lanes = 256
        chosen = spread(target_block(order, n_dp), depth, lanes, width)
        grads[order, depth : depth + GAIN_ROWS, 0:lanes] = nt(both, chosen).astype(BF)
        grads[order, depth : depth + GAIN_ROWS, lanes:] = jnp.zeros(
            (GAIN_ROWS, grads.shape[2] - lanes), BF
        )

    each(n_dp, gain_rows)
    copies = []
    for order in range(n_dp):
        copy = pltpu.make_async_copy(grads.at[order], g_outs[order], out_sems.at[order])
        copy.start()
        copies.append(copy)
    gather.finish()
    scatter.finish()
    for copy in copies:
        copy.wait()


def shaped(shape, dtype):
    return jax.ShapeDtypeStruct(shape, dtype)


def dma(count):
    return pltpu.SemaphoreType.DMA((count,))


def reaches(rows):
    return [min((turn + 1) * rows + PAD, 4 * rows) for turn in range(4)]


def params(which):
    return pltpu.CompilerParams(collective_id=which, has_side_effects=True, vmem_limit_bytes=LIMIT)


def cost(flops, moved):
    return pl.CostEstimate(flops=flops, bytes_accessed=moved, transcendentals=0)


def attn_forward(states, tables, shards):
    cosine, sine, spans, place = tables
    n_dp = len(shards)
    rows, width = states.shape
    depth = width // n_dp
    columns = shards[0].shape[1]
    heads = place.shape[1] // PAD
    reach = reaches(rows)
    length = 4 * rows
    results = pl.pallas_call(
        functools.partial(attn_forward_kernel, n_dp, depth),
        out_shape=[
            shaped((rows, width), F32),
            shaped((GAIN_ROWS, width), F32),
            shaped((4, rows, width), BF),
            shaped((length, 2 * heads * PAD), BF),
            shaped((length, place.shape[0]), BF),
        ]
        + [shaped((heads, rows, r), BF) for r in reach],
        in_specs=[VM] * 5 + [ANY] * n_dp,
        out_specs=[VM, VM] + [ANY] * 7,
        scratch_shapes=comm_scratch(rows, width)
        + [
            pltpu.VMEM((width, columns), BF),
            pltpu.VMEM((n_dp, GAIN_ROWS, 256), BF),
            pltpu.VMEM((width, 2 * heads * PAD), BF),
            pltpu.VMEM((length, 2 * heads * PAD), BF),
            pltpu.VMEM((length, heads * PAD), BF),
            pltpu.VMEM((length, place.shape[0]), BF),
        ]
        + [pltpu.VMEM((heads, rows, r), BF) for r in reach]
        + [dma(n_dp), dma(n_dp), dma(7)],
        compiler_params=params(0),
        cost_estimate=cost(20_000_000_000, 60_000_000),
        name="attn_forward",
    )(states, cosine, sine, spans, place, *shards)
    return results[0], results[1], results[2:]


def mlp_forward(middle, gains, shards):
    n_dp = len(shards)
    rows, width = middle.shape
    columns = shards[0].shape[1]
    units = columns // 3
    length = 4 * rows
    results = pl.pallas_call(
        functools.partial(mlp_forward_kernel, n_dp),
        out_shape=[
            shaped((rows, width), F32),
            shaped((4, rows, width), BF),
            shaped((length, 2 * units), BF),
            shaped((length, units), BF),
        ],
        in_specs=[VM] * 2 + [ANY] * n_dp,
        out_specs=[VM] + [ANY] * 3,
        scratch_shapes=comm_scratch(rows, width)
        + [
            pltpu.VMEM((width, columns), BF),
            pltpu.VMEM((length, 2 * units), BF),
            pltpu.VMEM((length, units), BF),
            dma(n_dp),
            dma(3),
        ],
        compiler_params=params(1),
        cost_estimate=cost(20_000_000_000, 60_000_000),
        name="mlp_forward",
    )(middle, gains, *shards)
    return results[0], results[1:]


def mlp_backward(grad, middle, gains, saved, shards):
    n_dp = len(shards)
    rows, width = middle.shape
    depth = width // n_dp
    columns = shards[0].shape[1]
    units = columns // 3
    length = 4 * rows
    results = pl.pallas_call(
        functools.partial(mlp_backward_kernel, n_dp, depth),
        out_shape=[shaped((rows, width), F32), shaped((8, width), F32)]
        + [shaped((depth, columns), BF)] * n_dp,
        in_specs=[VM] * 3 + [ANY] * (3 + n_dp),
        out_specs=[VM] * 2 + [ANY] * n_dp,
        scratch_shapes=comm_scratch(rows, width)
        + [
            pltpu.VMEM((width, columns), BF),
            pltpu.VMEM((4, rows, width), BF),
            pltpu.VMEM((width, length), BF),
            pltpu.VMEM((length, 2 * units), BF),
            pltpu.VMEM((length, units), BF),
            pltpu.VMEM((length, 2 * units), BF),
            pltpu.VMEM((n_dp, depth, columns), BF),
            dma(n_dp),
            dma(3),
            dma(n_dp),
        ],
        compiler_params=params(2),
        cost_estimate=cost(30_000_000_000, 60_000_000),
        name="mlp_backward",
    )(grad, middle, gains, *saved, *shards)
    return results[0], results[1], results[2:]


def attn_backward(grad, states, gains, dgain_mlp, tables, saved, shards):
    cosine, sine, _, place = tables
    n_dp = len(shards)
    rows, width = states.shape
    depth = width // n_dp
    columns = shards[0].shape[1]
    heads = place.shape[1] // PAD
    reach = reaches(rows)
    length = 4 * rows
    results = pl.pallas_call(
        functools.partial(attn_backward_kernel, n_dp, depth),
        out_shape=[shaped((rows, width), F32)]
        + [shaped((depth + GAIN_ROWS, columns), BF)] * n_dp,
        in_specs=[VM] * 7 + [ANY] * (7 + n_dp),
        out_specs=[VM] + [ANY] * n_dp,
        scratch_shapes=comm_scratch(rows, width)
        + [
            pltpu.VMEM((width, columns), BF),
            pltpu.VMEM((4, rows, width), BF),
            pltpu.VMEM((width, length), BF),
            pltpu.VMEM((length, 2 * heads * PAD), BF),
            pltpu.VMEM((length, place.shape[0]), BF),
        ]
        + [pltpu.VMEM((heads, rows, r), BF) for r in reach]
        + [
            pltpu.VMEM((length, heads * PAD), BF),
            pltpu.VMEM((length, heads * PAD), BF),
            pltpu.VMEM((length, heads * PAD), BF),
            pltpu.VMEM((length, heads // 2 * PAD), F32),
            pltpu.VMEM((length, heads // 2 * PAD), F32),
            pltpu.VMEM((length, 2 * place.shape[0]), BF),
            pltpu.VMEM((n_dp, depth + GAIN_ROWS, columns), BF),
            pltpu.VMEM((8, width), F32),
            dma(n_dp),
            dma(7),
            dma(n_dp),
        ],
        compiler_params=params(3),
        cost_estimate=cost(30_000_000_000, 60_000_000),
        name="attn_backward",
    )(grad, states, gains, dgain_mlp, cosine, sine, place, *saved, *shards)
    return results[0], results[1:]


def tables_of(documents, heads):
    length = documents.shape[0]
    places = jnp.arange(length, dtype=jnp.int32)
    head = jnp.sum((documents == 0).astype(jnp.int32))
    body_end = jnp.sum((documents <= 1).astype(jnp.int32))
    starts = jnp.where(documents == 0, 0, jnp.where(documents == 1, head, body_end))
    ends = jnp.where(documents == 0, head, jnp.where(documents == 1, body_end, length))
    offset = places - starts
    last = jnp.minimum(starts + (offset // BLOCK + 1) * BLOCK, ends)
    spans = jnp.stack([starts, last], axis=1)
    freqs = jnp.exp(
        jnp.arange(HALF, dtype=F32) * (-2.0 * math.log(rope_base) / HEAD_DIM)
    )
    angles = offset.astype(F32)[:, None] * freqs[None, :]
    gap = ((0, 0), (0, PAD // 2 - HALF))
    cos_half = jnp.pad(jnp.cos(angles), gap)
    sin_half = jnp.pad(jnp.sin(angles), gap)
    cosine = jnp.concatenate([cos_half, cos_half], axis=1)
    sine = jnp.concatenate([-sin_half, sin_half], axis=1)
    place = np.zeros((heads * HEAD_DIM, heads * PAD), np.float32)
    for row in range(heads * HEAD_DIM):
        which, column = divmod(row, HEAD_DIM)
        place[row, which * PAD + column + (PAD // 2 - HALF if column >= HALF else 0)] = 1.0
    return cosine, sine, spans, jnp.asarray(place, BF)


def pack_attn(gain_attn, query, key, value, output, gain_mlp):
    weights = jnp.concatenate([query, key, value, output.T], axis=1).astype(BF)
    depth, columns = weights.shape
    gains = jnp.stack([gain_attn, gain_mlp]).astype(BF)
    gains = jnp.pad(gains, ((0, GAIN_ROWS - 2), (0, columns - depth)))
    return jnp.concatenate([weights, gains], axis=0)


def pack_mlp(gate, up, down):
    return jnp.concatenate([gate, up, down.T], axis=1).astype(BF)


def across(value, count, shift, side):
    pairs = [
        (high * 2 + low, (high + shift) % count * 2 + (low + side) % 2)
        for high in range(count)
        for low in range(2)
    ]
    return lax.ppermute(value, "dp", pairs)


def fetch(pack, n_dp):
    count = n_dp // 2
    along = [pack] + [across(pack, count, shift, 0) for shift in range(1, count)]
    blocks = []
    for block in along:
        blocks += [block, across(block, count, 0, 1)]
    return blocks


def reduce_blocks(blocks):
    n_dp = len(blocks)
    count = n_dp // 2
    total = None
    for shift in range(count):
        arrived = across(blocks[2 * shift + 1], count, 0, 1)
        chunk = blocks[2 * shift].astype(F32) + arrived.astype(F32)
        if shift:
            chunk = across(chunk.astype(BF), count, shift, 0).astype(F32)
        total = chunk if total is None else total + chunk
    return total


def body(n_dp, states_in, documents, *rest):
    cotangent = rest[-1]
    layers = [rest[0:9], rest[9:18]]
    heads = layers[0][1].shape[1] // HEAD_DIM
    tables = tables_of(documents, heads)
    attn_packs = [pack_attn(w[0], w[1], w[2], w[3], w[4], w[5]) for w in layers]
    mlp_packs = [pack_mlp(w[6], w[7], w[8]) for w in layers]
    states = states_in
    kept = []
    for level in range(2):
        attn_shards = fetch(attn_packs[level], n_dp)
        mlp_shards = fetch(mlp_packs[level], n_dp)
        middle, gains, attn_saved = attn_forward(states, tables, attn_shards)
        result, mlp_saved = mlp_forward(middle, gains, mlp_shards)
        kept.append((states, middle, gains, attn_saved, mlp_saved, attn_shards, mlp_shards))
        states = result
    grad = cotangent
    parts = [None, None]
    for level in (1, 0):
        before, middle, gains, attn_saved, mlp_saved, attn_shards, mlp_shards = kept[level]
        (a_full, qkv, mixed, *probs) = attn_saved
        grad_middle, dgain_mlp, mlp_blocks = mlp_backward(grad, middle, gains, mlp_saved, mlp_shards)
        mlp_total = reduce_blocks(mlp_blocks)
        grad, attn_blocks = attn_backward(
            grad_middle, before, gains, dgain_mlp, tables, (a_full, qkv, mixed, *probs), attn_shards
        )
        attn_total = reduce_blocks(attn_blocks)
        parts[level] = (attn_total, mlp_total)
    depth = parts[0][1].shape[0]
    columns = [w.shape[1] for w in layers[0][1:4]]
    units = layers[0][6].shape[1]
    gains = lax.psum(
        jnp.concatenate([parts[level][0][depth : depth + 2, 0:depth] for level in range(2)], axis=0),
        "tensor",
    )
    outs = [states, grad]
    for level in range(2):
        attn_total, mlp_total = parts[level]
        attn_total = attn_total[0:depth]
        first = columns[0]
        second = first + columns[1]
        third = second + columns[2]
        outs += [
            gains[2 * level],
            attn_total[:, 0:first],
            attn_total[:, first:second],
            attn_total[:, second:third],
            attn_total[:, third:].T,
            gains[2 * level + 1],
            mlp_total[:, 0:units],
            mlp_total[:, units : 2 * units],
            mlp_total[:, 2 * units :].T,
        ]
    return tuple(outs)


def solution(mesh):
    layer = (
        P("dp"),
        P("dp", "tensor"),
        P("dp", "tensor"),
        P("dp", "tensor"),
        P("tensor", "dp"),
        P("dp"),
        P("dp", "tensor"),
        P("dp", "tensor"),
        P("tensor", "dp"),
    )
    rows = P(("dp", "tensor"), None)
    return jax.shard_map(
        functools.partial(body, mesh.shape["dp"]),
        mesh=mesh,
        in_specs=(rows, P("dp"), *layer, *layer, rows),
        out_specs=(rows, rows, *layer, *layer),
        check_vma=False,
    )
```

```python
import functools
import math
import types

import jax
import jax.numpy as jnp
import numpy as np
from jax import lax
from jax.experimental import pallas as pl
from jax.experimental.pallas import tpu as pltpu
from jax.sharding import PartitionSpec as P

HEAD_DIM = 96
HALF = HEAD_DIM // 2
BLOCK = 256
PAD = 128
GAIN_ROWS = 16
LIMIT = 60 * 1024 * 1024

epsilon = 1e-05
rope_base = 100000.0
masked_value = -1e30
scale = 1.0 / math.sqrt(HEAD_DIM)

BF = jnp.bfloat16
F32 = jnp.float32
MESH = pl.DeviceIdType.MESH
ANY = pl.BlockSpec(memory_space=pl.ANY)
VM = pl.BlockSpec(memory_space=pltpu.VMEM)


def nn(left, right):
    return lax.dot_general(left, right, (((1,), (0,)), ((), ())), preferred_element_type=F32)


def nt(left, right):
    return lax.dot_general(left, right, (((1,), (1,)), ((), ())), preferred_element_type=F32)


def tn(left, right):
    return lax.dot_general(left, right, (((0,), (0,)), ((), ())), preferred_element_type=F32)


def tile(index, size):
    return pl.ds(pl.multiple_of(index * size, size), size)


def each(count, body):
    def step(index, carry):
        body(index)
        return carry

    lax.fori_loop(0, count, step, 0)


class Group:
    def __init__(self):
        self.me = lax.axis_index("tensor")
        self.core_bit = lax.rem(self.me, 2)
        self.chip = self.me // 2
        self.core = self.me + 1 - 2 * self.core_bit
        self.other = lax.rem(self.me + 2, 4)

    def greet(self, barrier):
        for near in (self.core, self.other):
            pl.semaphore_signal(barrier, inc=1, device_id={"tensor": near}, device_id_type=MESH)

    def peers(self):
        return 2

    def remote(self, source, target, send, recv, device):
        return pltpu.make_async_remote_copy(
            src_ref=source,
            dst_ref=target,
            send_sem=send,
            recv_sem=recv,
            device_id={"tensor": device},
            device_id_type=MESH,
        )


class Gather:
    def __init__(self, group, full, send, recv):
        self.group, self.full, self.send, self.recv = group, full, send, recv
        half = full.shape[1] // 2
        mine = full.at[group.me]
        self.to_core = group.remote(mine, mine, send.at[0], recv.at[0], group.core)
        self.to_other = []
        self.onward = []
        for part in range(2):
            piece = full.at[group.me, pl.ds(part * half, half)]
            self.to_other.append(
                group.remote(piece, piece, send.at[1 + part], recv.at[1 + part], group.other)
            )
            piece = full.at[group.other, pl.ds(part * half, half)]
            self.onward.append(
                group.remote(piece, piece, send.at[3 + part], recv.at[3 + part], group.core)
            )

    def start(self):
        for copy in self.to_other:
            copy.start()
        self.to_core.start()

    def wait_chip(self):
        self.to_core.wait_recv()

    def forward(self):
        for here, there in zip(self.to_other, self.onward):
            here.wait_recv()
            there.start()

    def wait_other(self):
        for copy in self.onward:
            copy.wait_recv()

    def finish(self):
        self.to_core.wait_send()
        for copy in self.to_other + self.onward:
            copy.wait_send()


class Scatter:
    def __init__(self, group, parts, near, away, landed, send, recv):
        self.group, self.parts, self.near = group, parts, near
        self.away, self.landed = away, landed
        self.to_core = [
            group.remote(
                parts.at[turn, 1 - group.core_bit], near.at[turn], send.at[turn], recv.at[turn], group.core
            )
            for turn in range(2)
        ]
        half = away.shape[0] // 2
        self.to_other = [
            group.remote(
                away.at[pl.ds(part * half, half)],
                landed.at[pl.ds(part * half, half)],
                send.at[2 + part],
                recv.at[2 + part],
                group.other,
            )
            for part in range(2)
        ]

    def rows_of(self, turn):
        return 1 - self.group.chip if turn == 0 else self.group.chip

    def send_core(self, turn):
        self.to_core[turn].start()

    def send_away(self):
        self.to_core[0].wait_recv()
        half = self.away.shape[0] // 2
        for part in range(2):

            def add(index):
                rows = pl.ds(pl.multiple_of(part * half + index * 32, 32), 32)
                total = self.parts[0, self.group.core_bit, rows, :].astype(F32) + self.near[
                    0, rows, :
                ].astype(F32)
                self.away[rows, :] = total.astype(BF)

            each(half // 32, add)
            self.to_other[part].start()

    def wait(self):
        self.to_core[1].wait_recv()
        for copy in self.to_other:
            copy.wait_recv()

    def total(self, rows):
        return (
            self.parts[1, self.group.core_bit, rows, :].astype(F32)
            + self.near[1, rows, :].astype(F32)
            + self.landed[rows, :].astype(F32)
        )

    def finish(self):
        for copy in self.to_core + self.to_other:
            copy.wait_send()


class Line:
    def __init__(self, n_dp):
        mine = lax.axis_index("dp")
        self.count = n_dp // 2
        self.z, self.x = mine // 2, lax.rem(mine, 2)
        self.mine = mine
        self.pair = self.z * 2 + 1 - self.x
        self.up = jnp.minimum(self.z + 1, self.count - 1) * 2 + self.x
        self.down = jnp.maximum(self.z - 1, 0) * 2 + self.x
        self.has_up = self.z + 1 < self.count
        self.has_down = self.z > 0

    def greet(self, barrier):
        def hello(device):
            pl.semaphore_signal(barrier, inc=1, device_id={"dp": device}, device_id_type=MESH)

        hello(self.pair)
        pl.when(self.has_up)(lambda: hello(self.up))
        pl.when(self.has_down)(lambda: hello(self.down))

    def peers(self):
        return 1 + jnp.minimum(self.count - 1 - self.z, 1) + jnp.minimum(self.z, 1)

    def remote(self, source, target, send, recv, device):
        return pltpu.make_async_remote_copy(
            src_ref=source, dst_ref=target, send_sem=send, recv_sem=recv,
            device_id={"dp": device}, device_id_type=MESH)


class Fetch:
    def __init__(self, line, own, blocks, send, recv):
        self.line, self.own, self.blocks, self.send, self.recv = line, own, blocks, send, recv

    @staticmethod
    def scratch(n_dp):
        return [pltpu.SemaphoreType.DMA((n_dp, 3))] * 2

    def copy(self, slot, block, device, way):
        source = self.own if slot == 0 else self.blocks.at[block]
        return self.line.remote(
            source, self.blocks.at[block], self.send.at[slot, way], self.recv.at[slot, way], device)

    def upward(self, step):
        line = self.line
        return self.copy(step, jnp.maximum(line.z - step, 0) * 2 + line.x, line.up, 1)

    def downward(self, step):
        line = self.line
        return self.copy(step, jnp.minimum(line.z + step, line.count - 1) * 2 + line.x, line.down, 2)

    def sideways(self, step, low):
        line = self.line
        if low:
            return self.copy(step, jnp.maximum(line.z - step, 0) * 2 + line.x, line.pair, 0)
        return self.copy(line.count + step, jnp.minimum(line.z + step, line.count - 1) * 2 + line.x, line.pair, 0)

    def start(self):
        line = self.line
        pl.when(line.has_up)(lambda: self.upward(0).start())
        pl.when(line.has_down)(lambda: self.downward(0).start())
        self.sideways(0, True).start()

    def step(self, step):
        line = self.line

        @pl.when(line.z >= step)
        def _():
            self.upward_in(step).wait_recv()
            pl.when(line.has_up)(lambda: self.upward(step).start())
            self.sideways(step, True).start()

        @pl.when(line.z + step < line.count)
        def _():
            self.downward_in(step).wait_recv()
            pl.when(line.has_down)(lambda: self.downward(step).start())
            self.sideways(step, False).start()

    def upward_in(self, step):
        line = self.line
        return self.copy(step - 1, jnp.maximum(line.z - step, 0) * 2 + line.x, line.up, 1)

    def downward_in(self, step):
        line = self.line
        return self.copy(step - 1, jnp.minimum(line.z + step, line.count - 1) * 2 + line.x, line.down, 2)

    def finish(self):
        line = self.line
        for step in range(line.count):

            @pl.when(line.z >= step)
            def _():
                pl.when(line.has_up)(lambda: self.upward(step).wait_send())
                self.sideways(step, True).wait()

            @pl.when(line.z + step < line.count)
            def _():
                pl.when(line.has_down)(lambda: self.downward(step).wait_send())
                if step:
                    self.sideways(step, False).wait()

    def actions(self):
        return [self.start] + [functools.partial(self.step, s) for s in range(1, self.line.count)] + [self.finish]


class Reduce:
    def __init__(self, line, blocks, out, pair_in, line_in, mine, x_send, x_recv, z_send, z_recv, local):
        self.line, self.blocks, self.out = line, blocks, out
        self.pair_in, self.line_in, self.mine = pair_in, line_in, mine
        self.x_send, self.x_recv, self.z_send, self.z_recv, self.local = x_send, x_recv, z_send, z_recv, local

    @staticmethod
    def scratch(n_dp, rows, columns):
        count = n_dp // 2
        dma = pltpu.SemaphoreType.DMA
        return [
            pltpu.VMEM((count, rows, columns), BF),
            pltpu.VMEM((count + 1, rows, columns), BF),
            pltpu.VMEM((2, rows, columns), BF),
            dma((count,)), dma((count,)), dma((count,)), dma((count + 1,)), dma((2,)),
        ]

    def sideways(self, target):
        line = self.line
        return line.remote(self.blocks.at[target * 2 + 1 - line.x], self.pair_in.at[target],
                           self.x_send.at[target], self.x_recv.at[target], line.pair)

    def along(self, target, up):
        line = self.line
        slot = target + 1 if up else target
        return line.remote(self.pair_in.at[target], self.line_in.at[slot],
                           self.z_send.at[target], self.z_recv.at[slot], line.up if up else line.down)

    def load(self, target, slot):
        return pltpu.make_async_copy(self.blocks.at[target * 2 + self.line.x], self.mine.at[slot], self.local.at[slot])

    def above(self, step):
        return self.line.z + step < self.line.count, jnp.minimum(self.line.z + step, self.line.count - 1)

    def below(self, step):
        return self.line.z - step >= 0, jnp.maximum(self.line.z - step, 0)

    def fetch(self, step):
        there, target = self.above(step)
        pl.when(there)(lambda: self.load(target, 0).start())
        if step:
            there2, target2 = self.below(step)
            pl.when(there2)(lambda: self.load(target2, 1).start())

    def start(self):
        line = self.line
        for step in range(line.count - 1, 0, -1):
            for there, target in (self.above(step), self.below(step)):
                pl.when(there)(lambda: self.sideways(target).start())
        self.sideways(line.z).start()
        self.fetch(line.count - 1)

    def add(self, target, slot, more):
        rows = self.out.shape[0]

        def some(index):
            part = pl.ds(pl.multiple_of(index * 16, 16), 16)
            total = self.pair_in[target, part, :].astype(F32) + self.mine[slot, part, :].astype(F32)
            for other in more:
                total += self.line_in[other, part, :].astype(F32)
            self.pair_in[target, part, :] = total.astype(BF)

        each(rows // 16, some)

    def pass_on(self, target, slot, up):
        line = self.line
        self.load(target, slot).wait()
        self.sideways(target).wait_recv()
        fed = line.has_down if up else line.has_up

        @pl.when(fed)
        def _():
            self.along(target, up).wait_recv()
            self.add(target, slot, [target + 1 if up else target])

        pl.when(jnp.logical_not(fed))(lambda: self.add(target, slot, []))
        self.along(target, up).start()

    def step(self, step):
        for slot, (there, target) in enumerate((self.above(step), self.below(step))):
            pl.when(there)(lambda: self.pass_on(target, slot, slot == 0))
        self.fetch(step - 1)

    def close(self):
        line = self.line
        z = line.z
        self.load(z, 0).wait()
        self.sideways(z).wait_recv()
        rows = self.out.shape[0]

        def final(more):
            def some(index):
                part = pl.ds(pl.multiple_of(index * 16, 16), 16)
                total = self.pair_in[z, part, :].astype(F32) + self.mine[0, part, :].astype(F32)
                for other in more:
                    total += self.line_in[other, part, :].astype(F32)
                self.out[part, :] = total

            each(rows // 16, some)

        pl.when(line.has_down)(lambda: self.along(z, True).wait_recv())
        pl.when(line.has_up)(lambda: self.along(z, False).wait_recv())
        pl.when(jnp.logical_not(line.has_down))(lambda: final([z]))
        pl.when(jnp.logical_not(line.has_up))(lambda: final([z + 1]))
        pl.when(line.has_down & line.has_up)(lambda: final([z, z + 1]))
        for step in range(line.count - 1, 0, -1):
            for up, (there, target) in ((True, self.above(step)), (False, self.below(step))):

                @pl.when(there)
                def _():
                    self.sideways(target).wait_send()
                    self.along(target, up).wait_send()

        self.sideways(z).wait_send()

    def actions(self):
        return [self.start] + [functools.partial(self.step, s) for s in range(self.line.count - 1, 0, -1)] + [self.close]


def spread(block, depth, lanes, width):
    row = lax.broadcasted_iota(jnp.int32, (lanes, width), 0)
    column = lax.broadcasted_iota(jnp.int32, (lanes, width), 1)
    hit = (column - row == block * depth) & (row < depth)
    return jnp.where(hit, 1.0, 0.0).astype(BF)


def turn_half(values):
    return pltpu.roll(values, PAD // 2, 1)


def meet(*circles):
    barrier = pltpu.get_barrier_semaphore()
    for circle in circles:
        circle.greet(barrier)
    pl.semaphore_wait(barrier, sum(circle.peers() for circle in circles))


class Weights:
    def __init__(self, line, own, blocks, held, sems):
        self.copies = []
        depth = own.shape[0]
        count = line.count
        for index in range(2 * count):
            shift, side = index // 2, index % 2
            block = lax.rem(line.z + shift, count) * 2 + lax.rem(line.x + side, 2)
            source = blocks.at[block] if index else own
            rows = pl.ds(pl.multiple_of(block * depth, 16), depth)
            self.copies.append(pltpu.make_async_copy(source, held.at[rows], sems.at[index]))

    def start(self):
        for copy in self.copies:
            copy.start()

    def wait(self):
        for copy in self.copies:
            copy.wait()


class Pump:
    def __init__(self, tasks, plan):
        self.steps = [step for task in tasks for step in task.actions()]
        self.plan = list(plan)

    def __call__(self):
        count = self.plan.pop(0) if self.plan else 0
        self.do(count)

    def do(self, count):
        for step in self.steps[:count]:
            step()
        self.steps = self.steps[count:]

    def rest(self):
        self.do(len(self.steps))


def fetches_of(line, r, count):
    return [
        Fetch(
            line,
            getattr(r, f"own{i}"),
            getattr(r, f"blocks{i}"),
            getattr(r, f"fetch_send{i}"),
            getattr(r, f"fetch_recv{i}"),
        )
        for i in range(count)
    ]


def reduces_of(line, r, count):
    return [
        Reduce(
            line,
            getattr(r, f"sum{i}"),
            getattr(r, f"total{i}"),
            *[getattr(r, f"reduce{i}_{j}") for j in range(8)],
        )
        for i in range(count)
    ]


def comm_of(r):
    group = Group()
    gather = Gather(group, r.full, r.g_send, r.g_recv)
    scatter = Scatter(group, r.parts, r.near, r.away, r.landed, r.s_send, r.s_recv)
    return group, gather, scatter


def out_columns(scatter, turn, left_rows, right_tile, columns):
    product = nt(left_rows, right_tile)
    rows = product.shape[0] // 2
    scatter.parts[turn, 0, :, columns] = product[:rows].astype(BF)
    scatter.parts[turn, 1, :, columns] = product[rows:].astype(BF)


def norm_rows(source, gain, full, slot):
    def norm(index):
        part = tile(index, 32)
        values = source[part, :]
        factor = lax.rsqrt(jnp.mean(values * values, axis=-1, keepdims=True) + epsilon)
        full[slot, part, :] = (values * factor * gain).astype(BF)

    each(source.shape[0] // 32, norm)


def add_rows(scatter, source, target):
    def close(index):
        part = tile(index, 32)
        target[part, :] = source[part, :] + scatter.total(part)

    each(source.shape[0] // 32, close)


def attn_forward_kernel(first, level, fetch_count, plan, r):
    rows, width = r.x.shape
    n_dp, depth = r.w_sems.shape[0], r.own.shape[0]
    line = Line(n_dp)
    group, gather, scatter = comm_of(r)
    tasks = fetches_of(line, r, fetch_count)
    weights = Weights(line, r.own, r.blocks, r.held, r.w_sems)
    circles = (group, line) if first or tasks else (group,)
    meet(*circles)
    if first:
        lanes = r.gain_own.shape[1]
        gain_fetch = Fetch(line, r.gain_own, r.gain_blocks, r.gain_send, r.gain_recv)
        weight_fetch = Fetch(line, r.own, r.blocks, r.weight_send, r.weight_recv)
        gain_fetch.start()
        weight_fetch.start()
        for step in gain_fetch.actions()[1:]:
            step()
        r.gains[...] = jnp.zeros_like(r.gains)

        def gather_gain(block):
            chosen = spread(block, depth, lanes, width)

            @pl.when(block == line.mine)
            def _():
                r.gains[...] += nn(r.gain_own[...], chosen)

            @pl.when(block != line.mine)
            def _():
                r.gains[...] += nn(r.gain_blocks[block], chosen)

        each(n_dp, gather_gain)
        norm_rows(r.x, r.gains[2 * level : 2 * level + 1, :], r.full, group.me)
        gather.start()
        for step in weight_fetch.actions()[1:-1]:
            step()
        pump = Pump(tasks, plan)
        pump()
        weight_fetch.finish()
        weights.start()
    else:
        weights.start()
        pump = Pump(tasks, plan)
        pump()
        norm_rows(r.x, r.gains[2 * level : 2 * level + 1, :], r.full, group.me)
        gather.start()
    weights.wait()
    place = r.place[...]
    heads = place.shape[1] // PAD
    compact_width, head_width = place.shape
    padded, qkv, mixed, compact, held = r.padded, r.qkv, r.mixed, r.compact, r.held

    def pad(index):
        part = tile(index, 256)
        padded[part, 0:head_width] = nn(held[part, 0:compact_width], place).astype(BF)
        padded[part, head_width : 2 * head_width] = nn(
            held[part, compact_width : 2 * compact_width], place
        ).astype(BF)

    each(width // 256, pad)

    def project(chip):
        left = r.full[pl.ds(2 * chip, 2)].reshape(2 * rows, width)
        where = tile(chip, 2 * rows)
        cosine, sine = r.cosine[where, :], r.sine[where, :]

        def turned(index):
            columns = tile(index, 2 * PAD)
            product = nn(left, padded[:, columns])
            for half in range(2):
                u = product[:, half * PAD : (half + 1) * PAD]
                qkv[where, tile(2 * index + half, PAD)] = (u * cosine + turn_half(u) * sine).astype(BF)

        each(3 * heads // 4, turned)
        columns = pl.ds(3 * heads // 2 * PAD, heads // 2 * PAD)
        qkv[where, columns] = nn(left, padded[:, columns]).astype(BF)

    gather.wait_chip()
    project(group.chip)
    pump()
    gather.forward()
    pump()
    gather.wait_other()
    project(1 - group.chip)
    copies = [
        pltpu.make_async_copy(r.full, r.a_out, r.out_sems.at[0]),
        pltpu.make_async_copy(qkv, r.qkv_out, r.out_sems.at[1]),
    ]
    for copy in copies:
        copy.start()
    pump()
    kv_at = heads * PAD
    value_at = kv_at + heads // 2 * PAD
    for turn in range(4):
        prob = getattr(r, f"prob{turn}")
        reach = prob.shape[2]
        where = pl.ds(turn * rows, rows)

        def attend(head):
            query = qkv[where, tile(head, PAD)]
            key = qkv[0:reach, pl.ds(pl.multiple_of(kv_at + head // 2 * PAD, PAD), PAD)]
            value = qkv[0:reach, pl.ds(pl.multiple_of(value_at + head // 2 * PAD, PAD), PAD)]
            scores = nt(query, key) * scale
            place_of = lax.broadcasted_iota(jnp.int32, scores.shape, 1)
            begin = r.spans[where, 0:1]
            end = r.spans[where, 1:2]
            scores = jnp.where((place_of >= begin) & (place_of < end), scores, masked_value)
            exponent = jnp.exp(scores - jnp.max(scores, axis=-1, keepdims=True))
            summed = jnp.sum(exponent, axis=-1, keepdims=True)
            low = (exponent * (1.0 / summed)).astype(BF)
            prob[head] = low
            mixed[where, tile(head, PAD)] = nn(low, value).astype(BF)

        each(heads, attend)
        copy = pltpu.make_async_copy(prob, getattr(r, f"p_out{turn}"), r.out_sems.at[2 + turn])
        copy.start()
        copies.append(copy)
        compact[where, :] = nt(mixed[where, :], place).astype(BF)
        pump()
    copy = pltpu.make_async_copy(compact, r.o_out, r.out_sems.at[6])
    copy.start()
    copies.append(copy)
    for turn in range(2):
        left = compact[tile(scatter.rows_of(turn), 2 * rows), :]

        def part_of(index):
            columns = tile(index, 256)
            out_columns(scatter, turn, left, held[columns, 2 * compact_width :], columns)

        each(width // 256, part_of)
        scatter.send_core(turn)
        if turn == 0:
            scatter.send_away()
        pump()
    scatter.wait()
    pump()
    add_rows(scatter, r.x, r.middle)
    pump.rest()
    gather.finish()
    scatter.finish()
    for copy in copies:
        copy.wait()


def mlp_forward_kernel(level, fetch_count, plan, r):
    rows, width = r.middle.shape
    units = r.hid.shape[1]
    line = Line(r.wide_sems.shape[0])
    group, gather, scatter = comm_of(r)
    tasks = fetches_of(line, r, fetch_count)
    wide, held, gu, hid = r.wide, r.held, r.gu, r.hid
    weights = [
        Weights(line, r.wide_own, r.wide_blocks, wide, r.wide_sems),
        Weights(line, r.own, r.blocks, held, r.w_sems),
    ]
    meet(*((group, line) if tasks else (group,)))
    for each_of in weights:
        each_of.start()
    pump = Pump(tasks, plan)
    pump()
    norm_rows(r.middle, r.gains[2 * level + 1 : 2 * level + 2, :], r.full, group.me)
    gather.start()
    weights[0].wait()

    def expand(chip):
        left = r.full[pl.ds(2 * chip, 2)].reshape(2 * rows, width)
        where = tile(chip, 2 * rows)

        def unit(index):
            columns = tile(index, 256)
            further = pl.ds(pl.multiple_of(units + index * 256, 256), 256)
            gate = nn(left, wide[:, columns])
            up = nn(left, wide[:, further])
            hid[where, columns] = (gate / (1.0 + jnp.exp(-gate)) * up).astype(BF)
            gu[where, columns] = gate.astype(BF)
            gu[where, further] = up.astype(BF)

        each(units // 256, unit)

    gather.wait_chip()
    expand(group.chip)
    pump()
    gather.forward()
    pump()
    gather.wait_other()
    expand(1 - group.chip)
    copies = [
        pltpu.make_async_copy(r.full, r.m_out, r.out_sems.at[0]),
        pltpu.make_async_copy(gu, r.gu_out, r.out_sems.at[1]),
        pltpu.make_async_copy(hid, r.hid_out, r.out_sems.at[2]),
    ]
    for copy in copies:
        copy.start()
    pump()
    weights[1].wait()
    for turn in range(2):
        left = hid[tile(scatter.rows_of(turn), 2 * rows), :]

        def part_of(index):
            columns = tile(index, 256)
            out_columns(scatter, turn, left, held[columns, :], columns)

        each(width // 256, part_of)
        scatter.send_core(turn)
        if turn == 0:
            scatter.send_away()
        pump()
    scatter.wait()
    pump()
    add_rows(scatter, r.middle, r.result)
    pump.rest()
    gather.finish()
    scatter.finish()
    for copy in copies:
        copy.wait()


def flip(source, target, slot):
    _, rows, width = source.shape

    def block(index):
        columns = tile(index, 256)
        target[columns, slot * rows : (slot + 1) * rows] = source[slot, :, columns].T

    each(width // 256, block)


def flip_pairs(source, target, slot):
    rows, width = source.shape[2:]

    def block(index):
        columns = tile(index, 256)
        target[columns, slot * rows : (slot + 1) * rows] = source[slot // 2, slot % 2, :, columns].T

    each(width // 256, block)


def close_back(scatter, grad_in_ref, state_ref, gain, grad_out, dgain):
    rows = state_ref.shape[0]
    dgain[...] = jnp.zeros_like(dgain)

    def close(index):
        part = tile(index, 32)
        values = state_ref[part, :]
        factor = lax.rsqrt(jnp.mean(values * values, axis=-1, keepdims=True) + epsilon)
        normed = values * factor
        grad_in = scatter.total(part)
        dgain[...] += jnp.sum((grad_in * normed).reshape(4, 8, -1), axis=0)
        grad_norm = grad_in * gain
        inner = jnp.mean(grad_norm * normed, axis=-1, keepdims=True)
        grad_out[part, :] = grad_in_ref[part, :] + factor * (grad_norm - normed * inner)

    each(rows // 32, close)


def mlp_backward_kernel(level, reduce_count, plan, r):
    rows, width = r.middle.shape
    units = r.hid.shape[1]
    n_dp = r.wide_sems.shape[0]
    depth = width // n_dp
    line = Line(n_dp)
    group, gather, scatter = comm_of(r)
    tasks = reduces_of(line, r, reduce_count)
    wide, held, gu, hid, flipped = r.wide, r.held, r.gu, r.hid, r.flipped
    weights = [
        Weights(line, r.own, r.blocks, held, r.w_sems),
        Weights(line, r.wide_own, r.wide_blocks, wide, r.wide_sems),
    ]
    fetches = [
        pltpu.make_async_copy(r.m_in, r.parts, r.in_sems.at[0]),
        pltpu.make_async_copy(r.gu_in, gu, r.in_sems.at[1]),
        pltpu.make_async_copy(r.hid_in, hid, r.in_sems.at[2]),
    ]
    meet(*((group, line) if tasks else (group,)))
    for copy in fetches + weights:
        copy.start()
    pump = Pump(tasks, plan)
    pump()
    r.full[group.me] = r.grad[...].astype(BF)
    gather.start()
    fetches[0].wait()
    for slot in range(4):
        flip_pairs(r.parts, flipped, slot)
    pump()
    for copy in weights + fetches[1:]:
        copy.wait()

    def inward(chip):
        left = r.full[pl.ds(2 * chip, 2)].reshape(2 * rows, width)
        where = tile(chip, 2 * rows)

        def unit(index):
            columns = tile(index, 256)
            further = pl.ds(pl.multiple_of(units + index * 256, 256), 256)
            grad = nn(left, held[:, columns])
            gate = gu[where, columns].astype(F32)
            up = gu[where, further].astype(F32)
            sig = 1.0 / (1.0 + jnp.exp(-gate))
            gu[where, columns] = (grad * up * sig * (1.0 + gate * (1.0 - sig))).astype(BF)
            gu[where, further] = (grad * gate * sig).astype(BF)

        each(units // 256, unit)

    gather.wait_chip()
    inward(group.chip)
    pump()
    gather.forward()
    pump()
    gather.wait_other()
    inward(1 - group.chip)
    pump()
    for turn in range(2):
        where = tile(scatter.rows_of(turn), 2 * rows)

        def part_of(index):
            columns = tile(index, 256)
            out_columns(scatter, turn, gu[where, :], wide[columns, :], columns)

        each(width // 256, part_of)
        scatter.send_core(turn)
        if turn == 0:
            scatter.send_away()
        pump()

    def grads_of(block, target, slot, right):
        left = flipped[pl.ds(pl.multiple_of(block * depth, 16), depth), :]

        def some(index):
            columns = tile(index, 512)
            target[slot, :, columns] = nn(left, right[:, columns]).astype(BF)

        each(right.shape[1] // 512, some)

    half = n_dp // 2
    copies = []
    for part in range(2):
        for copy in copies:
            copy.wait()
        each(half, lambda slot: grads_of(part * half + slot, r.wide_grads, slot, gu))
        copies = [
            pltpu.make_async_copy(r.wide_grads, r.wide_out.at[pl.ds(part * half, half)], r.out_sems.at[part])
        ]
        copies[0].start()
        pump()
    for slot in range(4):
        flip(r.full, flipped, slot)
    each(n_dp, lambda block: grads_of(block, r.grads, block, hid))
    copies.append(pltpu.make_async_copy(r.grads, r.grads_out, r.out_sems.at[2]))
    copies[-1].start()
    pump()
    scatter.wait()
    pump()
    close_back(
        scatter, r.grad, r.middle, r.gains[2 * level + 1 : 2 * level + 2, :], r.grad_out, r.dgain
    )
    pump.rest()
    gather.finish()
    scatter.finish()
    for copy in copies:
        copy.wait()


def attn_backward_kernel(level, reduce_count, plan, r):
    rows, width = r.x.shape
    n_dp = r.w_sems.shape[0]
    depth = width // n_dp
    line = Line(n_dp)
    group, gather, scatter = comm_of(r)
    tasks = reduces_of(line, r, reduce_count)
    held, qkv, compact, flipped = r.held, r.qkv, r.compact, r.flipped
    probs = [getattr(r, f"prob{turn}") for turn in range(4)]
    weights = Weights(line, r.own, r.blocks, held, r.w_sems)
    fetches = [
        pltpu.make_async_copy(r.a_in, r.parts, r.in_sems.at[0]),
        pltpu.make_async_copy(r.o_in, compact, r.in_sems.at[1]),
        pltpu.make_async_copy(r.qkv_in, qkv, r.in_sems.at[2]),
    ] + [
        pltpu.make_async_copy(getattr(r, f"p_in{turn}"), probs[turn], r.in_sems.at[3 + turn])
        for turn in range(4)
    ]
    meet(*((group, line) if tasks else (group,)))
    fetches[0].start()
    weights.start()
    for copy in fetches[1:]:
        copy.start()
    pump = Pump(tasks, plan)
    pump()
    r.full[group.me] = r.grad[...].astype(BF)
    gather.start()
    fetches[0].wait()
    for slot in range(4):
        flip_pairs(r.parts, flipped, slot)
    pump()
    weights.wait()
    for copy in fetches[1:]:
        copy.wait()
    place = r.place[...]
    heads = place.shape[1] // PAD
    compact_width, head_width = place.shape

    def inward(chip):
        left = r.full[pl.ds(2 * chip, 2)].reshape(2 * rows, width)
        where = tile(chip, 2 * rows)
        grad = nn(left, held[:, 2 * compact_width :]).astype(BF)
        r.grad_mixed[where, :] = nn(grad, place).astype(BF)

    gather.wait_chip()
    inward(group.chip)
    pump()
    gather.forward()
    pump()
    gather.wait_other()
    inward(1 - group.chip)
    kv_at = heads * PAD
    value_at = kv_at + heads // 2 * PAD
    r.grad_k[...] = jnp.zeros_like(r.grad_k)
    r.grad_v[...] = jnp.zeros_like(r.grad_v)
    for turn, prob in enumerate(probs):
        reach = prob.shape[2]
        where = pl.ds(turn * rows, rows)
        cosine, sine = r.cosine[where, :], r.sine[where, :]

        def attend(head):
            mine = tile(head, PAD)
            shared = tile(head // 2, PAD)
            query = qkv[where, mine]
            key = qkv[0:reach, pl.ds(pl.multiple_of(kv_at + head // 2 * PAD, PAD), PAD)]
            value = qkv[0:reach, pl.ds(pl.multiple_of(value_at + head // 2 * PAD, PAD), PAD)]
            grad = r.grad_mixed[where, mine]
            low = prob[head]
            grad_prob = nt(grad, value)
            weight = low.astype(F32)
            inner = jnp.sum(weight * grad_prob, axis=-1, keepdims=True)
            grad_score = (weight * (grad_prob - inner)).astype(BF)
            u = nn(grad_score, key) * scale
            r.grad_q[where, mine] = (u * cosine - turn_half(u) * sine).astype(BF)
            r.grad_k[0:reach, shared] += tn(grad_score, query)
            r.grad_v[0:reach, shared] += tn(low, grad)

        each(heads, attend)
        pump()
    for pair in range(heads // 2):
        columns = pl.ds(pair * PAD, PAD)
        u = r.grad_k[:, columns] * scale
        r.grad_kv[:, columns] = (u * r.cosine[...] - turn_half(u) * r.sine[...]).astype(BF)
        r.grad_kv[:, pl.ds((heads // 2 + pair) * PAD, PAD)] = r.grad_v[:, columns].astype(BF)
    grad_low = r.grad_low
    grad_low[:, 0:compact_width] = nt(r.grad_q[...], place).astype(BF)
    grad_low[:, compact_width : 2 * compact_width] = nt(r.grad_kv[...], place).astype(BF)
    for turn in range(2):
        where = tile(scatter.rows_of(turn), 2 * rows)

        def part_of(index):
            columns = tile(index, 256)
            out_columns(
                scatter, turn, grad_low[where, :], held[columns, 0 : 2 * compact_width], columns
            )

        each(width // 256, part_of)
        scatter.send_core(turn)
        if turn == 0:
            scatter.send_away()
        pump()
    grads = r.grads

    def grads_of(block, begin, right):
        left = flipped[pl.ds(pl.multiple_of(block * depth, 16), depth), :]
        grads[block, :, begin : begin + right.shape[1]] = nn(left, right[...]).astype(BF)

    each(n_dp, lambda block: grads_of(block, 0, grad_low))
    for slot in range(4):
        flip(r.full, flipped, slot)
    each(n_dp, lambda block: grads_of(block, 2 * compact_width, compact))
    copy = pltpu.make_async_copy(grads, r.grads_out, r.out_sems.at[0])
    copy.start()
    pump()
    scatter.wait()
    pump()
    close_back(scatter, r.grad, r.x, r.gains[2 * level : 2 * level + 1, :], r.grad_out, r.dgain)
    pump.rest()
    gather.finish()
    scatter.finish()
    copy.wait()


def last_kernel(reduce_count, r):
    n_dp, _, lanes = r.gain_blocks.shape
    width = r.rows.shape[1]
    depth = width // n_dp
    line = Line(n_dp)
    group = Group()
    tasks = reduces_of(line, r, reduce_count)
    gains = Reduce(line, r.gain_blocks, r.gain_total, *[getattr(r, f"gain{j}") for j in range(8)])
    meet(group, line)
    for task in tasks:
        task.start()
    for row in range(4):
        r.rows[row : row + 1, :] = jnp.sum(getattr(r, f"dgain{row}")[...], axis=0, keepdims=True)
    r.rows[4:8, :] = jnp.zeros((4, width), F32)
    for turn, device in enumerate((group.core, group.other)):
        copy = group.remote(r.rows, r.others.at[turn], r.row_send.at[turn], r.row_recv.at[turn], device)
        copy.start()
        copy.wait()
        r.rows[...] += r.others[turn]
    both = jnp.concatenate([r.rows[...], jnp.zeros((GAIN_ROWS - 8, width), F32)], axis=0).astype(BF)

    def gain_rows(block):
        r.gain_blocks[block] = nt(both, spread(block, depth, lanes, width)).astype(BF)

    each(n_dp, gain_rows)
    gains.start()
    for task in tasks:
        for step in task.actions()[1:]:
            step()
    for step in gains.actions()[1:]:
        step()


def shaped(shape, dtype):
    return jax.ShapeDtypeStruct(shape, dtype)


def dma(count):
    return pltpu.SemaphoreType.DMA((count,))


def vmem(*shape, dtype=BF):
    return pltpu.VMEM(shape, dtype)


def reaches(rows):
    return [min((turn + 1) * rows + PAD, 4 * rows) for turn in range(4)]


def launch(kernel, which, name, ins, outs, scratch):
    names = list(ins) + list(outs) + list(scratch)

    def entry(*refs):
        kernel(types.SimpleNamespace(**dict(zip(names, refs))))

    results = pl.pallas_call(
        entry,
        out_shape=[shape for shape, _ in outs.values()],
        in_specs=[spec for _, spec in ins.values()],
        out_specs=[spec for _, spec in outs.values()],
        scratch_shapes=list(scratch.values()),
        compiler_params=pltpu.CompilerParams(
            collective_id=which, has_side_effects=True, vmem_limit_bytes=LIMIT
        ),
        cost_estimate=pl.CostEstimate(
            flops=20_000_000_000, bytes_accessed=60_000_000, transcendentals=0
        ),
        name=name,
    )(*[array for array, _ in ins.values()])
    return dict(zip(outs, results))


def comm_scratch(rows, width):
    return dict(
        full=vmem(4, rows, width),
        parts=vmem(2, 2, rows, width),
        near=vmem(2, rows, width),
        away=vmem(rows, width),
        landed=vmem(rows, width),
        g_send=dma(5),
        g_recv=dma(5),
        s_send=dma(4),
        s_recv=dma(4),
    )


def blocks_of(pack, n_dp):
    return shaped((n_dp,) + pack.shape, pack.dtype)


def fetch_refs(packs, n_dp):
    ins, outs, scratch = {}, {}, {}
    for i, pack in enumerate(packs):
        ins[f"own{i}"] = (pack, ANY)
        outs[f"blocks{i}"] = (blocks_of(pack, n_dp), ANY)
        scratch[f"fetch_send{i}"], scratch[f"fetch_recv{i}"] = Fetch.scratch(n_dp)
    return ins, outs, scratch


def reduce_refs(sums):
    ins, outs, scratch = {}, {}, {}
    for i, blocks in enumerate(sums):
        n_dp, depth, columns = blocks.shape
        ins[f"sum{i}"] = (blocks, ANY)
        outs[f"total{i}"] = (shaped((depth, columns), F32), VM)
        for j, each_of in enumerate(Reduce.scratch(n_dp, depth, columns)):
            scratch[f"reduce{i}_{j}"] = each_of
    return ins, outs, scratch


def totals(out, count):
    return [out[f"total{i}"] for i in range(count)]


def fetched(out, count):
    return [out[f"blocks{i}"] for i in range(count)]


def attn_forward(level, which, states, tables, gains, pack, blocks, packs, plan, gain_pack=None):
    cosine, sine, spans, place = tables
    rows, width = states.shape
    first = blocks is None
    n_dp = width // pack.shape[0]
    columns = pack.shape[1]
    heads = place.shape[1] // PAD
    length = 4 * rows
    ins = dict(
        x=(states, VM), cosine=(cosine, VM), sine=(sine, VM), spans=(spans, VM), place=(place, VM), own=(pack, ANY)
    )
    outs = dict(
        middle=(shaped((rows, width), F32), VM),
        a_out=(shaped((4, rows, width), BF), ANY),
        qkv_out=(shaped((length, 2 * heads * PAD), BF), ANY),
        o_out=(shaped((length, place.shape[0]), BF), ANY),
    )
    scratch = comm_scratch(rows, width) | dict(
        held=vmem(width, columns),
        padded=vmem(width, 2 * heads * PAD),
        qkv=vmem(length, 2 * heads * PAD),
        mixed=vmem(length, heads * PAD),
        compact=vmem(length, place.shape[0]),
        w_sems=dma(n_dp),
        out_sems=dma(7),
    )
    for turn, reach in enumerate(reaches(rows)):
        outs[f"p_out{turn}"] = (shaped((heads, rows, reach), BF), ANY)
        scratch[f"prob{turn}"] = vmem(heads, rows, reach)
    if first:
        ins["gain_own"] = (gain_pack, VM)
        outs["gains"] = (shaped((gain_pack.shape[0], width), F32), VM)
        outs["blocks"] = (blocks_of(pack, n_dp), ANY)
        scratch["gain_blocks"] = vmem(n_dp, *gain_pack.shape)
        scratch["gain_send"], scratch["gain_recv"] = Fetch.scratch(n_dp)
        scratch["weight_send"], scratch["weight_recv"] = Fetch.scratch(n_dp)
    else:
        ins["gains"] = (gains, VM)
        ins["blocks"] = (blocks, ANY)
    more = fetch_refs(packs, n_dp)
    return launch(
        functools.partial(attn_forward_kernel, first, level, len(packs), plan),
        which, f"attn_forward_{level}", ins | more[0], outs | more[1], scratch | more[2],
    )


def mlp_refs(rows, width, wide, down):
    n_dp = width // wide[0].shape[0]
    units = down[0].shape[1]
    ins = dict(wide_own=(wide[0], ANY), wide_blocks=(wide[1], ANY), own=(down[0], ANY), blocks=(down[1], ANY))
    scratch = comm_scratch(rows, width) | dict(
        wide=vmem(width, 2 * units),
        held=vmem(width, units),
        gu=vmem(4 * rows, 2 * units),
        hid=vmem(4 * rows, units),
        wide_sems=dma(n_dp),
        w_sems=dma(n_dp),
    )
    return n_dp, units, ins, scratch


def mlp_forward(level, which, middle, gains, wide, down, packs, plan):
    rows, width = middle.shape
    n_dp, units, ins, scratch = mlp_refs(rows, width, wide, down)
    ins |= dict(middle=(middle, VM), gains=(gains, VM))
    outs = dict(
        result=(shaped((rows, width), F32), VM),
        m_out=(shaped((4, rows, width), BF), ANY),
        gu_out=(shaped((4 * rows, 2 * units), BF), ANY),
        hid_out=(shaped((4 * rows, units), BF), ANY),
    )
    scratch |= dict(out_sems=dma(3))
    more = fetch_refs(packs, n_dp)
    return launch(
        functools.partial(mlp_forward_kernel, level, len(packs), plan),
        which, f"mlp_forward_{level}", ins | more[0], outs | more[1], scratch | more[2],
    )


def mlp_backward(level, which, grad, middle, gains, saved, wide, down, sums, plan):
    rows, width = middle.shape
    n_dp, units, ins, scratch = mlp_refs(rows, width, wide, down)
    depth = width // n_dp
    ins |= dict(
        grad=(grad, VM), middle=(middle, VM), gains=(gains, VM),
        m_in=(saved["m_out"].reshape(2, 2, rows, width), ANY), gu_in=(saved["gu_out"], ANY), hid_in=(saved["hid_out"], ANY),
    )
    outs = dict(
        grad_out=(shaped((rows, width), F32), VM),
        dgain=(shaped((8, width), F32), VM),
        wide_out=(shaped((n_dp, depth, 2 * units), BF), ANY),
        grads_out=(shaped((n_dp, depth, units), BF), ANY),
    )
    scratch |= dict(
        flipped=vmem(width, 4 * rows),
        wide_grads=vmem(n_dp // 2, depth, 2 * units),
        grads=vmem(n_dp, depth, units),
        in_sems=dma(3),
        out_sems=dma(3),
    )
    more = reduce_refs(sums)
    return launch(
        functools.partial(mlp_backward_kernel, level, len(sums), plan),
        which, f"mlp_backward_{level}", ins | more[0], outs | more[1], scratch | more[2],
    )


def attn_backward(level, which, grad, states, gains, tables, saved, weights, sums, plan):
    cosine, sine, _, place = tables
    pack, blocks = weights
    rows, width = states.shape
    depth, columns = pack.shape
    n_dp = width // depth
    heads = place.shape[1] // PAD
    length = 4 * rows
    ins = dict(
        grad=(grad, VM), x=(states, VM), gains=(gains, VM), cosine=(cosine, VM), sine=(sine, VM), place=(place, VM),
        own=(pack, ANY), blocks=(blocks, ANY),
        a_in=(saved["a_out"].reshape(2, 2, rows, width), ANY), qkv_in=(saved["qkv_out"], ANY), o_in=(saved["o_out"], ANY),
    )
    outs = dict(
        grad_out=(shaped((rows, width), F32), VM),
        dgain=(shaped((8, width), F32), VM),
        grads_out=(shaped((n_dp, depth, columns), BF), ANY),
    )
    scratch = comm_scratch(rows, width) | dict(
        held=vmem(width, columns),
        flipped=vmem(width, length),
        qkv=vmem(length, 2 * heads * PAD),
        compact=vmem(length, place.shape[0]),
        grad_mixed=vmem(length, heads * PAD),
        grad_q=vmem(length, heads * PAD),
        grad_kv=vmem(length, heads * PAD),
        grad_k=vmem(length, heads // 2 * PAD, dtype=F32),
        grad_v=vmem(length, heads // 2 * PAD, dtype=F32),
        grad_low=vmem(length, 2 * place.shape[0]),
        grads=vmem(n_dp, depth, columns),
        w_sems=dma(n_dp),
        in_sems=dma(7),
        out_sems=dma(1),
    )
    for turn, reach in enumerate(reaches(rows)):
        ins[f"p_in{turn}"] = (saved[f"p_out{turn}"], ANY)
        scratch[f"prob{turn}"] = vmem(heads, rows, reach)
    more = reduce_refs(sums)
    return launch(
        functools.partial(attn_backward_kernel, level, len(sums), plan),
        which, f"attn_backward_{level}", ins | more[0], outs | more[1], scratch | more[2],
    )


def last_sums(which, dgains, sums):
    n_dp = sums[0].shape[0]
    width = dgains[0].shape[1]
    ins = {f"dgain{i}": (dgain, VM) for i, dgain in enumerate(dgains)}
    outs = dict(gain_total=(shaped((GAIN_ROWS, 256), F32), VM))
    scratch = dict(
        gain_blocks=vmem(n_dp, GAIN_ROWS, 256),
        rows=vmem(8, width, dtype=F32),
        others=vmem(2, 8, width, dtype=F32),
        row_send=dma(2),
        row_recv=dma(2),
    )
    for j, each_of in enumerate(Reduce.scratch(n_dp, GAIN_ROWS, 256)):
        scratch[f"gain{j}"] = each_of
    more = reduce_refs(sums)
    return launch(
        functools.partial(last_kernel, len(sums)),
        which, "last_sums", ins | more[0], outs | more[1], scratch | more[2],
    )


def tables_of(documents, heads):
    length = documents.shape[0]
    places = jnp.arange(length, dtype=jnp.int32)
    head = jnp.sum((documents == 0).astype(jnp.int32))
    body_end = jnp.sum((documents <= 1).astype(jnp.int32))
    starts = jnp.where(documents == 0, 0, jnp.where(documents == 1, head, body_end))
    ends = jnp.where(documents == 0, head, jnp.where(documents == 1, body_end, length))
    offset = places - starts
    last = jnp.minimum(starts + (offset // BLOCK + 1) * BLOCK, ends)
    spans = jnp.stack([starts, last], axis=1)
    freqs = jnp.exp(
        jnp.arange(HALF, dtype=F32) * (-2.0 * math.log(rope_base) / HEAD_DIM)
    )
    angles = offset.astype(F32)[:, None] * freqs[None, :]
    gap = ((0, 0), (0, PAD // 2 - HALF))
    cos_half = jnp.pad(jnp.cos(angles), gap)
    sin_half = jnp.pad(jnp.sin(angles), gap)
    cosine = jnp.concatenate([cos_half, cos_half], axis=1)
    sine = jnp.concatenate([-sin_half, sin_half], axis=1)
    place = np.zeros((heads * HEAD_DIM, heads * PAD), np.float32)
    for row in range(heads * HEAD_DIM):
        which, column = divmod(row, HEAD_DIM)
        place[row, which * PAD + column + (PAD // 2 - HALF if column >= HALF else 0)] = 1.0
    return cosine, sine, spans, jnp.asarray(place, BF)


def pack_gains(gains):
    stacked = jnp.stack(gains).astype(BF)
    return jnp.pad(stacked, ((0, GAIN_ROWS - stacked.shape[0]), (0, 256 - stacked.shape[1])))


def body(states_in, documents, *rest):
    cotangent = rest[-1]
    one, two = rest[0:9], rest[9:18]
    heads = one[1].shape[1] // HEAD_DIM
    tables = tables_of(documents, heads)
    attn_pack = [jnp.concatenate([w[1], w[2], w[3], w[4].T], axis=1).astype(BF) for w in (one, two)]
    wide_pack = [jnp.concatenate([w[6], w[7]], axis=1).astype(BF) for w in (one, two)]
    down_pack = [w[8].T.astype(BF) for w in (one, two)]
    gain_pack = pack_gains([one[0], one[5], two[0], two[5]])

    attn1 = attn_forward(
        0, 0, states_in, tables, None, attn_pack[0], None, [wide_pack[0], down_pack[0]],
        [1, 0, 1, 0, 1, 0, 1, 1, 1, 1], gain_pack,
    )
    gains = attn1["gains"]
    wide1, down1 = fetched(attn1, 2)
    mlp1 = mlp_forward(
        0, 1, attn1["middle"], gains, (wide_pack[0], wide1), (down_pack[0], down1),
        [attn_pack[1], down_pack[1]], [1, 1, 1, 1, 2, 1, 1],
    )
    attn2_blocks, down2 = fetched(mlp1, 2)
    attn2 = attn_forward(
        1, 2, mlp1["result"], tables, gains, attn_pack[1], attn2_blocks, [wide_pack[1]],
        [1, 0, 1, 0, 0, 1, 0, 0, 1, 0, 0],
    )
    (wide2,) = fetched(attn2, 1)
    mlp2 = mlp_forward(1, 3, attn2["middle"], gains, (wide_pack[1], wide2), (down_pack[1], down2), [], [])

    back_mlp2 = mlp_backward(
        1, 4, cotangent, attn2["middle"], gains, mlp2, (wide_pack[1], wide2), (down_pack[1], down2), [], []
    )
    back_attn2 = attn_backward(
        1, 5, back_mlp2["grad_out"], mlp1["result"], gains, tables, attn2, (attn_pack[1], attn2_blocks),
        [back_mlp2["wide_out"]], [1, 0, 0, 1, 0, 1, 0, 0, 0, 1],
    )
    back_mlp1 = mlp_backward(
        0, 6, back_attn2["grad_out"], attn1["middle"], gains, mlp1, (wide_pack[0], wide1), (down_pack[0], down1),
        [back_mlp2["grads_out"], back_attn2["grads_out"]], [1, 1, 1, 1, 1, 1, 1, 0, 1, 0, 1],
    )
    back_attn1 = attn_backward(
        0, 7, back_mlp1["grad_out"], states_in, gains, tables, attn1, (attn_pack[0], attn1["blocks"]),
        [back_mlp1["wide_out"]], [1, 0, 0, 1, 0, 1, 0, 0, 0, 1],
    )
    last = last_sums(
        8,
        [back_attn1["dgain"], back_mlp1["dgain"], back_attn2["dgain"], back_mlp2["dgain"]],
        [back_mlp1["grads_out"], back_attn1["grads_out"]],
    )
    (wide_total2,) = totals(back_attn2, 1)
    down_total2, attn_total2 = totals(back_mlp1, 2)
    (wide_total1,) = totals(back_attn1, 1)
    down_total1, attn_total1 = totals(last, 2)
    gain_total = last["gain_total"]
    depth = down_total1.shape[0]
    bounds = [0]
    for w in one[1:4]:
        bounds.append(bounds[-1] + w.shape[1])
    units = one[6].shape[1]
    outs = [mlp2["result"], back_attn1["grad_out"]]
    for level, (attn_total, wide_total, down_total) in enumerate(
        ((attn_total1, wide_total1, down_total1), (attn_total2, wide_total2, down_total2))
    ):
        outs.append(gain_total[2 * level, 0:depth])
        outs += [attn_total[:, low:high] for low, high in zip(bounds, bounds[1:])]
        outs.append(attn_total[:, bounds[-1] :].T)
        outs.append(gain_total[2 * level + 1, 0:depth])
        outs += [wide_total[:, 0:units], wide_total[:, units:], down_total.T]
    return tuple(outs)


def solution(mesh):
    layer = (
        P("dp"),
        P("dp", "tensor"),
        P("dp", "tensor"),
        P("dp", "tensor"),
        P("tensor", "dp"),
        P("dp"),
        P("dp", "tensor"),
        P("dp", "tensor"),
        P("tensor", "dp"),
    )
    rows = P(("dp", "tensor"), None)
    return jax.shard_map(
        body,
        mesh=mesh,
        in_specs=(rows, P("dp"), *layer, *layer, rows),
        out_specs=(rows, rows, *layer, *layer),
        check_vma=False,
    )
```

```python
import functools
import math
import types

import jax
import jax.numpy as jnp
import numpy as np
from jax import lax
from jax.experimental import pallas as pl
from jax.experimental.pallas import tpu as pltpu
from jax.sharding import PartitionSpec as P

HEAD_DIM = 96
HALF = HEAD_DIM // 2
BLOCK = 256
PAD = 128
GAIN_ROWS = 16
LIMIT = 60 * 1024 * 1024

epsilon = 1e-05
rope_base = 100000.0
masked_value = -1e30
scale = 1.0 / math.sqrt(HEAD_DIM)

BF = jnp.bfloat16
F32 = jnp.float32
MESH = pl.DeviceIdType.MESH
ANY = pl.BlockSpec(memory_space=pl.ANY)
VM = pl.BlockSpec(memory_space=pltpu.VMEM)


def nn(left, right):
    return lax.dot_general(left, right, (((1,), (0,)), ((), ())), preferred_element_type=F32)


def nt(left, right):
    return lax.dot_general(left, right, (((1,), (1,)), ((), ())), preferred_element_type=F32)


def tn(left, right):
    return lax.dot_general(left, right, (((0,), (0,)), ((), ())), preferred_element_type=F32)


def tile(index, size):
    if isinstance(index, int):
        return pl.ds(index * size, size)
    return pl.ds(pl.multiple_of(index * size, size), size)


def each(count, body):
    def step(index, carry):
        body(index)
        return carry

    lax.fori_loop(0, count, step, 0)


class Group:
    def __init__(self):
        self.me = lax.axis_index("tensor")
        self.core_bit = lax.rem(self.me, 2)
        self.chip = self.me // 2
        self.core = self.me + 1 - 2 * self.core_bit
        self.other = lax.rem(self.me + 2, 4)

    def greet(self, barrier):
        for near in (self.core, self.other):
            pl.semaphore_signal(barrier, inc=1, device_id={"tensor": near}, device_id_type=MESH)

    def peers(self):
        return 2

    def remote(self, source, target, send, recv, device):
        return pltpu.make_async_remote_copy(
            src_ref=source,
            dst_ref=target,
            send_sem=send,
            recv_sem=recv,
            device_id={"tensor": device},
            device_id_type=MESH,
        )


class Gather:
    def __init__(self, group, full, send, recv):
        self.group, self.full, self.send, self.recv = group, full, send, recv
        half = full.shape[1] // 2
        mine = full.at[group.me]
        self.to_core = group.remote(mine, mine, send.at[0], recv.at[0], group.core)
        self.to_other = []
        self.onward = []
        for part in range(2):
            piece = full.at[group.me, pl.ds(part * half, half)]
            self.to_other.append(
                group.remote(piece, piece, send.at[1 + part], recv.at[1 + part], group.other)
            )
            piece = full.at[group.other, pl.ds(part * half, half)]
            self.onward.append(
                group.remote(piece, piece, send.at[3 + part], recv.at[3 + part], group.core)
            )

    def start(self):
        for copy in self.to_other:
            copy.start()
        self.to_core.start()

    def wait_chip(self):
        self.to_core.wait_recv()

    def forward(self):
        for here, there in zip(self.to_other, self.onward):
            here.wait_recv()
            there.start()

    def wait_other(self):
        for copy in self.onward:
            copy.wait_recv()

    def finish(self):
        self.to_core.wait_send()
        for copy in self.to_other + self.onward:
            copy.wait_send()


class Scatter:
    def __init__(self, group, parts, near, away, landed, send, recv):
        self.group, self.parts, self.near = group, parts, near
        self.away, self.landed = away, landed
        self.to_core = [
            group.remote(
                parts.at[turn, 1 - group.core_bit], near.at[turn], send.at[turn], recv.at[turn], group.core
            )
            for turn in range(2)
        ]
        half = away.shape[0] // 2
        self.to_other = [
            group.remote(
                away.at[pl.ds(part * half, half)],
                landed.at[pl.ds(part * half, half)],
                send.at[2 + part],
                recv.at[2 + part],
                group.other,
            )
            for part in range(2)
        ]

    def rows_of(self, turn):
        return 1 - self.group.chip if turn == 0 else self.group.chip

    def send_core(self, turn):
        self.to_core[turn].start()

    def send_away(self):
        self.to_core[0].wait_recv()
        half = self.away.shape[0] // 2
        for part in range(2):

            def add(index):
                rows = pl.ds(pl.multiple_of(part * half + index * 32, 32), 32)
                total = self.parts[0, self.group.core_bit, rows, :].astype(F32) + self.near[
                    0, rows, :
                ].astype(F32)
                self.away[rows, :] = total.astype(BF)

            each(half // 32, add)
            self.to_other[part].start()

    def wait(self):
        self.to_core[1].wait_recv()
        for copy in self.to_other:
            copy.wait_recv()

    def total(self, rows):
        return (
            self.parts[1, self.group.core_bit, rows, :].astype(F32)
            + self.near[1, rows, :].astype(F32)
            + self.landed[rows, :].astype(F32)
        )

    def finish(self):
        for copy in self.to_core + self.to_other:
            copy.wait_send()


class Line:
    def __init__(self, n_dp):
        mine = lax.axis_index("dp")
        self.count = n_dp // 2
        self.z, self.x = mine // 2, lax.rem(mine, 2)
        self.mine = mine
        self.pair = self.z * 2 + 1 - self.x
        self.up = jnp.minimum(self.z + 1, self.count - 1) * 2 + self.x
        self.down = jnp.maximum(self.z - 1, 0) * 2 + self.x
        self.has_up = self.z + 1 < self.count
        self.has_down = self.z > 0

    def greet(self, barrier):
        def hello(device):
            pl.semaphore_signal(barrier, inc=1, device_id={"dp": device}, device_id_type=MESH)

        hello(self.pair)
        pl.when(self.has_up)(lambda: hello(self.up))
        pl.when(self.has_down)(lambda: hello(self.down))

    def peers(self):
        return 1 + jnp.minimum(self.count - 1 - self.z, 1) + jnp.minimum(self.z, 1)

    def remote(self, source, target, send, recv, device):
        return pltpu.make_async_remote_copy(
            src_ref=source, dst_ref=target, send_sem=send, recv_sem=recv,
            device_id={"dp": device}, device_id_type=MESH)


class Fetch:
    def __init__(self, line, own, blocks, send, recv):
        self.line, self.own, self.blocks, self.send, self.recv = line, own, blocks, send, recv
        rows = own.shape[0]
        self.edge = max(rows // 6 // 16, 1) * 16 if rows > 32 else 0
        self.rows = rows

    @staticmethod
    def scratch(n_dp):
        return [pltpu.SemaphoreType.DMA((n_dp, 5))] * 2

    def low(self, step):
        return jnp.maximum(self.line.z - step, 0) * 2

    def high(self, step):
        return jnp.minimum(self.line.z + step, self.line.count - 1) * 2

    def copy(self, slot, block, device, way, rows=None):
        source = self.own if slot == 0 and way < 3 else self.blocks.at[block]
        target = self.blocks.at[block]
        if rows is not None:
            source, target = source.at[rows], target.at[rows]
        return self.line.remote(
            source, target, self.send.at[slot, way], self.recv.at[slot, way], device
        )

    def upward(self, step):
        return self.copy(step, self.low(step) + self.line.x, self.line.up, 1)

    def downward(self, step):
        return self.copy(step, self.high(step) + self.line.x, self.line.down, 2)

    def edge_up(self, step):
        block = self.low(step) + 1 - self.line.x
        return self.copy(step, block, self.line.up, 3, pl.ds(0, self.edge))

    def edge_down(self, step):
        block = self.high(step) + 1 - self.line.x
        return self.copy(step, block, self.line.down, 4, pl.ds(0, self.edge))

    def sideways(self, step, low):
        line = self.line
        rows = pl.ds(self.edge, self.rows - self.edge) if step and self.edge else None
        if low:
            return self.copy(step, self.low(step) + line.x, line.pair, 0, rows)
        return self.copy(line.count + step, self.high(step) + line.x, line.pair, 0, rows)

    def upward_in(self, step):
        return self.copy(step - 1, self.low(step) + self.line.x, self.line.up, 1)

    def downward_in(self, step):
        return self.copy(step - 1, self.high(step) + self.line.x, self.line.down, 2)

    def edge_up_in(self, step):
        block = self.low(step) + 1 - self.line.x
        return self.copy(step - 1, block, self.line.up, 3, pl.ds(0, self.edge))

    def edge_down_in(self, step):
        block = self.high(step) + 1 - self.line.x
        return self.copy(step - 1, block, self.line.down, 4, pl.ds(0, self.edge))

    def start(self):
        line = self.line
        pl.when(line.has_up)(lambda: self.upward(0).start())
        pl.when(line.has_down)(lambda: self.downward(0).start())
        self.sideways(0, True).start()

    def step(self, step):
        line = self.line

        @pl.when(line.z >= step)
        def _():
            self.upward_in(step).wait_recv()
            pl.when(line.has_up)(lambda: self.upward(step).start())
            self.sideways(step, True).start()

        @pl.when(line.z + step < line.count)
        def _():
            self.downward_in(step).wait_recv()
            pl.when(line.has_down)(lambda: self.downward(step).start())
            self.sideways(step, False).start()

        self.edges(step - 1)

    def edges(self, step):
        line = self.line
        if step == 0:
            self.sideways(0, True).wait_recv()
        if not self.edge:
            return
        if step == 0:
            pl.when(line.has_up)(lambda: self.edge_up(0).start())
            pl.when(line.has_down)(lambda: self.edge_down(0).start())
            return

        @pl.when(line.z >= step)
        def _():
            self.edge_up_in(step).wait_recv()
            pl.when(line.has_up)(lambda: self.edge_up(step).start())

        @pl.when(line.z + step < line.count)
        def _():
            self.edge_down_in(step).wait_recv()
            pl.when(line.has_down)(lambda: self.edge_down(step).start())

    def finish(self):
        line = self.line
        self.edges(line.count - 1)
        for step in range(line.count):

            @pl.when(line.z >= step)
            def _():
                @pl.when(line.has_up)
                def _():
                    self.upward(step).wait_send()
                    if self.edge:
                        self.edge_up(step).wait_send()

                self.sideways(step, True).wait_send()
                if step:
                    self.sideways(step, True).wait_recv()

            @pl.when(line.z + step < line.count)
            def _():
                @pl.when(line.has_down)
                def _():
                    self.downward(step).wait_send()
                    if self.edge:
                        self.edge_down(step).wait_send()

                if step:
                    self.sideways(step, False).wait()

    def actions(self):
        steps = [functools.partial(self.step, step) for step in range(1, self.line.count)]
        return [self.start] + steps + [self.finish]


class Reduce:
    def __init__(self, line, blocks, out, pair_in, line_in, mine, x_send, x_recv, z_send, z_recv, local):
        self.line, self.blocks, self.out = line, blocks, out
        self.pair_in, self.line_in, self.mine = pair_in, line_in, mine
        self.x_send, self.x_recv, self.z_send, self.z_recv, self.local = x_send, x_recv, z_send, z_recv, local

    @staticmethod
    def scratch(n_dp, rows, columns):
        count = n_dp // 2
        dma = pltpu.SemaphoreType.DMA
        return [
            pltpu.VMEM((count, rows, columns), BF),
            pltpu.VMEM((count + 1, rows, columns), BF),
            pltpu.VMEM((2, rows, columns), BF),
            dma((count,)), dma((count,)), dma((count,)), dma((count + 1,)), dma((2,)),
        ]

    def sideways(self, target):
        line = self.line
        return line.remote(self.blocks.at[target * 2 + 1 - line.x], self.pair_in.at[target],
                           self.x_send.at[target], self.x_recv.at[target], line.pair)

    def along(self, target, up):
        line = self.line
        slot = target + 1 if up else target
        return line.remote(self.pair_in.at[target], self.line_in.at[slot],
                           self.z_send.at[target], self.z_recv.at[slot], line.up if up else line.down)

    def load(self, target, slot):
        return pltpu.make_async_copy(self.blocks.at[target * 2 + self.line.x], self.mine.at[slot], self.local.at[slot])

    def above(self, step):
        return self.line.z + step < self.line.count, jnp.minimum(self.line.z + step, self.line.count - 1)

    def below(self, step):
        return self.line.z - step >= 0, jnp.maximum(self.line.z - step, 0)

    def fetch(self, step):
        there, target = self.above(step)
        pl.when(there)(lambda: self.load(target, 0).start())
        if step:
            there2, target2 = self.below(step)
            pl.when(there2)(lambda: self.load(target2, 1).start())

    def start(self):
        line = self.line
        for step in range(line.count - 1, 0, -1):
            for there, target in (self.above(step), self.below(step)):
                pl.when(there)(lambda: self.sideways(target).start())
        self.sideways(line.z).start()
        self.fetch(line.count - 1)

    def add(self, target, slot, more):
        rows = self.out.shape[0]

        def some(index):
            part = pl.ds(pl.multiple_of(index * 16, 16), 16)
            total = self.pair_in[target, part, :].astype(F32) + self.mine[slot, part, :].astype(F32)
            for other in more:
                total += self.line_in[other, part, :].astype(F32)
            self.pair_in[target, part, :] = total.astype(BF)

        each(rows // 16, some)

    def pass_on(self, target, slot, up):
        line = self.line
        self.load(target, slot).wait()
        self.sideways(target).wait_recv()
        fed = line.has_down if up else line.has_up

        @pl.when(fed)
        def _():
            self.along(target, up).wait_recv()
            self.add(target, slot, [target + 1 if up else target])

        pl.when(jnp.logical_not(fed))(lambda: self.add(target, slot, []))
        self.along(target, up).start()

    def step(self, step):
        for slot, (there, target) in enumerate((self.above(step), self.below(step))):
            pl.when(there)(lambda: self.pass_on(target, slot, slot == 0))
        self.fetch(step - 1)

    def close(self):
        line = self.line
        z = line.z
        self.load(z, 0).wait()
        self.sideways(z).wait_recv()
        rows = self.out.shape[0]

        def final(more):
            def some(index):
                part = pl.ds(pl.multiple_of(index * 16, 16), 16)
                total = self.pair_in[z, part, :].astype(F32) + self.mine[0, part, :].astype(F32)
                for other in more:
                    total += self.line_in[other, part, :].astype(F32)
                self.out[part, :] = total

            each(rows // 16, some)

        pl.when(line.has_down)(lambda: self.along(z, True).wait_recv())
        pl.when(line.has_up)(lambda: self.along(z, False).wait_recv())
        pl.when(jnp.logical_not(line.has_down))(lambda: final([z]))
        pl.when(jnp.logical_not(line.has_up))(lambda: final([z + 1]))
        pl.when(line.has_down & line.has_up)(lambda: final([z, z + 1]))
        for step in range(line.count - 1, 0, -1):
            for up, (there, target) in ((True, self.above(step)), (False, self.below(step))):

                @pl.when(there)
                def _():
                    self.sideways(target).wait_send()
                    self.along(target, up).wait_send()

        self.sideways(z).wait_send()

    def actions(self):
        return [self.start] + [functools.partial(self.step, s) for s in range(self.line.count - 1, 0, -1)] + [self.close]


def spread(block, depth, lanes, width):
    row = lax.broadcasted_iota(jnp.int32, (lanes, width), 0)
    column = lax.broadcasted_iota(jnp.int32, (lanes, width), 1)
    hit = (column - row == block * depth) & (row < depth)
    return jnp.where(hit, 1.0, 0.0).astype(BF)


def turn_half(values):
    return pltpu.roll(values, PAD // 2, 1)


def meet(*circles):
    barrier = pltpu.get_barrier_semaphore()
    for circle in circles:
        circle.greet(barrier)
    pl.semaphore_wait(barrier, sum(circle.peers() for circle in circles))


class Weights:
    def __init__(self, line, own, blocks, held, sems, first=0):
        self.copies = []
        columns = pl.ds(first, own.shape[1])
        depth = own.shape[0]
        count = line.count
        for index in range(2 * count):
            shift, side = index // 2, index % 2
            block = lax.rem(line.z + shift, count) * 2 + lax.rem(line.x + side, 2)
            source = blocks.at[block] if index else own
            rows = pl.ds(pl.multiple_of(block * depth, 16), depth)
            self.copies.append(pltpu.make_async_copy(source, held.at[rows, columns], sems.at[index]))

    def start(self):
        for copy in self.copies:
            copy.start()

    def wait(self):
        for copy in self.copies:
            copy.wait()


class Pump:
    def __init__(self, tasks, plan):
        self.steps = [step for together in zip(*[task.actions() for task in tasks]) for step in together]
        self.plan = list(plan)

    def __call__(self):
        count = self.plan.pop(0) if self.plan else 0
        self.do(count)

    def do(self, count):
        for step in self.steps[:count]:
            step()
        self.steps = self.steps[count:]

    def rest(self):
        self.do(len(self.steps))


def fetches_of(line, r, count):
    return [
        Fetch(
            line,
            getattr(r, f"own{i}"),
            getattr(r, f"blocks{i}"),
            getattr(r, f"fetch_send{i}"),
            getattr(r, f"fetch_recv{i}"),
        )
        for i in range(count)
    ]


def reduces_of(line, r, count):
    return [
        Reduce(
            line,
            getattr(r, f"sum{i}"),
            getattr(r, f"total{i}"),
            *[getattr(r, f"reduce{i}_{j}") for j in range(8)],
        )
        for i in range(count)
    ]


def comm_of(r):
    group = Group()
    gather = Gather(group, r.full, r.g_send, r.g_recv)
    scatter = Scatter(group, r.parts, r.near, r.away, r.landed, r.s_send, r.s_recv)
    return group, gather, scatter


def out_columns(scatter, turn, left_rows, right_tile, columns):
    product = nt(left_rows, right_tile)
    rows = product.shape[0] // 2
    scatter.parts[turn, 0, :, columns] = product[:rows].astype(BF)
    scatter.parts[turn, 1, :, columns] = product[rows:].astype(BF)


def norm_rows(source, gain, full, slot):
    def norm(index):
        part = tile(index, 32)
        values = source[part, :]
        factor = lax.rsqrt(jnp.mean(values * values, axis=-1, keepdims=True) + epsilon)
        full[slot, part, :] = (values * factor * gain).astype(BF)

    each(source.shape[0] // 32, norm)


def add_rows(scatter, source, target):
    def close(index):
        part = tile(index, 32)
        target[part, :] = source[part, :] + scatter.total(part)

    each(source.shape[0] // 32, close)


def pack_attn(query, key, value, output, target):
    width, each_kv = query.shape[1], key.shape[1]
    target[:, 0:width] = query[...].astype(BF)
    both = jnp.concatenate([key[...], value[...]], axis=1)
    target[:, width : width + 2 * each_kv] = both.astype(BF)
    target[:, width + 2 * each_kv :] = output[...].astype(BF)


def count_rows(documents, below):
    hits = jnp.where(documents < below, 1.0, 0.0)
    return jnp.sum(jnp.sum(hits, axis=1, keepdims=True), axis=0, keepdims=True).astype(jnp.int32)


def starts_of(marks, places):
    head, body_end = marks[0:1, 0:1], marks[1:2, 0:1]
    return jnp.where(places < head, 0, jnp.where(places < body_end, head, body_end))


def make_tables(r):
    marks = jnp.concatenate([count_rows(r.documents[...], 1), count_rows(r.documents[...], 2)], axis=0)
    r.marks[0:2, :] = jnp.broadcast_to(marks, (2, PAD))
    r.marks[2:, :] = jnp.zeros((6, PAD), jnp.int32)

    def some(index):
        where = tile(index, 128)
        places = lax.broadcasted_iota(jnp.int32, (128, PAD), 0) + index * 128
        offset = places - starts_of(r.marks, places)
        angles = offset.astype(F32) * r.freqs[0:1, :]
        r.cosine[where, :] = jnp.cos(angles)
        r.sine[where, :] = jnp.sin(angles) * r.freqs[1:2, :]

    each(r.cosine.shape[0] // 128, some)


def attn_forward_kernel(first, level, fetch_count, plan, r):
    rows, width = r.x.shape
    n_dp, depth = r.w_sems.shape[0], r.own.shape[0]
    line = Line(n_dp)
    group, gather, scatter = comm_of(r)
    tasks = fetches_of(line, r, fetch_count)
    weights = Weights(line, r.own, r.blocks, r.held, r.w_sems)
    circles = (group, line) if first or tasks else (group,)
    meet(*circles)
    if first:
        raw = {}
        for name in ("gate0", "up0", "down0", "query1", "key1", "value1", "output1", "gate1", "up1", "down1"):
            raw[name] = pltpu.make_async_copy(
                getattr(r, "raw_" + name), getattr(r, name), r.raw_sems.at[len(raw)]
            )
            raw[name].start()
        lanes = r.gain_own.shape[1]
        r.gain_raw[...] = jnp.zeros_like(r.gain_raw)
        for row in range(4):
            r.gain_raw[row : row + 1, 0:depth] = getattr(r, f"gain{row}")[...]
        r.gain_own[...] = r.gain_raw[...].astype(BF)
        pack_attn(r.raw_query0, r.raw_key0, r.raw_value0, r.raw_output0, r.own)
        gain_fetch = Fetch(line, r.gain_own, r.gain_blocks, r.gain_send, r.gain_recv)
        weight_fetch = Fetch(line, r.own, r.blocks, r.weight_send, r.weight_recv)
        gain_fetch.start()
        weight_fetch.start()
        for step in gain_fetch.actions()[1:]:
            step()
        r.gains[...] = jnp.zeros_like(r.gains)

        def gather_gain(block):
            chosen = spread(block, depth, lanes, width)

            @pl.when(block == line.mine)
            def _():
                r.gains[...] += nn(r.gain_own[...], chosen)

            @pl.when(block != line.mine)
            def _():
                r.gains[...] += nn(r.gain_blocks[block], chosen)

        each(n_dp, gather_gain)
        norm_rows(r.x, r.gains[2 * level : 2 * level + 1, :], r.full, group.me)
        gather.start()
        for name in ("gate0", "up0"):
            raw[name].wait()
        r.own0[...] = r.gate0[...].astype(BF)
        r.own1[...] = r.up0[...].astype(BF)
        for step in weight_fetch.actions()[1:-1]:
            step()
        pump = Pump(tasks, plan)
        pump()
        make_tables(r)
        for name in list(raw)[2:]:
            raw[name].wait()
        pack_attn(r.query1, r.key1, r.value1, r.output1, r.attn_pack1)
        r.down_pack0[...] = r.down0[...].astype(BF)
        r.down_pack1[...] = r.down1[...].astype(BF)
        r.gate_pack1[...] = r.gate1[...].astype(BF)
        r.up_pack1[...] = r.up1[...].astype(BF)
        weight_fetch.finish()
        weights.start()
    else:
        weights.start()
        pump = Pump(tasks, plan)
        pump()
        norm_rows(r.x, r.gains[2 * level : 2 * level + 1, :], r.full, group.me)
        gather.start()
    weights.wait()
    place = r.place[...]
    heads = place.shape[1] // PAD
    compact_width, head_width = place.shape
    padded, qkv, mixed, compact, held = r.padded, r.qkv, r.mixed, r.compact, r.held

    def pad(index):
        part = tile(index, 256)
        padded[part, 0:head_width] = nn(held[part, 0:compact_width], place).astype(BF)
        padded[part, head_width : 2 * head_width] = nn(
            held[part, compact_width : 2 * compact_width], place
        ).astype(BF)

    each(width // 256, pad)

    def project(chip):
        left = r.full[pl.ds(2 * chip, 2)].reshape(2 * rows, width)
        where = tile(chip, 2 * rows)
        cosine, sine = r.cosine[where, :], r.sine[where, :]

        def turned(index):
            columns = tile(index, 2 * PAD)
            product = nn(left, padded[:, columns])
            for half in range(2):
                u = product[:, half * PAD : (half + 1) * PAD]
                qkv[where, tile(2 * index + half, PAD)] = (u * cosine + turn_half(u) * sine).astype(BF)

        each(3 * heads // 4, turned)
        columns = pl.ds(3 * heads // 2 * PAD, heads // 2 * PAD)
        qkv[where, columns] = nn(left, padded[:, columns]).astype(BF)

    gather.wait_chip()
    project(group.chip)
    pump()
    gather.forward()
    pump()
    gather.wait_other()
    project(1 - group.chip)
    copies = [
        pltpu.make_async_copy(r.full, r.a_out, r.out_sems.at[0]),
        pltpu.make_async_copy(qkv, r.qkv_out, r.out_sems.at[1]),
    ]
    for copy in copies:
        copy.start()
    pump()
    kv_at = heads * PAD
    value_at = kv_at + heads // 2 * PAD
    for turn in range(4):
        prob = getattr(r, f"prob{turn}")
        reach = prob.shape[2]
        where = pl.ds(turn * rows, rows)
        places = lax.broadcasted_iota(jnp.int32, (rows, PAD), 0) + turn * rows
        begin = starts_of(r.marks, places)
        head, body_end = r.marks[0:1, 0:1], r.marks[1:2, 0:1]
        end = jnp.where(places < head, head, jnp.where(places < body_end, body_end, 4 * rows))
        end = jnp.minimum(begin + ((places - begin) // BLOCK + 1) * BLOCK, end)
        place_of = lax.broadcasted_iota(jnp.int32, (rows, reach), 1)
        inside = (place_of >= begin[:, 0:1]) & (place_of < end[:, 0:1])
        r.bias[:, 0:reach] = jnp.where(inside, 0.0, masked_value)

        def attend(head):
            query = qkv[where, tile(head, PAD)]
            key = qkv[0:reach, pl.ds(kv_at + head // 2 * PAD, PAD)]
            value = qkv[0:reach, pl.ds(value_at + head // 2 * PAD, PAD)]
            scores = nt(query, key) * scale + r.bias[:, 0:reach]
            exponent = jnp.exp(scores - jnp.max(scores, axis=-1, keepdims=True))
            summed = jnp.sum(exponent, axis=-1, keepdims=True)
            low = (exponent * (1.0 / summed)).astype(BF)
            prob[head] = low
            mixed[where, tile(head, PAD)] = nn(low, value).astype(BF)

        for head in range(heads):
            attend(head)
        copy = pltpu.make_async_copy(prob, getattr(r, f"p_out{turn}"), r.out_sems.at[2 + turn])
        copy.start()
        copies.append(copy)
        compact[where, :] = nt(mixed[where, :], place).astype(BF)
        pump()
    copy = pltpu.make_async_copy(compact, r.o_out, r.out_sems.at[6])
    copy.start()
    copies.append(copy)
    for turn in range(2):
        left = compact[tile(scatter.rows_of(turn), 2 * rows), :]

        def part_of(index):
            columns = tile(index, 256)
            out_columns(scatter, turn, left, held[columns, 2 * compact_width :], columns)

        each(width // 256, part_of)
        scatter.send_core(turn)
        if turn == 0:
            scatter.send_away()
        pump()
    scatter.wait()
    pump()
    add_rows(scatter, r.x, r.middle)
    pump.rest()
    gather.finish()
    scatter.finish()
    for copy in copies:
        copy.wait()


def wide_of(line, r):
    return [
        Weights(line, r.gate_own, r.gate_blocks, r.wide, r.gate_sems),
        Weights(line, r.up_own, r.up_blocks, r.wide, r.up_sems, r.gate_own.shape[1]),
    ]


def mlp_forward_kernel(level, fetch_count, plan, r):
    rows, width = r.middle.shape
    units = r.hid.shape[1]
    line = Line(r.w_sems.shape[0])
    group, gather, scatter = comm_of(r)
    down = Fetch(line, r.own, r.blocks, r.down_send, r.down_recv)
    down_steps = down.actions()[1:-1]
    wide, held, gu, hid = r.wide, r.held, r.gu, r.hid
    wide_weights = wide_of(line, r)
    weights = Weights(line, r.own, r.blocks, held, r.w_sems)
    meet(group, line)
    down.start()
    for copy in wide_weights:
        copy.start()
    pump = Pump(fetches_of(line, r, fetch_count), plan)
    pump()
    norm_rows(r.middle, r.gains[2 * level + 1 : 2 * level + 2, :], r.full, group.me)
    gather.start()
    for copy in wide_weights:
        copy.wait()

    def expand(chip):
        left = r.full[pl.ds(2 * chip, 2)].reshape(2 * rows, width)
        where = tile(chip, 2 * rows)

        def unit(index):
            columns = tile(index, 256)
            further = pl.ds(pl.multiple_of(units + index * 256, 256), 256)
            gate = nn(left, wide[:, columns])
            up = nn(left, wide[:, further])
            hid[where, columns] = (gate / (1.0 + jnp.exp(-gate)) * up).astype(BF)
            gu[where, columns] = gate.astype(BF)
            gu[where, further] = up.astype(BF)

        each(units // 256, unit)

    gather.wait_chip()
    expand(group.chip)
    for step in down_steps[:1]:
        step()
    gather.forward()
    for step in down_steps[1:2]:
        step()
    pump()
    gather.wait_other()
    expand(1 - group.chip)
    for step in down_steps[2:]:
        step()
    pump()
    copies = [
        pltpu.make_async_copy(r.full, r.m_out, r.out_sems.at[0]),
        pltpu.make_async_copy(gu, r.gu_out, r.out_sems.at[1]),
        pltpu.make_async_copy(hid, r.hid_out, r.out_sems.at[2]),
    ]
    for copy in copies:
        copy.start()
    down.finish()
    weights.start()
    weights.wait()
    for turn in range(2):
        left = hid[tile(scatter.rows_of(turn), 2 * rows), :]

        def part_of(index):
            columns = tile(index, 256)
            out_columns(scatter, turn, left, held[columns, :], columns)

        each(width // 256, part_of)
        scatter.send_core(turn)
        if turn == 0:
            scatter.send_away()
        pump()
    scatter.wait()
    pump()
    add_rows(scatter, r.middle, r.result)
    pump.rest()
    gather.finish()
    scatter.finish()
    for copy in copies:
        copy.wait()


def weight_grads(source, right, target, columns):
    width = source.shape[-1]
    depth = target.shape[1]
    chunk = math.lcm(depth, PAD)

    def some(index):
        left = source[..., tile(index, chunk)].reshape(right.shape[0], chunk)
        product = tn(left, right[...]).astype(BF)
        for part in range(chunk // depth):
            rows = slice(part * depth, (part + 1) * depth)
            target[index * (chunk // depth) + part, :, columns] = product[rows]

    each(width // chunk, some)


def close_back(scatter, grad_in_ref, state_ref, gain, grad_out, dgain):
    rows = state_ref.shape[0]
    dgain[...] = jnp.zeros_like(dgain)

    def close(index):
        part = tile(index, 32)
        values = state_ref[part, :]
        factor = lax.rsqrt(jnp.mean(values * values, axis=-1, keepdims=True) + epsilon)
        normed = values * factor
        grad_in = scatter.total(part)
        dgain[...] += jnp.sum((grad_in * normed).reshape(4, 8, -1), axis=0)
        grad_norm = grad_in * gain
        inner = jnp.mean(grad_norm * normed, axis=-1, keepdims=True)
        grad_out[part, :] = grad_in_ref[part, :] + factor * (grad_norm - normed * inner)

    each(rows // 32, close)


def mlp_backward_kernel(level, reduce_count, plan, r):
    rows, width = r.middle.shape
    units = r.hid.shape[1]
    n_dp = r.w_sems.shape[0]
    line = Line(n_dp)
    group, gather, scatter = comm_of(r)
    wide, held, gu, hid = r.wide, r.held, r.gu, r.hid
    weights = [
        Weights(line, r.own, r.blocks, held, r.w_sems),
        *wide_of(line, r),
    ]
    fetches = [
        pltpu.make_async_copy(r.hid_in, hid, r.in_sems.at[2]),
        pltpu.make_async_copy(r.gu_in, gu, r.in_sems.at[1]),
        pltpu.make_async_copy(r.m_in, r.m_full, r.in_sems.at[0]),
    ]
    down = Reduce(line, r.grads, r.down_total, *[getattr(r, f"down{j}") for j in range(8)])
    meet(group, line)
    pump = Pump(reduces_of(line, r, reduce_count), plan)
    pump.steps += down.actions()[1:]
    pump()
    for copy in weights[:1] + fetches + weights[1:]:
        copy.start()
    r.full[group.me] = r.grad[...].astype(BF)
    gather.start()
    for copy in weights[:1] + fetches[:2]:
        copy.wait()

    def inward(chip):
        left = r.full[pl.ds(2 * chip, 2)].reshape(2 * rows, width)
        where = tile(chip, 2 * rows)

        def unit(index):
            columns = tile(index, 256)
            further = pl.ds(pl.multiple_of(units + index * 256, 256), 256)
            grad = nn(left, held[:, columns])
            gate = gu[where, columns].astype(F32)
            up = gu[where, further].astype(F32)
            sig = 1.0 / (1.0 + jnp.exp(-gate))
            gu[where, columns] = (grad * up * sig * (1.0 + gate * (1.0 - sig))).astype(BF)
            gu[where, further] = (grad * gate * sig).astype(BF)

        each(units // 256, unit)

    gather.wait_chip()
    inward(group.chip)
    pump()
    gather.forward()
    pump()
    gather.wait_other()
    weight_grads(r.full, hid, r.grads, slice(0, units))
    down.start()
    inward(1 - group.chip)
    for copy in weights[1:] + fetches[2:]:
        copy.wait()
    pump()
    for turn in range(2):
        where = tile(scatter.rows_of(turn), 2 * rows)

        def part_of(index):
            columns = tile(index, 256)
            out_columns(scatter, turn, gu[where, :], wide[columns, :], columns)

        each(width // 256, part_of)
        scatter.send_core(turn)
        if turn == 0:
            scatter.send_away()
        pump()
    for part in range(2):
        columns = slice(part * units, (part + 1) * units)
        weight_grads(r.m_full, gu.at[:, columns], r.wide_grads, columns)
        pump()
    copies = [pltpu.make_async_copy(r.wide_grads, r.wide_out, r.out_sems.at[0])]
    copies[0].start()
    scatter.wait()
    pump()
    close_back(
        scatter, r.grad, r.middle, r.gains[2 * level + 1 : 2 * level + 2, :], r.grad_out, r.dgain
    )
    pump.rest()
    gather.finish()
    scatter.finish()
    for copy in copies:
        copy.wait()


def attn_backward_kernel(level, reduce_count, plan, r):
    rows, width = r.x.shape
    n_dp = r.w_sems.shape[0]
    depth = width // n_dp
    line = Line(n_dp)
    group, gather, scatter = comm_of(r)
    tasks = reduces_of(line, r, reduce_count)
    held, qkv, compact = r.held, r.qkv, r.compact
    probs = [getattr(r, f"prob{turn}") for turn in range(4)]
    weights = Weights(line, r.own, r.blocks, held, r.w_sems)
    fetches = [
        pltpu.make_async_copy(r.a_in, r.a_full, r.in_sems.at[0]),
        pltpu.make_async_copy(r.o_in, compact, r.in_sems.at[1]),
        pltpu.make_async_copy(r.qkv_in, qkv, r.in_sems.at[2]),
    ] + [
        pltpu.make_async_copy(getattr(r, f"p_in{turn}"), probs[turn], r.in_sems.at[3 + turn])
        for turn in range(4)
    ]
    meet(*((group, line) if tasks else (group,)))
    weights.start()
    for copy in fetches:
        copy.start()
    pump = Pump(tasks, plan)
    pump()
    r.full[group.me] = r.grad[...].astype(BF)
    gather.start()
    pump()
    weights.wait()
    for copy in fetches:
        copy.wait()
    place = r.place[...]
    heads = place.shape[1] // PAD
    compact_width, head_width = place.shape

    def inward(chip):
        left = r.full[pl.ds(2 * chip, 2)].reshape(2 * rows, width)
        where = tile(chip, 2 * rows)
        grad = nn(left, held[:, 2 * compact_width :]).astype(BF)
        r.grad_mixed[where, :] = nn(grad, place).astype(BF)

    gather.wait_chip()
    inward(group.chip)
    pump()
    gather.forward()
    pump()
    gather.wait_other()
    inward(1 - group.chip)
    kv_at = heads * PAD
    value_at = kv_at + heads // 2 * PAD
    r.grad_k[...] = jnp.zeros_like(r.grad_k)
    r.grad_v[...] = jnp.zeros_like(r.grad_v)
    for turn, prob in enumerate(probs):
        reach = prob.shape[2]
        where = pl.ds(turn * rows, rows)
        cosine, sine = r.cosine[where, :], r.sine[where, :]

        def attend(head):
            mine = tile(head, PAD)
            shared = tile(head // 2, PAD)
            query = qkv[where, mine]
            key = qkv[0:reach, pl.ds(kv_at + head // 2 * PAD, PAD)]
            value = qkv[0:reach, pl.ds(value_at + head // 2 * PAD, PAD)]
            grad = r.grad_mixed[where, mine]
            low = prob[head]
            grad_prob = nt(grad, value)
            weight = low.astype(F32)
            inner = jnp.sum(weight * grad_prob, axis=-1, keepdims=True)
            grad_score = (weight * (grad_prob - inner)).astype(BF)
            u = nn(grad_score, key) * scale
            r.grad_q[where, mine] = (u * cosine - turn_half(u) * sine).astype(BF)
            r.grad_k[0:reach, shared] += tn(grad_score, query)
            r.grad_v[0:reach, shared] += tn(low, grad)

        for head in range(heads):
            attend(head)
        pump()
    for pair in range(heads // 2):
        columns = pl.ds(pair * PAD, PAD)
        u = r.grad_k[:, columns] * scale
        r.grad_kv[:, columns] = (u * r.cosine[...] - turn_half(u) * r.sine[...]).astype(BF)
        r.grad_kv[:, pl.ds((heads // 2 + pair) * PAD, PAD)] = r.grad_v[:, columns].astype(BF)
    grad_low = r.grad_low
    grad_low[:, 0:compact_width] = nt(r.grad_q[...], place).astype(BF)
    grad_low[:, compact_width : 2 * compact_width] = nt(r.grad_kv[...], place).astype(BF)
    for turn in range(2):
        where = tile(scatter.rows_of(turn), 2 * rows)

        def part_of(index):
            columns = tile(index, 256)
            out_columns(
                scatter, turn, grad_low[where, :], held[columns, 0 : 2 * compact_width], columns
            )

        each(width // 256, part_of)
        scatter.send_core(turn)
        if turn == 0:
            scatter.send_away()
        pump()
    grads = r.grads
    weight_grads(r.a_full, grad_low, grads, slice(0, 2 * compact_width))
    weight_grads(r.full, compact, grads, slice(2 * compact_width, 3 * compact_width))
    copy = pltpu.make_async_copy(grads, r.grads_out, r.out_sems.at[0])
    copy.start()
    pump()
    scatter.wait()
    pump()
    close_back(scatter, r.grad, r.x, r.gains[2 * level : 2 * level + 1, :], r.grad_out, r.dgain)
    pump.rest()
    gather.finish()
    scatter.finish()
    copy.wait()


def last_kernel(reduce_count, r):
    n_dp, _, lanes = r.gain_blocks.shape
    width = r.rows.shape[1]
    depth = width // n_dp
    line = Line(n_dp)
    group = Group()
    tasks = reduces_of(line, r, reduce_count)
    gains = Reduce(line, r.gain_blocks, r.gain_total, *[getattr(r, f"gain{j}") for j in range(8)])
    meet(group, line)
    for task in tasks:
        task.start()
    for row in range(4):
        r.rows[row : row + 1, :] = jnp.sum(getattr(r, f"dgain{row}")[...], axis=0, keepdims=True)
    r.rows[4:8, :] = jnp.zeros((4, width), F32)
    for turn, device in enumerate((group.core, group.other)):
        copy = group.remote(r.rows, r.others.at[turn], r.row_send.at[turn], r.row_recv.at[turn], device)
        copy.start()
        copy.wait()
        r.rows[...] += r.others[turn]
    both = jnp.concatenate([r.rows[...], jnp.zeros((GAIN_ROWS - 8, width), F32)], axis=0).astype(BF)

    def gain_rows(block):
        r.gain_blocks[block] = nt(both, spread(block, depth, lanes, width)).astype(BF)

    each(n_dp, gain_rows)
    gains.start()
    for task in tasks:
        for step in task.actions()[1:]:
            step()
    for step in gains.actions()[1:]:
        step()


def shaped(shape, dtype):
    return jax.ShapeDtypeStruct(shape, dtype)


def dma(count):
    return pltpu.SemaphoreType.DMA((count,))


def vmem(*shape, dtype=BF):
    return pltpu.VMEM(shape, dtype)


def reaches(rows):
    return [min((turn + 1) * rows + PAD, 4 * rows) for turn in range(4)]


def launch(kernel, which, name, ins, outs, scratch):
    names = list(ins) + list(outs) + list(scratch)

    def entry(*refs):
        kernel(types.SimpleNamespace(**dict(zip(names, refs))))

    results = pl.pallas_call(
        entry,
        out_shape=[shape for shape, _ in outs.values()],
        in_specs=[spec for _, spec in ins.values()],
        out_specs=[spec for _, spec in outs.values()],
        scratch_shapes=list(scratch.values()),
        compiler_params=pltpu.CompilerParams(
            collective_id=which, has_side_effects=True, vmem_limit_bytes=LIMIT
        ),
        cost_estimate=pl.CostEstimate(
            flops=20_000_000_000, bytes_accessed=60_000_000, transcendentals=0
        ),
        name=name,
    )(*[array for array, _ in ins.values()])
    return types.SimpleNamespace(**dict(zip(outs, results)))


def comm_scratch(rows, width):
    return dict(
        full=vmem(4, rows, width),
        parts=vmem(2, 2, rows, width),
        near=vmem(2, rows, width),
        away=vmem(rows, width),
        landed=vmem(rows, width),
        g_send=dma(5),
        g_recv=dma(5),
        s_send=dma(4),
        s_recv=dma(4),
    )


def blocks_of(pack, n_dp):
    return shaped((n_dp,) + pack.shape, pack.dtype)


def fetch_refs(packs, n_dp):
    ins, outs, scratch = {}, {}, {}
    for i, pack in enumerate(packs):
        ins[f"own{i}"] = (pack, ANY)
        outs[f"blocks{i}"] = (blocks_of(pack, n_dp), ANY)
        scratch[f"fetch_send{i}"], scratch[f"fetch_recv{i}"] = Fetch.scratch(n_dp)
    return ins, outs, scratch


def reduce_refs(sums):
    ins, outs, scratch = {}, {}, {}
    for i, blocks in enumerate(sums):
        n_dp, depth, columns = blocks.shape
        ins[f"sum{i}"] = (blocks, ANY)
        outs[f"total{i}"] = (shaped((depth, columns), F32), VM)
        for j, each_of in enumerate(Reduce.scratch(n_dp, depth, columns)):
            scratch[f"reduce{i}_{j}"] = each_of
    return ins, outs, scratch


def totals(out, count):
    return [getattr(out, f"total{i}") for i in range(count)]


def fetched(out, count):
    return [getattr(out, f"blocks{i}") for i in range(count)]


def attn_forward(level, which, states, tables, place, gains, pack, blocks, packs, plan, raw=None):
    rows, width = states.shape
    first = raw is not None
    if first:
        depth, columns = raw["raw_query0"].shape[0], 3 * raw["raw_query0"].shape[1]
        pack = shaped((depth, columns), BF)
    depth, columns = pack.shape
    n_dp = width // depth
    heads = place.shape[1] // PAD
    length = 4 * rows
    ins = dict(x=(states, VM), place=(place, VM))
    outs = dict(
        middle=(shaped((rows, width), F32), VM),
        a_out=(shaped((4, rows, width), BF), ANY),
        qkv_out=(shaped((length, 2 * heads * PAD), BF), ANY),
        o_out=(shaped((length, place.shape[0]), BF), ANY),
    )
    scratch = comm_scratch(rows, width) | dict(
        held=vmem(width, columns),
        padded=vmem(width, 2 * heads * PAD),
        qkv=vmem(length, 2 * heads * PAD),
        mixed=vmem(length, heads * PAD),
        compact=vmem(length, place.shape[0]),
        bias=vmem(rows, length, dtype=F32),
        w_sems=dma(n_dp),
        out_sems=dma(7),
    )
    for turn, reach in enumerate(reaches(rows)):
        outs[f"p_out{turn}"] = (shaped((heads, rows, reach), BF), ANY)
        scratch[f"prob{turn}"] = vmem(heads, rows, reach)
    if first:
        units = raw["raw_gate0"].shape[1]
        now = ("raw_query0", "raw_key0", "raw_value0", "raw_output0")
        for name, array in raw.items():
            late = name.startswith("raw_") and name not in now
            ins[name] = (array, ANY if late else VM)
            if late:
                scratch[name[4:]] = vmem(*array.shape, dtype=F32)
        outs |= dict(
            gains=(shaped((GAIN_ROWS, width), F32), VM),
            blocks=(blocks_of(pack, n_dp), ANY),
            own=(pack, VM),
            own0=(shaped((depth, units), BF), VM),
            own1=(shaped((depth, units), BF), VM),
            blocks0=(shaped((n_dp, depth, units), BF), ANY),
            blocks1=(shaped((n_dp, depth, units), BF), ANY),
            down_pack0=(shaped((depth, units), BF), VM),
            attn_pack1=(pack, VM),
            gate_pack1=(shaped((depth, units), BF), VM),
            up_pack1=(shaped((depth, units), BF), VM),
            down_pack1=(shaped((depth, units), BF), VM),
            cosine=(shaped((length, PAD), F32), VM),
            sine=(shaped((length, PAD), F32), VM),
            marks=(shaped((8, PAD), jnp.int32), VM),
        )
        scratch["gain_raw"] = vmem(GAIN_ROWS, 256, dtype=F32)
        scratch["gain_own"] = vmem(GAIN_ROWS, 256)
        scratch["gain_blocks"] = vmem(n_dp, GAIN_ROWS, 256)
        scratch["raw_sems"] = dma(10)
        for name, tail in (("gain", ""), ("weight", ""), ("fetch", "0"), ("fetch", "1")):
            scratch[f"{name}_send{tail}"], scratch[f"{name}_recv{tail}"] = Fetch.scratch(n_dp)
        more = {}, {}, {}
    else:
        cosine, sine, marks = tables
        ins |= dict(
            gains=(gains, VM), cosine=(cosine, VM), sine=(sine, VM), marks=(marks, VM), own=(pack, ANY), blocks=(blocks, ANY)
        )
        more = fetch_refs(packs, n_dp)
    return launch(
        functools.partial(attn_forward_kernel, first, level, 2 if first else len(packs), plan),
        which, f"attn_forward_{level}", ins | more[0], outs | more[1], scratch | more[2],
    )


def mlp_refs(rows, width, wide, own):
    depth, units = own.shape
    n_dp = width // depth
    ins = dict(own=(own, ANY))
    ins |= {name: (array, ANY) for name, array in wide.items()}
    scratch = comm_scratch(rows, width) | dict(
        wide=vmem(width, 2 * units),
        held=vmem(width, units),
        gu=vmem(4 * rows, 2 * units),
        hid=vmem(4 * rows, units),
        gate_sems=dma(n_dp),
        up_sems=dma(n_dp),
        w_sems=dma(n_dp),
    )
    return n_dp, units, ins, scratch


def mlp_forward(level, which, middle, gains, wide, down_own, packs, plan):
    rows, width = middle.shape
    n_dp, units, ins, scratch = mlp_refs(rows, width, wide, down_own)
    ins |= dict(middle=(middle, VM), gains=(gains, VM))
    outs = dict(
        result=(shaped((rows, width), F32), VM),
        m_out=(shaped((4, rows, width), BF), ANY),
        gu_out=(shaped((4 * rows, 2 * units), BF), ANY),
        hid_out=(shaped((4 * rows, units), BF), ANY),
        blocks=(blocks_of(down_own, n_dp), ANY),
    )
    scratch |= dict(out_sems=dma(3))
    scratch["down_send"], scratch["down_recv"] = Fetch.scratch(n_dp)
    more = fetch_refs(packs, n_dp)
    return launch(
        functools.partial(mlp_forward_kernel, level, len(packs), plan),
        which, f"mlp_forward_{level}", ins | more[0], outs | more[1], scratch | more[2],
    )


def mlp_backward(level, which, grad, middle, gains, saved, wide, down, sums, plan):
    rows, width = middle.shape
    n_dp, units, ins, scratch = mlp_refs(rows, width, wide, down[0])
    depth = width // n_dp
    ins |= dict(
        blocks=(down[1], ANY),
        grad=(grad, VM), middle=(middle, VM), gains=(gains, VM),
        m_in=(saved.m_out, ANY), gu_in=(saved.gu_out, ANY), hid_in=(saved.hid_out, ANY),
    )
    outs = dict(
        grad_out=(shaped((rows, width), F32), VM),
        dgain=(shaped((8, width), F32), VM),
        wide_out=(shaped((n_dp, depth, 2 * units), BF), ANY),
        down_total=(shaped((depth, units), F32), VM),
    )
    scratch |= dict(
        m_full=vmem(4, rows, width),
        wide_grads=vmem(n_dp, depth, 2 * units),
        grads=vmem(n_dp, depth, units),
        in_sems=dma(3),
        out_sems=dma(3),
    )
    for j, each_of in enumerate(Reduce.scratch(n_dp, depth, units)):
        scratch[f"down{j}"] = each_of
    more = reduce_refs(sums)
    return launch(
        functools.partial(mlp_backward_kernel, level, len(sums), plan),
        which, f"mlp_backward_{level}", ins | more[0], outs | more[1], scratch | more[2],
    )


def attn_backward(level, which, grad, states, gains, tables, place, saved, weights, sums, plan):
    cosine, sine, _ = tables
    pack, blocks = weights
    rows, width = states.shape
    depth, columns = pack.shape
    n_dp = width // depth
    heads = place.shape[1] // PAD
    length = 4 * rows
    ins = dict(
        grad=(grad, VM), x=(states, VM), gains=(gains, VM), cosine=(cosine, VM), sine=(sine, VM), place=(place, VM),
        own=(pack, ANY), blocks=(blocks, ANY),
        a_in=(saved.a_out, ANY), qkv_in=(saved.qkv_out, ANY), o_in=(saved.o_out, ANY),
    )
    outs = dict(
        grad_out=(shaped((rows, width), F32), VM),
        dgain=(shaped((8, width), F32), VM),
        grads_out=(shaped((n_dp, depth, columns), BF), ANY),
    )
    scratch = comm_scratch(rows, width) | dict(
        held=vmem(width, columns),
        a_full=vmem(4, rows, width),
        qkv=vmem(length, 2 * heads * PAD),
        compact=vmem(length, place.shape[0]),
        grad_mixed=vmem(length, heads * PAD),
        grad_q=vmem(length, heads * PAD),
        grad_kv=vmem(length, heads * PAD),
        grad_k=vmem(length, heads // 2 * PAD, dtype=F32),
        grad_v=vmem(length, heads // 2 * PAD, dtype=F32),
        grad_low=vmem(length, 2 * place.shape[0]),
        grads=vmem(n_dp, depth, columns),
        w_sems=dma(n_dp),
        in_sems=dma(7),
        out_sems=dma(1),
    )
    for turn, reach in enumerate(reaches(rows)):
        ins[f"p_in{turn}"] = (getattr(saved, f"p_out{turn}"), ANY)
        scratch[f"prob{turn}"] = vmem(heads, rows, reach)
    more = reduce_refs(sums)
    return launch(
        functools.partial(attn_backward_kernel, level, len(sums), plan),
        which, f"attn_backward_{level}", ins | more[0], outs | more[1], scratch | more[2],
    )


def last_sums(which, dgains, sums):
    n_dp = sums[0].shape[0]
    width = dgains[0].shape[1]
    ins = {f"dgain{i}": (dgain, VM) for i, dgain in enumerate(dgains)}
    outs = dict(gain_total=(shaped((GAIN_ROWS, 256), F32), VM))
    scratch = dict(
        gain_blocks=vmem(n_dp, GAIN_ROWS, 256),
        rows=vmem(8, width, dtype=F32),
        others=vmem(2, 8, width, dtype=F32),
        row_send=dma(2),
        row_recv=dma(2),
    )
    for j, each_of in enumerate(Reduce.scratch(n_dp, GAIN_ROWS, 256)):
        scratch[f"gain{j}"] = each_of
    more = reduce_refs(sums)
    return launch(
        functools.partial(last_kernel, len(sums)),
        which, "last_sums", ins | more[0], outs | more[1], scratch | more[2],
    )


def constants(heads):
    place = np.zeros((heads * HEAD_DIM, heads * PAD), np.float32)
    for row in range(heads * HEAD_DIM):
        which, column = divmod(row, HEAD_DIM)
        place[row, which * PAD + column + (PAD // 2 - HALF if column >= HALF else 0)] = 1.0
    freqs = np.zeros((8, PAD), np.float32)
    for start in (0, PAD // 2):
        freqs[0, start : start + HALF] = np.exp(np.arange(HALF) * (-2.0 * math.log(rope_base) / HEAD_DIM))
    freqs[1, 0 : PAD // 2] = -1.0
    freqs[1, PAD // 2 :] = 1.0
    return jnp.asarray(place, BF), jnp.asarray(freqs)


def body(states_in, documents, *rest):
    cotangent = rest[-1]
    one, two = rest[0:9], rest[9:18]
    heads = one[1].shape[1] // HEAD_DIM
    place, freqs = constants(heads)
    raw = dict(documents=documents.reshape(-1, PAD), freqs=freqs)
    for level, w in enumerate((one, two)):
        raw[f"gain{2 * level}"] = w[0].reshape(1, -1)
        raw[f"gain{2 * level + 1}"] = w[5].reshape(1, -1)
        for name, array in zip(("query", "key", "value", "output", "", "gate", "up", "down"), w[1:]):
            if name:
                raw[f"raw_{name}{level}"] = array.T if name in ("output", "down") else array

    attn1 = attn_forward(
        0, 0, states_in, None, place, None, None, None, None, [2, 1, 0, 1, 0, 0, 1, 0, 0, 2, 1], raw
    )
    tables = (attn1.cosine, attn1.sine, attn1.marks)
    attn_pack = [attn1.own, attn1.attn_pack1]
    down_pack = [attn1.down_pack0, attn1.down_pack1]
    gains = attn1.gains
    wide1 = dict(
        gate_own=attn1.own0, gate_blocks=attn1.blocks0, up_own=attn1.own1, up_blocks=attn1.blocks1
    )
    mlp1 = mlp_forward(
        0, 1, attn1.middle, gains, wide1, down_pack[0], [attn_pack[1]], [0, 0, 1, 1, 2, 0]
    )
    down1 = (down_pack[0], mlp1.blocks)
    (attn2_blocks,) = fetched(mlp1, 1)
    attn2 = attn_forward(
        1, 2, mlp1.result, tables, place, gains, attn_pack[1], attn2_blocks, [attn1.gate_pack1, attn1.up_pack1],
        [2, 1, 1, 0, 0, 0, 1, 0, 0, 2, 1],
    )
    wide2 = dict(
        gate_own=attn1.gate_pack1, gate_blocks=attn2.blocks0, up_own=attn1.up_pack1, up_blocks=attn2.blocks1
    )
    mlp2 = mlp_forward(1, 3, attn2.middle, gains, wide2, down_pack[1], [], [])
    down2 = (down_pack[1], mlp2.blocks)

    back_mlp2 = mlp_backward(
        1, 4, cotangent, attn2.middle, gains, mlp2, wide2, down2, [], [0, 0, 0, 0, 0, 1, 1, 1]
    )
    back_attn2 = attn_backward(
        1, 5, back_mlp2.grad_out, mlp1.result, gains, tables, place, attn2, (attn_pack[1], attn2_blocks),
        [back_mlp2.wide_out], [1, 0, 0, 1, 0, 1, 0, 0, 0, 1],
    )
    back_mlp1 = mlp_backward(
        0, 6, back_attn2.grad_out, attn1.middle, gains, mlp1, wide1, down1,
        [back_attn2.grads_out], [1, 1, 1, 1, 1, 1, 0, 1, 1],
    )
    back_attn1 = attn_backward(
        0, 7, back_mlp1.grad_out, states_in, gains, tables, place, attn1, (attn_pack[0], attn1.blocks),
        [back_mlp1.wide_out], [1, 0, 0, 1, 0, 0, 1, 0, 0, 1],
    )
    last = last_sums(
        8,
        [back_attn1.dgain, back_mlp1.dgain, back_attn2.dgain, back_mlp2.dgain],
        [back_attn1.grads_out],
    )
    (wide_total2,) = totals(back_attn2, 1)
    (attn_total2,) = totals(back_mlp1, 1)
    (wide_total1,) = totals(back_attn1, 1)
    (attn_total1,) = totals(last, 1)
    down_total1, down_total2 = back_mlp1.down_total, back_mlp2.down_total
    gain_total = last.gain_total
    depth = down_total1.shape[0]
    bounds = [0]
    for w in one[1:4]:
        bounds.append(bounds[-1] + w.shape[1])
    units = one[6].shape[1]
    outs = [mlp2.result, back_attn1.grad_out]
    for level, (attn_total, wide_total, down_total) in enumerate(
        ((attn_total1, wide_total1, down_total1), (attn_total2, wide_total2, down_total2))
    ):
        outs.append(gain_total[2 * level, 0:depth])
        outs += [attn_total[:, low:high] for low, high in zip(bounds, bounds[1:])]
        outs.append(attn_total[:, bounds[-1] :].T)
        outs.append(gain_total[2 * level + 1, 0:depth])
        outs += [wide_total[:, 0:units], wide_total[:, units:], down_total.T]
    return tuple(outs)


def solution(mesh):
    layer = (
        P("dp"),
        P("dp", "tensor"),
        P("dp", "tensor"),
        P("dp", "tensor"),
        P("tensor", "dp"),
        P("dp"),
        P("dp", "tensor"),
        P("dp", "tensor"),
        P("tensor", "dp"),
    )
    rows = P(("dp", "tensor"), None)
    return jax.shard_map(
        body,
        mesh=mesh,
        in_specs=(rows, P("dp"), *layer, *layer, rows),
        out_specs=(rows, rows, *layer, *layer),
        check_vma=False,
    )
```

```python
import functools
import math
import types

import jax
import jax.numpy as jnp
import numpy as np
from jax import lax
from jax.experimental import pallas as pl
from jax.experimental.pallas import tpu as pltpu
from jax.sharding import PartitionSpec as P

HEAD_DIM = 96
HALF = HEAD_DIM // 2
BLOCK = 256
PAD = 128
GAIN_ROWS = 16
LIMIT = 60 * 1024 * 1024

epsilon = 1e-05
rope_base = 100000.0
masked_value = -1e30
scale = 1.0 / math.sqrt(HEAD_DIM)

BF = jnp.bfloat16
F32 = jnp.float32
MESH = pl.DeviceIdType.MESH
ANY = pl.BlockSpec(memory_space=pl.ANY)
VM = pl.BlockSpec(memory_space=pltpu.VMEM)


def nn(left, right):
    return lax.dot_general(left, right, (((1,), (0,)), ((), ())), preferred_element_type=F32)


def nt(left, right):
    return lax.dot_general(left, right, (((1,), (1,)), ((), ())), preferred_element_type=F32)


def tn(left, right):
    return lax.dot_general(left, right, (((0,), (0,)), ((), ())), preferred_element_type=F32)


def tile(index, size):
    if isinstance(index, int):
        return pl.ds(index * size, size)
    return pl.ds(pl.multiple_of(index * size, size), size)


def each(count, body):
    def step(index, carry):
        body(index)
        return carry

    lax.fori_loop(0, count, step, 0)


class Group:
    def __init__(self):
        self.me = lax.axis_index("tensor")
        self.core_bit = lax.rem(self.me, 2)
        self.chip = self.me // 2
        self.core = self.me + 1 - 2 * self.core_bit
        self.other = lax.rem(self.me + 2, 4)

    def greet(self, barrier):
        for near in (self.core, self.other):
            pl.semaphore_signal(barrier, inc=1, device_id={"tensor": near}, device_id_type=MESH)

    def peers(self):
        return 2

    def remote(self, source, target, send, recv, device):
        return pltpu.make_async_remote_copy(
            src_ref=source,
            dst_ref=target,
            send_sem=send,
            recv_sem=recv,
            device_id={"tensor": device},
            device_id_type=MESH,
        )


class Gather:
    def __init__(self, group, full, send, recv):
        self.group, self.full, self.send, self.recv = group, full, send, recv
        half = full.shape[1] // 2
        mine = full.at[group.me]
        self.to_core = group.remote(mine, mine, send.at[0], recv.at[0], group.core)
        self.to_other = []
        self.onward = []
        for part in range(2):
            piece = full.at[group.me, pl.ds(part * half, half)]
            self.to_other.append(
                group.remote(piece, piece, send.at[1 + part], recv.at[1 + part], group.other)
            )
            piece = full.at[group.other, pl.ds(part * half, half)]
            self.onward.append(
                group.remote(piece, piece, send.at[3 + part], recv.at[3 + part], group.core)
            )

    def start(self):
        for copy in self.to_other:
            copy.start()
        self.to_core.start()

    def wait_chip(self):
        self.to_core.wait_recv()

    def forward(self):
        for here, there in zip(self.to_other, self.onward):
            here.wait_recv()
            there.start()

    def wait_other(self):
        for copy in self.onward:
            copy.wait_recv()

    def finish(self):
        self.to_core.wait_send()
        for copy in self.to_other + self.onward:
            copy.wait_send()


class Scatter:
    def __init__(self, group, parts, near, away, landed, send, recv):
        self.group, self.parts, self.near = group, parts, near
        self.away, self.landed = away, landed
        self.to_core = [
            group.remote(
                parts.at[turn, 1 - group.core_bit], near.at[turn], send.at[turn], recv.at[turn], group.core
            )
            for turn in range(2)
        ]
        half = away.shape[0] // 2
        self.to_other = [
            group.remote(
                away.at[pl.ds(part * half, half)],
                landed.at[pl.ds(part * half, half)],
                send.at[2 + part],
                recv.at[2 + part],
                group.other,
            )
            for part in range(2)
        ]

    def rows_of(self, turn):
        return 1 - self.group.chip if turn == 0 else self.group.chip

    def send_core(self, turn):
        self.to_core[turn].start()

    def send_away(self):
        self.to_core[0].wait_recv()
        half = self.away.shape[0] // 2
        for part in range(2):

            def add(index):
                rows = pl.ds(pl.multiple_of(part * half + index * 32, 32), 32)
                total = self.parts[0, self.group.core_bit, rows, :].astype(F32) + self.near[
                    0, rows, :
                ].astype(F32)
                self.away[rows, :] = total.astype(BF)

            each(half // 32, add)
            self.to_other[part].start()

    def wait(self):
        self.to_core[1].wait_recv()
        for copy in self.to_other:
            copy.wait_recv()

    def total(self, rows):
        return (
            self.parts[1, self.group.core_bit, rows, :].astype(F32)
            + self.near[1, rows, :].astype(F32)
            + self.landed[rows, :].astype(F32)
        )

    def finish(self):
        for copy in self.to_core + self.to_other:
            copy.wait_send()


class Line:
    def __init__(self, n_dp):
        mine = lax.axis_index("dp")
        self.count = n_dp // 2
        self.z, self.x = mine // 2, lax.rem(mine, 2)
        self.mine = mine
        self.pair = self.z * 2 + 1 - self.x
        self.up = jnp.minimum(self.z + 1, self.count - 1) * 2 + self.x
        self.down = jnp.maximum(self.z - 1, 0) * 2 + self.x
        self.has_up = self.z + 1 < self.count
        self.has_down = self.z > 0

    def greet(self, barrier):
        def hello(device):
            pl.semaphore_signal(barrier, inc=1, device_id={"dp": device}, device_id_type=MESH)

        hello(self.pair)
        pl.when(self.has_up)(lambda: hello(self.up))
        pl.when(self.has_down)(lambda: hello(self.down))

    def peers(self):
        return 1 + jnp.minimum(self.count - 1 - self.z, 1) + jnp.minimum(self.z, 1)

    def remote(self, source, target, send, recv, device):
        return pltpu.make_async_remote_copy(
            src_ref=source, dst_ref=target, send_sem=send, recv_sem=recv,
            device_id={"dp": device}, device_id_type=MESH)


class Fetch:
    def __init__(self, line, own, blocks, send, recv):
        self.line, self.own, self.blocks, self.send, self.recv = line, own, blocks, send, recv
        rows = own.shape[0]
        self.edge = max(rows // 6 // 16, 1) * 16 if rows > 32 else 0
        self.rows = rows

    @staticmethod
    def scratch(n_dp):
        return [pltpu.SemaphoreType.DMA((n_dp, 5))] * 2

    def low(self, step):
        return jnp.maximum(self.line.z - step, 0) * 2

    def high(self, step):
        return jnp.minimum(self.line.z + step, self.line.count - 1) * 2

    def copy(self, slot, block, device, way, rows=None):
        source = self.own if slot == 0 and way < 3 else self.blocks.at[block]
        target = self.blocks.at[block]
        if rows is not None:
            source, target = source.at[rows], target.at[rows]
        return self.line.remote(
            source, target, self.send.at[slot, way], self.recv.at[slot, way], device
        )

    def upward(self, step):
        return self.copy(step, self.low(step) + self.line.x, self.line.up, 1)

    def downward(self, step):
        return self.copy(step, self.high(step) + self.line.x, self.line.down, 2)

    def edge_up(self, step):
        block = self.low(step) + 1 - self.line.x
        return self.copy(step, block, self.line.up, 3, pl.ds(0, self.edge))

    def edge_down(self, step):
        block = self.high(step) + 1 - self.line.x
        return self.copy(step, block, self.line.down, 4, pl.ds(0, self.edge))

    def sideways(self, step, low):
        line = self.line
        rows = pl.ds(self.edge, self.rows - self.edge) if step and self.edge else None
        if low:
            return self.copy(step, self.low(step) + line.x, line.pair, 0, rows)
        return self.copy(line.count + step, self.high(step) + line.x, line.pair, 0, rows)

    def upward_in(self, step):
        return self.copy(step - 1, self.low(step) + self.line.x, self.line.up, 1)

    def downward_in(self, step):
        return self.copy(step - 1, self.high(step) + self.line.x, self.line.down, 2)

    def edge_up_in(self, step):
        block = self.low(step) + 1 - self.line.x
        return self.copy(step - 1, block, self.line.up, 3, pl.ds(0, self.edge))

    def edge_down_in(self, step):
        block = self.high(step) + 1 - self.line.x
        return self.copy(step - 1, block, self.line.down, 4, pl.ds(0, self.edge))

    def start(self):
        line = self.line
        pl.when(line.has_up)(lambda: self.upward(0).start())
        pl.when(line.has_down)(lambda: self.downward(0).start())
        self.sideways(0, True).start()

    def step(self, step):
        line = self.line

        @pl.when(line.z >= step)
        def _():
            self.upward_in(step).wait_recv()
            pl.when(line.has_up)(lambda: self.upward(step).start())
            self.sideways(step, True).start()

        @pl.when(line.z + step < line.count)
        def _():
            self.downward_in(step).wait_recv()
            pl.when(line.has_down)(lambda: self.downward(step).start())
            self.sideways(step, False).start()

        self.edges(step - 1)

    def edges(self, step):
        line = self.line
        if step == 0:
            self.sideways(0, True).wait_recv()
        if not self.edge:
            return
        if step == 0:
            pl.when(line.has_up)(lambda: self.edge_up(0).start())
            pl.when(line.has_down)(lambda: self.edge_down(0).start())
            return

        @pl.when(line.z >= step)
        def _():
            self.edge_up_in(step).wait_recv()
            pl.when(line.has_up)(lambda: self.edge_up(step).start())

        @pl.when(line.z + step < line.count)
        def _():
            self.edge_down_in(step).wait_recv()
            pl.when(line.has_down)(lambda: self.edge_down(step).start())

    def finish(self):
        line = self.line
        self.edges(line.count - 1)
        for step in range(line.count):

            @pl.when(line.z >= step)
            def _():
                @pl.when(line.has_up)
                def _():
                    self.upward(step).wait_send()
                    if self.edge:
                        self.edge_up(step).wait_send()

                self.sideways(step, True).wait_send()
                if step:
                    self.sideways(step, True).wait_recv()

            @pl.when(line.z + step < line.count)
            def _():
                @pl.when(line.has_down)
                def _():
                    self.downward(step).wait_send()
                    if self.edge:
                        self.edge_down(step).wait_send()

                if step:
                    self.sideways(step, False).wait()

    def actions(self):
        steps = [functools.partial(self.step, step) for step in range(1, self.line.count)]
        return [self.start] + steps + [self.finish]


class Reduce:
    def __init__(self, line, blocks, out, pair_in, line_in, mine, x_send, x_recv, z_send, z_recv, local):
        self.line, self.blocks, self.out = line, blocks, out
        self.pair_in, self.line_in, self.mine = pair_in, line_in, mine
        self.x_send, self.x_recv, self.z_send, self.z_recv, self.local = x_send, x_recv, z_send, z_recv, local

    @staticmethod
    def scratch(n_dp, rows, columns):
        count = n_dp // 2
        dma = pltpu.SemaphoreType.DMA
        return [
            pltpu.VMEM((count, rows, columns), BF),
            pltpu.VMEM((count + 1, rows, columns), BF),
            pltpu.VMEM((2, rows, columns), BF),
            dma((count,)), dma((count,)), dma((count,)), dma((count + 1,)), dma((2,)),
        ]

    def sideways(self, target):
        line = self.line
        return line.remote(self.blocks.at[target * 2 + 1 - line.x], self.pair_in.at[target],
                           self.x_send.at[target], self.x_recv.at[target], line.pair)

    def along(self, target, up):
        line = self.line
        slot = target + 1 if up else target
        return line.remote(self.pair_in.at[target], self.line_in.at[slot],
                           self.z_send.at[target], self.z_recv.at[slot], line.up if up else line.down)

    def load(self, target, slot):
        return pltpu.make_async_copy(self.blocks.at[target * 2 + self.line.x], self.mine.at[slot], self.local.at[slot])

    def above(self, step):
        return self.line.z + step < self.line.count, jnp.minimum(self.line.z + step, self.line.count - 1)

    def below(self, step):
        return self.line.z - step >= 0, jnp.maximum(self.line.z - step, 0)

    def fetch(self, step):
        there, target = self.above(step)
        pl.when(there)(lambda: self.load(target, 0).start())
        if step:
            there2, target2 = self.below(step)
            pl.when(there2)(lambda: self.load(target2, 1).start())

    def start(self):
        line = self.line
        for step in range(line.count - 1, 0, -1):
            for there, target in (self.above(step), self.below(step)):
                pl.when(there)(lambda: self.sideways(target).start())
        self.sideways(line.z).start()
        self.fetch(line.count - 1)

    def add(self, target, slot, more):
        rows = self.out.shape[0]

        def some(index):
            part = pl.ds(pl.multiple_of(index * 16, 16), 16)
            total = self.pair_in[target, part, :].astype(F32) + self.mine[slot, part, :].astype(F32)
            for other in more:
                total += self.line_in[other, part, :].astype(F32)
            self.pair_in[target, part, :] = total.astype(BF)

        each(rows // 16, some)

    def pass_on(self, target, slot, up):
        line = self.line
        self.load(target, slot).wait()
        self.sideways(target).wait_recv()
        fed = line.has_down if up else line.has_up

        @pl.when(fed)
        def _():
            self.along(target, up).wait_recv()
            self.add(target, slot, [target + 1 if up else target])

        pl.when(jnp.logical_not(fed))(lambda: self.add(target, slot, []))
        self.along(target, up).start()

    def step(self, step):
        for slot, (there, target) in enumerate((self.above(step), self.below(step))):
            pl.when(there)(lambda: self.pass_on(target, slot, slot == 0))
        self.fetch(step - 1)

    def close(self):
        line = self.line
        z = line.z
        self.load(z, 0).wait()
        self.sideways(z).wait_recv()
        rows = self.out.shape[0]

        def final(more):
            def some(index):
                part = pl.ds(pl.multiple_of(index * 16, 16), 16)
                total = self.pair_in[z, part, :].astype(F32) + self.mine[0, part, :].astype(F32)
                for other in more:
                    total += self.line_in[other, part, :].astype(F32)
                self.out[part, :] = total

            each(rows // 16, some)

        pl.when(line.has_down)(lambda: self.along(z, True).wait_recv())
        pl.when(line.has_up)(lambda: self.along(z, False).wait_recv())
        pl.when(jnp.logical_not(line.has_down))(lambda: final([z]))
        pl.when(jnp.logical_not(line.has_up))(lambda: final([z + 1]))
        pl.when(line.has_down & line.has_up)(lambda: final([z, z + 1]))
        for step in range(line.count - 1, 0, -1):
            for up, (there, target) in ((True, self.above(step)), (False, self.below(step))):

                @pl.when(there)
                def _():
                    self.sideways(target).wait_send()
                    self.along(target, up).wait_send()

        self.sideways(z).wait_send()

    def actions(self):
        return [self.start] + [functools.partial(self.step, s) for s in range(self.line.count - 1, 0, -1)] + [self.close]


def spread(block, depth, lanes, width):
    row = lax.broadcasted_iota(jnp.int32, (lanes, width), 0)
    column = lax.broadcasted_iota(jnp.int32, (lanes, width), 1)
    hit = (column - row == block * depth) & (row < depth)
    return jnp.where(hit, 1.0, 0.0).astype(BF)


def turn_half(values):
    return pltpu.roll(values, PAD // 2, 1)


def meet(*circles):
    barrier = pltpu.get_barrier_semaphore()
    for circle in circles:
        circle.greet(barrier)
    pl.semaphore_wait(barrier, sum(circle.peers() for circle in circles))


class Weights:
    def __init__(self, line, own, blocks, held, sems, first=0):
        self.copies = []
        columns = pl.ds(first, own.shape[1])
        depth = own.shape[0]
        count = line.count
        for index in range(2 * count):
            shift, side = index // 2, index % 2
            block = lax.rem(line.z + shift, count) * 2 + lax.rem(line.x + side, 2)
            source = blocks.at[block] if index else own
            rows = pl.ds(pl.multiple_of(block * depth, 16), depth)
            self.copies.append(pltpu.make_async_copy(source, held.at[rows, columns], sems.at[index]))

    def start(self):
        for copy in self.copies:
            copy.start()

    def wait(self):
        for copy in self.copies:
            copy.wait()


class Pump:
    def __init__(self, tasks, plan):
        self.steps = [step for together in zip(*[task.actions() for task in tasks]) for step in together]
        self.plan = list(plan)

    def __call__(self):
        count = self.plan.pop(0) if self.plan else 0
        self.do(count)

    def do(self, count):
        for step in self.steps[:count]:
            step()
        self.steps = self.steps[count:]

    def rest(self):
        self.do(len(self.steps))


def fetches_of(line, r, count):
    return [
        Fetch(
            line,
            getattr(r, f"own{i}"),
            getattr(r, f"blocks{i}"),
            getattr(r, f"fetch_send{i}"),
            getattr(r, f"fetch_recv{i}"),
        )
        for i in range(count)
    ]


def reduces_of(line, r, count):
    return [
        Reduce(
            line,
            getattr(r, f"sum{i}"),
            getattr(r, f"total{i}"),
            *[getattr(r, f"reduce{i}_{j}") for j in range(8)],
        )
        for i in range(count)
    ]


def comm_of(r):
    group = Group()
    gather = Gather(group, r.full, r.g_send, r.g_recv)
    scatter = Scatter(group, r.parts, r.near, r.away, r.landed, r.s_send, r.s_recv)
    return group, gather, scatter


def out_columns(scatter, turn, left_rows, right_tile, columns):
    product = nt(left_rows, right_tile)
    rows = product.shape[0] // 2
    scatter.parts[turn, 0, :, columns] = product[:rows].astype(BF)
    scatter.parts[turn, 1, :, columns] = product[rows:].astype(BF)


def norm_rows(source, gain, full, slot):
    def norm(index):
        part = tile(index, 32)
        values = source[part, :]
        factor = lax.rsqrt(jnp.mean(values * values, axis=-1, keepdims=True) + epsilon)
        full[slot, part, :] = (values * factor * gain).astype(BF)

    each(source.shape[0] // 32, norm)


def add_rows(scatter, source, target):
    def close(index):
        part = tile(index, 32)
        target[part, :] = source[part, :] + scatter.total(part)

    each(source.shape[0] // 32, close)


def pack_attn(query, key, value, output, target):
    width, each_kv = query.shape[1], key.shape[1]
    target[:, 0:width] = query[...].astype(BF)
    both = jnp.concatenate([key[...], value[...]], axis=1)
    target[:, width : width + 2 * each_kv] = both.astype(BF)
    target[:, width + 2 * each_kv :] = output[...].astype(BF)


def count_rows(documents, below):
    hits = jnp.where(documents < below, 1.0, 0.0)
    return jnp.sum(jnp.sum(hits, axis=1, keepdims=True), axis=0, keepdims=True).astype(jnp.int32)


def starts_of(marks, places):
    head, body_end = marks[0:1, 0:1], marks[1:2, 0:1]
    return jnp.where(places < head, 0, jnp.where(places < body_end, head, body_end))


def make_tables(r):
    marks = jnp.concatenate([count_rows(r.documents[...], 1), count_rows(r.documents[...], 2)], axis=0)
    r.marks[0:2, :] = jnp.broadcast_to(marks, (2, PAD))
    r.marks[2:, :] = jnp.zeros((6, PAD), jnp.int32)

    def some(index):
        where = tile(index, 128)
        places = lax.broadcasted_iota(jnp.int32, (128, PAD), 0) + index * 128
        offset = places - starts_of(r.marks, places)
        angles = offset.astype(F32) * r.freqs[0:1, :]
        r.cosine[where, :] = jnp.cos(angles)
        r.sine[where, :] = jnp.sin(angles) * r.freqs[1:2, :]

    each(r.cosine.shape[0] // 128, some)


def attn_forward_kernel(first, level, fetch_count, plan, r):
    rows, width = r.x.shape
    n_dp, depth = r.w_sems.shape[0], r.own.shape[0]
    line = Line(n_dp)
    group, gather, scatter = comm_of(r)
    tasks = fetches_of(line, r, fetch_count)
    weights = Weights(line, r.own, r.blocks, r.held, r.w_sems)
    circles = (group, line) if first or tasks else (group,)
    meet(*circles)
    if first:
        raw = {}
        for name in ("gate0", "up0", "down0", "query1", "key1", "value1", "output1", "gate1", "up1", "down1"):
            raw[name] = pltpu.make_async_copy(
                getattr(r, "raw_" + name), getattr(r, name), r.raw_sems.at[len(raw)]
            )
            raw[name].start()
        lanes = r.gain_own.shape[1]
        r.gain_raw[...] = jnp.zeros_like(r.gain_raw)
        for row in range(4):
            r.gain_raw[row : row + 1, 0:depth] = getattr(r, f"gain{row}")[...]
        r.gain_own[...] = r.gain_raw[...].astype(BF)
        pack_attn(r.raw_query0, r.raw_key0, r.raw_value0, r.raw_output0, r.own)
        gain_fetch = Fetch(line, r.gain_own, r.gain_blocks, r.gain_send, r.gain_recv)
        weight_fetch = Fetch(line, r.own, r.blocks, r.weight_send, r.weight_recv)
        gain_fetch.start()
        weight_fetch.start()
        for step in gain_fetch.actions()[1:]:
            step()
        r.gains[...] = jnp.zeros_like(r.gains)

        def gather_gain(block):
            chosen = spread(block, depth, lanes, width)

            @pl.when(block == line.mine)
            def _():
                r.gains[...] += nn(r.gain_own[...], chosen)

            @pl.when(block != line.mine)
            def _():
                r.gains[...] += nn(r.gain_blocks[block], chosen)

        each(n_dp, gather_gain)
        norm_rows(r.x, r.gains[2 * level : 2 * level + 1, :], r.full, group.me)
        gather.start()
        weight_steps = weight_fetch.actions()[1:-1]
        for step in weight_steps[:1]:
            step()
        ahead = Gather(group, r.ahead, r.a_send, r.a_recv)
        r.ahead[group.me] = r.cotangent[...].astype(BF)
        ahead.start()
        for name in ("gate0", "up0"):
            raw[name].wait()
        r.own0[...] = r.gate0[...].astype(BF)
        r.own1[...] = r.up0[...].astype(BF)
        for step in weight_steps[1:]:
            step()
        pump = Pump(tasks, plan)
        pump()
        make_tables(r)
        for name in list(raw)[2:]:
            raw[name].wait()
        pack_attn(r.query1, r.key1, r.value1, r.output1, r.attn_pack1)
        r.down_pack0[...] = r.down0[...].astype(BF)
        r.down_pack1[...] = r.down1[...].astype(BF)
        r.gate_pack1[...] = r.gate1[...].astype(BF)
        r.up_pack1[...] = r.up1[...].astype(BF)
        weight_fetch.finish()
        weights.start()
    else:
        weights.start()
        pump = Pump(tasks, plan)
        pump()
        norm_rows(r.x, r.gains[2 * level : 2 * level + 1, :], r.full, group.me)
        gather.start()
    weights.wait()
    place = r.place[...]
    heads = place.shape[1] // PAD
    compact_width, head_width = place.shape
    padded, qkv, mixed, compact, held = r.padded, r.qkv, r.mixed, r.compact, r.held

    def pad(index):
        part = tile(index, 256)
        padded[part, 0:head_width] = nn(held[part, 0:compact_width], place).astype(BF)
        padded[part, head_width : 2 * head_width] = nn(
            held[part, compact_width : 2 * compact_width], place
        ).astype(BF)

    each(width // 256, pad)

    def project(chip):
        left = r.full[pl.ds(2 * chip, 2)].reshape(2 * rows, width)
        where = tile(chip, 2 * rows)
        cosine, sine = r.cosine[where, :], r.sine[where, :]

        def turned(index):
            columns = tile(index, 2 * PAD)
            product = nn(left, padded[:, columns])
            for half in range(2):
                u = product[:, half * PAD : (half + 1) * PAD]
                qkv[where, tile(2 * index + half, PAD)] = (u * cosine + turn_half(u) * sine).astype(BF)

        each(3 * heads // 4, turned)
        columns = pl.ds(3 * heads // 2 * PAD, heads // 2 * PAD)
        qkv[where, columns] = nn(left, padded[:, columns]).astype(BF)

    gather.wait_chip()
    project(group.chip)
    pump()
    gather.forward()
    pump()
    gather.wait_other()
    project(1 - group.chip)
    copies = [
        pltpu.make_async_copy(r.full, r.a_out, r.out_sems.at[0]),
        pltpu.make_async_copy(qkv, r.qkv_out, r.out_sems.at[1]),
    ]
    for copy in copies:
        copy.start()
    if first:
        ahead.wait_chip()
        ahead.forward()
    pump()
    kv_at = heads * PAD
    value_at = kv_at + heads // 2 * PAD
    for turn in range(4):
        prob = getattr(r, f"prob{turn}")
        reach = prob.shape[2]
        where = pl.ds(turn * rows, rows)
        places = lax.broadcasted_iota(jnp.int32, (rows, PAD), 0) + turn * rows
        begin = starts_of(r.marks, places)
        head, body_end = r.marks[0:1, 0:1], r.marks[1:2, 0:1]
        end = jnp.where(places < head, head, jnp.where(places < body_end, body_end, 4 * rows))
        end = jnp.minimum(begin + ((places - begin) // BLOCK + 1) * BLOCK, end)
        place_of = lax.broadcasted_iota(jnp.int32, (rows, reach), 1)
        inside = (place_of >= begin[:, 0:1]) & (place_of < end[:, 0:1])
        r.bias[:, 0:reach] = jnp.where(inside, 0.0, masked_value)

        def attend(head):
            query = qkv[where, tile(head, PAD)]
            key = qkv[0:reach, pl.ds(kv_at + head // 2 * PAD, PAD)]
            value = qkv[0:reach, pl.ds(value_at + head // 2 * PAD, PAD)]
            scores = nt(query, key) * scale + r.bias[:, 0:reach]
            exponent = jnp.exp(scores - jnp.max(scores, axis=-1, keepdims=True))
            summed = jnp.sum(exponent, axis=-1, keepdims=True)
            low = (exponent * (1.0 / summed)).astype(BF)
            prob[head] = low
            mixed[where, tile(head, PAD)] = nn(low, value).astype(BF)

        for head in range(heads):
            attend(head)
        copy = pltpu.make_async_copy(prob, getattr(r, f"p_out{turn}"), r.out_sems.at[2 + turn])
        copy.start()
        copies.append(copy)
        compact[where, :] = nt(mixed[where, :], place).astype(BF)
        pump()
    copies.append(pltpu.make_async_copy(compact, r.o_out, r.out_sems.at[6]))
    copies[-1].start()
    if first:
        ahead.wait_other()
        copies.append(pltpu.make_async_copy(r.ahead, r.ahead_out, r.out_sems.at[7]))
        copies[-1].start()
        ahead.finish()
    for turn in range(2):
        left = compact[tile(scatter.rows_of(turn), 2 * rows), :]

        def part_of(index):
            columns = tile(index, 256)
            out_columns(scatter, turn, left, held[columns, 2 * compact_width :], columns)

        each(width // 256, part_of)
        scatter.send_core(turn)
        if turn == 0:
            scatter.send_away()
        pump()
    scatter.wait()
    pump()
    add_rows(scatter, r.x, r.middle)
    pump.rest()
    gather.finish()
    scatter.finish()
    for copy in copies:
        copy.wait()


def wide_of(line, r):
    return [
        Weights(line, r.gate_own, r.gate_blocks, r.wide, r.gate_sems),
        Weights(line, r.up_own, r.up_blocks, r.wide, r.up_sems, r.gate_own.shape[1]),
    ]


def mlp_forward_kernel(level, fetch_count, plan, r):
    rows, width = r.middle.shape
    units = r.hid.shape[1]
    line = Line(r.w_sems.shape[0])
    group, gather, scatter = comm_of(r)
    down = Fetch(line, r.own, r.blocks, r.down_send, r.down_recv)
    down_steps = down.actions()[1:-1]
    wide, held, gu, hid = r.wide, r.held, r.gu, r.hid
    wide_weights = wide_of(line, r)
    weights = Weights(line, r.own, r.blocks, held, r.w_sems)
    meet(group, line)
    down.start()
    for copy in wide_weights:
        copy.start()
    pump = Pump(fetches_of(line, r, fetch_count), plan)
    pump()
    norm_rows(r.middle, r.gains[2 * level + 1 : 2 * level + 2, :], r.full, group.me)
    gather.start()
    for copy in wide_weights:
        copy.wait()

    def expand(chip):
        left = r.full[pl.ds(2 * chip, 2)].reshape(2 * rows, width)
        where = tile(chip, 2 * rows)

        def unit(index):
            columns = tile(index, 256)
            further = pl.ds(pl.multiple_of(units + index * 256, 256), 256)
            gate = nn(left, wide[:, columns])
            up = nn(left, wide[:, further])
            hid[where, columns] = (gate / (1.0 + jnp.exp(-gate)) * up).astype(BF)
            gu[where, columns] = gate.astype(BF)
            gu[where, further] = up.astype(BF)

        each(units // 256, unit)

    gather.wait_chip()
    expand(group.chip)
    for step in down_steps[:1]:
        step()
    gather.forward()
    for step in down_steps[1:2]:
        step()
    pump()
    gather.wait_other()
    expand(1 - group.chip)
    for step in down_steps[2:]:
        step()
    pump()
    copies = [
        pltpu.make_async_copy(r.full, r.m_out, r.out_sems.at[0]),
        pltpu.make_async_copy(gu, r.gu_out, r.out_sems.at[1]),
        pltpu.make_async_copy(hid, r.hid_out, r.out_sems.at[2]),
    ]
    for copy in copies:
        copy.start()
    down.finish()
    weights.start()
    weights.wait()
    for turn in range(2):
        left = hid[tile(scatter.rows_of(turn), 2 * rows), :]

        def part_of(index):
            columns = tile(index, 256)
            out_columns(scatter, turn, left, held[columns, :], columns)

        each(width // 256, part_of)
        scatter.send_core(turn)
        if turn == 0:
            scatter.send_away()
        pump()
    scatter.wait()
    pump()
    add_rows(scatter, r.middle, r.result)
    pump.rest()
    gather.finish()
    scatter.finish()
    for copy in copies:
        copy.wait()


def weight_grads(source, right, target, columns):
    width = source.shape[-1]
    depth = target.shape[1]
    chunk = math.lcm(depth, PAD)

    def some(index):
        left = source[..., tile(index, chunk)].reshape(right.shape[0], chunk)
        product = tn(left, right[...]).astype(BF)
        for part in range(chunk // depth):
            rows = slice(part * depth, (part + 1) * depth)
            target[index * (chunk // depth) + part, :, columns] = product[rows]

    each(width // chunk, some)


def close_back(scatter, grad_in_ref, state_ref, gain, grad_out, dgain):
    rows = state_ref.shape[0]
    dgain[...] = jnp.zeros_like(dgain)

    def close(index):
        part = tile(index, 32)
        values = state_ref[part, :]
        factor = lax.rsqrt(jnp.mean(values * values, axis=-1, keepdims=True) + epsilon)
        normed = values * factor
        grad_in = scatter.total(part)
        dgain[...] += jnp.sum((grad_in * normed).reshape(4, 8, -1), axis=0)
        grad_norm = grad_in * gain
        inner = jnp.mean(grad_norm * normed, axis=-1, keepdims=True)
        grad_out[part, :] = grad_in_ref[part, :] + factor * (grad_norm - normed * inner)

    each(rows // 32, close)


def mlp_backward_kernel(level, reduce_count, plan, ready, r):
    rows, width = r.middle.shape
    units = r.hid.shape[1]
    n_dp = r.w_sems.shape[0]
    line = Line(n_dp)
    group, gather, scatter = comm_of(r)
    wide, held, gu, hid = r.wide, r.held, r.gu, r.hid
    weights = [
        Weights(line, r.own, r.blocks, held, r.w_sems),
        *wide_of(line, r),
    ]
    fetches = [
        pltpu.make_async_copy(r.hid_in, hid, r.in_sems.at[2]),
        pltpu.make_async_copy(r.gu_in, gu, r.in_sems.at[1]),
        pltpu.make_async_copy(r.m_in, r.m_full, r.in_sems.at[0]),
    ]
    down = Reduce(line, r.grads, r.down_total, *[getattr(r, f"down{j}") for j in range(8)])
    meet(group, line)
    pump = Pump(reduces_of(line, r, reduce_count), plan)
    pump.steps += down.actions()[1:]
    pump()
    for copy in weights[:1] + fetches + weights[1:]:
        copy.start()
    if ready:
        whole = pltpu.make_async_copy(r.ahead_in, r.full, r.in_sems.at[3])
        whole.start()
    else:
        r.full[group.me] = r.grad[...].astype(BF)
        gather.start()
    for copy in weights[:1] + fetches[:2]:
        copy.wait()

    def inward(chip):
        left = r.full[pl.ds(2 * chip, 2)].reshape(2 * rows, width)
        where = tile(chip, 2 * rows)

        def unit(index):
            columns = tile(index, 256)
            further = pl.ds(pl.multiple_of(units + index * 256, 256), 256)
            grad = nn(left, held[:, columns])
            gate = gu[where, columns].astype(F32)
            up = gu[where, further].astype(F32)
            sig = 1.0 / (1.0 + jnp.exp(-gate))
            gu[where, columns] = (grad * up * sig * (1.0 + gate * (1.0 - sig))).astype(BF)
            gu[where, further] = (grad * gate * sig).astype(BF)

        each(units // 256, unit)

    if ready:
        whole.wait()
    else:
        gather.wait_chip()
        inward(group.chip)
        pump()
        gather.forward()
        pump()
        gather.wait_other()
    weight_grads(r.full, hid, r.grads, slice(0, units))
    down.start()
    if ready:
        inward(group.chip)
    inward(1 - group.chip)
    for copy in weights[1:] + fetches[2:]:
        copy.wait()
    pump()
    for turn in range(2):
        where = tile(scatter.rows_of(turn), 2 * rows)

        def part_of(index):
            columns = tile(index, 256)
            out_columns(scatter, turn, gu[where, :], wide[columns, :], columns)

        each(width // 256, part_of)
        scatter.send_core(turn)
        if turn == 0:
            scatter.send_away()
        pump()
    for part in range(2):
        columns = slice(part * units, (part + 1) * units)
        weight_grads(r.m_full, gu.at[:, columns], r.wide_grads, columns)
        pump()
    copies = [pltpu.make_async_copy(r.wide_grads, r.wide_out, r.out_sems.at[0])]
    copies[0].start()
    scatter.wait()
    pump()
    close_back(
        scatter, r.grad, r.middle, r.gains[2 * level + 1 : 2 * level + 2, :], r.grad_out, r.dgain
    )
    pump.rest()
    if not ready:
        gather.finish()
    scatter.finish()
    for copy in copies:
        copy.wait()


def attn_backward_kernel(level, reduce_count, plan, final, r):
    rows, width = r.x.shape
    n_dp = r.w_sems.shape[0]
    depth = width // n_dp
    line = Line(n_dp)
    group, gather, scatter = comm_of(r)
    tasks = reduces_of(line, r, reduce_count)
    held, qkv, compact = r.held, r.qkv, r.compact
    probs = [getattr(r, f"prob{turn}") for turn in range(4)]
    weights = Weights(line, r.own, r.blocks, held, r.w_sems)
    fetches = [
        pltpu.make_async_copy(r.a_in, r.a_full, r.in_sems.at[0]),
        pltpu.make_async_copy(r.o_in, compact, r.in_sems.at[1]),
        pltpu.make_async_copy(r.qkv_in, qkv, r.in_sems.at[2]),
    ] + [
        pltpu.make_async_copy(getattr(r, f"p_in{turn}"), probs[turn], r.in_sems.at[3 + turn])
        for turn in range(4)
    ]
    meet(*((group, line) if tasks else (group,)))
    weights.start()
    for copy in fetches:
        copy.start()
    pump = Pump(tasks, plan)
    pump()
    r.full[group.me] = r.grad[...].astype(BF)
    gather.start()
    pump()
    weights.wait()
    for copy in fetches:
        copy.wait()
    place = r.place[...]
    heads = place.shape[1] // PAD
    compact_width, head_width = place.shape

    def inward(chip):
        left = r.full[pl.ds(2 * chip, 2)].reshape(2 * rows, width)
        where = tile(chip, 2 * rows)
        grad = nn(left, held[:, 2 * compact_width :]).astype(BF)
        r.grad_mixed[where, :] = nn(grad, place).astype(BF)

    gather.wait_chip()
    inward(group.chip)
    pump()
    gather.forward()
    pump()
    gather.wait_other()
    inward(1 - group.chip)
    kv_at = heads * PAD
    value_at = kv_at + heads // 2 * PAD
    r.grad_k[...] = jnp.zeros_like(r.grad_k)
    r.grad_v[...] = jnp.zeros_like(r.grad_v)
    for turn, prob in enumerate(probs):
        reach = prob.shape[2]
        where = pl.ds(turn * rows, rows)
        cosine, sine = r.cosine[where, :], r.sine[where, :]

        def attend(head):
            mine = tile(head, PAD)
            shared = tile(head // 2, PAD)
            query = qkv[where, mine]
            key = qkv[0:reach, pl.ds(kv_at + head // 2 * PAD, PAD)]
            value = qkv[0:reach, pl.ds(value_at + head // 2 * PAD, PAD)]
            grad = r.grad_mixed[where, mine]
            low = prob[head]
            grad_prob = nt(grad, value)
            weight = low.astype(F32)
            inner = jnp.sum(weight * grad_prob, axis=-1, keepdims=True)
            grad_score = (weight * (grad_prob - inner)).astype(BF)
            u = nn(grad_score, key) * scale
            r.grad_q[where, mine] = (u * cosine - turn_half(u) * sine).astype(BF)
            r.grad_k[0:reach, shared] += tn(grad_score, query)
            r.grad_v[0:reach, shared] += tn(low, grad)

        for head in range(heads):
            attend(head)
        pump()
    for pair in range(heads // 2):
        columns = pl.ds(pair * PAD, PAD)
        u = r.grad_k[:, columns] * scale
        r.grad_kv[:, columns] = (u * r.cosine[...] - turn_half(u) * r.sine[...]).astype(BF)
        r.grad_kv[:, pl.ds((heads // 2 + pair) * PAD, PAD)] = r.grad_v[:, columns].astype(BF)
    grad_low = r.grad_low
    grad_low[:, 0:compact_width] = nt(r.grad_q[...], place).astype(BF)
    grad_low[:, compact_width : 2 * compact_width] = nt(r.grad_kv[...], place).astype(BF)
    for turn in range(2):
        where = tile(scatter.rows_of(turn), 2 * rows)

        def part_of(index):
            columns = tile(index, 256)
            out_columns(
                scatter, turn, grad_low[where, :], held[columns, 0 : 2 * compact_width], columns
            )

        each(width // 256, part_of)
        scatter.send_core(turn)
        if turn == 0:
            scatter.send_away()
        pump()
    grads = r.grads
    weight_grads(r.a_full, grad_low, grads, slice(0, 2 * compact_width))
    weight_grads(r.full, compact, grads, slice(2 * compact_width, 3 * compact_width))
    if not final:
        copy = pltpu.make_async_copy(grads, r.grads_out, r.out_sems.at[0])
        copy.start()
    pump()
    scatter.wait()
    pump()
    close_back(scatter, r.grad, r.x, r.gains[2 * level : 2 * level + 1, :], r.grad_out, r.dgain)
    if final:
        attn = Reduce(line, grads, r.attn_total, *[getattr(r, f"attn{j}") for j in range(8)])
        gains = gain_sums(line, group, r)
        gains.start()
        attn.start()
        pump.rest()
        for step in gains.actions()[1:] + attn.actions()[1:]:
            step()
    pump.rest()
    gather.finish()
    scatter.finish()
    if not final:
        copy.wait()


def gain_sums(line, group, r):
    n_dp, _, lanes = r.gain_blocks.shape
    width = r.rows.shape[1]
    depth = width // n_dp
    for row, part in enumerate((r.dgain, r.dgain1, r.dgain2, r.dgain3)):
        r.rows[row : row + 1, :] = jnp.sum(part[...], axis=0, keepdims=True)
    r.rows[4:8, :] = jnp.zeros((4, width), F32)
    for turn, device in enumerate((group.core, group.other)):
        copy = group.remote(r.rows, r.others.at[turn], r.row_send.at[turn], r.row_recv.at[turn], device)
        copy.start()
        copy.wait()
        r.rows[...] += r.others[turn]
    both = jnp.concatenate([r.rows[...], jnp.zeros((GAIN_ROWS - 8, width), F32)], axis=0).astype(BF)

    def gain_rows(block):
        r.gain_blocks[block] = nt(both, spread(block, depth, lanes, width)).astype(BF)

    each(n_dp, gain_rows)
    return Reduce(line, r.gain_blocks, r.gain_total, *[getattr(r, f"gain{j}") for j in range(8)])


def shaped(shape, dtype):
    return jax.ShapeDtypeStruct(shape, dtype)


def dma(count):
    return pltpu.SemaphoreType.DMA((count,))


def vmem(*shape, dtype=BF):
    return pltpu.VMEM(shape, dtype)


def reaches(rows):
    return [min((turn + 1) * rows + PAD, 4 * rows) for turn in range(4)]


def launch(kernel, which, name, ins, outs, scratch):
    names = list(ins) + list(outs) + list(scratch)

    def entry(*refs):
        kernel(types.SimpleNamespace(**dict(zip(names, refs))))

    results = pl.pallas_call(
        entry,
        out_shape=[shape for shape, _ in outs.values()],
        in_specs=[spec for _, spec in ins.values()],
        out_specs=[spec for _, spec in outs.values()],
        scratch_shapes=list(scratch.values()),
        compiler_params=pltpu.CompilerParams(
            collective_id=which, has_side_effects=True, vmem_limit_bytes=LIMIT
        ),
        cost_estimate=pl.CostEstimate(
            flops=20_000_000_000, bytes_accessed=60_000_000, transcendentals=0
        ),
        name=name,
    )(*[array for array, _ in ins.values()])
    return types.SimpleNamespace(**dict(zip(outs, results)))


def comm_scratch(rows, width):
    return dict(
        full=vmem(4, rows, width),
        parts=vmem(2, 2, rows, width),
        near=vmem(2, rows, width),
        away=vmem(rows, width),
        landed=vmem(rows, width),
        g_send=dma(5),
        g_recv=dma(5),
        s_send=dma(4),
        s_recv=dma(4),
    )


def blocks_of(pack, n_dp):
    return shaped((n_dp,) + pack.shape, pack.dtype)


def fetch_refs(packs, n_dp):
    ins, outs, scratch = {}, {}, {}
    for i, pack in enumerate(packs):
        ins[f"own{i}"] = (pack, ANY)
        outs[f"blocks{i}"] = (blocks_of(pack, n_dp), ANY)
        scratch[f"fetch_send{i}"], scratch[f"fetch_recv{i}"] = Fetch.scratch(n_dp)
    return ins, outs, scratch


def reduce_refs(sums):
    ins, outs, scratch = {}, {}, {}
    for i, blocks in enumerate(sums):
        n_dp, depth, columns = blocks.shape
        ins[f"sum{i}"] = (blocks, ANY)
        outs[f"total{i}"] = (shaped((depth, columns), F32), VM)
        for j, each_of in enumerate(Reduce.scratch(n_dp, depth, columns)):
            scratch[f"reduce{i}_{j}"] = each_of
    return ins, outs, scratch


def totals(out, count):
    return [getattr(out, f"total{i}") for i in range(count)]


def fetched(out, count):
    return [getattr(out, f"blocks{i}") for i in range(count)]


def attn_forward(level, which, states, tables, place, gains, pack, blocks, packs, plan, raw=None):
    rows, width = states.shape
    first = raw is not None
    if first:
        depth, columns = raw["raw_query0"].shape[0], 3 * raw["raw_query0"].shape[1]
        pack = shaped((depth, columns), BF)
    depth, columns = pack.shape
    n_dp = width // depth
    heads = place.shape[1] // PAD
    length = 4 * rows
    ins = dict(x=(states, VM), place=(place, VM))
    outs = dict(
        middle=(shaped((rows, width), F32), VM),
        a_out=(shaped((4, rows, width), BF), ANY),
        qkv_out=(shaped((length, 2 * heads * PAD), BF), ANY),
        o_out=(shaped((length, place.shape[0]), BF), ANY),
    )
    scratch = comm_scratch(rows, width) | dict(
        held=vmem(width, columns),
        padded=vmem(width, 2 * heads * PAD),
        qkv=vmem(length, 2 * heads * PAD),
        mixed=vmem(length, heads * PAD),
        compact=vmem(length, place.shape[0]),
        bias=vmem(rows, length, dtype=F32),
        w_sems=dma(n_dp),
        out_sems=dma(8),
    )
    for turn, reach in enumerate(reaches(rows)):
        outs[f"p_out{turn}"] = (shaped((heads, rows, reach), BF), ANY)
        scratch[f"prob{turn}"] = vmem(heads, rows, reach)
    if first:
        units = raw["raw_gate0"].shape[1]
        now = ("raw_query0", "raw_key0", "raw_value0", "raw_output0")
        for name, array in raw.items():
            late = name.startswith("raw_") and name not in now
            ins[name] = (array, ANY if late else VM)
            if late:
                scratch[name[4:]] = vmem(*array.shape, dtype=F32)
        outs |= dict(
            gains=(shaped((GAIN_ROWS, width), F32), VM),
            blocks=(blocks_of(pack, n_dp), ANY),
            own=(pack, VM),
            own0=(shaped((depth, units), BF), VM),
            own1=(shaped((depth, units), BF), VM),
            blocks0=(shaped((n_dp, depth, units), BF), ANY),
            blocks1=(shaped((n_dp, depth, units), BF), ANY),
            down_pack0=(shaped((depth, units), BF), VM),
            attn_pack1=(pack, VM),
            gate_pack1=(shaped((depth, units), BF), VM),
            up_pack1=(shaped((depth, units), BF), VM),
            down_pack1=(shaped((depth, units), BF), VM),
            cosine=(shaped((length, PAD), F32), VM),
            sine=(shaped((length, PAD), F32), VM),
            marks=(shaped((8, PAD), jnp.int32), VM),
            ahead_out=(shaped((4, rows, width), BF), ANY),
        )
        scratch |= dict(ahead=vmem(4, rows, width), a_send=dma(5), a_recv=dma(5))
        scratch["gain_raw"] = vmem(GAIN_ROWS, 256, dtype=F32)
        scratch["gain_own"] = vmem(GAIN_ROWS, 256)
        scratch["gain_blocks"] = vmem(n_dp, GAIN_ROWS, 256)
        scratch["raw_sems"] = dma(10)
        for name, tail in (("gain", ""), ("weight", ""), ("fetch", "0"), ("fetch", "1")):
            scratch[f"{name}_send{tail}"], scratch[f"{name}_recv{tail}"] = Fetch.scratch(n_dp)
        more = {}, {}, {}
    else:
        cosine, sine, marks = tables
        ins |= dict(
            gains=(gains, VM), cosine=(cosine, VM), sine=(sine, VM), marks=(marks, VM), own=(pack, ANY), blocks=(blocks, ANY)
        )
        more = fetch_refs(packs, n_dp)
    return launch(
        functools.partial(attn_forward_kernel, first, level, 2 if first else len(packs), plan),
        which, f"attn_forward_{level}", ins | more[0], outs | more[1], scratch | more[2],
    )


def mlp_refs(rows, width, wide, own):
    depth, units = own.shape
    n_dp = width // depth
    ins = dict(own=(own, ANY))
    ins |= {name: (array, ANY) for name, array in wide.items()}
    scratch = comm_scratch(rows, width) | dict(
        wide=vmem(width, 2 * units),
        held=vmem(width, units),
        gu=vmem(4 * rows, 2 * units),
        hid=vmem(4 * rows, units),
        gate_sems=dma(n_dp),
        up_sems=dma(n_dp),
        w_sems=dma(n_dp),
    )
    return n_dp, units, ins, scratch


def mlp_forward(level, which, middle, gains, wide, down_own, packs, plan):
    rows, width = middle.shape
    n_dp, units, ins, scratch = mlp_refs(rows, width, wide, down_own)
    ins |= dict(middle=(middle, VM), gains=(gains, VM))
    outs = dict(
        result=(shaped((rows, width), F32), VM),
        m_out=(shaped((4, rows, width), BF), ANY),
        gu_out=(shaped((4 * rows, 2 * units), BF), ANY),
        hid_out=(shaped((4 * rows, units), BF), ANY),
        blocks=(blocks_of(down_own, n_dp), ANY),
    )
    scratch |= dict(out_sems=dma(3))
    scratch["down_send"], scratch["down_recv"] = Fetch.scratch(n_dp)
    more = fetch_refs(packs, n_dp)
    return launch(
        functools.partial(mlp_forward_kernel, level, len(packs), plan),
        which, f"mlp_forward_{level}", ins | more[0], outs | more[1], scratch | more[2],
    )


def mlp_backward(level, which, grad, middle, gains, saved, wide, down, sums, plan, ahead=None):
    rows, width = middle.shape
    n_dp, units, ins, scratch = mlp_refs(rows, width, wide, down[0])
    depth = width // n_dp
    ins |= dict(
        blocks=(down[1], ANY),
        grad=(grad, VM), middle=(middle, VM), gains=(gains, VM),
        m_in=(saved.m_out, ANY), gu_in=(saved.gu_out, ANY), hid_in=(saved.hid_out, ANY),
    )
    outs = dict(
        grad_out=(shaped((rows, width), F32), VM),
        dgain=(shaped((8, width), F32), VM),
        wide_out=(shaped((n_dp, depth, 2 * units), BF), ANY),
        down_total=(shaped((depth, units), F32), VM),
    )
    scratch |= dict(
        m_full=vmem(4, rows, width),
        wide_grads=vmem(n_dp, depth, 2 * units),
        grads=vmem(n_dp, depth, units),
        in_sems=dma(4),
        out_sems=dma(3),
    )
    if ahead is not None:
        ins |= dict(ahead_in=(ahead, ANY))
    for j, each_of in enumerate(Reduce.scratch(n_dp, depth, units)):
        scratch[f"down{j}"] = each_of
    more = reduce_refs(sums)
    return launch(
        functools.partial(mlp_backward_kernel, level, len(sums), plan, ahead is not None),
        which, f"mlp_backward_{level}", ins | more[0], outs | more[1], scratch | more[2],
    )


def attn_backward(level, which, grad, states, gains, tables, place, saved, weights, sums, plan, dgains=()):
    cosine, sine, _ = tables
    pack, blocks = weights
    rows, width = states.shape
    depth, columns = pack.shape
    n_dp = width // depth
    heads = place.shape[1] // PAD
    length = 4 * rows
    ins = dict(
        grad=(grad, VM), x=(states, VM), gains=(gains, VM), cosine=(cosine, VM), sine=(sine, VM), place=(place, VM),
        own=(pack, ANY), blocks=(blocks, ANY),
        a_in=(saved.a_out, ANY), qkv_in=(saved.qkv_out, ANY), o_in=(saved.o_out, ANY),
    )
    outs = dict(
        grad_out=(shaped((rows, width), F32), VM),
        dgain=(shaped((8, width), F32), VM),
    )
    scratch = comm_scratch(rows, width) | dict(
        held=vmem(width, columns),
        a_full=vmem(4, rows, width),
        qkv=vmem(length, 2 * heads * PAD),
        compact=vmem(length, place.shape[0]),
        grad_mixed=vmem(length, heads * PAD),
        grad_q=vmem(length, heads * PAD),
        grad_kv=vmem(length, heads * PAD),
        grad_k=vmem(length, heads // 2 * PAD, dtype=F32),
        grad_v=vmem(length, heads // 2 * PAD, dtype=F32),
        grad_low=vmem(length, 2 * place.shape[0]),
        grads=vmem(n_dp, depth, columns),
        w_sems=dma(n_dp),
        in_sems=dma(7),
        out_sems=dma(1),
    )
    for turn, reach in enumerate(reaches(rows)):
        ins[f"p_in{turn}"] = (getattr(saved, f"p_out{turn}"), ANY)
        scratch[f"prob{turn}"] = vmem(heads, rows, reach)
    if dgains:
        ins |= {f"dgain{1 + i}": (dgain, VM) for i, dgain in enumerate(dgains)}
        outs |= dict(
            gain_total=(shaped((GAIN_ROWS, 256), F32), VM),
            attn_total=(shaped((depth, columns), F32), VM),
        )
        scratch |= dict(
            gain_blocks=vmem(n_dp, GAIN_ROWS, 256),
            rows=vmem(8, width, dtype=F32),
            others=vmem(2, 8, width, dtype=F32),
            row_send=dma(2),
            row_recv=dma(2),
        )
        for j, each_of in enumerate(Reduce.scratch(n_dp, GAIN_ROWS, 256)):
            scratch[f"gain{j}"] = each_of
        for j, each_of in enumerate(Reduce.scratch(n_dp, depth, columns)):
            scratch[f"attn{j}"] = each_of
    else:
        outs |= dict(grads_out=(shaped((n_dp, depth, columns), BF), ANY))
    more = reduce_refs(sums)
    return launch(
        functools.partial(attn_backward_kernel, level, len(sums), plan, bool(dgains)),
        which, f"attn_backward_{level}", ins | more[0], outs | more[1], scratch | more[2],
    )


def constants(heads):
    place = np.zeros((heads * HEAD_DIM, heads * PAD), np.float32)
    for row in range(heads * HEAD_DIM):
        which, column = divmod(row, HEAD_DIM)
        place[row, which * PAD + column + (PAD // 2 - HALF if column >= HALF else 0)] = 1.0
    freqs = np.zeros((8, PAD), np.float32)
    for start in (0, PAD // 2):
        freqs[0, start : start + HALF] = np.exp(np.arange(HALF) * (-2.0 * math.log(rope_base) / HEAD_DIM))
    freqs[1, 0 : PAD // 2] = -1.0
    freqs[1, PAD // 2 :] = 1.0
    return jnp.asarray(place, BF), jnp.asarray(freqs)


def body(states_in, documents, *rest):
    cotangent = rest[-1]
    one, two = rest[0:9], rest[9:18]
    heads = one[1].shape[1] // HEAD_DIM
    place, freqs = constants(heads)
    raw = dict(documents=documents.reshape(-1, PAD), freqs=freqs, cotangent=cotangent)
    for level, w in enumerate((one, two)):
        raw[f"gain{2 * level}"] = w[0].reshape(1, -1)
        raw[f"gain{2 * level + 1}"] = w[5].reshape(1, -1)
        for name, array in zip(("query", "key", "value", "output", "", "gate", "up", "down"), w[1:]):
            if name:
                raw[f"raw_{name}{level}"] = array.T if name in ("output", "down") else array

    attn1 = attn_forward(
        0, 0, states_in, None, place, None, None, None, None, [2, 1, 0, 1, 0, 0, 1, 0, 0, 2, 1], raw
    )
    tables = (attn1.cosine, attn1.sine, attn1.marks)
    attn_pack = [attn1.own, attn1.attn_pack1]
    down_pack = [attn1.down_pack0, attn1.down_pack1]
    gains = attn1.gains
    wide1 = dict(
        gate_own=attn1.own0, gate_blocks=attn1.blocks0, up_own=attn1.own1, up_blocks=attn1.blocks1
    )
    mlp1 = mlp_forward(
        0, 1, attn1.middle, gains, wide1, down_pack[0], [attn_pack[1]], [0, 0, 1, 1, 2, 0]
    )
    down1 = (down_pack[0], mlp1.blocks)
    (attn2_blocks,) = fetched(mlp1, 1)
    attn2 = attn_forward(
        1, 2, mlp1.result, tables, place, gains, attn_pack[1], attn2_blocks, [attn1.gate_pack1, attn1.up_pack1],
        [2, 1, 1, 0, 0, 0, 1, 0, 0, 2, 1],
    )
    wide2 = dict(
        gate_own=attn1.gate_pack1, gate_blocks=attn2.blocks0, up_own=attn1.up_pack1, up_blocks=attn2.blocks1
    )
    mlp2 = mlp_forward(1, 3, attn2.middle, gains, wide2, down_pack[1], [], [])
    down2 = (down_pack[1], mlp2.blocks)

    back_mlp2 = mlp_backward(
        1, 4, cotangent, attn2.middle, gains, mlp2, wide2, down2, [], [0, 0, 1, 0, 1, 1, 0],
        attn1.ahead_out,
    )
    back_attn2 = attn_backward(
        1, 5, back_mlp2.grad_out, mlp1.result, gains, tables, place, attn2, (attn_pack[1], attn2_blocks),
        [back_mlp2.wide_out], [1, 0, 0, 1, 0, 1, 0, 0, 0, 1],
    )
    back_mlp1 = mlp_backward(
        0, 6, back_attn2.grad_out, attn1.middle, gains, mlp1, wide1, down1,
        [back_attn2.grads_out], [1, 1, 1, 1, 1, 1, 0, 1, 1],
    )
    back_attn1 = attn_backward(
        0, 7, back_mlp1.grad_out, states_in, gains, tables, place, attn1, (attn_pack[0], attn1.blocks),
        [back_mlp1.wide_out], [1, 0, 0, 1, 0, 0, 1, 0, 0, 1],
        (back_mlp1.dgain, back_attn2.dgain, back_mlp2.dgain),
    )
    (wide_total2,) = totals(back_attn2, 1)
    (attn_total2,) = totals(back_mlp1, 1)
    (wide_total1,) = totals(back_attn1, 1)
    attn_total1 = back_attn1.attn_total
    down_total1, down_total2 = back_mlp1.down_total, back_mlp2.down_total
    gain_total = back_attn1.gain_total
    depth = down_total1.shape[0]
    bounds = [0]
    for w in one[1:4]:
        bounds.append(bounds[-1] + w.shape[1])
    units = one[6].shape[1]
    outs = [mlp2.result, back_attn1.grad_out]
    for level, (attn_total, wide_total, down_total) in enumerate(
        ((attn_total1, wide_total1, down_total1), (attn_total2, wide_total2, down_total2))
    ):
        outs.append(gain_total[2 * level, 0:depth])
        outs += [attn_total[:, low:high] for low, high in zip(bounds, bounds[1:])]
        outs.append(attn_total[:, bounds[-1] :].T)
        outs.append(gain_total[2 * level + 1, 0:depth])
        outs += [wide_total[:, 0:units], wide_total[:, units:], down_total.T]
    return tuple(outs)


def solution(mesh):
    layer = (
        P("dp"),
        P("dp", "tensor"),
        P("dp", "tensor"),
        P("dp", "tensor"),
        P("tensor", "dp"),
        P("dp"),
        P("dp", "tensor"),
        P("dp", "tensor"),
        P("tensor", "dp"),
    )
    rows = P(("dp", "tensor"), None)
    return jax.shard_map(
        body,
        mesh=mesh,
        in_specs=(rows, P("dp"), *layer, *layer, rows),
        out_specs=(rows, rows, *layer, *layer),
        check_vma=False,
    )
```

```python
import functools
import math
import types

import jax
import jax.numpy as jnp
import numpy as np
from jax import lax
from jax.experimental import pallas as pl
from jax.experimental.pallas import tpu as pltpu
from jax.sharding import PartitionSpec as P

HEAD_DIM = 96
HALF = HEAD_DIM // 2
BLOCK = 256
PAD = 128
GAIN_ROWS = 16
LIMIT = 60 * 1024 * 1024

epsilon = 1e-05
rope_base = 100000.0
masked_value = -1e30
scale = 1.0 / math.sqrt(HEAD_DIM)

BF = jnp.bfloat16
F32 = jnp.float32
MESH = pl.DeviceIdType.MESH
ANY = pl.BlockSpec(memory_space=pl.ANY)
VM = pl.BlockSpec(memory_space=pltpu.VMEM)
SELF = None


def nn(left, right):
    return lax.dot_general(left, right, (((1,), (0,)), ((), ())), preferred_element_type=F32)


def nt(left, right):
    return lax.dot_general(left, right, (((1,), (1,)), ((), ())), preferred_element_type=F32)


def tn(left, right):
    return lax.dot_general(left, right, (((0,), (0,)), ((), ())), preferred_element_type=F32)


def tile(index, size):
    if isinstance(index, int):
        return pl.ds(index * size, size)
    return pl.ds(pl.multiple_of(index * size, size), size)


def each(count, body):
    def step(index, carry):
        body(index)
        return carry

    lax.fori_loop(0, count, step, 0)


class Group:
    def __init__(self):
        self.me = lax.axis_index("tensor")
        self.core_bit = lax.rem(self.me, 2)
        self.chip = self.me // 2
        self.core = self.me + 1 - 2 * self.core_bit
        self.other = lax.rem(self.me + 2, 4)

    def greet(self, barrier):
        for near in (self.core, self.other):
            pl.semaphore_signal(barrier, inc=1, device_id={"tensor": near}, device_id_type=MESH)

    def peers(self):
        return 2

    def remote(self, source, target, send, recv, device):
        return pltpu.make_async_remote_copy(
            src_ref=source,
            dst_ref=target,
            send_sem=send,
            recv_sem=recv,
            device_id={"tensor": device},
            device_id_type=MESH,
        )


class Gather:
    def __init__(self, group, full, send, recv):
        self.group, self.full, self.send, self.recv = group, full, send, recv
        half = full.shape[1] // 2
        mine = full.at[group.me]
        self.to_core = group.remote(mine, mine, send.at[0], recv.at[0], group.core)
        self.to_other = []
        self.onward = []
        for part in range(2):
            piece = full.at[group.me, pl.ds(part * half, half)]
            self.to_other.append(
                group.remote(piece, piece, send.at[1 + part], recv.at[1 + part], group.other)
            )
            piece = full.at[group.other, pl.ds(part * half, half)]
            self.onward.append(
                group.remote(piece, piece, send.at[3 + part], recv.at[3 + part], group.core)
            )

    def start(self):
        for copy in self.to_other:
            copy.start()
        self.to_core.start()

    def wait_chip(self):
        self.to_core.wait_recv()

    def forward(self):
        for here, there in zip(self.to_other, self.onward):
            here.wait_recv()
            there.start()

    def wait_other(self):
        for copy in self.onward:
            copy.wait_recv()

    def finish(self):
        self.to_core.wait_send()
        for copy in self.to_other + self.onward:
            copy.wait_send()


class Scatter:
    def __init__(self, group, parts, near, away, landed, send, recv):
        self.group, self.parts, self.near = group, parts, near
        self.away, self.landed = away, landed
        self.to_core = [
            group.remote(
                parts.at[turn, 1 - group.core_bit], near.at[turn], send.at[turn], recv.at[turn], group.core
            )
            for turn in range(2)
        ]
        half = away.shape[0] // 2
        self.to_other = [
            group.remote(
                away.at[pl.ds(part * half, half)],
                landed.at[pl.ds(part * half, half)],
                send.at[2 + part],
                recv.at[2 + part],
                group.other,
            )
            for part in range(2)
        ]

    def rows_of(self, turn):
        return 1 - self.group.chip if turn == 0 else self.group.chip

    def send_core(self, turn):
        self.to_core[turn].start()

    def send_away(self):
        self.to_core[0].wait_recv()
        half = self.away.shape[0] // 2
        for part in range(2):

            def add(index):
                rows = pl.ds(pl.multiple_of(part * half + index * 32, 32), 32)
                total = self.parts[0, self.group.core_bit, rows, :].astype(F32) + self.near[
                    0, rows, :
                ].astype(F32)
                self.away[rows, :] = total.astype(BF)

            each(half // 32, add)
            self.to_other[part].start()

    def wait(self):
        self.to_core[1].wait_recv()
        for copy in self.to_other:
            copy.wait_recv()

    def total(self, rows):
        return (
            self.parts[1, self.group.core_bit, rows, :].astype(F32)
            + self.near[1, rows, :].astype(F32)
            + self.landed[rows, :].astype(F32)
        )

    def finish(self):
        for copy in self.to_core + self.to_other:
            copy.wait_send()


class Line:
    def __init__(self, n_dp):
        mine = lax.axis_index("dp")
        self.count = n_dp // 2
        self.z, self.x = mine // 2, lax.rem(mine, 2)
        self.mine = mine
        self.pair = self.z * 2 + 1 - self.x
        self.up = jnp.minimum(self.z + 1, self.count - 1) * 2 + self.x
        self.down = jnp.maximum(self.z - 1, 0) * 2 + self.x
        self.has_up = self.z + 1 < self.count
        self.has_down = self.z > 0

    def greet(self, barrier):
        def hello(device):
            pl.semaphore_signal(barrier, inc=1, device_id={"dp": device}, device_id_type=MESH)

        hello(self.pair)
        pl.when(self.has_up)(lambda: hello(self.up))
        pl.when(self.has_down)(lambda: hello(self.down))

    def peers(self):
        return 1 + jnp.minimum(self.count - 1 - self.z, 1) + jnp.minimum(self.z, 1)

    def remote(self, source, target, send, recv, device):
        return pltpu.make_async_remote_copy(
            src_ref=source, dst_ref=target, send_sem=send, recv_sem=recv,
            device_id={"dp": device}, device_id_type=MESH)


class Fetch:
    def __init__(self, line, own, blocks, send, recv):
        self.line, self.own, self.blocks, self.send, self.recv = line, own, blocks, send, recv
        rows = own.shape[0]
        self.edge = max(rows // 6 // 16, 1) * 16 if rows > 32 else 0
        self.rows = rows

    @staticmethod
    def scratch(n_dp):
        return [pltpu.SemaphoreType.DMA((n_dp, 5))] * 2

    def low(self, step):
        return jnp.maximum(self.line.z - step, 0) * 2

    def high(self, step):
        return jnp.minimum(self.line.z + step, self.line.count - 1) * 2

    def copy(self, slot, block, device, way, rows=None):
        source = self.own if slot == 0 and way < 3 else self.blocks.at[block]
        target = self.blocks.at[block]
        if rows is not None:
            source, target = source.at[rows], target.at[rows]
        return self.line.remote(
            source, target, self.send.at[slot, way], self.recv.at[slot, way], device
        )

    def upward(self, step):
        return self.copy(step, self.low(step) + self.line.x, self.line.up, 1)

    def downward(self, step):
        return self.copy(step, self.high(step) + self.line.x, self.line.down, 2)

    def edge_up(self, step):
        block = self.low(step) + 1 - self.line.x
        return self.copy(step, block, self.line.up, 3, pl.ds(0, self.edge))

    def edge_down(self, step):
        block = self.high(step) + 1 - self.line.x
        return self.copy(step, block, self.line.down, 4, pl.ds(0, self.edge))

    def sideways(self, step, low):
        line = self.line
        rows = pl.ds(self.edge, self.rows - self.edge) if step and self.edge else None
        if low:
            return self.copy(step, self.low(step) + line.x, line.pair, 0, rows)
        return self.copy(line.count + step, self.high(step) + line.x, line.pair, 0, rows)

    def upward_in(self, step):
        return self.copy(step - 1, self.low(step) + self.line.x, self.line.up, 1)

    def downward_in(self, step):
        return self.copy(step - 1, self.high(step) + self.line.x, self.line.down, 2)

    def edge_up_in(self, step):
        block = self.low(step) + 1 - self.line.x
        return self.copy(step - 1, block, self.line.up, 3, pl.ds(0, self.edge))

    def edge_down_in(self, step):
        block = self.high(step) + 1 - self.line.x
        return self.copy(step - 1, block, self.line.down, 4, pl.ds(0, self.edge))

    def start(self):
        line = self.line
        pl.when(line.has_up)(lambda: self.upward(0).start())
        pl.when(line.has_down)(lambda: self.downward(0).start())
        self.sideways(0, True).start()

    def step(self, step):
        line = self.line

        @pl.when(line.z >= step)
        def _():
            self.upward_in(step).wait_recv()
            pl.when(line.has_up)(lambda: self.upward(step).start())
            self.sideways(step, True).start()

        @pl.when(line.z + step < line.count)
        def _():
            self.downward_in(step).wait_recv()
            pl.when(line.has_down)(lambda: self.downward(step).start())
            self.sideways(step, False).start()

        self.edges(step - 1)

    def edges(self, step):
        line = self.line
        if step == 0:
            self.sideways(0, True).wait_recv()
        if not self.edge:
            return
        if step == 0:
            pl.when(line.has_up)(lambda: self.edge_up(0).start())
            pl.when(line.has_down)(lambda: self.edge_down(0).start())
            return

        @pl.when(line.z >= step)
        def _():
            self.edge_up_in(step).wait_recv()
            pl.when(line.has_up)(lambda: self.edge_up(step).start())

        @pl.when(line.z + step < line.count)
        def _():
            self.edge_down_in(step).wait_recv()
            pl.when(line.has_down)(lambda: self.edge_down(step).start())

    def finish(self):
        line = self.line
        self.edges(line.count - 1)
        for step in range(line.count):

            @pl.when(line.z >= step)
            def _():
                @pl.when(line.has_up)
                def _():
                    self.upward(step).wait_send()
                    if self.edge:
                        self.edge_up(step).wait_send()

                self.sideways(step, True).wait_send()
                if step:
                    self.sideways(step, True).wait_recv()

            @pl.when(line.z + step < line.count)
            def _():
                @pl.when(line.has_down)
                def _():
                    self.downward(step).wait_send()
                    if self.edge:
                        self.edge_down(step).wait_send()

                if step:
                    self.sideways(step, False).wait()

    def actions(self):
        steps = [functools.partial(self.step, step) for step in range(1, self.line.count)]
        return [self.start] + steps + [self.finish]


class Reduce:
    def __init__(self, line, blocks, out, pair_in, line_in, mine, x_send, x_recv, z_send, z_recv, local):
        self.line, self.blocks, self.out = line, blocks, out
        self.pair_in, self.line_in, self.mine = pair_in, line_in, mine
        self.x_send, self.x_recv, self.z_send, self.z_recv, self.local = x_send, x_recv, z_send, z_recv, local

    @staticmethod
    def scratch(n_dp, rows, columns):
        count = n_dp // 2
        dma = pltpu.SemaphoreType.DMA
        return [
            pltpu.VMEM((count, rows, columns), BF),
            pltpu.VMEM((count + 1, rows, columns), BF),
            pltpu.VMEM((2, rows, columns), BF),
            dma((count,)), dma((count,)), dma((count,)), dma((count + 1,)), dma((2,)),
        ]

    def sideways(self, target):
        line = self.line
        return line.remote(self.blocks.at[target * 2 + 1 - line.x], self.pair_in.at[target],
                           self.x_send.at[target], self.x_recv.at[target], line.pair)

    def along(self, target, up):
        line = self.line
        slot = target + 1 if up else target
        return line.remote(self.pair_in.at[target], self.line_in.at[slot],
                           self.z_send.at[target], self.z_recv.at[slot], line.up if up else line.down)

    def load(self, target, slot):
        return pltpu.make_async_copy(self.blocks.at[target * 2 + self.line.x], self.mine.at[slot], self.local.at[slot])

    def above(self, step):
        return self.line.z + step < self.line.count, jnp.minimum(self.line.z + step, self.line.count - 1)

    def below(self, step):
        return self.line.z - step >= 0, jnp.maximum(self.line.z - step, 0)

    def fetch(self, step):
        there, target = self.above(step)
        pl.when(there)(lambda: self.load(target, 0).start())
        if step:
            there2, target2 = self.below(step)
            pl.when(there2)(lambda: self.load(target2, 1).start())

    def start(self):
        line = self.line
        for step in range(line.count - 1, 0, -1):
            for there, target in (self.above(step), self.below(step)):
                pl.when(there)(lambda: self.sideways(target).start())
        self.sideways(line.z).start()
        self.fetch(line.count - 1)

    def add(self, target, slot, more):
        rows = self.out.shape[0]

        def some(index):
            part = pl.ds(pl.multiple_of(index * 16, 16), 16)
            total = self.pair_in[target, part, :].astype(F32) + self.mine[slot, part, :].astype(F32)
            for other in more:
                total += self.line_in[other, part, :].astype(F32)
            self.pair_in[target, part, :] = total.astype(BF)

        each(rows // 16, some)

    def pass_on(self, target, slot, up):
        line = self.line
        self.load(target, slot).wait()
        self.sideways(target).wait_recv()
        fed = line.has_down if up else line.has_up

        @pl.when(fed)
        def _():
            self.along(target, up).wait_recv()
            self.add(target, slot, [target + 1 if up else target])

        pl.when(jnp.logical_not(fed))(lambda: self.add(target, slot, []))
        self.along(target, up).start()

    def step(self, step):
        for slot, (there, target) in enumerate((self.above(step), self.below(step))):
            pl.when(there)(lambda: self.pass_on(target, slot, slot == 0))
        self.fetch(step - 1)

    def close(self):
        line = self.line
        z = line.z
        self.load(z, 0).wait()
        self.sideways(z).wait_recv()
        rows = self.out.shape[0]

        def final(more):
            def some(index):
                part = pl.ds(pl.multiple_of(index * 16, 16), 16)
                total = self.pair_in[z, part, :].astype(F32) + self.mine[0, part, :].astype(F32)
                for other in more:
                    total += self.line_in[other, part, :].astype(F32)
                self.out[part, :] = total

            each(rows // 16, some)

        pl.when(line.has_down)(lambda: self.along(z, True).wait_recv())
        pl.when(line.has_up)(lambda: self.along(z, False).wait_recv())
        pl.when(jnp.logical_not(line.has_down))(lambda: final([z]))
        pl.when(jnp.logical_not(line.has_up))(lambda: final([z + 1]))
        pl.when(line.has_down & line.has_up)(lambda: final([z, z + 1]))
        for step in range(line.count - 1, 0, -1):
            for up, (there, target) in ((True, self.above(step)), (False, self.below(step))):

                @pl.when(there)
                def _():
                    self.sideways(target).wait_send()
                    self.along(target, up).wait_send()

        self.sideways(z).wait_send()

    def actions(self):
        return [self.start] + [functools.partial(self.step, s) for s in range(self.line.count - 1, 0, -1)] + [self.close]


def spread(block, depth, lanes, width):
    row = lax.broadcasted_iota(jnp.int32, (lanes, width), 0)
    column = lax.broadcasted_iota(jnp.int32, (lanes, width), 1)
    hit = (column - row == block * depth) & (row < depth)
    return jnp.where(hit, 1.0, 0.0).astype(BF)


def turn_half(values):
    return pltpu.roll(values, PAD // 2, 1)


def meet(*circles):
    barrier = pltpu.get_barrier_semaphore()
    for circle in circles:
        circle.greet(barrier)
    pl.semaphore_wait(barrier, sum(circle.peers() for circle in circles))


class Weights:
    def __init__(self, line, own, blocks, held, sems, first=0):
        self.copies = []
        columns = pl.ds(first, own.shape[1])
        depth = own.shape[0]
        count = line.count
        for index in range(2 * count):
            shift, side = index // 2, index % 2
            block = lax.rem(line.z + shift, count) * 2 + lax.rem(line.x + side, 2)
            source = blocks.at[block] if index else own
            rows = pl.ds(pl.multiple_of(block * depth, 16), depth)
            self.copies.append(pltpu.make_async_copy(source, held.at[rows, columns], sems.at[index]))

    def start(self):
        for copy in self.copies:
            copy.start()

    def wait(self):
        for copy in self.copies:
            copy.wait()


def start_coming(r):
    for copy in r.coming.values():
        copy.start()


class Pump:
    def __init__(self, tasks, plan):
        self.steps = [step for together in zip(*[task.actions() for task in tasks]) for step in together]
        self.plan = list(plan)

    def __call__(self):
        count = self.plan.pop(0) if self.plan else 0
        self.do(count)

    def do(self, count):
        for step in self.steps[:count]:
            step()
        self.steps = self.steps[count:]

    def rest(self):
        self.do(len(self.steps))


def fetches_of(line, r, count):
    return [
        Fetch(
            line,
            getattr(r, f"own{i}"),
            getattr(r, f"blocks{i}"),
            getattr(r, f"fetch_send{i}"),
            getattr(r, f"fetch_recv{i}"),
        )
        for i in range(count)
    ]


def reduces_of(line, r, count):
    return [
        Reduce(
            line,
            getattr(r, f"sum{i}"),
            getattr(r, f"total{i}"),
            *[getattr(r, f"reduce{i}_{j}") for j in range(8)],
        )
        for i in range(count)
    ]


def comm_of(r):
    group = Group()
    gather = Gather(group, r.full, r.g_send, r.g_recv)
    scatter = Scatter(group, r.parts, r.near, r.away, r.landed, r.s_send, r.s_recv)
    return group, gather, scatter


def out_columns(scatter, turn, left_rows, right_tile, columns):
    product = nt(left_rows, right_tile)
    rows = product.shape[0] // 2
    scatter.parts[turn, 0, :, columns] = product[:rows].astype(BF)
    scatter.parts[turn, 1, :, columns] = product[rows:].astype(BF)


def norm_rows(source, gain, full, slot):
    def norm(index):
        part = tile(index, 32)
        values = source[part, :]
        factor = lax.rsqrt(jnp.mean(values * values, axis=-1, keepdims=True) + epsilon)
        full[slot, part, :] = (values * factor * gain).astype(BF)

    each(source.shape[0] // 32, norm)


def add_rows(scatter, source, target):
    def close(index):
        part = tile(index, 32)
        target[part, :] = source[part, :] + scatter.total(part)

    each(source.shape[0] // 32, close)


def pack_attn(query, key, value, output, target):
    width, each_kv = query.shape[1], key.shape[1]
    target[:, 0:width] = query[...].astype(BF)
    both = jnp.concatenate([key[...], value[...]], axis=1)
    target[:, width : width + 2 * each_kv] = both.astype(BF)
    target[:, width + 2 * each_kv :] = output[...].astype(BF)


def count_rows(documents, below):
    hits = jnp.where(documents < below, 1.0, 0.0)
    return jnp.sum(jnp.sum(hits, axis=1, keepdims=True), axis=0, keepdims=True).astype(jnp.int32)


def starts_of(marks, places):
    head, body_end = marks[0:1, 0:1], marks[1:2, 0:1]
    return jnp.where(places < head, 0, jnp.where(places < body_end, head, body_end))


def make_tables(r):
    marks = jnp.concatenate([count_rows(r.documents[...], 1), count_rows(r.documents[...], 2)], axis=0)
    r.marks[0:2, :] = jnp.broadcast_to(marks, (2, PAD))
    r.marks[2:, :] = jnp.zeros((6, PAD), jnp.int32)

    def some(index):
        where = tile(index, 128)
        places = lax.broadcasted_iota(jnp.int32, (128, PAD), 0) + index * 128
        offset = places - starts_of(r.marks, places)
        angles = offset.astype(F32) * r.freqs[0:1, :]
        r.cosine[where, :] = jnp.cos(angles)
        r.sine[where, :] = jnp.sin(angles) * r.freqs[1:2, :]

    each(r.cosine.shape[0] // 128, some)


def attn_forward_kernel(first, level, fetch_count, plan, r):
    rows, width = r.x.shape
    n_dp, depth = r.w_sems.shape[0], r.own.shape[0]
    line = Line(n_dp)
    group, gather, scatter = comm_of(r)
    tasks = fetches_of(line, r, fetch_count)
    weights = Weights(line, r.own, r.blocks, r.held, r.w_sems)
    circles = (group, line) if first or tasks else (group,)
    meet(*circles)
    if first:
        raw = {}
        for name in ("gate0", "up0", "down0", "query1", "key1", "value1", "output1", "gate1", "up1", "down1"):
            raw[name] = pltpu.make_async_copy(
                getattr(r, "raw_" + name), getattr(r, name), r.raw_sems.at[len(raw)]
            )
            raw[name].start()
        lanes = r.gain_own.shape[1]
        r.gain_raw[...] = jnp.zeros_like(r.gain_raw)
        for row in range(4):
            r.gain_raw[row : row + 1, 0:depth] = getattr(r, f"gain{row}")[...]
        r.gain_own[...] = r.gain_raw[...].astype(BF)
        pack_attn(r.raw_query0, r.raw_key0, r.raw_value0, r.raw_output0, r.own)
        start_coming(r)
        leave(r, "own")
        gain_fetch = Fetch(line, r.gain_own, r.gain_blocks, r.gain_send, r.gain_recv)
        weight_fetch = Fetch(line, r.own, r.blocks, r.weight_send, r.weight_recv)
        gain_fetch.start()
        weight_fetch.start()
        for step in gain_fetch.actions()[1:]:
            step()
        r.gains[...] = jnp.zeros_like(r.gains)

        def gather_gain(block):
            chosen = spread(block, depth, lanes, width)

            @pl.when(block == line.mine)
            def _():
                r.gains[...] += nn(r.gain_own[...], chosen)

            @pl.when(block != line.mine)
            def _():
                r.gains[...] += nn(r.gain_blocks[block], chosen)

        each(n_dp, gather_gain)
        come(r, "x")
        norm_rows(r.x, r.gains[2 * level : 2 * level + 1, :], r.full, group.me)
        gather.start()
        weight_steps = weight_fetch.actions()[1:-1]
        for step in weight_steps[:1]:
            step()
        ahead = Gather(group, r.ahead, r.a_send, r.a_recv)
        come(r, "cotangent")
        r.ahead[group.me] = r.cotangent[...].astype(BF)
        ahead.start()
        for name in ("gate0", "up0"):
            raw[name].wait()
        r.own0[...] = r.gate0[...].astype(BF)
        r.own1[...] = r.up0[...].astype(BF)
        leave(r, "own0", "own1")
        for step in weight_steps[1:]:
            step()
        pump = Pump(tasks, plan)
        pump()
        make_tables(r)
        for name in list(raw)[2:]:
            raw[name].wait()
        pack_attn(r.query1, r.key1, r.value1, r.output1, r.attn_pack1)
        r.down_pack0[...] = r.down0[...].astype(BF)
        r.down_pack1[...] = r.down1[...].astype(BF)
        r.gate_pack1[...] = r.gate1[...].astype(BF)
        r.up_pack1[...] = r.up1[...].astype(BF)
        leave(r, "down_pack0", "down_pack1", "attn_pack1", "gate_pack1", "up_pack1", "cosine", "sine")
        come(r, "place")
        weight_fetch.finish()
        weights.start()
    else:
        weights.start()
        pump = Pump(tasks, plan)
        pump()
        start_coming(r)
        norm_rows(r.x, r.gains[2 * level : 2 * level + 1, :], r.full, group.me)
        gather.start()
        come(r, "place", "cosine", "sine")
    weights.wait()
    place = r.place[...]
    heads = place.shape[1] // PAD
    compact_width, head_width = place.shape
    padded, qkv, mixed, compact, held = r.padded, r.qkv, r.mixed, r.compact, r.held

    def pad(index):
        part = tile(index, 256)
        padded[part, 0:head_width] = nn(held[part, 0:compact_width], place).astype(BF)
        padded[part, head_width : 2 * head_width] = nn(
            held[part, compact_width : 2 * compact_width], place
        ).astype(BF)

    each(width // 256, pad)

    def project(chip):
        left = r.full[pl.ds(2 * chip, 2)].reshape(2 * rows, width)
        where = tile(chip, 2 * rows)
        cosine, sine = r.cosine[where, :], r.sine[where, :]

        def turned(index):
            columns = tile(index, 2 * PAD)
            product = nn(left, padded[:, columns])
            for half in range(2):
                u = product[:, half * PAD : (half + 1) * PAD]
                qkv[where, tile(2 * index + half, PAD)] = (u * cosine + turn_half(u) * sine).astype(BF)

        each(3 * heads // 4, turned)
        columns = pl.ds(3 * heads // 2 * PAD, heads // 2 * PAD)
        qkv[where, columns] = nn(left, padded[:, columns]).astype(BF)

    gather.wait_chip()
    project(group.chip)
    pump()
    gather.forward()
    pump()
    gather.wait_other()
    project(1 - group.chip)
    copies = [
        pltpu.make_async_copy(r.full, r.a_out, r.out_sems.at[0]),
        pltpu.make_async_copy(qkv, r.qkv_out, r.out_sems.at[1]),
    ]
    for copy in copies:
        copy.start()
    if first:
        ahead.wait_chip()
        ahead.forward()
    pump()
    kv_at = heads * PAD
    value_at = kv_at + heads // 2 * PAD
    for turn in range(4):
        prob = getattr(r, f"prob{turn}")
        reach = prob.shape[2]
        where = pl.ds(turn * rows, rows)
        places = lax.broadcasted_iota(jnp.int32, (rows, PAD), 0) + turn * rows
        begin = starts_of(r.marks, places)
        head, body_end = r.marks[0:1, 0:1], r.marks[1:2, 0:1]
        end = jnp.where(places < head, head, jnp.where(places < body_end, body_end, 4 * rows))
        end = jnp.minimum(begin + ((places - begin) // BLOCK + 1) * BLOCK, end)
        place_of = lax.broadcasted_iota(jnp.int32, (rows, reach), 1)
        inside = (place_of >= begin[:, 0:1]) & (place_of < end[:, 0:1])
        r.bias[:, 0:reach] = jnp.where(inside, 0.0, masked_value)

        def attend(head):
            query = qkv[where, tile(head, PAD)]
            key = qkv[0:reach, pl.ds(kv_at + head // 2 * PAD, PAD)]
            value = qkv[0:reach, pl.ds(value_at + head // 2 * PAD, PAD)]
            scores = nt(query, key) * scale + r.bias[:, 0:reach]
            exponent = jnp.exp(scores - jnp.max(scores, axis=-1, keepdims=True))
            summed = jnp.sum(exponent, axis=-1, keepdims=True)
            low = (exponent * (1.0 / summed)).astype(BF)
            prob[head] = low
            mixed[where, tile(head, PAD)] = nn(low, value).astype(BF)

        for head in range(heads):
            attend(head)
        copy = pltpu.make_async_copy(prob, getattr(r, f"p_out{turn}"), r.out_sems.at[2 + turn])
        copy.start()
        copies.append(copy)
        compact[where, :] = nt(mixed[where, :], place).astype(BF)
        pump()
    copies.append(pltpu.make_async_copy(compact, r.o_out, r.out_sems.at[6]))
    copies[-1].start()
    if first:
        ahead.wait_other()
        copies.append(pltpu.make_async_copy(r.ahead, r.ahead_out, r.out_sems.at[7]))
        copies[-1].start()
        ahead.finish()
    for turn in range(2):
        left = compact[tile(scatter.rows_of(turn), 2 * rows), :]

        def part_of(index):
            columns = tile(index, 256)
            out_columns(scatter, turn, left, held[columns, 2 * compact_width :], columns)

        each(width // 256, part_of)
        scatter.send_core(turn)
        if turn == 0:
            scatter.send_away()
        pump()
    scatter.wait()
    pump()
    add_rows(scatter, r.x, r.middle)
    leave(r, "middle")
    pump.rest()
    gather.finish()
    scatter.finish()
    for copy in copies:
        copy.wait()


def wide_of(line, r):
    return [
        Weights(line, r.gate_own, r.gate_blocks, r.wide, r.gate_sems),
        Weights(line, r.up_own, r.up_blocks, r.wide, r.up_sems, r.gate_own.shape[1]),
    ]


def mlp_forward_kernel(level, fetch_count, plan, r):
    rows, width = r.middle.shape
    units = r.hid.shape[1]
    line = Line(r.w_sems.shape[0])
    group, gather, scatter = comm_of(r)
    down = Fetch(line, r.own, r.blocks, r.down_send, r.down_recv)
    down_steps = down.actions()[1:-1]
    wide, held, gu, hid = r.wide, r.held, r.gu, r.hid
    wide_weights = wide_of(line, r)
    weights = Weights(line, r.own, r.blocks, held, r.w_sems)
    meet(group, line)
    down.start()
    for copy in wide_weights:
        copy.start()
    pump = Pump(fetches_of(line, r, fetch_count), plan)
    pump()
    norm_rows(r.middle, r.gains[2 * level + 1 : 2 * level + 2, :], r.full, group.me)
    gather.start()
    for copy in wide_weights:
        copy.wait()

    def expand(chip):
        left = r.full[pl.ds(2 * chip, 2)].reshape(2 * rows, width)
        where = tile(chip, 2 * rows)

        def unit(index):
            columns = tile(index, 256)
            further = pl.ds(pl.multiple_of(units + index * 256, 256), 256)
            gate = nn(left, wide[:, columns])
            up = nn(left, wide[:, further])
            hid[where, columns] = (gate / (1.0 + jnp.exp(-gate)) * up).astype(BF)
            gu[where, columns] = gate.astype(BF)
            gu[where, further] = up.astype(BF)

        each(units // 256, unit)

    gather.wait_chip()
    expand(group.chip)
    for step in down_steps[:1]:
        step()
    gather.forward()
    for step in down_steps[1:2]:
        step()
    pump()
    gather.wait_other()
    expand(1 - group.chip)
    for step in down_steps[2:]:
        step()
    pump()
    copies = [
        pltpu.make_async_copy(r.full, r.m_out, r.out_sems.at[0]),
        pltpu.make_async_copy(gu, r.gu_out, r.out_sems.at[1]),
        pltpu.make_async_copy(hid, r.hid_out, r.out_sems.at[2]),
    ]
    for copy in copies:
        copy.start()
    down.finish()
    weights.start()
    weights.wait()
    for turn in range(2):
        left = hid[tile(scatter.rows_of(turn), 2 * rows), :]

        def part_of(index):
            columns = tile(index, 256)
            out_columns(scatter, turn, left, held[columns, :], columns)

        each(width // 256, part_of)
        scatter.send_core(turn)
        if turn == 0:
            scatter.send_away()
        pump()
    scatter.wait()
    pump()
    add_rows(scatter, r.middle, r.result)
    leave(r, "result")
    pump.rest()
    gather.finish()
    scatter.finish()
    for copy in copies:
        copy.wait()


def weight_grads(source, right, target, columns):
    width = source.shape[-1]
    depth = target.shape[1]
    chunk = math.lcm(depth, PAD)

    def some(index):
        left = source[..., tile(index, chunk)].reshape(right.shape[0], chunk)
        product = tn(left, right[...]).astype(BF)
        for part in range(chunk // depth):
            rows = slice(part * depth, (part + 1) * depth)
            target[index * (chunk // depth) + part, :, columns] = product[rows]

    each(width // chunk, some)


def close_back(scatter, grad_in_ref, state_ref, gain, grad_out, dgain):
    rows = state_ref.shape[0]
    dgain[...] = jnp.zeros_like(dgain)

    def close(index):
        part = tile(index, 32)
        values = state_ref[part, :]
        factor = lax.rsqrt(jnp.mean(values * values, axis=-1, keepdims=True) + epsilon)
        normed = values * factor
        grad_in = scatter.total(part)
        dgain[...] += jnp.sum((grad_in * normed).reshape(4, 8, -1), axis=0)
        grad_norm = grad_in * gain
        inner = jnp.mean(grad_norm * normed, axis=-1, keepdims=True)
        grad_out[part, :] = grad_in_ref[part, :] + factor * (grad_norm - normed * inner)

    each(rows // 32, close)


def mlp_backward_kernel(level, reduce_count, plan, ready, r):
    rows, width = r.middle.shape
    units = r.hid.shape[1]
    n_dp = r.w_sems.shape[0]
    line = Line(n_dp)
    group, gather, scatter = comm_of(r)
    wide, held, gu, hid = r.wide, r.held, r.gu, r.hid
    weights = [
        Weights(line, r.own, r.blocks, held, r.w_sems),
        *wide_of(line, r),
    ]
    fetches = [
        pltpu.make_async_copy(r.hid_in, hid, r.in_sems.at[2]),
        pltpu.make_async_copy(r.gu_in, gu, r.in_sems.at[1]),
        pltpu.make_async_copy(r.m_in, r.m_full, r.in_sems.at[0]),
    ]
    down = Reduce(line, r.grads, r.down_total, *[getattr(r, f"down{j}") for j in range(8)])
    meet(group, line)
    pump = Pump(reduces_of(line, r, reduce_count), plan)
    pump.steps += down.actions()[1:]
    pump()
    for copy in weights[:1] + fetches + weights[1:]:
        copy.start()
    start_coming(r)
    if ready:
        whole = pltpu.make_async_copy(r.ahead_in, r.full, r.in_sems.at[3])
        whole.start()
    else:
        r.full[group.me] = r.grad[...].astype(BF)
        gather.start()
    for copy in weights[:1] + fetches[:2]:
        copy.wait()

    def inward(chip):
        left = r.full[pl.ds(2 * chip, 2)].reshape(2 * rows, width)
        where = tile(chip, 2 * rows)

        def unit(index):
            columns = tile(index, 256)
            further = pl.ds(pl.multiple_of(units + index * 256, 256), 256)
            grad = nn(left, held[:, columns])
            gate = gu[where, columns].astype(F32)
            up = gu[where, further].astype(F32)
            sig = 1.0 / (1.0 + jnp.exp(-gate))
            gu[where, columns] = (grad * up * sig * (1.0 + gate * (1.0 - sig))).astype(BF)
            gu[where, further] = (grad * gate * sig).astype(BF)

        each(units // 256, unit)

    if ready:
        whole.wait()
    else:
        gather.wait_chip()
        inward(group.chip)
        pump()
        gather.forward()
        pump()
        gather.wait_other()
    weight_grads(r.full, hid, r.grads, slice(0, units))
    down.start()
    if ready:
        inward(group.chip)
    inward(1 - group.chip)
    for copy in weights[1:] + fetches[2:]:
        copy.wait()
    pump()
    for turn in range(2):
        where = tile(scatter.rows_of(turn), 2 * rows)

        def part_of(index):
            columns = tile(index, 256)
            out_columns(scatter, turn, gu[where, :], wide[columns, :], columns)

        each(width // 256, part_of)
        scatter.send_core(turn)
        if turn == 0:
            scatter.send_away()
        pump()
    for part in range(2):
        columns = slice(part * units, (part + 1) * units)
        weight_grads(r.m_full, gu.at[:, columns], r.wide_grads, columns)
        pump()
    copies = [pltpu.make_async_copy(r.wide_grads, r.wide_out, r.out_sems.at[0])]
    copies[0].start()
    scatter.wait()
    pump()
    come(r, *r.coming)
    close_back(
        scatter, r.grad, r.middle, r.gains[2 * level + 1 : 2 * level + 2, :], r.grad_out, r.dgain
    )
    leave(r, "grad_out")
    pump.rest()
    if not ready:
        gather.finish()
    scatter.finish()
    for copy in copies:
        copy.wait()


def attn_backward_kernel(level, reduce_count, plan, final, r):
    rows, width = r.x.shape
    n_dp = r.w_sems.shape[0]
    depth = width // n_dp
    line = Line(n_dp)
    group, gather, scatter = comm_of(r)
    tasks = reduces_of(line, r, reduce_count)
    held, qkv, compact = r.held, r.qkv, r.compact
    probs = [getattr(r, f"prob{turn}") for turn in range(4)]
    weights = Weights(line, r.own, r.blocks, held, r.w_sems)
    fetches = [
        pltpu.make_async_copy(r.a_in, r.a_full, r.in_sems.at[0]),
        pltpu.make_async_copy(r.o_in, compact, r.in_sems.at[1]),
        pltpu.make_async_copy(r.qkv_in, qkv, r.in_sems.at[2]),
    ] + [
        pltpu.make_async_copy(getattr(r, f"p_in{turn}"), probs[turn], r.in_sems.at[3 + turn])
        for turn in range(4)
    ]
    meet(*((group, line) if tasks else (group,)))
    pump = Pump(tasks, plan)
    pump()
    weights.start()
    for copy in fetches:
        copy.start()
    start_coming(r)
    r.full[group.me] = r.grad[...].astype(BF)
    gather.start()
    pump()
    weights.wait()
    for copy in fetches:
        copy.wait()
    come(r, *r.coming)
    place = r.place[...]
    heads = place.shape[1] // PAD
    compact_width, head_width = place.shape

    def inward(chip):
        left = r.full[pl.ds(2 * chip, 2)].reshape(2 * rows, width)
        where = tile(chip, 2 * rows)
        grad = nn(left, held[:, 2 * compact_width :]).astype(BF)
        r.grad_mixed[where, :] = nn(grad, place).astype(BF)

    gather.wait_chip()
    inward(group.chip)
    pump()
    gather.forward()
    pump()
    gather.wait_other()
    inward(1 - group.chip)
    kv_at = heads * PAD
    value_at = kv_at + heads // 2 * PAD
    r.grad_k[...] = jnp.zeros_like(r.grad_k)
    r.grad_v[...] = jnp.zeros_like(r.grad_v)
    for turn, prob in enumerate(probs):
        reach = prob.shape[2]
        where = pl.ds(turn * rows, rows)
        cosine, sine = r.cosine[where, :], r.sine[where, :]

        def attend(head):
            mine = tile(head, PAD)
            shared = tile(head // 2, PAD)
            query = qkv[where, mine]
            key = qkv[0:reach, pl.ds(kv_at + head // 2 * PAD, PAD)]
            value = qkv[0:reach, pl.ds(value_at + head // 2 * PAD, PAD)]
            grad = r.grad_mixed[where, mine]
            low = prob[head]
            grad_prob = nt(grad, value)
            weight = low.astype(F32)
            inner = jnp.sum(weight * grad_prob, axis=-1, keepdims=True)
            grad_score = (weight * (grad_prob - inner)).astype(BF)
            u = nn(grad_score, key) * scale
            r.grad_q[where, mine] = (u * cosine - turn_half(u) * sine).astype(BF)
            r.grad_k[0:reach, shared] += tn(grad_score, query)
            r.grad_v[0:reach, shared] += tn(low, grad)

        for head in range(heads):
            attend(head)
        pump()
    for pair in range(heads // 2):
        columns = pl.ds(pair * PAD, PAD)
        u = r.grad_k[:, columns] * scale
        r.grad_kv[:, columns] = (u * r.cosine[...] - turn_half(u) * r.sine[...]).astype(BF)
        r.grad_kv[:, pl.ds((heads // 2 + pair) * PAD, PAD)] = r.grad_v[:, columns].astype(BF)
    grad_low = r.grad_low
    grad_low[:, 0:compact_width] = nt(r.grad_q[...], place).astype(BF)
    grad_low[:, compact_width : 2 * compact_width] = nt(r.grad_kv[...], place).astype(BF)
    for turn in range(2):
        where = tile(scatter.rows_of(turn), 2 * rows)

        def part_of(index):
            columns = tile(index, 256)
            out_columns(
                scatter, turn, grad_low[where, :], held[columns, 0 : 2 * compact_width], columns
            )

        each(width // 256, part_of)
        scatter.send_core(turn)
        if turn == 0:
            scatter.send_away()
        pump()
    grads = r.grads
    weight_grads(r.a_full, grad_low, grads, slice(0, 2 * compact_width))
    weight_grads(r.full, compact, grads, slice(2 * compact_width, 3 * compact_width))
    if not final:
        copy = pltpu.make_async_copy(grads, r.grads_out, r.out_sems.at[0])
        copy.start()
    pump()
    scatter.wait()
    pump()
    close_back(scatter, r.grad, r.x, r.gains[2 * level : 2 * level + 1, :], r.grad_out, r.dgain)
    leave(r, "grad_out")
    if final:
        attn = Reduce(line, grads, r.attn_total, *[getattr(r, f"attn{j}") for j in range(8)])
        gains = gain_sums(line, group, r)
        gains.start()
        attn.start()
        pump.rest()
        for step in gains.actions()[1:] + attn.actions()[1:]:
            step()
    pump.rest()
    gather.finish()
    scatter.finish()
    if not final:
        copy.wait()


def gain_sums(line, group, r):
    n_dp, _, lanes = r.gain_blocks.shape
    width = r.rows.shape[1]
    depth = width // n_dp
    for row, part in enumerate((r.dgain, r.dgain1, r.dgain2, r.dgain3)):
        r.rows[row : row + 1, :] = jnp.sum(part[...], axis=0, keepdims=True)
    r.rows[4:8, :] = jnp.zeros((4, width), F32)
    for turn, device in enumerate((group.core, group.other)):
        copy = group.remote(r.rows, r.others.at[turn], r.row_send.at[turn], r.row_recv.at[turn], device)
        copy.start()
        copy.wait()
        r.rows[...] += r.others[turn]
    both = jnp.concatenate([r.rows[...], jnp.zeros((GAIN_ROWS - 8, width), F32)], axis=0).astype(BF)

    def gain_rows(block):
        r.gain_blocks[block] = nt(both, spread(block, depth, lanes, width)).astype(BF)

    each(n_dp, gain_rows)
    return Reduce(line, r.gain_blocks, r.gain_total, *[getattr(r, f"gain{j}") for j in range(8)])


def shaped(shape, dtype):
    return jax.ShapeDtypeStruct(shape, dtype)


def dma(count):
    return pltpu.SemaphoreType.DMA((count,))


def vmem(*shape, dtype=BF):
    return pltpu.VMEM(shape, dtype)


def reaches(rows):
    return [min((turn + 1) * rows + PAD, 4 * rows) for turn in range(4)]


def come(r, *names):
    for name in names:
        r.coming[name].wait()


def leave(r, *names):
    for name in names:
        r.leaving[name].start()


def launch(kernel, which, name, ins, outs, scratch):
    late = [each_of for each_of, (_, spec) in ins.items() if spec is SELF]
    early = [each_of for each_of, (_, spec) in outs.items() if spec is SELF]
    names = [n + "_" * (n in late) for n in ins] + [n + "_" * (n in early) for n in outs]
    scratch = scratch | {n: vmem(*ins[n][0].shape, dtype=ins[n][0].dtype) for n in late}
    scratch |= {n: vmem(*outs[n][0].shape, dtype=outs[n][0].dtype) for n in early}
    scratch["own_sems"] = dma(len(late) + len(early) + 1)
    names += list(scratch)

    def entry(*refs):
        r = types.SimpleNamespace(**dict(zip(names, refs)))
        sems = iter(range(len(late) + len(early)))
        r.coming = {
            n: pltpu.make_async_copy(getattr(r, n + "_"), getattr(r, n), r.own_sems.at[next(sems)]) for n in late
        }
        r.leaving = {
            n: pltpu.make_async_copy(getattr(r, n), getattr(r, n + "_"), r.own_sems.at[next(sems)]) for n in early
        }
        kernel(r)
        for copy in r.leaving.values():
            copy.wait()

    results = pl.pallas_call(
        entry,
        out_shape=[shape for shape, _ in outs.values()],
        in_specs=[ANY if spec is SELF else spec for _, spec in ins.values()],
        out_specs=[ANY if spec is SELF else spec for _, spec in outs.values()],
        scratch_shapes=list(scratch.values()),
        compiler_params=pltpu.CompilerParams(
            collective_id=which, has_side_effects=True, vmem_limit_bytes=LIMIT
        ),
        cost_estimate=pl.CostEstimate(
            flops=20_000_000_000, bytes_accessed=60_000_000, transcendentals=0
        ),
        name=name,
    )(*[array for array, _ in ins.values()])
    return types.SimpleNamespace(**dict(zip(outs, results)))


def comm_scratch(rows, width):
    return dict(
        full=vmem(4, rows, width),
        parts=vmem(2, 2, rows, width),
        near=vmem(2, rows, width),
        away=vmem(rows, width),
        landed=vmem(rows, width),
        g_send=dma(5),
        g_recv=dma(5),
        s_send=dma(4),
        s_recv=dma(4),
    )


def blocks_of(pack, n_dp):
    return shaped((n_dp,) + pack.shape, pack.dtype)


def fetch_refs(packs, n_dp):
    ins, outs, scratch = {}, {}, {}
    for i, pack in enumerate(packs):
        ins[f"own{i}"] = (pack, ANY)
        outs[f"blocks{i}"] = (blocks_of(pack, n_dp), ANY)
        scratch[f"fetch_send{i}"], scratch[f"fetch_recv{i}"] = Fetch.scratch(n_dp)
    return ins, outs, scratch


def reduce_refs(sums):
    ins, outs, scratch = {}, {}, {}
    for i, blocks in enumerate(sums):
        n_dp, depth, columns = blocks.shape
        ins[f"sum{i}"] = (blocks, ANY)
        outs[f"total{i}"] = (shaped((depth, columns), F32), VM)
        for j, each_of in enumerate(Reduce.scratch(n_dp, depth, columns)):
            scratch[f"reduce{i}_{j}"] = each_of
    return ins, outs, scratch


def totals(out, count):
    return [getattr(out, f"total{i}") for i in range(count)]


def fetched(out, count):
    return [getattr(out, f"blocks{i}") for i in range(count)]


def attn_forward(level, which, states, tables, place, gains, pack, blocks, packs, plan, raw=None):
    rows, width = states.shape
    first = raw is not None
    if first:
        depth, columns = raw["raw_query0"].shape[0], 3 * raw["raw_query0"].shape[1]
        pack = shaped((depth, columns), BF)
    depth, columns = pack.shape
    n_dp = width // depth
    heads = place.shape[1] // PAD
    length = 4 * rows
    ins = dict(x=(states, SELF if first else VM), place=(place, SELF))
    outs = dict(
        middle=(shaped((rows, width), F32), SELF),
        a_out=(shaped((4, rows, width), BF), ANY),
        qkv_out=(shaped((length, 2 * heads * PAD), BF), ANY),
        o_out=(shaped((length, place.shape[0]), BF), ANY),
    )
    scratch = comm_scratch(rows, width) | dict(
        held=vmem(width, columns),
        padded=vmem(width, 2 * heads * PAD),
        qkv=vmem(length, 2 * heads * PAD),
        mixed=vmem(length, heads * PAD),
        compact=vmem(length, place.shape[0]),
        bias=vmem(rows, length, dtype=F32),
        w_sems=dma(n_dp),
        out_sems=dma(8),
    )
    for turn, reach in enumerate(reaches(rows)):
        outs[f"p_out{turn}"] = (shaped((heads, rows, reach), BF), ANY)
        scratch[f"prob{turn}"] = vmem(heads, rows, reach)
    if first:
        units = raw["raw_gate0"].shape[1]
        now = ("raw_query0", "raw_key0", "raw_value0", "raw_output0")
        for name, array in raw.items():
            late = name.startswith("raw_") and name not in now
            ins[name] = (array, ANY if late else SELF if array.shape == states.shape else VM)
            if late:
                scratch[name[4:]] = vmem(*array.shape, dtype=F32)
        outs |= dict(
            gains=(shaped((GAIN_ROWS, width), F32), VM),
            blocks=(blocks_of(pack, n_dp), ANY),
            own=(pack, SELF),
            own0=(shaped((depth, units), BF), SELF),
            own1=(shaped((depth, units), BF), SELF),
            blocks0=(shaped((n_dp, depth, units), BF), ANY),
            blocks1=(shaped((n_dp, depth, units), BF), ANY),
            down_pack0=(shaped((depth, units), BF), SELF),
            attn_pack1=(pack, SELF),
            gate_pack1=(shaped((depth, units), BF), SELF),
            up_pack1=(shaped((depth, units), BF), SELF),
            down_pack1=(shaped((depth, units), BF), SELF),
            cosine=(shaped((length, PAD), F32), SELF),
            sine=(shaped((length, PAD), F32), SELF),
            marks=(shaped((8, PAD), jnp.int32), VM),
            ahead_out=(shaped((4, rows, width), BF), ANY),
        )
        scratch |= dict(ahead=vmem(4, rows, width), a_send=dma(5), a_recv=dma(5))
        scratch["gain_raw"] = vmem(GAIN_ROWS, 256, dtype=F32)
        scratch["gain_own"] = vmem(GAIN_ROWS, 256)
        scratch["gain_blocks"] = vmem(n_dp, GAIN_ROWS, 256)
        scratch["raw_sems"] = dma(10)
        for name, tail in (("gain", ""), ("weight", ""), ("fetch", "0"), ("fetch", "1")):
            scratch[f"{name}_send{tail}"], scratch[f"{name}_recv{tail}"] = Fetch.scratch(n_dp)
        more = {}, {}, {}
    else:
        cosine, sine, marks = tables
        ins |= dict(
            gains=(gains, VM), cosine=(cosine, SELF), sine=(sine, SELF), marks=(marks, VM), own=(pack, ANY), blocks=(blocks, ANY)
        )
        more = fetch_refs(packs, n_dp)
    return launch(
        functools.partial(attn_forward_kernel, first, level, 2 if first else len(packs), plan),
        which, f"attn_forward_{level}", ins | more[0], outs | more[1], scratch | more[2],
    )


def mlp_refs(rows, width, wide, own):
    depth, units = own.shape
    n_dp = width // depth
    ins = dict(own=(own, ANY))
    ins |= {name: (array, ANY) for name, array in wide.items()}
    scratch = comm_scratch(rows, width) | dict(
        wide=vmem(width, 2 * units),
        held=vmem(width, units),
        gu=vmem(4 * rows, 2 * units),
        hid=vmem(4 * rows, units),
        gate_sems=dma(n_dp),
        up_sems=dma(n_dp),
        w_sems=dma(n_dp),
    )
    return n_dp, units, ins, scratch


def mlp_forward(level, which, middle, gains, wide, down_own, packs, plan):
    rows, width = middle.shape
    n_dp, units, ins, scratch = mlp_refs(rows, width, wide, down_own)
    ins |= dict(middle=(middle, VM), gains=(gains, VM))
    outs = dict(
        result=(shaped((rows, width), F32), SELF),
        m_out=(shaped((4, rows, width), BF), ANY),
        gu_out=(shaped((4 * rows, 2 * units), BF), ANY),
        hid_out=(shaped((4 * rows, units), BF), ANY),
        blocks=(blocks_of(down_own, n_dp), ANY),
    )
    scratch |= dict(out_sems=dma(3))
    scratch["down_send"], scratch["down_recv"] = Fetch.scratch(n_dp)
    more = fetch_refs(packs, n_dp)
    return launch(
        functools.partial(mlp_forward_kernel, level, len(packs), plan),
        which, f"mlp_forward_{level}", ins | more[0], outs | more[1], scratch | more[2],
    )


def mlp_backward(level, which, grad, middle, gains, saved, wide, down, sums, plan, ahead=None):
    rows, width = middle.shape
    n_dp, units, ins, scratch = mlp_refs(rows, width, wide, down[0])
    depth = width // n_dp
    ins |= dict(
        blocks=(down[1], ANY),
        grad=(grad, VM if ahead is None else SELF), middle=(middle, SELF), gains=(gains, VM),
        m_in=(saved.m_out, ANY), gu_in=(saved.gu_out, ANY), hid_in=(saved.hid_out, ANY),
    )
    outs = dict(
        grad_out=(shaped((rows, width), F32), SELF),
        dgain=(shaped((8, width), F32), VM),
        wide_out=(shaped((n_dp, depth, 2 * units), BF), ANY),
        down_total=(shaped((depth, units), F32), VM),
    )
    scratch |= dict(
        m_full=vmem(4, rows, width),
        wide_grads=vmem(n_dp, depth, 2 * units),
        grads=vmem(n_dp, depth, units),
        in_sems=dma(4),
        out_sems=dma(3),
    )
    if ahead is not None:
        ins |= dict(ahead_in=(ahead, ANY))
    for j, each_of in enumerate(Reduce.scratch(n_dp, depth, units)):
        scratch[f"down{j}"] = each_of
    more = reduce_refs(sums)
    return launch(
        functools.partial(mlp_backward_kernel, level, len(sums), plan, ahead is not None),
        which, f"mlp_backward_{level}", ins | more[0], outs | more[1], scratch | more[2],
    )


def attn_backward(level, which, grad, states, gains, tables, place, saved, weights, sums, plan, dgains=()):
    cosine, sine, _ = tables
    pack, blocks = weights
    rows, width = states.shape
    depth, columns = pack.shape
    n_dp = width // depth
    heads = place.shape[1] // PAD
    length = 4 * rows
    ins = dict(
        grad=(grad, VM), x=(states, SELF), gains=(gains, VM), cosine=(cosine, SELF), sine=(sine, SELF), place=(place, SELF),
        own=(pack, ANY), blocks=(blocks, ANY),
        a_in=(saved.a_out, ANY), qkv_in=(saved.qkv_out, ANY), o_in=(saved.o_out, ANY),
    )
    outs = dict(
        grad_out=(shaped((rows, width), F32), SELF),
        dgain=(shaped((8, width), F32), VM),
    )
    scratch = comm_scratch(rows, width) | dict(
        held=vmem(width, columns),
        a_full=vmem(4, rows, width),
        qkv=vmem(length, 2 * heads * PAD),
        compact=vmem(length, place.shape[0]),
        grad_mixed=vmem(length, heads * PAD),
        grad_q=vmem(length, heads * PAD),
        grad_kv=vmem(length, heads * PAD),
        grad_k=vmem(length, heads // 2 * PAD, dtype=F32),
        grad_v=vmem(length, heads // 2 * PAD, dtype=F32),
        grad_low=vmem(length, 2 * place.shape[0]),
        grads=vmem(n_dp, depth, columns),
        w_sems=dma(n_dp),
        in_sems=dma(7),
        out_sems=dma(1),
    )
    for turn, reach in enumerate(reaches(rows)):
        ins[f"p_in{turn}"] = (getattr(saved, f"p_out{turn}"), ANY)
        scratch[f"prob{turn}"] = vmem(heads, rows, reach)
    if dgains:
        ins |= {f"dgain{1 + i}": (dgain, VM) for i, dgain in enumerate(dgains)}
        outs |= dict(
            gain_total=(shaped((GAIN_ROWS, 256), F32), VM),
            attn_total=(shaped((depth, columns), F32), VM),
        )
        scratch |= dict(
            gain_blocks=vmem(n_dp, GAIN_ROWS, 256),
            rows=vmem(8, width, dtype=F32),
            others=vmem(2, 8, width, dtype=F32),
            row_send=dma(2),
            row_recv=dma(2),
        )
        for j, each_of in enumerate(Reduce.scratch(n_dp, GAIN_ROWS, 256)):
            scratch[f"gain{j}"] = each_of
        for j, each_of in enumerate(Reduce.scratch(n_dp, depth, columns)):
            scratch[f"attn{j}"] = each_of
    else:
        outs |= dict(grads_out=(shaped((n_dp, depth, columns), BF), ANY))
    more = reduce_refs(sums)
    return launch(
        functools.partial(attn_backward_kernel, level, len(sums), plan, bool(dgains)),
        which, f"attn_backward_{level}", ins | more[0], outs | more[1], scratch | more[2],
    )


def constants(heads):
    place = np.zeros((heads * HEAD_DIM, heads * PAD), np.float32)
    for row in range(heads * HEAD_DIM):
        which, column = divmod(row, HEAD_DIM)
        place[row, which * PAD + column + (PAD // 2 - HALF if column >= HALF else 0)] = 1.0
    freqs = np.zeros((8, PAD), np.float32)
    for start in (0, PAD // 2):
        freqs[0, start : start + HALF] = np.exp(np.arange(HALF) * (-2.0 * math.log(rope_base) / HEAD_DIM))
    freqs[1, 0 : PAD // 2] = -1.0
    freqs[1, PAD // 2 :] = 1.0
    return jnp.asarray(place, BF), jnp.asarray(freqs)


def body(states_in, documents, *rest):
    cotangent = rest[-1]
    one, two = rest[0:9], rest[9:18]
    heads = one[1].shape[1] // HEAD_DIM
    place, freqs = constants(heads)
    raw = dict(documents=documents.reshape(-1, PAD), freqs=freqs, cotangent=cotangent)
    for level, w in enumerate((one, two)):
        raw[f"gain{2 * level}"] = w[0].reshape(1, -1)
        raw[f"gain{2 * level + 1}"] = w[5].reshape(1, -1)
        for name, array in zip(("query", "key", "value", "output", "", "gate", "up", "down"), w[1:]):
            if name:
                raw[f"raw_{name}{level}"] = array.T if name in ("output", "down") else array

    attn1 = attn_forward(
        0, 0, states_in, None, place, None, None, None, None, [2, 1, 0, 1, 0, 0, 1, 0, 0, 2, 1], raw
    )
    tables = (attn1.cosine, attn1.sine, attn1.marks)
    attn_pack = [attn1.own, attn1.attn_pack1]
    down_pack = [attn1.down_pack0, attn1.down_pack1]
    gains = attn1.gains
    wide1 = dict(
        gate_own=attn1.own0, gate_blocks=attn1.blocks0, up_own=attn1.own1, up_blocks=attn1.blocks1
    )
    mlp1 = mlp_forward(
        0, 1, attn1.middle, gains, wide1, down_pack[0], [attn_pack[1]], [0, 0, 1, 1, 2, 0]
    )
    down1 = (down_pack[0], mlp1.blocks)
    (attn2_blocks,) = fetched(mlp1, 1)
    attn2 = attn_forward(
        1, 2, mlp1.result, tables, place, gains, attn_pack[1], attn2_blocks, [attn1.gate_pack1, attn1.up_pack1],
        [2, 1, 1, 0, 0, 0, 1, 0, 0, 2, 1],
    )
    wide2 = dict(
        gate_own=attn1.gate_pack1, gate_blocks=attn2.blocks0, up_own=attn1.up_pack1, up_blocks=attn2.blocks1
    )
    mlp2 = mlp_forward(1, 3, attn2.middle, gains, wide2, down_pack[1], [], [])
    down2 = (down_pack[1], mlp2.blocks)

    back_mlp2 = mlp_backward(
        1, 4, cotangent, attn2.middle, gains, mlp2, wide2, down2, [], [0, 0, 1, 0, 1, 1, 0],
        attn1.ahead_out,
    )
    back_attn2 = attn_backward(
        1, 5, back_mlp2.grad_out, mlp1.result, gains, tables, place, attn2, (attn_pack[1], attn2_blocks),
        [back_mlp2.wide_out], [1, 0, 0, 1, 0, 1, 0, 0, 0, 1],
    )
    back_mlp1 = mlp_backward(
        0, 6, back_attn2.grad_out, attn1.middle, gains, mlp1, wide1, down1,
        [back_attn2.grads_out], [1, 1, 1, 1, 1, 1, 0, 1, 1],
    )
    back_attn1 = attn_backward(
        0, 7, back_mlp1.grad_out, states_in, gains, tables, place, attn1, (attn_pack[0], attn1.blocks),
        [back_mlp1.wide_out], [1, 0, 0, 1, 0, 0, 1, 0, 0, 1],
        (back_mlp1.dgain, back_attn2.dgain, back_mlp2.dgain),
    )
    (wide_total2,) = totals(back_attn2, 1)
    (attn_total2,) = totals(back_mlp1, 1)
    (wide_total1,) = totals(back_attn1, 1)
    attn_total1 = back_attn1.attn_total
    down_total1, down_total2 = back_mlp1.down_total, back_mlp2.down_total
    gain_total = back_attn1.gain_total
    depth = down_total1.shape[0]
    bounds = [0]
    for w in one[1:4]:
        bounds.append(bounds[-1] + w.shape[1])
    units = one[6].shape[1]
    outs = [mlp2.result, back_attn1.grad_out]
    for level, (attn_total, wide_total, down_total) in enumerate(
        ((attn_total1, wide_total1, down_total1), (attn_total2, wide_total2, down_total2))
    ):
        outs.append(gain_total[2 * level, 0:depth])
        outs += [attn_total[:, low:high] for low, high in zip(bounds, bounds[1:])]
        outs.append(attn_total[:, bounds[-1] :].T)
        outs.append(gain_total[2 * level + 1, 0:depth])
        outs += [wide_total[:, 0:units], wide_total[:, units:], down_total.T]
    return tuple(outs)


def solution(mesh):
    layer = (
        P("dp"),
        P("dp", "tensor"),
        P("dp", "tensor"),
        P("dp", "tensor"),
        P("tensor", "dp"),
        P("dp"),
        P("dp", "tensor"),
        P("dp", "tensor"),
        P("tensor", "dp"),
    )
    rows = P(("dp", "tensor"), None)
    return jax.shard_map(
        body,
        mesh=mesh,
        in_specs=(rows, P("dp"), *layer, *layer, rows),
        out_specs=(rows, rows, *layer, *layer),
        check_vma=False,
    )
```

```python
import functools
import math
import types

import jax
import jax.numpy as jnp
import numpy as np
from jax import lax
from jax.experimental import pallas as pl
from jax.experimental.pallas import tpu as pltpu
from jax.sharding import PartitionSpec as P

HEAD_DIM = 96
HALF = HEAD_DIM // 2
BLOCK = 256
PAD = 128
GAIN_ROWS = 16
LIMIT = 60 * 1024 * 1024

epsilon = 1e-05
rope_base = 100000.0
masked_value = -1e30
scale = 1.0 / math.sqrt(HEAD_DIM)

BF = jnp.bfloat16
F32 = jnp.float32
MESH = pl.DeviceIdType.MESH
ANY = pl.BlockSpec(memory_space=pl.ANY)
VM = pl.BlockSpec(memory_space=pltpu.VMEM)
SELF = None


def nn(left, right):
    return lax.dot_general(left, right, (((1,), (0,)), ((), ())), preferred_element_type=F32)


def nt(left, right):
    return lax.dot_general(left, right, (((1,), (1,)), ((), ())), preferred_element_type=F32)


def tn(left, right):
    return lax.dot_general(left, right, (((0,), (0,)), ((), ())), preferred_element_type=F32)


def tile(index, size):
    if isinstance(index, int):
        return pl.ds(index * size, size)
    return pl.ds(pl.multiple_of(index * size, size), size)


def each(count, body):
    def step(index, carry):
        body(index)
        return carry

    lax.fori_loop(0, count, step, 0)


class Group:
    def __init__(self):
        self.me = lax.axis_index("tensor")
        self.core_bit = lax.rem(self.me, 2)
        self.chip = self.me // 2
        self.core = self.me + 1 - 2 * self.core_bit
        self.other = lax.rem(self.me + 2, 4)

    def greet(self, barrier):
        for near in (self.core, self.other):
            pl.semaphore_signal(barrier, inc=1, device_id={"tensor": near}, device_id_type=MESH)

    def peers(self):
        return 2

    def remote(self, source, target, send, recv, device):
        return pltpu.make_async_remote_copy(
            src_ref=source,
            dst_ref=target,
            send_sem=send,
            recv_sem=recv,
            device_id={"tensor": device},
            device_id_type=MESH,
        )


class Gather:
    def __init__(self, group, full, send, recv):
        self.group, self.full, self.send, self.recv = group, full, send, recv
        half = full.shape[1] // 2
        mine = full.at[group.me]
        self.to_core = group.remote(mine, mine, send.at[0], recv.at[0], group.core)
        self.to_other = []
        self.onward = []
        for part in range(2):
            piece = full.at[group.me, pl.ds(part * half, half)]
            self.to_other.append(
                group.remote(piece, piece, send.at[1 + part], recv.at[1 + part], group.other)
            )
            piece = full.at[group.other, pl.ds(part * half, half)]
            self.onward.append(
                group.remote(piece, piece, send.at[3 + part], recv.at[3 + part], group.core)
            )

    def start(self):
        for copy in self.to_other:
            copy.start()
        self.to_core.start()

    def wait_chip(self):
        self.to_core.wait_recv()

    def forward(self):
        for here, there in zip(self.to_other, self.onward):
            here.wait_recv()
            there.start()

    def wait_other(self):
        for copy in self.onward:
            copy.wait_recv()

    def finish(self):
        self.to_core.wait_send()
        for copy in self.to_other + self.onward:
            copy.wait_send()


class Scatter:
    def __init__(self, group, parts, near, away, landed, send, recv):
        self.group, self.parts, self.near = group, parts, near
        self.away, self.landed = away, landed
        self.to_core = [
            group.remote(
                parts.at[turn, 1 - group.core_bit], near.at[turn], send.at[turn], recv.at[turn], group.core
            )
            for turn in range(2)
        ]
        half = away.shape[0] // 2
        self.to_other = [
            group.remote(
                away.at[pl.ds(part * half, half)],
                landed.at[pl.ds(part * half, half)],
                send.at[2 + part],
                recv.at[2 + part],
                group.other,
            )
            for part in range(2)
        ]

    def rows_of(self, turn):
        return 1 - self.group.chip if turn == 0 else self.group.chip

    def send_core(self, turn):
        self.to_core[turn].start()

    def send_away(self):
        self.to_core[0].wait_recv()
        half = self.away.shape[0] // 2
        for part in range(2):

            def add(index):
                rows = pl.ds(pl.multiple_of(part * half + index * 32, 32), 32)
                total = self.parts[0, self.group.core_bit, rows, :].astype(F32) + self.near[
                    0, rows, :
                ].astype(F32)
                self.away[rows, :] = total.astype(BF)

            each(half // 32, add)
            self.to_other[part].start()

    def wait(self):
        self.to_core[1].wait_recv()
        for copy in self.to_other:
            copy.wait_recv()

    def total(self, rows):
        return (
            self.parts[1, self.group.core_bit, rows, :].astype(F32)
            + self.near[1, rows, :].astype(F32)
            + self.landed[rows, :].astype(F32)
        )

    def finish(self):
        for copy in self.to_core + self.to_other:
            copy.wait_send()


class Line:
    def __init__(self, n_dp):
        mine = lax.axis_index("dp")
        self.count = n_dp // 2
        self.z, self.x = mine // 2, lax.rem(mine, 2)
        self.mine = mine
        self.pair = self.z * 2 + 1 - self.x
        self.up = jnp.minimum(self.z + 1, self.count - 1) * 2 + self.x
        self.down = jnp.maximum(self.z - 1, 0) * 2 + self.x
        self.has_up = self.z + 1 < self.count
        self.has_down = self.z > 0

    def greet(self, barrier):
        def hello(device):
            pl.semaphore_signal(barrier, inc=1, device_id={"dp": device}, device_id_type=MESH)

        hello(self.pair)
        pl.when(self.has_up)(lambda: hello(self.up))
        pl.when(self.has_down)(lambda: hello(self.down))

    def peers(self):
        return 1 + jnp.minimum(self.count - 1 - self.z, 1) + jnp.minimum(self.z, 1)

    def remote(self, source, target, send, recv, device):
        return pltpu.make_async_remote_copy(
            src_ref=source, dst_ref=target, send_sem=send, recv_sem=recv,
            device_id={"dp": device}, device_id_type=MESH)


class Fetch:
    def __init__(self, line, own, blocks, send, recv):
        self.line, self.own, self.blocks, self.send, self.recv = line, own, blocks, send, recv
        rows = own.shape[0]
        self.edge = max(rows // 6 // 16, 1) * 16 if rows > 32 else 0
        self.rows = rows

    @staticmethod
    def scratch(n_dp):
        return [pltpu.SemaphoreType.DMA((n_dp, 5))] * 2

    def low(self, step):
        return jnp.maximum(self.line.z - step, 0) * 2

    def high(self, step):
        return jnp.minimum(self.line.z + step, self.line.count - 1) * 2

    def copy(self, slot, block, device, way, rows=None):
        source = self.own if slot == 0 and way < 3 else self.blocks.at[block]
        target = self.blocks.at[block]
        if rows is not None:
            source, target = source.at[rows], target.at[rows]
        return self.line.remote(
            source, target, self.send.at[slot, way], self.recv.at[slot, way], device
        )

    def upward(self, step):
        return self.copy(step, self.low(step) + self.line.x, self.line.up, 1)

    def downward(self, step):
        return self.copy(step, self.high(step) + self.line.x, self.line.down, 2)

    def edge_up(self, step):
        block = self.low(step) + 1 - self.line.x
        return self.copy(step, block, self.line.up, 3, pl.ds(0, self.edge))

    def edge_down(self, step):
        block = self.high(step) + 1 - self.line.x
        return self.copy(step, block, self.line.down, 4, pl.ds(0, self.edge))

    def sideways(self, step, low):
        line = self.line
        rows = pl.ds(self.edge, self.rows - self.edge) if step and self.edge else None
        if low:
            return self.copy(step, self.low(step) + line.x, line.pair, 0, rows)
        return self.copy(line.count + step, self.high(step) + line.x, line.pair, 0, rows)

    def upward_in(self, step):
        return self.copy(step - 1, self.low(step) + self.line.x, self.line.up, 1)

    def downward_in(self, step):
        return self.copy(step - 1, self.high(step) + self.line.x, self.line.down, 2)

    def edge_up_in(self, step):
        block = self.low(step) + 1 - self.line.x
        return self.copy(step - 1, block, self.line.up, 3, pl.ds(0, self.edge))

    def edge_down_in(self, step):
        block = self.high(step) + 1 - self.line.x
        return self.copy(step - 1, block, self.line.down, 4, pl.ds(0, self.edge))

    def start(self):
        line = self.line
        pl.when(line.has_up)(lambda: self.upward(0).start())
        pl.when(line.has_down)(lambda: self.downward(0).start())
        self.sideways(0, True).start()

    def step(self, step):
        line = self.line

        @pl.when(line.z >= step)
        def _():
            self.upward_in(step).wait_recv()
            pl.when(line.has_up)(lambda: self.upward(step).start())
            self.sideways(step, True).start()

        @pl.when(line.z + step < line.count)
        def _():
            self.downward_in(step).wait_recv()
            pl.when(line.has_down)(lambda: self.downward(step).start())
            self.sideways(step, False).start()

        self.edges(step - 1)

    def edges(self, step):
        line = self.line
        if step == 0:
            self.sideways(0, True).wait_recv()
        if not self.edge:
            return
        if step == 0:
            pl.when(line.has_up)(lambda: self.edge_up(0).start())
            pl.when(line.has_down)(lambda: self.edge_down(0).start())
            return

        @pl.when(line.z >= step)
        def _():
            self.edge_up_in(step).wait_recv()
            pl.when(line.has_up)(lambda: self.edge_up(step).start())

        @pl.when(line.z + step < line.count)
        def _():
            self.edge_down_in(step).wait_recv()
            pl.when(line.has_down)(lambda: self.edge_down(step).start())

    def finish(self):
        line = self.line
        self.edges(line.count - 1)
        for step in range(line.count):

            @pl.when(line.z >= step)
            def _():
                @pl.when(line.has_up)
                def _():
                    self.upward(step).wait_send()
                    if self.edge:
                        self.edge_up(step).wait_send()

                self.sideways(step, True).wait_send()
                if step:
                    self.sideways(step, True).wait_recv()

            @pl.when(line.z + step < line.count)
            def _():
                @pl.when(line.has_down)
                def _():
                    self.downward(step).wait_send()
                    if self.edge:
                        self.edge_down(step).wait_send()

                if step:
                    self.sideways(step, False).wait()

    def actions(self):
        steps = [functools.partial(self.step, step) for step in range(1, self.line.count)]
        return [self.start] + steps + [self.finish]


class Reduce:
    def __init__(self, line, blocks, out, pair_in, line_in, mine, x_send, x_recv, z_send, z_recv, local):
        self.line, self.blocks, self.out = line, blocks, out
        self.pair_in, self.line_in, self.mine = pair_in, line_in, mine
        self.x_send, self.x_recv, self.z_send, self.z_recv, self.local = x_send, x_recv, z_send, z_recv, local

    @staticmethod
    def scratch(n_dp, rows, columns):
        count = n_dp // 2
        dma = pltpu.SemaphoreType.DMA
        return [
            pltpu.VMEM((count, rows, columns), BF),
            pltpu.VMEM((count + 1, rows, columns), BF),
            pltpu.VMEM((2, rows, columns), BF),
            dma((count,)), dma((count,)), dma((count,)), dma((count + 1,)), dma((2,)),
        ]

    def sideways(self, target):
        line = self.line
        return line.remote(self.blocks.at[target * 2 + 1 - line.x], self.pair_in.at[target],
                           self.x_send.at[target], self.x_recv.at[target], line.pair)

    def along(self, target, up):
        line = self.line
        slot = target + 1 if up else target
        return line.remote(self.pair_in.at[target], self.line_in.at[slot],
                           self.z_send.at[target], self.z_recv.at[slot], line.up if up else line.down)

    def load(self, target, slot):
        return pltpu.make_async_copy(self.blocks.at[target * 2 + self.line.x], self.mine.at[slot], self.local.at[slot])

    def above(self, step):
        return self.line.z + step < self.line.count, jnp.minimum(self.line.z + step, self.line.count - 1)

    def below(self, step):
        return self.line.z - step >= 0, jnp.maximum(self.line.z - step, 0)

    def fetch(self, step):
        there, target = self.above(step)
        pl.when(there)(lambda: self.load(target, 0).start())
        if step:
            there2, target2 = self.below(step)
            pl.when(there2)(lambda: self.load(target2, 1).start())

    def start(self):
        line = self.line
        for step in range(line.count - 1, 0, -1):
            for there, target in (self.above(step), self.below(step)):
                pl.when(there)(lambda: self.sideways(target).start())
        self.sideways(line.z).start()
        self.fetch(line.count - 1)

    def add(self, target, slot, more):
        rows = self.out.shape[0]

        def some(index):
            part = pl.ds(pl.multiple_of(index * 16, 16), 16)
            total = self.pair_in[target, part, :].astype(F32) + self.mine[slot, part, :].astype(F32)
            for other in more:
                total += self.line_in[other, part, :].astype(F32)
            self.pair_in[target, part, :] = total.astype(BF)

        each(rows // 16, some)

    def pass_on(self, target, slot, up):
        line = self.line
        self.load(target, slot).wait()
        self.sideways(target).wait_recv()
        fed = line.has_down if up else line.has_up

        @pl.when(fed)
        def _():
            self.along(target, up).wait_recv()
            self.add(target, slot, [target + 1 if up else target])

        pl.when(jnp.logical_not(fed))(lambda: self.add(target, slot, []))
        self.along(target, up).start()

    def step(self, step):
        for slot, (there, target) in enumerate((self.above(step), self.below(step))):
            pl.when(there)(lambda: self.pass_on(target, slot, slot == 0))
        self.fetch(step - 1)

    def close(self):
        line = self.line
        z = line.z
        self.load(z, 0).wait()
        self.sideways(z).wait_recv()
        rows = self.out.shape[0]

        def final(more):
            def some(index):
                part = pl.ds(pl.multiple_of(index * 16, 16), 16)
                total = self.pair_in[z, part, :].astype(F32) + self.mine[0, part, :].astype(F32)
                for other in more:
                    total += self.line_in[other, part, :].astype(F32)
                self.out[part, :] = total

            each(rows // 16, some)

        pl.when(line.has_down)(lambda: self.along(z, True).wait_recv())
        pl.when(line.has_up)(lambda: self.along(z, False).wait_recv())
        pl.when(jnp.logical_not(line.has_down))(lambda: final([z]))
        pl.when(jnp.logical_not(line.has_up))(lambda: final([z + 1]))
        pl.when(line.has_down & line.has_up)(lambda: final([z, z + 1]))
        for step in range(line.count - 1, 0, -1):
            for up, (there, target) in ((True, self.above(step)), (False, self.below(step))):

                @pl.when(there)
                def _():
                    self.sideways(target).wait_send()
                    self.along(target, up).wait_send()

        self.sideways(z).wait_send()

    def actions(self):
        return [self.start] + [functools.partial(self.step, s) for s in range(self.line.count - 1, 0, -1)] + [self.close]


def spread(block, depth, lanes, width):
    row = lax.broadcasted_iota(jnp.int32, (lanes, width), 0)
    column = lax.broadcasted_iota(jnp.int32, (lanes, width), 1)
    hit = (column - row == block * depth) & (row < depth)
    return jnp.where(hit, 1.0, 0.0).astype(BF)


def turn_half(values):
    return pltpu.roll(values, PAD // 2, 1)


def meet(*circles):
    barrier = pltpu.get_barrier_semaphore()
    for circle in circles:
        circle.greet(barrier)
    pl.semaphore_wait(barrier, sum(circle.peers() for circle in circles))


class Weights:
    def __init__(self, line, own, blocks, held, sems, first=0):
        self.copies = []
        columns = pl.ds(first, own.shape[1])
        depth = own.shape[0]
        count = line.count
        for index in range(2 * count):
            shift, side = index // 2, index % 2
            block = lax.rem(line.z + shift, count) * 2 + lax.rem(line.x + side, 2)
            source = blocks.at[block] if index else own
            rows = pl.ds(pl.multiple_of(block * depth, 16), depth)
            self.copies.append(pltpu.make_async_copy(source, held.at[rows, columns], sems.at[index]))

    def start(self):
        for copy in self.copies:
            copy.start()

    def wait(self):
        for copy in self.copies:
            copy.wait()


def start_coming(r):
    for copy in r.coming.values():
        copy.start()


class Pump:
    def __init__(self, tasks, plan):
        self.steps = [step for together in zip(*[task.actions() for task in tasks]) for step in together]
        self.plan = list(plan)

    def __call__(self):
        count = self.plan.pop(0) if self.plan else 0
        self.do(count)

    def do(self, count):
        for step in self.steps[:count]:
            step()
        self.steps = self.steps[count:]

    def rest(self):
        self.do(len(self.steps))


def fetches_of(line, r, count):
    return [
        Fetch(
            line,
            getattr(r, f"own{i}"),
            getattr(r, f"blocks{i}"),
            getattr(r, f"fetch_send{i}"),
            getattr(r, f"fetch_recv{i}"),
        )
        for i in range(count)
    ]


def reduces_of(line, r, count):
    return [
        Reduce(
            line,
            getattr(r, f"sum{i}"),
            getattr(r, f"total{i}"),
            *[getattr(r, f"reduce{i}_{j}") for j in range(8)],
        )
        for i in range(count)
    ]


def comm_of(r):
    group = Group()
    gather = Gather(group, r.full, r.g_send, r.g_recv)
    scatter = Scatter(group, r.parts, r.near, r.away, r.landed, r.s_send, r.s_recv)
    return group, gather, scatter


def out_columns(scatter, turn, left_rows, right_tile, columns):
    product = nt(left_rows, right_tile)
    rows = product.shape[0] // 2
    scatter.parts[turn, 0, :, columns] = product[:rows].astype(BF)
    scatter.parts[turn, 1, :, columns] = product[rows:].astype(BF)


def norm_rows(source, gain, full, slot):
    def norm(index):
        part = tile(index, 32)
        values = source[part, :]
        factor = lax.rsqrt(jnp.mean(values * values, axis=-1, keepdims=True) + epsilon)
        full[slot, part, :] = (values * factor * gain).astype(BF)

    each(source.shape[0] // 32, norm)


def add_rows(scatter, source, target):
    def close(index):
        part = tile(index, 32)
        target[part, :] = source[part, :] + scatter.total(part)

    each(source.shape[0] // 32, close)


def pack_attn(query, key, value, output, target):
    width, each_kv = query.shape[1], key.shape[1]
    target[:, 0:width] = query[...].astype(BF)
    both = jnp.concatenate([key[...], value[...]], axis=1)
    target[:, width : width + 2 * each_kv] = both.astype(BF)
    target[:, width + 2 * each_kv :] = output[...].astype(BF)


def count_rows(documents, below):
    hits = jnp.where(documents < below, 1.0, 0.0)
    return jnp.sum(jnp.sum(hits, axis=1, keepdims=True), axis=0, keepdims=True).astype(jnp.int32)


def starts_of(marks, places):
    head, body_end = marks[0:1, 0:1], marks[1:2, 0:1]
    return jnp.where(places < head, 0, jnp.where(places < body_end, head, body_end))


def make_tables(r):
    marks = jnp.concatenate([count_rows(r.documents[...], 1), count_rows(r.documents[...], 2)], axis=0)
    r.marks[0:2, :] = jnp.broadcast_to(marks, (2, PAD))
    r.marks[2:, :] = jnp.zeros((6, PAD), jnp.int32)

    def some(index):
        where = tile(index, 128)
        places = lax.broadcasted_iota(jnp.int32, (128, PAD), 0) + index * 128
        offset = places - starts_of(r.marks, places)
        angles = offset.astype(F32) * r.freqs[0:1, :]
        r.cosine[where, :] = jnp.cos(angles)
        r.sine[where, :] = jnp.sin(angles) * r.freqs[1:2, :]

    each(r.cosine.shape[0] // 128, some)


def attn_forward_kernel(first, level, fetch_count, plan, r):
    rows, width = r.x.shape
    n_dp, depth = r.w_sems.shape[0], r.own.shape[0]
    line = Line(n_dp)
    group, gather, scatter = comm_of(r)
    tasks = fetches_of(line, r, fetch_count)
    weights = Weights(line, r.own, r.blocks, r.held, r.w_sems)
    circles = (group, line) if first or tasks else (group,)
    meet(*circles)
    if first:
        raw = {}
        for name in ("gate0", "up0", "down0", "query1", "key1", "value1", "output1", "gate1", "up1", "down1"):
            raw[name] = pltpu.make_async_copy(
                getattr(r, "raw_" + name), getattr(r, name), r.raw_sems.at[len(raw)]
            )
            raw[name].start()
        lanes = r.gain_own.shape[1]
        r.gain_raw[...] = jnp.zeros_like(r.gain_raw)
        for row in range(4):
            r.gain_raw[row : row + 1, 0:depth] = getattr(r, f"gain{row}")[...]
        r.gain_own[...] = r.gain_raw[...].astype(BF)
        pack_attn(r.raw_query0, r.raw_key0, r.raw_value0, r.raw_output0, r.own)
        start_coming(r)
        leave(r, "own")
        gain_fetch = Fetch(line, r.gain_own, r.gain_blocks, r.gain_send, r.gain_recv)
        weight_fetch = Fetch(line, r.own, r.blocks, r.weight_send, r.weight_recv)
        gain_fetch.start()
        weight_fetch.start()
        for step in gain_fetch.actions()[1:]:
            step()
        r.gains[...] = jnp.zeros_like(r.gains)

        def gather_gain(block):
            chosen = spread(block, depth, lanes, width)

            @pl.when(block == line.mine)
            def _():
                r.gains[...] += nn(r.gain_own[...], chosen)

            @pl.when(block != line.mine)
            def _():
                r.gains[...] += nn(r.gain_blocks[block], chosen)

        each(n_dp, gather_gain)
        come(r, "x")
        norm_rows(r.x, r.gains[2 * level : 2 * level + 1, :], r.full, group.me)
        gather.start()
        weight_steps = weight_fetch.actions()[1:-1]
        for step in weight_steps[:1]:
            step()
        ahead = Gather(group, r.ahead, r.a_send, r.a_recv)
        come(r, "cotangent")
        r.ahead[group.me] = r.cotangent[...].astype(BF)
        ahead.start()
        for name in ("gate0", "up0"):
            raw[name].wait()
        r.own0[...] = r.gate0[...].astype(BF)
        r.own1[...] = r.up0[...].astype(BF)
        leave(r, "own0", "own1")
        for step in weight_steps[1:]:
            step()
        pump = Pump(tasks, plan)
        pump()
        make_tables(r)
        for name in list(raw)[2:]:
            raw[name].wait()
        pack_attn(r.query1, r.key1, r.value1, r.output1, r.attn_pack1)
        r.down_pack0[...] = r.down0[...].astype(BF)
        r.down_pack1[...] = r.down1[...].astype(BF)
        r.gate_pack1[...] = r.gate1[...].astype(BF)
        r.up_pack1[...] = r.up1[...].astype(BF)
        leave(r, *list(r.leaving)[4:])
        come(r, "place")
        weight_fetch.finish()
        weights.start()
    else:
        weights.start()
        pump = Pump(tasks, plan)
        pump()
        start_coming(r)
        norm_rows(r.x, r.gains[2 * level : 2 * level + 1, :], r.full, group.me)
        gather.start()
        come(r, "place", "cosine", "sine")
    weights.wait()
    place = r.place[...]
    heads = place.shape[1] // PAD
    compact_width, head_width = place.shape
    padded, qkv, mixed, compact, held = r.padded, r.qkv, r.mixed, r.compact, r.held

    def pad(index):
        part = tile(index, 256)
        padded[part, 0:head_width] = nn(held[part, 0:compact_width], place).astype(BF)
        padded[part, head_width : 2 * head_width] = nn(
            held[part, compact_width : 2 * compact_width], place
        ).astype(BF)

    each(width // 256, pad)

    def project(chip):
        left = r.full[pl.ds(2 * chip, 2)].reshape(2 * rows, width)
        where = tile(chip, 2 * rows)
        cosine, sine = r.cosine[where, :], r.sine[where, :]

        def turned(index):
            columns = tile(index, 2 * PAD)
            product = nn(left, padded[:, columns])
            for half in range(2):
                u = product[:, half * PAD : (half + 1) * PAD]
                qkv[where, tile(2 * index + half, PAD)] = (u * cosine + turn_half(u) * sine).astype(BF)

        each(3 * heads // 4, turned)
        columns = pl.ds(3 * heads // 2 * PAD, heads // 2 * PAD)
        qkv[where, columns] = nn(left, padded[:, columns]).astype(BF)

    gather.wait_chip()
    project(group.chip)
    pump()
    gather.forward()
    pump()
    gather.wait_other()
    project(1 - group.chip)
    copies = [
        pltpu.make_async_copy(r.full, r.a_out, r.out_sems.at[0]),
        pltpu.make_async_copy(qkv, r.qkv_out, r.out_sems.at[1]),
    ]
    for copy in copies:
        copy.start()
    if first:
        ahead.wait_chip()
        ahead.forward()
    pump()
    kv_at = heads * PAD
    value_at = kv_at + heads // 2 * PAD
    for turn in range(4):
        prob = getattr(r, f"prob{turn}")
        reach = prob.shape[2]
        where = pl.ds(turn * rows, rows)
        places = lax.broadcasted_iota(jnp.int32, (rows, PAD), 0) + turn * rows
        begin = starts_of(r.marks, places)
        head, body_end = r.marks[0:1, 0:1], r.marks[1:2, 0:1]
        end = jnp.where(places < head, head, jnp.where(places < body_end, body_end, 4 * rows))
        end = jnp.minimum(begin + ((places - begin) // BLOCK + 1) * BLOCK, end)
        place_of = lax.broadcasted_iota(jnp.int32, (rows, reach), 1)
        inside = (place_of >= begin[:, 0:1]) & (place_of < end[:, 0:1])
        r.bias[:, 0:reach] = jnp.where(inside, 0.0, masked_value)

        def attend(head):
            query = qkv[where, tile(head, PAD)]
            key = qkv[0:reach, pl.ds(kv_at + head // 2 * PAD, PAD)]
            value = qkv[0:reach, pl.ds(value_at + head // 2 * PAD, PAD)]
            scores = nt(query, key) * scale + r.bias[:, 0:reach]
            exponent = jnp.exp(scores - jnp.max(scores, axis=-1, keepdims=True))
            summed = jnp.sum(exponent, axis=-1, keepdims=True)
            low = (exponent * (1.0 / summed)).astype(BF)
            prob[head] = low
            mixed[where, tile(head, PAD)] = nn(low, value).astype(BF)

        for head in range(heads):
            attend(head)
        copy = pltpu.make_async_copy(prob, getattr(r, f"p_out{turn}"), r.out_sems.at[2 + turn])
        copy.start()
        copies.append(copy)
        compact[where, :] = nt(mixed[where, :], place).astype(BF)
        pump()
    copies.append(pltpu.make_async_copy(compact, r.o_out, r.out_sems.at[6]))
    copies[-1].start()
    if first:
        ahead.wait_other()
        copies.append(pltpu.make_async_copy(r.ahead, r.ahead_out, r.out_sems.at[7]))
        copies[-1].start()
        ahead.finish()
    for turn in range(2):
        left = compact[tile(scatter.rows_of(turn), 2 * rows), :]

        def part_of(index):
            columns = tile(index, 256)
            out_columns(scatter, turn, left, held[columns, 2 * compact_width :], columns)

        each(width // 256, part_of)
        scatter.send_core(turn)
        if turn == 0:
            scatter.send_away()
        pump()
    scatter.wait()
    pump()
    add_rows(scatter, r.x, r.middle)
    leave(r, "middle")
    pump.rest()
    gather.finish()
    scatter.finish()
    for copy in copies:
        copy.wait()


def wide_of(line, r):
    return [
        Weights(line, r.gate_own, r.gate_blocks, r.wide, r.gate_sems),
        Weights(line, r.up_own, r.up_blocks, r.wide, r.up_sems, r.gate_own.shape[1]),
    ]


def mlp_forward_kernel(level, fetch_count, plan, r):
    rows, width = r.middle.shape
    units = r.hid.shape[1]
    line = Line(r.w_sems.shape[0])
    group, gather, scatter = comm_of(r)
    down = Fetch(line, r.own, r.blocks, r.down_send, r.down_recv)
    down_steps = down.actions()[1:-1]
    wide, held, gu, hid = r.wide, r.held, r.gu, r.hid
    wide_weights = wide_of(line, r)
    weights = Weights(line, r.own, r.blocks, held, r.w_sems)
    meet(group, line)
    down.start()
    for copy in wide_weights:
        copy.start()
    pump = Pump(fetches_of(line, r, fetch_count), plan)
    pump()
    norm_rows(r.middle, r.gains[2 * level + 1 : 2 * level + 2, :], r.full, group.me)
    gather.start()
    for copy in wide_weights:
        copy.wait()

    def expand(chip):
        left = r.full[pl.ds(2 * chip, 2)].reshape(2 * rows, width)
        where = tile(chip, 2 * rows)

        def unit(index):
            columns = tile(index, 256)
            further = pl.ds(pl.multiple_of(units + index * 256, 256), 256)
            gate = nn(left, wide[:, columns])
            up = nn(left, wide[:, further])
            hid[where, columns] = (gate / (1.0 + jnp.exp(-gate)) * up).astype(BF)
            gu[where, columns] = gate.astype(BF)
            gu[where, further] = up.astype(BF)

        each(units // 256, unit)

    gather.wait_chip()
    expand(group.chip)
    for step in down_steps[:1]:
        step()
    gather.forward()
    for step in down_steps[1:2]:
        step()
    pump()
    gather.wait_other()
    expand(1 - group.chip)
    for step in down_steps[2:]:
        step()
    pump()
    copies = [
        pltpu.make_async_copy(r.full, r.m_out, r.out_sems.at[0]),
        pltpu.make_async_copy(gu, r.gu_out, r.out_sems.at[1]),
        pltpu.make_async_copy(hid, r.hid_out, r.out_sems.at[2]),
    ]
    for copy in copies:
        copy.start()
    down.finish()
    weights.start()
    weights.wait()
    for turn in range(2):
        left = hid[tile(scatter.rows_of(turn), 2 * rows), :]

        def part_of(index):
            columns = tile(index, 256)
            out_columns(scatter, turn, left, held[columns, :], columns)

        each(width // 256, part_of)
        scatter.send_core(turn)
        if turn == 0:
            scatter.send_away()
        pump()
    scatter.wait()
    pump()
    add_rows(scatter, r.middle, r.result)
    leave(r, "result")
    pump.rest()
    gather.finish()
    scatter.finish()
    for copy in copies:
        copy.wait()


def weight_grads(source, right, target, columns):
    width = source.shape[-1]
    depth = target.shape[1]
    chunk = math.lcm(depth, PAD)

    def some(index):
        left = source[..., tile(index, chunk)].reshape(right.shape[0], chunk)
        product = tn(left, right[...]).astype(BF)
        for part in range(chunk // depth):
            rows = slice(part * depth, (part + 1) * depth)
            target[index * (chunk // depth) + part, :, columns] = product[rows]

    each(width // chunk, some)


def close_back(scatter, grad_in_ref, state_ref, gain, grad_out, dgain):
    rows = state_ref.shape[0]
    dgain[...] = jnp.zeros_like(dgain)

    def close(index):
        part = tile(index, 32)
        values = state_ref[part, :]
        factor = lax.rsqrt(jnp.mean(values * values, axis=-1, keepdims=True) + epsilon)
        normed = values * factor
        grad_in = scatter.total(part)
        dgain[...] += jnp.sum((grad_in * normed).reshape(4, 8, -1), axis=0)
        grad_norm = grad_in * gain
        inner = jnp.mean(grad_norm * normed, axis=-1, keepdims=True)
        grad_out[part, :] = grad_in_ref[part, :] + factor * (grad_norm - normed * inner)

    each(rows // 32, close)


def mlp_backward_kernel(level, reduce_count, plan, ready, r):
    rows, width = r.middle.shape
    units = r.hid.shape[1]
    n_dp = r.w_sems.shape[0]
    line = Line(n_dp)
    group, gather, scatter = comm_of(r)
    wide, held, gu, hid = r.wide, r.held, r.gu, r.hid
    weights = [
        Weights(line, r.own, r.blocks, held, r.w_sems),
        *wide_of(line, r),
    ]
    fetches = [
        pltpu.make_async_copy(r.hid_in, hid, r.in_sems.at[2]),
        pltpu.make_async_copy(r.gu_in, gu, r.in_sems.at[1]),
        pltpu.make_async_copy(r.m_in, r.m_full, r.in_sems.at[0]),
    ]
    down = Reduce(line, r.grads, r.down_total, *[getattr(r, f"down{j}") for j in range(8)])
    meet(group, line)
    pump = Pump(reduces_of(line, r, reduce_count), plan)
    pump.steps += down.actions()[1:]
    pump()
    for copy in weights[:1] + fetches + weights[1:]:
        copy.start()
    start_coming(r)
    if ready:
        whole = pltpu.make_async_copy(r.ahead_in, r.full, r.in_sems.at[3])
        whole.start()
    else:
        r.full[group.me] = r.grad[...].astype(BF)
        gather.start()
    for copy in weights[:1] + fetches[:2]:
        copy.wait()

    def inward(chip):
        left = r.full[pl.ds(2 * chip, 2)].reshape(2 * rows, width)
        where = tile(chip, 2 * rows)

        def unit(index):
            columns = tile(index, 256)
            further = pl.ds(pl.multiple_of(units + index * 256, 256), 256)
            grad = nn(left, held[:, columns])
            gate = gu[where, columns].astype(F32)
            up = gu[where, further].astype(F32)
            sig = 1.0 / (1.0 + jnp.exp(-gate))
            gu[where, columns] = (grad * up * sig * (1.0 + gate * (1.0 - sig))).astype(BF)
            gu[where, further] = (grad * gate * sig).astype(BF)

        each(units // 256, unit)

    if ready:
        whole.wait()
    else:
        gather.wait_chip()
        inward(group.chip)
        pump()
        gather.forward()
        pump()
        gather.wait_other()
    weight_grads(r.full, hid, r.grads, slice(0, units))
    down.start()
    if ready:
        inward(group.chip)
    inward(1 - group.chip)
    for copy in weights[1:] + fetches[2:]:
        copy.wait()
    pump()
    for turn in range(2):
        where = tile(scatter.rows_of(turn), 2 * rows)

        def part_of(index):
            columns = tile(index, 256)
            out_columns(scatter, turn, gu[where, :], wide[columns, :], columns)

        each(width // 256, part_of)
        scatter.send_core(turn)
        if turn == 0:
            scatter.send_away()
        pump()
    for part in range(2):
        columns = slice(part * units, (part + 1) * units)
        weight_grads(r.m_full, gu.at[:, columns], r.wide_grads, columns)
        pump()
    copies = [pltpu.make_async_copy(r.wide_grads, r.wide_out, r.out_sems.at[0])]
    copies[0].start()
    scatter.wait()
    pump()
    come(r, *r.coming)
    close_back(
        scatter, r.grad, r.middle, r.gains[2 * level + 1 : 2 * level + 2, :], r.grad_out, r.dgain
    )
    leave(r, "grad_out")
    pump.rest()
    if not ready:
        gather.finish()
    scatter.finish()
    for copy in copies:
        copy.wait()


def attn_backward_kernel(level, reduce_count, plan, final, r):
    rows, width = r.x.shape
    n_dp = r.w_sems.shape[0]
    depth = width // n_dp
    line = Line(n_dp)
    group, gather, scatter = comm_of(r)
    tasks = reduces_of(line, r, reduce_count)
    held, qkv, compact = r.held, r.qkv, r.compact
    probs = [getattr(r, f"prob{turn}") for turn in range(4)]
    weights = Weights(line, r.own, r.blocks, held, r.w_sems)
    fetches = [
        pltpu.make_async_copy(r.a_in, r.a_full, r.in_sems.at[0]),
        pltpu.make_async_copy(r.o_in, compact, r.in_sems.at[1]),
        pltpu.make_async_copy(r.qkv_in, qkv, r.in_sems.at[2]),
    ] + [
        pltpu.make_async_copy(getattr(r, f"p_in{turn}"), probs[turn], r.in_sems.at[3 + turn])
        for turn in range(4)
    ]
    meet(*((group, line) if tasks else (group,)))
    pump = Pump(tasks, plan)
    pump()
    weights.start()
    for copy in fetches:
        copy.start()
    start_coming(r)
    r.full[group.me] = r.grad[...].astype(BF)
    gather.start()
    pump()
    weights.wait()
    for copy in fetches:
        copy.wait()
    come(r, *r.coming)
    place = r.place[...]
    heads = place.shape[1] // PAD
    compact_width, head_width = place.shape

    def inward(chip):
        left = r.full[pl.ds(2 * chip, 2)].reshape(2 * rows, width)
        where = tile(chip, 2 * rows)
        grad = nn(left, held[:, 2 * compact_width :]).astype(BF)
        r.grad_mixed[where, :] = nn(grad, place).astype(BF)

    gather.wait_chip()
    inward(group.chip)
    pump()
    gather.forward()
    pump()
    gather.wait_other()
    inward(1 - group.chip)
    kv_at = heads * PAD
    value_at = kv_at + heads // 2 * PAD
    r.grad_k[...] = jnp.zeros_like(r.grad_k)
    r.grad_v[...] = jnp.zeros_like(r.grad_v)
    for turn, prob in enumerate(probs):
        reach = prob.shape[2]
        where = pl.ds(turn * rows, rows)
        cosine, sine = r.cosine[where, :], r.sine[where, :]

        def attend(head):
            mine = tile(head, PAD)
            shared = tile(head // 2, PAD)
            query = qkv[where, mine]
            key = qkv[0:reach, pl.ds(kv_at + head // 2 * PAD, PAD)]
            value = qkv[0:reach, pl.ds(value_at + head // 2 * PAD, PAD)]
            grad = r.grad_mixed[where, mine]
            low = prob[head]
            grad_prob = nt(grad, value)
            weight = low.astype(F32)
            inner = jnp.sum(weight * grad_prob, axis=-1, keepdims=True)
            grad_score = (weight * (grad_prob - inner)).astype(BF)
            u = nn(grad_score, key) * scale
            r.grad_q[where, mine] = (u * cosine - turn_half(u) * sine).astype(BF)
            r.grad_k[0:reach, shared] += tn(grad_score, query)
            r.grad_v[0:reach, shared] += tn(low, grad)

        for head in range(heads):
            attend(head)
        pump()
    for pair in range(heads // 2):
        columns = pl.ds(pair * PAD, PAD)
        u = r.grad_k[:, columns] * scale
        r.grad_kv[:, columns] = (u * r.cosine[...] - turn_half(u) * r.sine[...]).astype(BF)
        r.grad_kv[:, pl.ds((heads // 2 + pair) * PAD, PAD)] = r.grad_v[:, columns].astype(BF)
    grad_low = r.grad_low
    grad_low[:, 0:compact_width] = nt(r.grad_q[...], place).astype(BF)
    grad_low[:, compact_width : 2 * compact_width] = nt(r.grad_kv[...], place).astype(BF)
    for turn in range(2):
        where = tile(scatter.rows_of(turn), 2 * rows)

        def part_of(index):
            columns = tile(index, 256)
            out_columns(
                scatter, turn, grad_low[where, :], held[columns, 0 : 2 * compact_width], columns
            )

        each(width // 256, part_of)
        scatter.send_core(turn)
        if turn == 0:
            scatter.send_away()
        pump()
    grads = r.grads
    weight_grads(r.a_full, grad_low, grads, slice(0, 2 * compact_width))
    weight_grads(r.full, compact, grads, slice(2 * compact_width, 3 * compact_width))
    if not final:
        copy = pltpu.make_async_copy(grads, r.grads_out, r.out_sems.at[0])
        copy.start()
    pump()
    scatter.wait()
    pump()
    close_back(scatter, r.grad, r.x, r.gains[2 * level : 2 * level + 1, :], r.grad_out, r.dgain)
    leave(r, "grad_out")
    if final:
        attn = Reduce(line, grads, r.attn_total, *[getattr(r, f"attn{j}") for j in range(8)])
        gains = gain_sums(line, group, r)
        gains.start()
        attn.start()
        pump.rest()
        for step in gains.actions()[1:] + attn.actions()[1:]:
            step()
    pump.rest()
    gather.finish()
    scatter.finish()
    if not final:
        copy.wait()


def gain_sums(line, group, r):
    n_dp, _, lanes = r.gain_blocks.shape
    width = r.rows.shape[1]
    depth = width // n_dp
    for row, part in enumerate((r.dgain, r.dgain1, r.dgain2, r.dgain3)):
        r.rows[row : row + 1, :] = jnp.sum(part[...], axis=0, keepdims=True)
    r.rows[4:8, :] = jnp.zeros((4, width), F32)
    for turn, device in enumerate((group.core, group.other)):
        copy = group.remote(r.rows, r.others.at[turn], r.row_send.at[turn], r.row_recv.at[turn], device)
        copy.start()
        copy.wait()
        r.rows[...] += r.others[turn]
    both = jnp.concatenate([r.rows[...], jnp.zeros((GAIN_ROWS - 8, width), F32)], axis=0).astype(BF)

    def gain_rows(block):
        r.gain_blocks[block] = nt(both, spread(block, depth, lanes, width)).astype(BF)

    each(n_dp, gain_rows)
    return Reduce(line, r.gain_blocks, r.gain_total, *[getattr(r, f"gain{j}") for j in range(8)])


def shaped(shape, dtype):
    return jax.ShapeDtypeStruct(shape, dtype)


def dma(count):
    return pltpu.SemaphoreType.DMA((count,))


def vmem(*shape, dtype=BF):
    return pltpu.VMEM(shape, dtype)


def reaches(rows):
    return [min((turn + 1) * rows + PAD, 4 * rows) for turn in range(4)]


def come(r, *names):
    for name in names:
        r.coming[name].wait()


def leave(r, *names):
    for name in names:
        r.leaving[name].start()


def launch(kernel, which, ins, outs, scratch):
    late = [each_of for each_of, (_, spec) in ins.items() if spec is SELF]
    early = [each_of for each_of, (_, spec) in outs.items() if spec is SELF]
    names = [n + "_" * (n in late) for n in ins] + [n + "_" * (n in early) for n in outs]
    scratch = scratch | {n: vmem(*ins[n][0].shape, dtype=ins[n][0].dtype) for n in late}
    scratch |= {n: vmem(*outs[n][0].shape, dtype=outs[n][0].dtype) for n in early}
    scratch["own_sems"] = dma(len(late) + len(early) + 1)
    names += list(scratch)

    def entry(*refs):
        r = types.SimpleNamespace(**dict(zip(names, refs)))
        sems = iter(range(len(late) + len(early)))
        r.coming = {
            n: pltpu.make_async_copy(getattr(r, n + "_"), getattr(r, n), r.own_sems.at[next(sems)]) for n in late
        }
        r.leaving = {
            n: pltpu.make_async_copy(getattr(r, n), getattr(r, n + "_"), r.own_sems.at[next(sems)]) for n in early
        }
        kernel(r)
        for copy in r.leaving.values():
            copy.wait()

    results = pl.pallas_call(
        entry,
        out_shape=[shape for shape, _ in outs.values()],
        in_specs=[ANY if spec is SELF else spec for _, spec in ins.values()],
        out_specs=[ANY if spec is SELF else spec for _, spec in outs.values()],
        scratch_shapes=list(scratch.values()),
        compiler_params=pltpu.CompilerParams(
            collective_id=which, has_side_effects=which is not None, vmem_limit_bytes=LIMIT
        ),
        cost_estimate=pl.CostEstimate(
            flops=20_000_000_000, bytes_accessed=60_000_000, transcendentals=0
        ),
        name=kernel.func.__name__,
    )(*[array for array, _ in ins.values()])
    return types.SimpleNamespace(**dict(zip(outs, results)))


def comm_scratch(rows, width):
    return dict(
        full=vmem(4, rows, width),
        parts=vmem(2, 2, rows, width),
        near=vmem(2, rows, width),
        away=vmem(rows, width),
        landed=vmem(rows, width),
        g_send=dma(5),
        g_recv=dma(5),
        s_send=dma(4),
        s_recv=dma(4),
    )


def blocks_of(pack, n_dp):
    return shaped((n_dp,) + pack.shape, pack.dtype)


def fetch_refs(packs, n_dp):
    ins, outs, scratch = {}, {}, {}
    for i, pack in enumerate(packs):
        ins[f"own{i}"] = (pack, ANY)
        outs[f"blocks{i}"] = (blocks_of(pack, n_dp), ANY)
        scratch[f"fetch_send{i}"], scratch[f"fetch_recv{i}"] = Fetch.scratch(n_dp)
    return ins, outs, scratch


def reduce_refs(sums):
    ins, outs, scratch = {}, {}, {}
    for i, blocks in enumerate(sums):
        n_dp, depth, columns = blocks.shape
        ins[f"sum{i}"] = (blocks, ANY)
        outs[f"total{i}"] = (shaped((depth, columns), F32), VM)
        for j, each_of in enumerate(Reduce.scratch(n_dp, depth, columns)):
            scratch[f"reduce{i}_{j}"] = each_of
    return ins, outs, scratch


def totals(out, count):
    return [getattr(out, f"total{i}") for i in range(count)]


def fetched(out, count):
    return [getattr(out, f"blocks{i}") for i in range(count)]


def attn_forward(level, which, states, tables, place, gains, pack, blocks, packs, plan, raw=None):
    rows, width = states.shape
    first = raw is not None
    if first:
        depth, columns = raw["raw_query0"].shape[0], 3 * raw["raw_query0"].shape[1]
        pack = shaped((depth, columns), BF)
    depth, columns = pack.shape
    n_dp = width // depth
    heads = place.shape[1] // PAD
    length = 4 * rows
    ins = dict(x=(states, SELF if first else VM), place=(place, SELF))
    outs = dict(
        middle=(shaped((rows, width), F32), SELF),
        a_out=(shaped((4, rows, width), BF), ANY),
        qkv_out=(shaped((length, 2 * heads * PAD), BF), ANY),
        o_out=(shaped((length, place.shape[0]), BF), ANY),
    )
    scratch = comm_scratch(rows, width) | dict(
        held=vmem(width, columns),
        padded=vmem(width, 2 * heads * PAD),
        qkv=vmem(length, 2 * heads * PAD),
        mixed=vmem(length, heads * PAD),
        compact=vmem(length, place.shape[0]),
        bias=vmem(rows, length, dtype=F32),
        w_sems=dma(n_dp),
        out_sems=dma(8),
    )
    for turn, reach in enumerate(reaches(rows)):
        outs[f"p_out{turn}"] = (shaped((heads, rows, reach), BF), ANY)
        scratch[f"prob{turn}"] = vmem(heads, rows, reach)
    if first:
        units = raw["raw_gate0"].shape[1]
        now = ("raw_query0", "raw_key0", "raw_value0", "raw_output0")
        for name, array in raw.items():
            late = name.startswith("raw_") and name not in now
            ins[name] = (array, ANY if late else SELF if array.shape == states.shape else VM)
            if late:
                scratch[name[4:]] = vmem(*array.shape, dtype=F32)
        outs |= dict(
            gains=(shaped((GAIN_ROWS, width), F32), VM),
            blocks=(blocks_of(pack, n_dp), ANY),
            own=(pack, SELF),
            own0=(shaped((depth, units), BF), SELF),
            own1=(shaped((depth, units), BF), SELF),
            blocks0=(shaped((n_dp, depth, units), BF), ANY),
            blocks1=(shaped((n_dp, depth, units), BF), ANY),
            down_pack0=(shaped((depth, units), BF), SELF),
            attn_pack1=(pack, SELF),
            gate_pack1=(shaped((depth, units), BF), SELF),
            up_pack1=(shaped((depth, units), BF), SELF),
            down_pack1=(shaped((depth, units), BF), SELF),
            cosine=(shaped((length, PAD), F32), SELF),
            sine=(shaped((length, PAD), F32), SELF),
            marks=(shaped((8, PAD), jnp.int32), VM),
            ahead_out=(shaped((4, rows, width), BF), ANY),
        )
        scratch |= dict(ahead=vmem(4, rows, width), a_send=dma(5), a_recv=dma(5))
        scratch["gain_raw"] = vmem(GAIN_ROWS, 256, dtype=F32)
        scratch["gain_own"] = vmem(GAIN_ROWS, 256)
        scratch["gain_blocks"] = vmem(n_dp, GAIN_ROWS, 256)
        scratch["raw_sems"] = dma(10)
        for name, tail in (("gain", ""), ("weight", ""), ("fetch", "0"), ("fetch", "1")):
            scratch[f"{name}_send{tail}"], scratch[f"{name}_recv{tail}"] = Fetch.scratch(n_dp)
        more = {}, {}, {}
    else:
        cosine, sine, marks = tables
        ins |= dict(
            gains=(gains, VM), cosine=(cosine, SELF), sine=(sine, SELF), marks=(marks, VM), own=(pack, ANY), blocks=(blocks, ANY)
        )
        more = fetch_refs(packs, n_dp)
    return launch(
        functools.partial(attn_forward_kernel, first, level, 2 if first else len(packs), plan),
        which, ins | more[0], outs | more[1], scratch | more[2],
    )


def mlp_refs(rows, width, wide, own):
    depth, units = own.shape
    n_dp = width // depth
    ins = dict(own=(own, ANY))
    ins |= {name: (array, ANY) for name, array in wide.items()}
    scratch = comm_scratch(rows, width) | dict(
        wide=vmem(width, 2 * units),
        held=vmem(width, units),
        gu=vmem(4 * rows, 2 * units),
        hid=vmem(4 * rows, units),
        gate_sems=dma(n_dp),
        up_sems=dma(n_dp),
        w_sems=dma(n_dp),
    )
    return n_dp, units, ins, scratch


def mlp_forward(level, which, middle, gains, wide, down_own, packs, plan):
    rows, width = middle.shape
    n_dp, units, ins, scratch = mlp_refs(rows, width, wide, down_own)
    ins |= dict(middle=(middle, VM), gains=(gains, VM))
    outs = dict(
        result=(shaped((rows, width), F32), SELF),
        m_out=(shaped((4, rows, width), BF), ANY),
        gu_out=(shaped((4 * rows, 2 * units), BF), ANY),
        hid_out=(shaped((4 * rows, units), BF), ANY),
        blocks=(blocks_of(down_own, n_dp), ANY),
    )
    scratch |= dict(out_sems=dma(3))
    scratch["down_send"], scratch["down_recv"] = Fetch.scratch(n_dp)
    more = fetch_refs(packs, n_dp)
    return launch(
        functools.partial(mlp_forward_kernel, level, len(packs), plan),
        which, ins | more[0], outs | more[1], scratch | more[2],
    )


def mlp_backward(level, which, grad, middle, gains, saved, wide, down, sums, plan, ahead=None):
    rows, width = middle.shape
    n_dp, units, ins, scratch = mlp_refs(rows, width, wide, down[0])
    depth = width // n_dp
    ins |= dict(
        blocks=(down[1], ANY),
        grad=(grad, VM if ahead is None else SELF), middle=(middle, SELF), gains=(gains, VM),
        m_in=(saved.m_out, ANY), gu_in=(saved.gu_out, ANY), hid_in=(saved.hid_out, ANY),
    )
    outs = dict(
        grad_out=(shaped((rows, width), F32), SELF),
        dgain=(shaped((8, width), F32), VM),
        wide_out=(shaped((n_dp, depth, 2 * units), BF), ANY),
        down_total=(shaped((depth, units), F32), VM),
    )
    scratch |= dict(
        m_full=vmem(4, rows, width),
        wide_grads=vmem(n_dp, depth, 2 * units),
        grads=vmem(n_dp, depth, units),
        in_sems=dma(4),
        out_sems=dma(3),
    )
    if ahead is not None:
        ins |= dict(ahead_in=(ahead, ANY))
    for j, each_of in enumerate(Reduce.scratch(n_dp, depth, units)):
        scratch[f"down{j}"] = each_of
    more = reduce_refs(sums)
    return launch(
        functools.partial(mlp_backward_kernel, level, len(sums), plan, ahead is not None),
        which, ins | more[0], outs | more[1], scratch | more[2],
    )


def attn_backward(level, which, grad, states, gains, tables, place, saved, weights, sums, plan, dgains=()):
    cosine, sine, _ = tables
    pack, blocks = weights
    rows, width = states.shape
    depth, columns = pack.shape
    n_dp = width // depth
    heads = place.shape[1] // PAD
    length = 4 * rows
    ins = dict(
        grad=(grad, VM), x=(states, SELF), gains=(gains, VM), cosine=(cosine, SELF), sine=(sine, SELF), place=(place, SELF),
        own=(pack, ANY), blocks=(blocks, ANY),
        a_in=(saved.a_out, ANY), qkv_in=(saved.qkv_out, ANY), o_in=(saved.o_out, ANY),
    )
    outs = dict(
        grad_out=(shaped((rows, width), F32), SELF),
        dgain=(shaped((8, width), F32), VM),
    )
    scratch = comm_scratch(rows, width) | dict(
        held=vmem(width, columns),
        a_full=vmem(4, rows, width),
        qkv=vmem(length, 2 * heads * PAD),
        compact=vmem(length, place.shape[0]),
        grad_mixed=vmem(length, heads * PAD),
        grad_q=vmem(length, heads * PAD),
        grad_kv=vmem(length, heads * PAD),
        grad_k=vmem(length, heads // 2 * PAD, dtype=F32),
        grad_v=vmem(length, heads // 2 * PAD, dtype=F32),
        grad_low=vmem(length, 2 * place.shape[0]),
        grads=vmem(n_dp, depth, columns),
        w_sems=dma(n_dp),
        in_sems=dma(7),
        out_sems=dma(1),
    )
    for turn, reach in enumerate(reaches(rows)):
        ins[f"p_in{turn}"] = (getattr(saved, f"p_out{turn}"), ANY)
        scratch[f"prob{turn}"] = vmem(heads, rows, reach)
    if dgains:
        ins |= {f"dgain{1 + i}": (dgain, VM) for i, dgain in enumerate(dgains)}
        outs |= dict(
            gain_total=(shaped((GAIN_ROWS, 256), F32), VM),
            attn_total=(shaped((depth, columns), F32), VM),
        )
        scratch |= dict(
            gain_blocks=vmem(n_dp, GAIN_ROWS, 256),
            rows=vmem(8, width, dtype=F32),
            others=vmem(2, 8, width, dtype=F32),
            row_send=dma(2),
            row_recv=dma(2),
        )
        for j, each_of in enumerate(Reduce.scratch(n_dp, GAIN_ROWS, 256)):
            scratch[f"gain{j}"] = each_of
        for j, each_of in enumerate(Reduce.scratch(n_dp, depth, columns)):
            scratch[f"attn{j}"] = each_of
    else:
        outs |= dict(grads_out=(shaped((n_dp, depth, columns), BF), ANY))
    more = reduce_refs(sums)
    return launch(
        functools.partial(attn_backward_kernel, level, len(sums), plan, bool(dgains)),
        which, ins | more[0], outs | more[1], scratch | more[2],
    )


def unpack_kernel(bounds, r):
    start_coming(r)
    copies = []

    def put(source, target):
        copies.append(pltpu.make_async_copy(source, target, r.put_sems.at[len(copies)]))
        copies[-1].start()

    low, middle, high, end = bounds
    for level in (1, 0):
        wide, down, attn, apart = (getattr(r, f"{n}{level}") for n in ("wide", "down", "attn", "apart"))
        query, key, value, output, gate, up, lower = (getattr(r, f"out{level}_{i}") for i in range(7))
        units = wide.shape[1] // 2
        come(r, f"wide{level}")
        put(wide.at[:, pl.ds(0, units)], gate)
        put(wide.at[:, pl.ds(units, units)], up)
        come(r, f"down{level}")
        put(down, lower)
        come(r, f"attn{level}")
        put(attn.at[:, pl.ds(0, low)], query)
        put(attn.at[:, pl.ds(high, end - high)], output)
        apart[0] = attn[:, low:middle]
        apart[1] = attn[:, middle:high]
        put(apart.at[0], key)
        put(apart.at[1], value)
    for name in ("x", "y"):
        come(r, name)
        put(getattr(r, name), getattr(r, name + "out"))
    for copy in copies:
        copy.wait()


def unpack(states, grad, bounds, attn, wide, down):
    ins = dict(x=(states, SELF), y=(grad, SELF))
    outs = dict(xout=(shaped(states.shape, F32), ANY), yout=(shaped(grad.shape, F32), ANY))
    scratch = dict(put_sems=dma(16))
    depth, units = down[0].shape
    low, middle, high, end = bounds
    for level in range(2):
        ins |= {
            f"wide{level}": (wide[level], SELF),
            f"down{level}": (down[level], SELF),
            f"attn{level}": (attn[level], SELF),
        }
        widths = (low, middle - low, high - middle, end - high, units, units, units)
        outs |= {f"out{level}_{i}": (shaped((depth, each_of), F32), ANY) for i, each_of in enumerate(widths)}
        scratch[f"apart{level}"] = vmem(2, depth, middle - low, dtype=F32)
    out = launch(functools.partial(unpack_kernel, bounds), None, ins, outs, scratch)
    return [out.xout, out.yout] + [[getattr(out, f"out{level}_{i}") for i in range(7)] for level in range(2)]


def constants(heads):
    place = np.zeros((heads * HEAD_DIM, heads * PAD), np.float32)
    for row in range(heads * HEAD_DIM):
        which, column = divmod(row, HEAD_DIM)
        place[row, which * PAD + column + (PAD // 2 - HALF if column >= HALF else 0)] = 1.0
    freqs = np.zeros((8, PAD), np.float32)
    for start in (0, PAD // 2):
        freqs[0, start : start + HALF] = np.exp(np.arange(HALF) * (-2.0 * math.log(rope_base) / HEAD_DIM))
    freqs[1, 0 : PAD // 2] = -1.0
    freqs[1, PAD // 2 :] = 1.0
    return jnp.asarray(place, BF), jnp.asarray(freqs)


def body(states_in, documents, *rest):
    cotangent = rest[-1]
    one, two = rest[0:9], rest[9:18]
    heads = one[1].shape[1] // HEAD_DIM
    place, freqs = constants(heads)
    raw = dict(documents=documents.reshape(-1, PAD), freqs=freqs, cotangent=cotangent)
    for level, w in enumerate((one, two)):
        raw[f"gain{2 * level}"] = w[0].reshape(1, -1)
        raw[f"gain{2 * level + 1}"] = w[5].reshape(1, -1)
        for name, array in zip(("query", "key", "value", "output", "", "gate", "up", "down"), w[1:]):
            if name:
                raw[f"raw_{name}{level}"] = array.T if name in ("output", "down") else array

    attn1 = attn_forward(
        0, 0, states_in, None, place, None, None, None, None, [2, 1, 0, 1, 0, 0, 1, 0, 0, 2, 1], raw
    )
    tables = (attn1.cosine, attn1.sine, attn1.marks)
    attn_pack = [attn1.own, attn1.attn_pack1]
    down_pack = [attn1.down_pack0, attn1.down_pack1]
    gains = attn1.gains
    wide1 = dict(
        gate_own=attn1.own0, gate_blocks=attn1.blocks0, up_own=attn1.own1, up_blocks=attn1.blocks1
    )
    mlp1 = mlp_forward(
        0, 1, attn1.middle, gains, wide1, down_pack[0], [attn_pack[1]], [0, 0, 1, 1, 2, 0]
    )
    down1 = (down_pack[0], mlp1.blocks)
    (attn2_blocks,) = fetched(mlp1, 1)
    attn2 = attn_forward(
        1, 2, mlp1.result, tables, place, gains, attn_pack[1], attn2_blocks, [attn1.gate_pack1, attn1.up_pack1],
        [2, 1, 1, 0, 0, 0, 1, 0, 0, 2, 1],
    )
    wide2 = dict(
        gate_own=attn1.gate_pack1, gate_blocks=attn2.blocks0, up_own=attn1.up_pack1, up_blocks=attn2.blocks1
    )
    mlp2 = mlp_forward(1, 3, attn2.middle, gains, wide2, down_pack[1], [], [])
    down2 = (down_pack[1], mlp2.blocks)

    back_mlp2 = mlp_backward(
        1, 4, cotangent, attn2.middle, gains, mlp2, wide2, down2, [], [0, 0, 1, 0, 1, 1, 0],
        attn1.ahead_out,
    )
    back_attn2 = attn_backward(
        1, 5, back_mlp2.grad_out, mlp1.result, gains, tables, place, attn2, (attn_pack[1], attn2_blocks),
        [back_mlp2.wide_out], [1, 0, 0, 1, 0, 1, 0, 0, 0, 1],
    )
    back_mlp1 = mlp_backward(
        0, 6, back_attn2.grad_out, attn1.middle, gains, mlp1, wide1, down1,
        [back_attn2.grads_out], [1, 1, 1, 1, 1, 1, 0, 1, 1],
    )
    back_attn1 = attn_backward(
        0, 7, back_mlp1.grad_out, states_in, gains, tables, place, attn1, (attn_pack[0], attn1.blocks),
        [back_mlp1.wide_out], [1, 0, 0, 1, 0, 0, 1, 0, 0, 1],
        (back_mlp1.dgain, back_attn2.dgain, back_mlp2.dgain),
    )
    (wide_total2,) = totals(back_attn2, 1)
    (attn_total2,) = totals(back_mlp1, 1)
    (wide_total1,) = totals(back_attn1, 1)
    attn_total1 = back_attn1.attn_total
    down_total1, down_total2 = back_mlp1.down_total, back_mlp2.down_total
    gain_total = back_attn1.gain_total
    depth = down_total1.shape[0]
    bounds = [0]
    for w in one[1:4]:
        bounds.append(bounds[-1] + w.shape[1])
    bounds = (*bounds[1:], attn_total1.shape[1])
    states, grad, *layers = unpack(
        mlp2.result, back_attn1.grad_out, bounds,
        (attn_total1, attn_total2), (wide_total1, wide_total2), (down_total1, down_total2),
    )
    outs = [states, grad]
    for level, (query, key, value, output, gate, up, down) in enumerate(layers):
        outs += [gain_total[2 * level, 0:depth], query, key, value, output.T]
        outs += [gain_total[2 * level + 1, 0:depth], gate, up, down.T]
    return tuple(outs)


def solution(mesh):
    layer = (
        P("dp"),
        P("dp", "tensor"),
        P("dp", "tensor"),
        P("dp", "tensor"),
        P("tensor", "dp"),
        P("dp"),
        P("dp", "tensor"),
        P("dp", "tensor"),
        P("tensor", "dp"),
    )
    rows = P(("dp", "tensor"), None)
    return jax.shard_map(
        body,
        mesh=mesh,
        in_specs=(rows, P("dp"), *layer, *layer, rows),
        out_specs=(rows, rows, *layer, *layer),
        check_vma=False,
    )
```

```python
import functools
import math
import types

import jax
import jax.numpy as jnp
import numpy as np
from jax import lax
from jax.experimental import pallas as pl
from jax.experimental.pallas import tpu as pltpu
from jax.sharding import PartitionSpec as P

HEAD_DIM = 96
HALF = HEAD_DIM // 2
BLOCK = 256
PAD = 128
GAIN_ROWS = 16
LIMIT = 60 * 1024 * 1024

epsilon = 1e-05
rope_base = 100000.0
masked_value = -1e30
scale = 1.0 / math.sqrt(HEAD_DIM)

BF = jnp.bfloat16
F32 = jnp.float32
MESH = pl.DeviceIdType.MESH
ANY = pl.BlockSpec(memory_space=pl.ANY)
VM = pl.BlockSpec(memory_space=pltpu.VMEM)
SELF = None


def nn(left, right):
    return lax.dot_general(left, right, (((1,), (0,)), ((), ())), preferred_element_type=F32)


def nt(left, right):
    return lax.dot_general(left, right, (((1,), (1,)), ((), ())), preferred_element_type=F32)


def tn(left, right):
    return lax.dot_general(left, right, (((0,), (0,)), ((), ())), preferred_element_type=F32)


def tile(index, size):
    if isinstance(index, int):
        return pl.ds(index * size, size)
    return pl.ds(pl.multiple_of(index * size, size), size)


def each(count, body):
    def step(index, carry):
        body(index)
        return carry

    lax.fori_loop(0, count, step, 0)


class Group:
    def __init__(self):
        self.me = lax.axis_index("tensor")
        self.core_bit = lax.rem(self.me, 2)
        self.chip = self.me // 2
        self.core = self.me + 1 - 2 * self.core_bit
        self.other = lax.rem(self.me + 2, 4)

    def greet(self, barrier):
        for near in (self.core, self.other):
            pl.semaphore_signal(barrier, inc=1, device_id={"tensor": near}, device_id_type=MESH)

    def peers(self):
        return 2

    def remote(self, source, target, send, recv, device):
        return pltpu.make_async_remote_copy(
            src_ref=source,
            dst_ref=target,
            send_sem=send,
            recv_sem=recv,
            device_id={"tensor": device},
            device_id_type=MESH,
        )


class Gather:
    def __init__(self, group, full, send, recv):
        self.group, self.full, self.send, self.recv = group, full, send, recv
        half = full.shape[1] // 2
        mine = full.at[group.me]
        self.to_core = group.remote(mine, mine, send.at[0], recv.at[0], group.core)
        self.to_other = []
        self.onward = []
        for part in range(2):
            piece = full.at[group.me, pl.ds(part * half, half)]
            self.to_other.append(
                group.remote(piece, piece, send.at[1 + part], recv.at[1 + part], group.other)
            )
            piece = full.at[group.other, pl.ds(part * half, half)]
            self.onward.append(
                group.remote(piece, piece, send.at[3 + part], recv.at[3 + part], group.core)
            )

    def start(self):
        for copy in self.to_other:
            copy.start()
        self.to_core.start()

    def wait_chip(self):
        self.to_core.wait_recv()

    def forward(self):
        for here, there in zip(self.to_other, self.onward):
            here.wait_recv()
            there.start()

    def wait_other(self):
        for copy in self.onward:
            copy.wait_recv()

    def finish(self):
        self.to_core.wait_send()
        for copy in self.to_other + self.onward:
            copy.wait_send()


class Scatter:
    def __init__(self, group, parts, near, away, landed, send, recv):
        self.group, self.parts, self.near = group, parts, near
        self.away, self.landed = away, landed
        self.to_core = [
            group.remote(
                parts.at[turn, 1 - group.core_bit], near.at[turn], send.at[turn], recv.at[turn], group.core
            )
            for turn in range(2)
        ]
        half = away.shape[0] // 2
        self.to_other = [
            group.remote(
                away.at[pl.ds(part * half, half)],
                landed.at[pl.ds(part * half, half)],
                send.at[2 + part],
                recv.at[2 + part],
                group.other,
            )
            for part in range(2)
        ]

    def rows_of(self, turn):
        return 1 - self.group.chip if turn == 0 else self.group.chip

    def send_core(self, turn):
        self.to_core[turn].start()

    def send_away(self):
        self.to_core[0].wait_recv()
        half = self.away.shape[0] // 2
        for part in range(2):

            def add(index):
                rows = pl.ds(pl.multiple_of(part * half + index * 32, 32), 32)
                total = self.parts[0, self.group.core_bit, rows, :].astype(F32) + self.near[
                    0, rows, :
                ].astype(F32)
                self.away[rows, :] = total.astype(BF)

            each(half // 32, add)
            self.to_other[part].start()

    def wait(self):
        self.to_core[1].wait_recv()
        for copy in self.to_other:
            copy.wait_recv()

    def total(self, rows):
        return (
            self.parts[1, self.group.core_bit, rows, :].astype(F32)
            + self.near[1, rows, :].astype(F32)
            + self.landed[rows, :].astype(F32)
        )

    def finish(self):
        for copy in self.to_core + self.to_other:
            copy.wait_send()


class Line:
    def __init__(self, n_dp):
        mine = lax.axis_index("dp")
        self.count = n_dp // 2
        self.z, self.x = mine // 2, lax.rem(mine, 2)
        self.mine = mine
        self.pair = self.z * 2 + 1 - self.x
        self.up = jnp.minimum(self.z + 1, self.count - 1) * 2 + self.x
        self.down = jnp.maximum(self.z - 1, 0) * 2 + self.x
        self.has_up = self.z + 1 < self.count
        self.has_down = self.z > 0

    def greet(self, barrier):
        def hello(device):
            pl.semaphore_signal(barrier, inc=1, device_id={"dp": device}, device_id_type=MESH)

        hello(self.pair)
        pl.when(self.has_up)(lambda: hello(self.up))
        pl.when(self.has_down)(lambda: hello(self.down))

    def peers(self):
        return 1 + jnp.minimum(self.count - 1 - self.z, 1) + jnp.minimum(self.z, 1)

    def remote(self, source, target, send, recv, device):
        return pltpu.make_async_remote_copy(
            src_ref=source, dst_ref=target, send_sem=send, recv_sem=recv,
            device_id={"dp": device}, device_id_type=MESH)


class Fetch:
    def __init__(self, line, own, blocks, send, recv):
        self.line, self.own, self.blocks, self.send, self.recv = line, own, blocks, send, recv
        rows = own.shape[0]
        self.edge = max(rows // 6 // 16, 1) * 16 if rows > 32 else 0
        self.rows = rows

    @staticmethod
    def scratch(n_dp):
        return [pltpu.SemaphoreType.DMA((n_dp, 5))] * 2

    def low(self, step):
        return jnp.maximum(self.line.z - step, 0) * 2

    def high(self, step):
        return jnp.minimum(self.line.z + step, self.line.count - 1) * 2

    def copy(self, slot, block, device, way, rows=None):
        source = self.own if slot == 0 and way < 3 else self.blocks.at[block]
        target = self.blocks.at[block]
        if rows is not None:
            source, target = source.at[rows], target.at[rows]
        return self.line.remote(
            source, target, self.send.at[slot, way], self.recv.at[slot, way], device
        )

    def upward(self, step):
        return self.copy(step, self.low(step) + self.line.x, self.line.up, 1)

    def downward(self, step):
        return self.copy(step, self.high(step) + self.line.x, self.line.down, 2)

    def edge_up(self, step):
        block = self.low(step) + 1 - self.line.x
        return self.copy(step, block, self.line.up, 3, pl.ds(0, self.edge))

    def edge_down(self, step):
        block = self.high(step) + 1 - self.line.x
        return self.copy(step, block, self.line.down, 4, pl.ds(0, self.edge))

    def sideways(self, step, low):
        line = self.line
        rows = pl.ds(self.edge, self.rows - self.edge) if step and self.edge else None
        if low:
            return self.copy(step, self.low(step) + line.x, line.pair, 0, rows)
        return self.copy(line.count + step, self.high(step) + line.x, line.pair, 0, rows)

    def upward_in(self, step):
        return self.copy(step - 1, self.low(step) + self.line.x, self.line.up, 1)

    def downward_in(self, step):
        return self.copy(step - 1, self.high(step) + self.line.x, self.line.down, 2)

    def edge_up_in(self, step):
        block = self.low(step) + 1 - self.line.x
        return self.copy(step - 1, block, self.line.up, 3, pl.ds(0, self.edge))

    def edge_down_in(self, step):
        block = self.high(step) + 1 - self.line.x
        return self.copy(step - 1, block, self.line.down, 4, pl.ds(0, self.edge))

    def start(self):
        line = self.line
        pl.when(line.has_up)(lambda: self.upward(0).start())
        pl.when(line.has_down)(lambda: self.downward(0).start())
        self.sideways(0, True).start()

    def step(self, step):
        line = self.line

        @pl.when(line.z >= step)
        def _():
            self.upward_in(step).wait_recv()
            pl.when(line.has_up)(lambda: self.upward(step).start())
            self.sideways(step, True).start()

        @pl.when(line.z + step < line.count)
        def _():
            self.downward_in(step).wait_recv()
            pl.when(line.has_down)(lambda: self.downward(step).start())
            self.sideways(step, False).start()

        self.edges(step - 1)

    def edges(self, step):
        line = self.line
        if step == 0:
            self.sideways(0, True).wait_recv()
        if not self.edge:
            return
        if step == 0:
            pl.when(line.has_up)(lambda: self.edge_up(0).start())
            pl.when(line.has_down)(lambda: self.edge_down(0).start())
            return

        @pl.when(line.z >= step)
        def _():
            self.edge_up_in(step).wait_recv()
            pl.when(line.has_up)(lambda: self.edge_up(step).start())

        @pl.when(line.z + step < line.count)
        def _():
            self.edge_down_in(step).wait_recv()
            pl.when(line.has_down)(lambda: self.edge_down(step).start())

    def finish(self):
        line = self.line
        self.edges(line.count - 1)
        for step in range(line.count):

            @pl.when(line.z >= step)
            def _():
                @pl.when(line.has_up)
                def _():
                    self.upward(step).wait_send()
                    if self.edge:
                        self.edge_up(step).wait_send()

                self.sideways(step, True).wait_send()
                if step:
                    self.sideways(step, True).wait_recv()

            @pl.when(line.z + step < line.count)
            def _():
                @pl.when(line.has_down)
                def _():
                    self.downward(step).wait_send()
                    if self.edge:
                        self.edge_down(step).wait_send()

                if step:
                    self.sideways(step, False).wait()

    def actions(self):
        steps = [functools.partial(self.step, step) for step in range(1, self.line.count)]
        return [self.start] + steps + [self.finish]


class Reduce:
    def __init__(self, line, blocks, out, pair_in, line_in, mine, x_send, x_recv, z_send, z_recv, local):
        self.line, self.blocks, self.out = line, blocks, out
        self.pair_in, self.line_in, self.mine = pair_in, line_in, mine
        self.x_send, self.x_recv, self.z_send, self.z_recv, self.local = x_send, x_recv, z_send, z_recv, local

    @staticmethod
    def scratch(n_dp, rows, columns):
        count = n_dp // 2
        dma = pltpu.SemaphoreType.DMA
        return [
            pltpu.VMEM((count, rows, columns), BF),
            pltpu.VMEM((count + 1, rows, columns), BF),
            pltpu.VMEM((2, rows, columns), BF),
            dma((count,)), dma((count,)), dma((count,)), dma((count + 1,)), dma((2,)),
        ]

    def sideways(self, target):
        line = self.line
        return line.remote(self.blocks.at[target * 2 + 1 - line.x], self.pair_in.at[target],
                           self.x_send.at[target], self.x_recv.at[target], line.pair)

    def along(self, target, up):
        line = self.line
        slot = target + 1 if up else target
        return line.remote(self.pair_in.at[target], self.line_in.at[slot],
                           self.z_send.at[target], self.z_recv.at[slot], line.up if up else line.down)

    def load(self, target, slot):
        return pltpu.make_async_copy(self.blocks.at[target * 2 + self.line.x], self.mine.at[slot], self.local.at[slot])

    def above(self, step):
        return self.line.z + step < self.line.count, jnp.minimum(self.line.z + step, self.line.count - 1)

    def below(self, step):
        return self.line.z - step >= 0, jnp.maximum(self.line.z - step, 0)

    def fetch(self, step):
        there, target = self.above(step)
        pl.when(there)(lambda: self.load(target, 0).start())
        if step:
            there2, target2 = self.below(step)
            pl.when(there2)(lambda: self.load(target2, 1).start())

    def start(self):
        line = self.line
        for step in range(line.count - 1, 0, -1):
            for there, target in (self.above(step), self.below(step)):
                pl.when(there)(lambda: self.sideways(target).start())
        self.sideways(line.z).start()
        self.fetch(line.count - 1)

    def add(self, target, slot, more):
        rows = self.out.shape[0]

        def some(index):
            part = pl.ds(pl.multiple_of(index * 16, 16), 16)
            total = self.pair_in[target, part, :].astype(F32) + self.mine[slot, part, :].astype(F32)
            for other in more:
                total += self.line_in[other, part, :].astype(F32)
            self.pair_in[target, part, :] = total.astype(BF)

        each(rows // 16, some)

    def pass_on(self, target, slot, up):
        line = self.line
        self.load(target, slot).wait()
        self.sideways(target).wait_recv()
        fed = line.has_down if up else line.has_up

        @pl.when(fed)
        def _():
            self.along(target, up).wait_recv()
            self.add(target, slot, [target + 1 if up else target])

        pl.when(jnp.logical_not(fed))(lambda: self.add(target, slot, []))
        self.along(target, up).start()

    def step(self, step):
        for slot, (there, target) in enumerate((self.above(step), self.below(step))):
            pl.when(there)(lambda: self.pass_on(target, slot, slot == 0))
        self.fetch(step - 1)

    def close(self):
        line = self.line
        z = line.z
        self.load(z, 0).wait()
        self.sideways(z).wait_recv()
        rows = self.out.shape[0]

        def final(more):
            def some(index):
                part = pl.ds(pl.multiple_of(index * 16, 16), 16)
                total = self.pair_in[z, part, :].astype(F32) + self.mine[0, part, :].astype(F32)
                for other in more:
                    total += self.line_in[other, part, :].astype(F32)
                self.out[part, :] = total

            each(rows // 16, some)

        pl.when(line.has_down)(lambda: self.along(z, True).wait_recv())
        pl.when(line.has_up)(lambda: self.along(z, False).wait_recv())
        pl.when(jnp.logical_not(line.has_down))(lambda: final([z]))
        pl.when(jnp.logical_not(line.has_up))(lambda: final([z + 1]))
        pl.when(line.has_down & line.has_up)(lambda: final([z, z + 1]))
        for step in range(line.count - 1, 0, -1):
            for up, (there, target) in ((True, self.above(step)), (False, self.below(step))):

                @pl.when(there)
                def _():
                    self.sideways(target).wait_send()
                    self.along(target, up).wait_send()

        self.sideways(z).wait_send()

    def actions(self):
        return [self.start] + [functools.partial(self.step, s) for s in range(self.line.count - 1, 0, -1)] + [self.close]


def spread(block, depth, lanes, width):
    row = lax.broadcasted_iota(jnp.int32, (lanes, width), 0)
    column = lax.broadcasted_iota(jnp.int32, (lanes, width), 1)
    hit = (column - row == block * depth) & (row < depth)
    return jnp.where(hit, 1.0, 0.0).astype(BF)


def turn_half(values):
    return pltpu.roll(values, PAD // 2, 1)


def meet(*circles):
    barrier = pltpu.get_barrier_semaphore()
    for circle in circles:
        circle.greet(barrier)
    pl.semaphore_wait(barrier, sum(circle.peers() for circle in circles))


class Weights:
    def __init__(self, line, own, blocks, held, sems, first=0):
        self.copies = []
        columns = pl.ds(first, own.shape[1])
        depth = own.shape[0]
        count = line.count
        for index in range(2 * count):
            shift, side = index // 2, index % 2
            block = lax.rem(line.z + shift, count) * 2 + lax.rem(line.x + side, 2)
            source = blocks.at[block] if index else own
            rows = pl.ds(pl.multiple_of(block * depth, 16), depth)
            self.copies.append(pltpu.make_async_copy(source, held.at[rows, columns], sems.at[index]))

    def start(self):
        for copy in self.copies:
            copy.start()

    def wait(self):
        for copy in self.copies:
            copy.wait()


def start_coming(r):
    for copy in r.coming.values():
        copy.start()


class Pump:
    def __init__(self, tasks, plan):
        self.steps = [step for together in zip(*[task.actions() for task in tasks]) for step in together]
        self.plan = list(plan)

    def __call__(self):
        count = self.plan.pop(0) if self.plan else 0
        self.do(count)

    def do(self, count):
        for step in self.steps[:count]:
            step()
        self.steps = self.steps[count:]

    def rest(self):
        self.do(len(self.steps))


def fetches_of(line, r, count):
    return [
        Fetch(
            line,
            getattr(r, f"own{i}"),
            getattr(r, f"blocks{i}"),
            getattr(r, f"fetch_send{i}"),
            getattr(r, f"fetch_recv{i}"),
        )
        for i in range(count)
    ]


def reduces_of(line, r, count):
    return [
        Reduce(
            line,
            getattr(r, f"sum{i}"),
            getattr(r, f"total{i}"),
            *[getattr(r, f"reduce{i}_{j}") for j in range(8)],
        )
        for i in range(count)
    ]


def comm_of(r):
    group = Group()
    gather = Gather(group, r.full, r.g_send, r.g_recv)
    scatter = Scatter(group, r.parts, r.near, r.away, r.landed, r.s_send, r.s_recv)
    return group, gather, scatter


def out_columns(scatter, turn, left_rows, right_tile, columns):
    product = nt(left_rows, right_tile)
    rows = product.shape[0] // 2
    scatter.parts[turn, 0, :, columns] = product[:rows].astype(BF)
    scatter.parts[turn, 1, :, columns] = product[rows:].astype(BF)


def norm_rows(source, gain, full, slot):
    def norm(index):
        part = tile(index, 32)
        values = source[part, :]
        factor = lax.rsqrt(jnp.mean(values * values, axis=-1, keepdims=True) + epsilon)
        full[slot, part, :] = (values * factor * gain).astype(BF)

    each(source.shape[0] // 32, norm)


def add_rows(scatter, source, target):
    def close(index):
        part = tile(index, 32)
        target[part, :] = source[part, :] + scatter.total(part)

    each(source.shape[0] // 32, close)


def pack_attn(query, key, value, output, target):
    width, each_kv = query.shape[1], key.shape[1]
    target[:, 0:width] = query[...].astype(BF)
    both = jnp.concatenate([key[...], value[...]], axis=1)
    target[:, width : width + 2 * each_kv] = both.astype(BF)
    target[:, width + 2 * each_kv :] = output[...].astype(BF)


def count_rows(documents, below):
    hits = jnp.where(documents < below, 1.0, 0.0)
    return jnp.sum(jnp.sum(hits, axis=1, keepdims=True), axis=0, keepdims=True).astype(jnp.int32)


def starts_of(marks, places):
    head, body_end = marks[0:1, 0:1], marks[1:2, 0:1]
    return jnp.where(places < head, 0, jnp.where(places < body_end, head, body_end))


def make_tables(r):
    marks = jnp.concatenate([count_rows(r.documents[...], 1), count_rows(r.documents[...], 2)], axis=0)
    r.marks[0:2, :] = jnp.broadcast_to(marks, (2, PAD))
    r.marks[2:, :] = jnp.zeros((6, PAD), jnp.int32)

    def some(index):
        where = tile(index, 128)
        places = lax.broadcasted_iota(jnp.int32, (128, PAD), 0) + index * 128
        offset = places - starts_of(r.marks, places)
        angles = offset.astype(F32) * r.freqs[0:1, :]
        r.cosine[where, :] = jnp.cos(angles)
        r.sine[where, :] = jnp.sin(angles) * r.freqs[1:2, :]

    each(r.cosine.shape[0] // 128, some)


def attn_forward_kernel(first, level, fetch_count, plan, r):
    rows, width = r.x.shape
    n_dp, depth = r.w_sems.shape[0], r.own.shape[0]
    line = Line(n_dp)
    group, gather, scatter = comm_of(r)
    tasks = fetches_of(line, r, fetch_count)
    weights = Weights(line, r.own, r.blocks, r.held, r.w_sems)
    circles = (group, line) if first or tasks else (group,)
    meet(*circles)
    if first:
        raw = {}
        for name in ("gate0", "up0", "down0", "query1", "key1", "value1", "output1", "gate1", "up1", "down1"):
            raw[name] = pltpu.make_async_copy(
                getattr(r, "raw_" + name), getattr(r, name), r.raw_sems.at[len(raw)]
            )
            raw[name].start()
        lanes = r.gain_own.shape[1]
        r.gain_raw[...] = jnp.zeros_like(r.gain_raw)
        for row in range(4):
            r.gain_raw[row : row + 1, 0:depth] = getattr(r, f"gain{row}")[...]
        r.gain_own[...] = r.gain_raw[...].astype(BF)
        pack_attn(r.raw_query0, r.raw_key0, r.raw_value0, r.raw_output0, r.own)
        start_coming(r)
        leave(r, "own")
        gain_fetch = Fetch(line, r.gain_own, r.gain_blocks, r.gain_send, r.gain_recv)
        weight_fetch = Fetch(line, r.own, r.blocks, r.weight_send, r.weight_recv)
        gain_fetch.start()
        weight_fetch.start()
        for step in gain_fetch.actions()[1:]:
            step()
        r.gains[...] = jnp.zeros_like(r.gains)

        def gather_gain(block):
            chosen = spread(block, depth, lanes, width)

            @pl.when(block == line.mine)
            def _():
                r.gains[...] += nn(r.gain_own[...], chosen)

            @pl.when(block != line.mine)
            def _():
                r.gains[...] += nn(r.gain_blocks[block], chosen)

        each(n_dp, gather_gain)
        come(r, "x")
        norm_rows(r.x, r.gains[2 * level : 2 * level + 1, :], r.full, group.me)
        gather.start()
        weight_steps = weight_fetch.actions()[1:-1]
        for step in weight_steps[:1]:
            step()
        ahead = Gather(group, r.ahead, r.a_send, r.a_recv)
        come(r, "cotangent")
        r.ahead[group.me] = r.cotangent[...].astype(BF)
        ahead.start()
        for name in ("gate0", "up0"):
            raw[name].wait()
        r.own0[...] = r.gate0[...].astype(BF)
        r.own1[...] = r.up0[...].astype(BF)
        leave(r, "own0", "own1")
        for step in weight_steps[1:]:
            step()
        pump = Pump(tasks, plan)
        pump()
        make_tables(r)
        for name in list(raw)[2:]:
            raw[name].wait()
        pack_attn(r.query1, r.key1, r.value1, r.output1, r.attn_pack1)
        r.down_pack0[...] = r.down0[...].astype(BF)
        r.down_pack1[...] = r.down1[...].astype(BF)
        r.gate_pack1[...] = r.gate1[...].astype(BF)
        r.up_pack1[...] = r.up1[...].astype(BF)
        leave(r, *list(r.leaving)[4:])
        come(r, "place")
        weight_fetch.finish()
        weights.start()
    else:
        weights.start()
        pump = Pump(tasks, plan)
        pump()
        start_coming(r)
        norm_rows(r.x, r.gains[2 * level : 2 * level + 1, :], r.full, group.me)
        gather.start()
        come(r, "place", "cosine", "sine")
    weights.wait()
    place = r.place[...]
    heads = place.shape[1] // PAD
    compact_width, head_width = place.shape
    padded, qkv, mixed, compact, held = r.padded, r.qkv, r.mixed, r.compact, r.held

    def pad(index):
        part = tile(index, 256)
        padded[part, 0:head_width] = nn(held[part, 0:compact_width], place).astype(BF)
        padded[part, head_width : 2 * head_width] = nn(
            held[part, compact_width : 2 * compact_width], place
        ).astype(BF)

    each(width // 256, pad)

    def project(chip):
        left = r.full[pl.ds(2 * chip, 2)].reshape(2 * rows, width)
        where = tile(chip, 2 * rows)
        cosine, sine = r.cosine[where, :], r.sine[where, :]

        def turned(index):
            columns = tile(index, 2 * PAD)
            product = nn(left, padded[:, columns])
            for half in range(2):
                u = product[:, half * PAD : (half + 1) * PAD]
                qkv[where, tile(2 * index + half, PAD)] = (u * cosine + turn_half(u) * sine).astype(BF)

        each(3 * heads // 4, turned)
        columns = pl.ds(3 * heads // 2 * PAD, heads // 2 * PAD)
        qkv[where, columns] = nn(left, padded[:, columns]).astype(BF)

    gather.wait_chip()
    project(group.chip)
    pump()
    gather.forward()
    pump()
    gather.wait_other()
    project(1 - group.chip)
    copies = [
        pltpu.make_async_copy(r.full, r.a_out, r.out_sems.at[0]),
        pltpu.make_async_copy(qkv, r.qkv_out, r.out_sems.at[1]),
    ]
    for copy in copies:
        copy.start()
    if first:
        ahead.wait_chip()
        ahead.forward()
    pump()
    kv_at = heads * PAD
    value_at = kv_at + heads // 2 * PAD
    for turn in range(4):
        prob = getattr(r, f"prob{turn}")
        reach = prob.shape[2]
        where = pl.ds(turn * rows, rows)
        places = lax.broadcasted_iota(jnp.int32, (rows, PAD), 0) + turn * rows
        begin = starts_of(r.marks, places)
        head, body_end = r.marks[0:1, 0:1], r.marks[1:2, 0:1]
        end = jnp.where(places < head, head, jnp.where(places < body_end, body_end, 4 * rows))
        end = jnp.minimum(begin + ((places - begin) // BLOCK + 1) * BLOCK, end)
        place_of = lax.broadcasted_iota(jnp.int32, (rows, reach), 1)
        inside = (place_of >= begin[:, 0:1]) & (place_of < end[:, 0:1])
        r.bias[:, 0:reach] = jnp.where(inside, 0.0, masked_value)

        def attend(head):
            query = qkv[where, tile(head, PAD)]
            key = qkv[0:reach, pl.ds(kv_at + head // 2 * PAD, PAD)]
            value = qkv[0:reach, pl.ds(value_at + head // 2 * PAD, PAD)]
            scores = nt(query, key) * scale + r.bias[:, 0:reach]
            exponent = jnp.exp(scores - jnp.max(scores, axis=-1, keepdims=True))
            summed = jnp.sum(exponent, axis=-1, keepdims=True)
            low = (exponent * (1.0 / summed)).astype(BF)
            prob[head] = low
            mixed[where, tile(head, PAD)] = nn(low, value).astype(BF)

        for head in range(heads):
            attend(head)
        copy = pltpu.make_async_copy(prob, getattr(r, f"p_out{turn}"), r.out_sems.at[2 + turn])
        copy.start()
        copies.append(copy)
        compact[where, :] = nt(mixed[where, :], place).astype(BF)
        pump()
    copies.append(pltpu.make_async_copy(compact, r.o_out, r.out_sems.at[6]))
    copies[-1].start()
    if first:
        ahead.wait_other()
        copies.append(pltpu.make_async_copy(r.ahead, r.ahead_out, r.out_sems.at[7]))
        copies[-1].start()
        ahead.finish()
    for turn in range(2):
        left = compact[tile(scatter.rows_of(turn), 2 * rows), :]

        def part_of(index):
            columns = tile(index, 256)
            out_columns(scatter, turn, left, held[columns, 2 * compact_width :], columns)

        each(width // 256, part_of)
        scatter.send_core(turn)
        if turn == 0:
            scatter.send_away()
        pump()
    scatter.wait()
    pump()
    add_rows(scatter, r.x, r.middle)
    leave(r, "middle")
    pump.rest()
    gather.finish()
    scatter.finish()
    for copy in copies:
        copy.wait()


def wide_of(line, r):
    return [
        Weights(line, r.gate_own, r.gate_blocks, r.wide, r.gate_sems),
        Weights(line, r.up_own, r.up_blocks, r.wide, r.up_sems, r.gate_own.shape[1]),
    ]


def mlp_forward_kernel(level, fetch_count, plan, r):
    rows, width = r.middle.shape
    units = r.hid.shape[1]
    line = Line(r.w_sems.shape[0])
    group, gather, scatter = comm_of(r)
    down = Fetch(line, r.own, r.blocks, r.down_send, r.down_recv)
    down_steps = down.actions()[1:-1]
    wide, held, gu, hid = r.wide, r.held, r.gu, r.hid
    wide_weights = wide_of(line, r)
    weights = Weights(line, r.own, r.blocks, held, r.w_sems)
    meet(group, line)
    down.start()
    for copy in wide_weights:
        copy.start()
    pump = Pump(fetches_of(line, r, fetch_count), plan)
    pump()
    norm_rows(r.middle, r.gains[2 * level + 1 : 2 * level + 2, :], r.full, group.me)
    gather.start()
    for copy in wide_weights:
        copy.wait()

    def expand(chip):
        left = r.full[pl.ds(2 * chip, 2)].reshape(2 * rows, width)
        where = tile(chip, 2 * rows)

        def unit(index):
            columns = tile(index, 256)
            further = pl.ds(pl.multiple_of(units + index * 256, 256), 256)
            gate = nn(left, wide[:, columns])
            up = nn(left, wide[:, further])
            hid[where, columns] = (gate / (1.0 + jnp.exp(-gate)) * up).astype(BF)
            gu[where, columns] = gate.astype(BF)
            gu[where, further] = up.astype(BF)

        each(units // 256, unit)

    gather.wait_chip()
    expand(group.chip)
    for step in down_steps[:1]:
        step()
    gather.forward()
    for step in down_steps[1:2]:
        step()
    pump()
    gather.wait_other()
    expand(1 - group.chip)
    for step in down_steps[2:]:
        step()
    pump()
    copies = [
        pltpu.make_async_copy(r.full, r.m_out, r.out_sems.at[0]),
        pltpu.make_async_copy(gu, r.gu_out, r.out_sems.at[1]),
        pltpu.make_async_copy(hid, r.hid_out, r.out_sems.at[2]),
    ]
    for copy in copies:
        copy.start()
    down.finish()
    weights.start()
    weights.wait()
    for turn in range(2):
        left = hid[tile(scatter.rows_of(turn), 2 * rows), :]

        def part_of(index):
            columns = tile(index, 256)
            out_columns(scatter, turn, left, held[columns, :], columns)

        each(width // 256, part_of)
        scatter.send_core(turn)
        if turn == 0:
            scatter.send_away()
        pump()
    scatter.wait()
    pump()
    add_rows(scatter, r.middle, r.result)
    leave(r, "result")
    pump.rest()
    gather.finish()
    scatter.finish()
    for copy in copies:
        copy.wait()


def weight_grads(source, right, target, columns):
    width = source.shape[-1]
    depth = target.shape[1]
    chunk = math.lcm(depth, PAD)

    def some(index):
        left = source[..., tile(index, chunk)].reshape(right.shape[0], chunk)
        product = tn(left, right[...]).astype(BF)
        for part in range(chunk // depth):
            rows = slice(part * depth, (part + 1) * depth)
            target[index * (chunk // depth) + part, :, columns] = product[rows]

    each(width // chunk, some)


def close_back(scatter, grad_in_ref, state_ref, gain, grad_out, dgain):
    rows = state_ref.shape[0]
    dgain[...] = jnp.zeros_like(dgain)

    def close(index):
        part = tile(index, 32)
        values = state_ref[part, :]
        factor = lax.rsqrt(jnp.mean(values * values, axis=-1, keepdims=True) + epsilon)
        normed = values * factor
        grad_in = scatter.total(part)
        dgain[...] += jnp.sum((grad_in * normed).reshape(4, 8, -1), axis=0)
        grad_norm = grad_in * gain
        inner = jnp.mean(grad_norm * normed, axis=-1, keepdims=True)
        grad_out[part, :] = grad_in_ref[part, :] + factor * (grad_norm - normed * inner)

    each(rows // 32, close)


def mlp_backward_kernel(level, reduce_count, plan, ready, r):
    rows, width = r.middle.shape
    units = r.hid.shape[1]
    n_dp = r.w_sems.shape[0]
    line = Line(n_dp)
    group, gather, scatter = comm_of(r)
    wide, held, gu, hid = r.wide, r.held, r.gu, r.hid
    weights = [
        Weights(line, r.own, r.blocks, held, r.w_sems),
        *wide_of(line, r),
    ]
    fetches = [
        pltpu.make_async_copy(r.hid_in, hid, r.in_sems.at[2]),
        pltpu.make_async_copy(r.gu_in, gu, r.in_sems.at[1]),
        pltpu.make_async_copy(r.m_in, r.m_full, r.in_sems.at[0]),
    ]
    down = Reduce(line, r.grads, r.down_total, *[getattr(r, f"down{j}") for j in range(8)])
    meet(group, line)
    pump = Pump(reduces_of(line, r, reduce_count), plan)
    pump.steps += down.actions()[1:]
    pump()
    for copy in weights[:1] + fetches + weights[1:]:
        copy.start()
    start_coming(r)
    if ready:
        whole = pltpu.make_async_copy(r.ahead_in, r.full, r.in_sems.at[3])
        whole.start()
    else:
        r.full[group.me] = r.grad[...].astype(BF)
        gather.start()
    for copy in weights[:1] + fetches[:2]:
        copy.wait()

    def inward(chip):
        left = r.full[pl.ds(2 * chip, 2)].reshape(2 * rows, width)
        where = tile(chip, 2 * rows)

        def unit(index):
            columns = tile(index, 256)
            further = pl.ds(pl.multiple_of(units + index * 256, 256), 256)
            grad = nn(left, held[:, columns])
            gate = gu[where, columns].astype(F32)
            up = gu[where, further].astype(F32)
            sig = 1.0 / (1.0 + jnp.exp(-gate))
            gu[where, columns] = (grad * up * sig * (1.0 + gate * (1.0 - sig))).astype(BF)
            gu[where, further] = (grad * gate * sig).astype(BF)

        each(units // 256, unit)

    if ready:
        whole.wait()
    else:
        gather.wait_chip()
        inward(group.chip)
        pump()
        gather.forward()
        pump()
        gather.wait_other()
    weight_grads(r.full, hid, r.grads, slice(0, units))
    down.start()
    if ready:
        inward(group.chip)
    inward(1 - group.chip)
    for copy in weights[1:] + fetches[2:]:
        copy.wait()
    pump()
    for turn in range(2):
        where = tile(scatter.rows_of(turn), 2 * rows)

        def part_of(index):
            columns = tile(index, 256)
            out_columns(scatter, turn, gu[where, :], wide[columns, :], columns)

        each(width // 256, part_of)
        scatter.send_core(turn)
        if turn == 0:
            scatter.send_away()
        pump()
    for part in range(2):
        columns = slice(part * units, (part + 1) * units)
        weight_grads(r.m_full, gu.at[:, columns], r.wide_grads, columns)
        pump()
    copies = [pltpu.make_async_copy(r.wide_grads, r.wide_out, r.out_sems.at[0])]
    copies[0].start()
    scatter.wait()
    pump()
    come(r, *r.coming)
    close_back(
        scatter, r.grad, r.middle, r.gains[2 * level + 1 : 2 * level + 2, :], r.grad_out, r.dgain
    )
    leave(r, "grad_out")
    pump.rest()
    if not ready:
        gather.finish()
    scatter.finish()
    for copy in copies:
        copy.wait()


def attn_backward_kernel(level, reduce_count, plan, final, r):
    rows, width = r.x.shape
    n_dp = r.w_sems.shape[0]
    depth = width // n_dp
    line = Line(n_dp)
    group, gather, scatter = comm_of(r)
    tasks = reduces_of(line, r, reduce_count)
    held, qkv, compact = r.held, r.qkv, r.compact
    probs = [getattr(r, f"prob{turn}") for turn in range(4)]
    weights = Weights(line, r.own, r.blocks, held, r.w_sems)
    fetches = [
        pltpu.make_async_copy(r.a_in, r.a_full, r.in_sems.at[0]),
        pltpu.make_async_copy(r.o_in, compact, r.in_sems.at[1]),
        pltpu.make_async_copy(r.qkv_in, qkv, r.in_sems.at[2]),
    ] + [
        pltpu.make_async_copy(getattr(r, f"p_in{turn}"), probs[turn], r.in_sems.at[3 + turn])
        for turn in range(4)
    ]
    meet(*((group, line) if tasks else (group,)))
    pump = Pump(tasks, plan)
    pump()
    weights.start()
    for copy in fetches:
        copy.start()
    start_coming(r)
    r.full[group.me] = r.grad[...].astype(BF)
    gather.start()
    pump()
    weights.wait()
    for copy in fetches:
        copy.wait()
    come(r, *r.coming)
    place = r.place[...]
    heads = place.shape[1] // PAD
    compact_width, head_width = place.shape

    def inward(chip):
        left = r.full[pl.ds(2 * chip, 2)].reshape(2 * rows, width)
        where = tile(chip, 2 * rows)
        grad = nn(left, held[:, 2 * compact_width :]).astype(BF)
        r.grad_mixed[where, :] = nn(grad, place).astype(BF)

    gather.wait_chip()
    inward(group.chip)
    pump()
    gather.forward()
    pump()
    gather.wait_other()
    inward(1 - group.chip)
    kv_at = heads * PAD
    value_at = kv_at + heads // 2 * PAD
    r.grad_k[...] = jnp.zeros_like(r.grad_k)
    r.grad_v[...] = jnp.zeros_like(r.grad_v)
    for turn, prob in enumerate(probs):
        reach = prob.shape[2]
        where = pl.ds(turn * rows, rows)
        cosine, sine = r.cosine[where, :], r.sine[where, :]

        def attend(head):
            mine = tile(head, PAD)
            shared = tile(head // 2, PAD)
            query = qkv[where, mine]
            key = qkv[0:reach, pl.ds(kv_at + head // 2 * PAD, PAD)]
            value = qkv[0:reach, pl.ds(value_at + head // 2 * PAD, PAD)]
            grad = r.grad_mixed[where, mine]
            low = prob[head]
            grad_prob = nt(grad, value)
            weight = low.astype(F32)
            inner = jnp.sum(weight * grad_prob, axis=-1, keepdims=True)
            grad_score = (weight * (grad_prob - inner)).astype(BF)
            u = nn(grad_score, key) * scale
            r.grad_q[where, mine] = (u * cosine - turn_half(u) * sine).astype(BF)
            r.grad_k[0:reach, shared] += tn(grad_score, query)
            r.grad_v[0:reach, shared] += tn(low, grad)

        for head in range(heads):
            attend(head)
        pump()
    for pair in range(heads // 2):
        columns = pl.ds(pair * PAD, PAD)
        u = r.grad_k[:, columns] * scale
        r.grad_kv[:, columns] = (u * r.cosine[...] - turn_half(u) * r.sine[...]).astype(BF)
        r.grad_kv[:, pl.ds((heads // 2 + pair) * PAD, PAD)] = r.grad_v[:, columns].astype(BF)
    grad_low = r.grad_low
    grad_low[:, 0:compact_width] = nt(r.grad_q[...], place).astype(BF)
    grad_low[:, compact_width : 2 * compact_width] = nt(r.grad_kv[...], place).astype(BF)
    for turn in range(2):
        where = tile(scatter.rows_of(turn), 2 * rows)

        def part_of(index):
            columns = tile(index, 256)
            out_columns(
                scatter, turn, grad_low[where, :], held[columns, 0 : 2 * compact_width], columns
            )

        each(width // 256, part_of)
        scatter.send_core(turn)
        if turn == 0:
            scatter.send_away()
        pump()
    grads = r.grads
    weight_grads(r.a_full, grad_low, grads, slice(0, 2 * compact_width))
    weight_grads(r.full, compact, grads, slice(2 * compact_width, 3 * compact_width))
    if not final:
        copy = pltpu.make_async_copy(grads, r.grads_out, r.out_sems.at[0])
        copy.start()
    pump()
    scatter.wait()
    pump()
    close_back(scatter, r.grad, r.x, r.gains[2 * level : 2 * level + 1, :], r.grad_out, r.dgain)
    leave(r, "grad_out")
    if final:
        attn = Reduce(line, grads, r.attn_total, *[getattr(r, f"attn{j}") for j in range(8)])
        gains = gain_sums(line, group, r)
        gains.start()
        attn.start()
        pump.rest()
        for step in gains.actions()[1:] + attn.actions()[1:]:
            step()
    pump.rest()
    gather.finish()
    scatter.finish()
    if not final:
        copy.wait()


def gain_sums(line, group, r):
    n_dp, _, lanes = r.gain_blocks.shape
    width = r.rows.shape[1]
    depth = width // n_dp
    for row, part in enumerate((r.dgain, r.dgain1, r.dgain2, r.dgain3)):
        r.rows[row : row + 1, :] = jnp.sum(part[...], axis=0, keepdims=True)
    r.rows[4:8, :] = jnp.zeros((4, width), F32)
    for turn, device in enumerate((group.core, group.other)):
        copy = group.remote(r.rows, r.others.at[turn], r.row_send.at[turn], r.row_recv.at[turn], device)
        copy.start()
        copy.wait()
        r.rows[...] += r.others[turn]
    both = jnp.concatenate([r.rows[...], jnp.zeros((GAIN_ROWS - 8, width), F32)], axis=0).astype(BF)

    def gain_rows(block):
        r.gain_blocks[block] = nt(both, spread(block, depth, lanes, width)).astype(BF)

    each(n_dp, gain_rows)
    return Reduce(line, r.gain_blocks, r.gain_total, *[getattr(r, f"gain{j}") for j in range(8)])


def shaped(shape, dtype):
    return jax.ShapeDtypeStruct(shape, dtype)


def dma(count):
    return pltpu.SemaphoreType.DMA((count,))


def vmem(*shape, dtype=BF):
    return pltpu.VMEM(shape, dtype)


def reaches(rows):
    return [min((turn + 1) * rows + PAD, 4 * rows) for turn in range(4)]


def come(r, *names):
    for name in names:
        r.coming[name].wait()


def leave(r, *names):
    for name in names:
        r.leaving[name].start()


def launch(kernel, which, ins, outs, scratch):
    late = [each_of for each_of, (_, spec) in ins.items() if spec is SELF]
    early = [each_of for each_of, (_, spec) in outs.items() if spec is SELF]
    names = [n + "_" * (n in late) for n in ins] + [n + "_" * (n in early) for n in outs]
    scratch = scratch | {n: vmem(*ins[n][0].shape, dtype=ins[n][0].dtype) for n in late}
    scratch |= {n: vmem(*outs[n][0].shape, dtype=outs[n][0].dtype) for n in early}
    scratch["own_sems"] = dma(len(late) + len(early) + 1)
    names += list(scratch)

    def entry(*refs):
        r = types.SimpleNamespace(**dict(zip(names, refs)))
        sems = iter(range(len(late) + len(early)))
        r.coming = {
            n: pltpu.make_async_copy(getattr(r, n + "_"), getattr(r, n), r.own_sems.at[next(sems)]) for n in late
        }
        r.leaving = {
            n: pltpu.make_async_copy(getattr(r, n), getattr(r, n + "_"), r.own_sems.at[next(sems)]) for n in early
        }
        kernel(r)
        for copy in r.leaving.values():
            copy.wait()

    results = pl.pallas_call(
        entry,
        out_shape=[shape for shape, _ in outs.values()],
        in_specs=[ANY if spec is SELF else spec for _, spec in ins.values()],
        out_specs=[ANY if spec is SELF else spec for _, spec in outs.values()],
        scratch_shapes=list(scratch.values()),
        compiler_params=pltpu.CompilerParams(
            collective_id=which, has_side_effects=which is not None, vmem_limit_bytes=LIMIT
        ),
        cost_estimate=pl.CostEstimate(
            flops=20_000_000_000, bytes_accessed=60_000_000, transcendentals=0
        ),
        name=kernel.func.__name__,
    )(*[array for array, _ in ins.values()])
    return types.SimpleNamespace(**dict(zip(outs, results)))


def comm_scratch(rows, width):
    return dict(
        full=vmem(4, rows, width),
        parts=vmem(2, 2, rows, width),
        near=vmem(2, rows, width),
        away=vmem(rows, width),
        landed=vmem(rows, width),
        g_send=dma(5),
        g_recv=dma(5),
        s_send=dma(4),
        s_recv=dma(4),
    )


def blocks_of(pack, n_dp):
    return shaped((n_dp,) + pack.shape, pack.dtype)


def fetch_refs(packs, n_dp):
    ins, outs, scratch = {}, {}, {}
    for i, pack in enumerate(packs):
        ins[f"own{i}"] = (pack, ANY)
        outs[f"blocks{i}"] = (blocks_of(pack, n_dp), ANY)
        scratch[f"fetch_send{i}"], scratch[f"fetch_recv{i}"] = Fetch.scratch(n_dp)
    return ins, outs, scratch


def reduce_refs(sums):
    ins, outs, scratch = {}, {}, {}
    for i, blocks in enumerate(sums):
        n_dp, depth, columns = blocks.shape
        ins[f"sum{i}"] = (blocks, ANY)
        outs[f"total{i}"] = (shaped((depth, columns), F32), VM)
        for j, each_of in enumerate(Reduce.scratch(n_dp, depth, columns)):
            scratch[f"reduce{i}_{j}"] = each_of
    return ins, outs, scratch


def totals(out, count):
    return [getattr(out, f"total{i}") for i in range(count)]


def fetched(out, count):
    return [getattr(out, f"blocks{i}") for i in range(count)]


def attn_forward(level, which, states, tables, place, gains, pack, blocks, packs, plan, raw=None):
    rows, width = states.shape
    first = raw is not None
    if first:
        depth, columns = raw["raw_query0"].shape[0], 3 * raw["raw_query0"].shape[1]
        pack = shaped((depth, columns), BF)
    depth, columns = pack.shape
    n_dp = width // depth
    heads = place.shape[1] // PAD
    length = 4 * rows
    ins = dict(x=(states, SELF if first else VM), place=(place, SELF))
    outs = dict(
        middle=(shaped((rows, width), F32), SELF),
        a_out=(shaped((4, rows, width), BF), ANY),
        qkv_out=(shaped((length, 2 * heads * PAD), BF), ANY),
        o_out=(shaped((length, place.shape[0]), BF), ANY),
    )
    scratch = comm_scratch(rows, width) | dict(
        held=vmem(width, columns),
        padded=vmem(width, 2 * heads * PAD),
        qkv=vmem(length, 2 * heads * PAD),
        mixed=vmem(length, heads * PAD),
        compact=vmem(length, place.shape[0]),
        bias=vmem(rows, length, dtype=F32),
        w_sems=dma(n_dp),
        out_sems=dma(8),
    )
    for turn, reach in enumerate(reaches(rows)):
        outs[f"p_out{turn}"] = (shaped((heads, rows, reach), BF), ANY)
        scratch[f"prob{turn}"] = vmem(heads, rows, reach)
    if first:
        units = raw["raw_gate0"].shape[1]
        now = ("raw_query0", "raw_key0", "raw_value0", "raw_output0")
        for name, array in raw.items():
            late = name.startswith("raw_") and name not in now
            ins[name] = (array, ANY if late else SELF if array.shape == states.shape else VM)
            if late:
                scratch[name[4:]] = vmem(*array.shape, dtype=F32)
        outs |= dict(
            gains=(shaped((GAIN_ROWS, width), F32), VM),
            blocks=(blocks_of(pack, n_dp), ANY),
            own=(pack, SELF),
            own0=(shaped((depth, units), BF), SELF),
            own1=(shaped((depth, units), BF), SELF),
            blocks0=(shaped((n_dp, depth, units), BF), ANY),
            blocks1=(shaped((n_dp, depth, units), BF), ANY),
            down_pack0=(shaped((depth, units), BF), SELF),
            attn_pack1=(pack, SELF),
            gate_pack1=(shaped((depth, units), BF), SELF),
            up_pack1=(shaped((depth, units), BF), SELF),
            down_pack1=(shaped((depth, units), BF), SELF),
            cosine=(shaped((length, PAD), F32), SELF),
            sine=(shaped((length, PAD), F32), SELF),
            marks=(shaped((8, PAD), jnp.int32), VM),
            ahead_out=(shaped((4, rows, width), BF), ANY),
        )
        scratch |= dict(ahead=vmem(4, rows, width), a_send=dma(5), a_recv=dma(5))
        scratch["gain_raw"] = vmem(GAIN_ROWS, 256, dtype=F32)
        scratch["gain_own"] = vmem(GAIN_ROWS, 256)
        scratch["gain_blocks"] = vmem(n_dp, GAIN_ROWS, 256)
        scratch["raw_sems"] = dma(10)
        for name, tail in (("gain", ""), ("weight", ""), ("fetch", "0"), ("fetch", "1")):
            scratch[f"{name}_send{tail}"], scratch[f"{name}_recv{tail}"] = Fetch.scratch(n_dp)
        more = {}, {}, {}
    else:
        cosine, sine, marks = tables
        ins |= dict(
            gains=(gains, VM), cosine=(cosine, SELF), sine=(sine, SELF), marks=(marks, VM), own=(pack, ANY), blocks=(blocks, ANY)
        )
        more = fetch_refs(packs, n_dp)
    return launch(
        functools.partial(attn_forward_kernel, first, level, 2 if first else len(packs), plan),
        which, ins | more[0], outs | more[1], scratch | more[2],
    )


def mlp_refs(rows, width, wide, own):
    depth, units = own.shape
    n_dp = width // depth
    ins = dict(own=(own, ANY))
    ins |= {name: (array, ANY) for name, array in wide.items()}
    scratch = comm_scratch(rows, width) | dict(
        wide=vmem(width, 2 * units),
        held=vmem(width, units),
        gu=vmem(4 * rows, 2 * units),
        hid=vmem(4 * rows, units),
        gate_sems=dma(n_dp),
        up_sems=dma(n_dp),
        w_sems=dma(n_dp),
    )
    return n_dp, units, ins, scratch


def mlp_forward(level, which, middle, gains, wide, down_own, packs, plan):
    rows, width = middle.shape
    n_dp, units, ins, scratch = mlp_refs(rows, width, wide, down_own)
    ins |= dict(middle=(middle, VM), gains=(gains, VM))
    outs = dict(
        result=(shaped((rows, width), F32), SELF),
        m_out=(shaped((4, rows, width), BF), ANY),
        gu_out=(shaped((4 * rows, 2 * units), BF), ANY),
        hid_out=(shaped((4 * rows, units), BF), ANY),
        blocks=(blocks_of(down_own, n_dp), ANY),
    )
    scratch |= dict(out_sems=dma(3))
    scratch["down_send"], scratch["down_recv"] = Fetch.scratch(n_dp)
    more = fetch_refs(packs, n_dp)
    return launch(
        functools.partial(mlp_forward_kernel, level, len(packs), plan),
        which, ins | more[0], outs | more[1], scratch | more[2],
    )


def mlp_backward(level, which, grad, middle, gains, saved, wide, down, sums, plan, ahead=None):
    rows, width = middle.shape
    n_dp, units, ins, scratch = mlp_refs(rows, width, wide, down[0])
    depth = width // n_dp
    ins |= dict(
        blocks=(down[1], ANY),
        grad=(grad, VM if ahead is None else SELF), middle=(middle, SELF), gains=(gains, VM),
        m_in=(saved.m_out, ANY), gu_in=(saved.gu_out, ANY), hid_in=(saved.hid_out, ANY),
    )
    outs = dict(
        grad_out=(shaped((rows, width), F32), SELF),
        dgain=(shaped((8, width), F32), VM),
        wide_out=(shaped((n_dp, depth, 2 * units), BF), ANY),
        down_total=(shaped((depth, units), F32), VM),
    )
    scratch |= dict(
        m_full=vmem(4, rows, width),
        wide_grads=vmem(n_dp, depth, 2 * units),
        grads=vmem(n_dp, depth, units),
        in_sems=dma(4),
        out_sems=dma(3),
    )
    if ahead is not None:
        ins |= dict(ahead_in=(ahead, ANY))
    for j, each_of in enumerate(Reduce.scratch(n_dp, depth, units)):
        scratch[f"down{j}"] = each_of
    more = reduce_refs(sums)
    return launch(
        functools.partial(mlp_backward_kernel, level, len(sums), plan, ahead is not None),
        which, ins | more[0], outs | more[1], scratch | more[2],
    )


def attn_backward(level, which, grad, states, gains, tables, place, saved, weights, sums, plan, dgains=()):
    cosine, sine, _ = tables
    pack, blocks = weights
    rows, width = states.shape
    depth, columns = pack.shape
    n_dp = width // depth
    heads = place.shape[1] // PAD
    length = 4 * rows
    ins = dict(
        grad=(grad, VM), x=(states, SELF), gains=(gains, VM), cosine=(cosine, SELF), sine=(sine, SELF), place=(place, SELF),
        own=(pack, ANY), blocks=(blocks, ANY),
        a_in=(saved.a_out, ANY), qkv_in=(saved.qkv_out, ANY), o_in=(saved.o_out, ANY),
    )
    outs = dict(
        grad_out=(shaped((rows, width), F32), SELF),
        dgain=(shaped((8, width), F32), VM),
    )
    scratch = comm_scratch(rows, width) | dict(
        held=vmem(width, columns),
        a_full=vmem(4, rows, width),
        qkv=vmem(length, 2 * heads * PAD),
        compact=vmem(length, place.shape[0]),
        grad_mixed=vmem(length, heads * PAD),
        grad_q=vmem(length, heads * PAD),
        grad_kv=vmem(length, heads * PAD),
        grad_k=vmem(length, heads // 2 * PAD, dtype=F32),
        grad_v=vmem(length, heads // 2 * PAD, dtype=F32),
        grad_low=vmem(length, 2 * place.shape[0]),
        grads=vmem(n_dp, depth, columns),
        w_sems=dma(n_dp),
        in_sems=dma(7),
        out_sems=dma(1),
    )
    for turn, reach in enumerate(reaches(rows)):
        ins[f"p_in{turn}"] = (getattr(saved, f"p_out{turn}"), ANY)
        scratch[f"prob{turn}"] = vmem(heads, rows, reach)
    if dgains:
        ins |= {f"dgain{1 + i}": (dgain, VM) for i, dgain in enumerate(dgains)}
        outs |= dict(
            gain_total=(shaped((GAIN_ROWS, 256), F32), VM),
            attn_total=(shaped((depth, columns), F32), VM),
        )
        scratch |= dict(
            gain_blocks=vmem(n_dp, GAIN_ROWS, 256),
            rows=vmem(8, width, dtype=F32),
            others=vmem(2, 8, width, dtype=F32),
            row_send=dma(2),
            row_recv=dma(2),
        )
        for j, each_of in enumerate(Reduce.scratch(n_dp, GAIN_ROWS, 256)):
            scratch[f"gain{j}"] = each_of
        for j, each_of in enumerate(Reduce.scratch(n_dp, depth, columns)):
            scratch[f"attn{j}"] = each_of
    else:
        outs |= dict(grads_out=(shaped((n_dp, depth, columns), BF), ANY))
    more = reduce_refs(sums)
    return launch(
        functools.partial(attn_backward_kernel, level, len(sums), plan, bool(dgains)),
        which, ins | more[0], outs | more[1], scratch | more[2],
    )


def unpack_kernel(bounds, r):
    start_coming(r)
    copies = []

    def put(source, target):
        copies.append(pltpu.make_async_copy(source, target, r.put_sems.at[len(copies)]))
        copies[-1].start()

    low, middle, high, end = bounds
    for level in (1, 0):
        wide, down, attn, apart = (getattr(r, f"{n}{level}") for n in ("wide", "down", "attn", "apart"))
        query, key, value, output, gate, up, lower = (getattr(r, f"out{level}_{i}") for i in range(7))
        units = wide.shape[1] // 2
        come(r, f"wide{level}")
        put(wide.at[:, pl.ds(0, units)], gate)
        put(wide.at[:, pl.ds(units, units)], up)
        come(r, f"down{level}")
        put(down, lower)
        come(r, f"attn{level}")
        put(attn.at[:, pl.ds(0, low)], query)
        put(attn.at[:, pl.ds(high, end - high)], output)
        apart[0] = attn[:, low:middle]
        apart[1] = attn[:, middle:high]
        put(apart.at[0], key)
        put(apart.at[1], value)
    for name in ("x", "y"):
        come(r, name)
        put(getattr(r, name), getattr(r, name + "out"))
    for copy in copies:
        copy.wait()


def unpack(states, grad, bounds, attn, wide, down):
    ins = dict(x=(states, SELF), y=(grad, SELF))
    outs = dict(xout=(shaped(states.shape, F32), ANY), yout=(shaped(grad.shape, F32), ANY))
    scratch = dict(put_sems=dma(16))
    depth, units = down[0].shape
    low, middle, high, end = bounds
    for level in range(2):
        ins |= {
            f"wide{level}": (wide[level], SELF),
            f"down{level}": (down[level], SELF),
            f"attn{level}": (attn[level], SELF),
        }
        widths = (low, middle - low, high - middle, end - high, units, units, units)
        outs |= {f"out{level}_{i}": (shaped((depth, each_of), F32), ANY) for i, each_of in enumerate(widths)}
        scratch[f"apart{level}"] = vmem(2, depth, middle - low, dtype=F32)
    out = launch(functools.partial(unpack_kernel, bounds), None, ins, outs, scratch)
    return [out.xout, out.yout] + [[getattr(out, f"out{level}_{i}") for i in range(7)] for level in range(2)]


def constants(heads):
    place = np.zeros((heads * HEAD_DIM, heads * PAD), np.float32)
    for row in range(heads * HEAD_DIM):
        which, column = divmod(row, HEAD_DIM)
        place[row, which * PAD + column + (PAD // 2 - HALF if column >= HALF else 0)] = 1.0
    freqs = np.zeros((8, PAD), np.float32)
    for start in (0, PAD // 2):
        freqs[0, start : start + HALF] = np.exp(np.arange(HALF) * (-2.0 * math.log(rope_base) / HEAD_DIM))
    freqs[1, 0 : PAD // 2] = -1.0
    freqs[1, PAD // 2 :] = 1.0
    return jnp.asarray(place, BF), jnp.asarray(freqs)


def body(states_in, documents, *rest):
    cotangent = rest[-1]
    one, two = rest[0:9], rest[9:18]
    heads = one[1].shape[1] // HEAD_DIM
    place, freqs = constants(heads)
    raw = dict(documents=documents.reshape(-1, PAD), freqs=freqs, cotangent=cotangent)
    for level, w in enumerate((one, two)):
        raw[f"gain{2 * level}"] = w[0].reshape(1, -1)
        raw[f"gain{2 * level + 1}"] = w[5].reshape(1, -1)
        for name, array in zip(("query", "key", "value", "output", "", "gate", "up", "down"), w[1:]):
            if name:
                raw[f"raw_{name}{level}"] = array.T if name in ("output", "down") else array

    attn1 = attn_forward(
        0, 0, states_in, None, place, None, None, None, None, [2, 1, 0, 1, 0, 0, 1, 0, 0, 2, 1], raw
    )
    tables = (attn1.cosine, attn1.sine, attn1.marks)
    attn_pack = [attn1.own, attn1.attn_pack1]
    down_pack = [attn1.down_pack0, attn1.down_pack1]
    gains = attn1.gains
    wide1 = dict(
        gate_own=attn1.own0, gate_blocks=attn1.blocks0, up_own=attn1.own1, up_blocks=attn1.blocks1
    )
    mlp1 = mlp_forward(
        0, 1, attn1.middle, gains, wide1, down_pack[0], [attn_pack[1]], [0, 0, 1, 1, 2, 0]
    )
    down1 = (down_pack[0], mlp1.blocks)
    (attn2_blocks,) = fetched(mlp1, 1)
    attn2 = attn_forward(
        1, 2, mlp1.result, tables, place, gains, attn_pack[1], attn2_blocks, [attn1.gate_pack1, attn1.up_pack1],
        [2, 1, 1, 0, 0, 0, 1, 0, 0, 2, 1],
    )
    wide2 = dict(
        gate_own=attn1.gate_pack1, gate_blocks=attn2.blocks0, up_own=attn1.up_pack1, up_blocks=attn2.blocks1
    )
    mlp2 = mlp_forward(1, 3, attn2.middle, gains, wide2, down_pack[1], [], [])
    down2 = (down_pack[1], mlp2.blocks)

    back_mlp2 = mlp_backward(
        1, 4, cotangent, attn2.middle, gains, mlp2, wide2, down2, [], [0, 0, 1, 0, 1, 1, 0],
        attn1.ahead_out,
    )
    back_attn2 = attn_backward(
        1, 5, back_mlp2.grad_out, mlp1.result, gains, tables, place, attn2, (attn_pack[1], attn2_blocks),
        [back_mlp2.wide_out], [1, 0, 0, 1, 0, 0, 1, 0, 0, 1],
    )
    back_mlp1 = mlp_backward(
        0, 6, back_attn2.grad_out, attn1.middle, gains, mlp1, wide1, down1,
        [back_attn2.grads_out], [1, 1, 1, 1, 1, 1, 0, 1, 1],
    )
    back_attn1 = attn_backward(
        0, 7, back_mlp1.grad_out, states_in, gains, tables, place, attn1, (attn_pack[0], attn1.blocks),
        [back_mlp1.wide_out], [1, 0, 0, 1, 0, 0, 1, 0, 0, 1],
        (back_mlp1.dgain, back_attn2.dgain, back_mlp2.dgain),
    )
    (wide_total2,) = totals(back_attn2, 1)
    (attn_total2,) = totals(back_mlp1, 1)
    (wide_total1,) = totals(back_attn1, 1)
    attn_total1 = back_attn1.attn_total
    down_total1, down_total2 = back_mlp1.down_total, back_mlp2.down_total
    gain_total = back_attn1.gain_total
    depth = down_total1.shape[0]
    bounds = [0]
    for w in one[1:4]:
        bounds.append(bounds[-1] + w.shape[1])
    bounds = (*bounds[1:], attn_total1.shape[1])
    states, grad, *layers = unpack(
        mlp2.result, back_attn1.grad_out, bounds,
        (attn_total1, attn_total2), (wide_total1, wide_total2), (down_total1, down_total2),
    )
    outs = [states, grad]
    for level, (query, key, value, output, gate, up, down) in enumerate(layers):
        outs += [gain_total[2 * level, 0:depth], query, key, value, output.T]
        outs += [gain_total[2 * level + 1, 0:depth], gate, up, down.T]
    return tuple(outs)


def solution(mesh):
    layer = (
        P("dp"),
        P("dp", "tensor"),
        P("dp", "tensor"),
        P("dp", "tensor"),
        P("tensor", "dp"),
        P("dp"),
        P("dp", "tensor"),
        P("dp", "tensor"),
        P("tensor", "dp"),
    )
    rows = P(("dp", "tensor"), None)
    return jax.shard_map(
        body,
        mesh=mesh,
        in_specs=(rows, P("dp"), *layer, *layer, rows),
        out_specs=(rows, rows, *layer, *layer),
        check_vma=False,
    )
```
